32 devices in a mesh: section: 2 (over y), expert: 8 (over z, x), tensor: 2 (over core).
Axes of the slice: x: 2, y: 2, z: 4, core: 2. Of those that a mesh axis runs over, the one named last changes fastest.
Arguments:
- inputs: float32 [2, 4096, 768], P(None, ('expert', 'tensor')), may hold values from -6 to 6
- cotangent: float32 [2, 4096, 768], P(None, ('expert', 'tensor')), may hold values from -6 to 6
- prev_logits: float32 [2, 2, 4096, 12], P('section', None, ('expert', 'tensor')), may hold values from -3 to 3
- lengths: int32 [2, 8, 4], P(None, 'expert'), may hold values from 1 to 456, 512 in all within a row
- routes: int32 [2, 2, 4096, 2], P('section', None, ('expert', 'tensor')), may hold values from 0 to 11, all different within a row; in each aligned block of 256 rows (0 to 255, 256 to 511, ..., all dimensions but the last counted through in order) at most 98 rows name the same one
- slot_order: int32 [2, 2, 16, 256], P('section', None, ('expert', 'tensor')), may hold values from 0 to 255, each once within a row
- norm_gain1: float32 [2, 768], P('section'), may hold values from 0.5 to 1.5
- w_query: bfloat16 [2, 768, 768], P('section', None, 'tensor'), may hold values from -0.21875 to 0.21875
- w_key: bfloat16 [2, 768, 768], P('section', None, 'tensor'), may hold values from -0.21875 to 0.21875
- w_value: bfloat16 [2, 768, 768], P('section', None, 'tensor'), may hold values from -0.21875 to 0.21875
- w_out: bfloat16 [2, 768, 768], P('section', 'tensor'), may hold values from -0.625 to 0.625
- norm_gain2: float32 [2, 768], P('section'), may hold values from 0.5 to 1.5
- router: float32 [2, 768, 12], P('section'), may hold values from -0.109375 to 0.109375
- router_residual: float32 [2, 12, 12], P('section'), may hold values from -1.75 to 1.75
- const_gate: float32 [2, 2, 768], P('section'), may hold values from -0.21875 to 0.21875
- const_value: float32 [2, 2, 768], P('section'), may hold values from -5 to 5
- expert_gate: bfloat16 [2, 8, 768, 2048], P('section', 'expert', None, 'tensor'), may hold values from -0.21875 to 0.21875
- expert_up: bfloat16 [2, 8, 768, 2048], P('section', 'expert', None, 'tensor'), may hold values from -0.21875 to 0.21875
- expert_down: bfloat16 [2, 8, 2048, 768], P('section', 'expert', 'tensor'), may hold values from -0.125 to 0.125
Outputs:
- layer_outputs: float32 [2, 2, 4096, 768], P('section', None, ('expert', 'tensor'))
- input_grads: float32 [2, 2, 4096, 768], P('section', None, ('expert', 'tensor'))
- logit_grads: float32 [2, 2, 4096, 12], P('section', None, ('expert', 'tensor'))
- norm_gain1_grad: float32 [2, 768], P('section')
- w_query_grad: float32 [2, 768, 768], P('section', None, 'tensor')
- w_key_grad: float32 [2, 768, 768], P('section', None, 'tensor')
- w_value_grad: float32 [2, 768, 768], P('section', None, 'tensor')
- w_out_grad: float32 [2, 768, 768], P('section', 'tensor')
- norm_gain2_grad: float32 [2, 768], P('section')
- router_grad: float32 [2, 768, 12], P('section')
- router_residual_grad: float32 [2, 12, 12], P('section')
- const_gate_grad: float32 [2, 2, 768], P('section')
- const_value_grad: float32 [2, 2, 768], P('section')
- expert_gate_grad: float32 [2, 8, 768, 2048], P('section', 'expert', None, 'tensor')
- expert_up_grad: float32 [2, 8, 768, 2048], P('section', 'expert', None, 'tensor')
- expert_down_grad: float32 [2, 8, 2048, 768], P('section', 'expert', 'tensor')
The draws below stay inside these ranges and needn't reach their ends.
Inputs may be any that keep to these rules, and one draw needn't show every extreme that they name: In each micro-batch and block, the first 3 entries are the lengths of the sequences packed in order into the block's 512 rows and the last is the number of padding rows at its end; the entries sum to 512 and the largest is exactly 456. `routes`: each row names two different choices: 0 to 7 are feed-forward experts, 8 the zero expert, 9 the copy expert, 10 and 11 the constant experts. Within the 256 rows of one device no choice is named by more than 98 rows, and every choice is named somewhere. `slot_order`: for each layer, micro-batch and device, a permutation of 0 to 256 - 1 over the device's rows.
All inputs are finite; a program needn't handle non-finite values.
Results may differ from the reference program's by a relative error of at most 0.028.
Values may be sent and summed in bfloat16 or wider, within the bound.
A program may use at most 256 MiB of HBM per device.

```python
import math
from functools import partial
import jax
import jax.numpy as jnp
import numpy as np
from jax import lax

D = 768
HEADS = 12
HEAD_DIM = 64
FF = 2048
TOK_DEV = 256
MB = 2
SEQS = 3
EXPERTS = 8
CHOICES = 12
CAP = 49
ROUTE_MOST = 98
SEQ_ROWS = 512
SEQ_MOST = 456
TOKENS = 4096
N_SECTION = 2
N_EXPERT = 8
N_TENSOR = 2


def shard_levels(rng, shape, cuts, low, largest):
    factor_of, own = 1.0, jax.random.fold_in(rng, 6)
    for dim, parts in cuts:
        steps = jnp.exp(jax.random.uniform(jax.random.fold_in(own, dim), (parts,), jnp.float32, low / len(cuts), largest / len(cuts)))
        factor_of = factor_of * jnp.repeat(steps, shape[dim] // parts).reshape([-1 if axis == dim else 1 for axis in range(len(shape))])
    return factor_of


def split_up(number_of, total, limit, lean):
    weights = [(1 << 20) // math.isqrt(standing ** lean) + 1 for standing in range(2, number_of + 1)]
    rest, counts = total - limit - (number_of - 1), [1] * (number_of - 1)
    while rest > 0:
        candidates = [i for i in range(number_of - 1) if counts[i] < limit]
        whole, left = sum([weights[i] for i in candidates]), rest
        for i in candidates:
            extra = min(limit - counts[i], max(1, left * weights[i] // whole), rest)
            counts[i] = counts[i] + extra
            rest = rest - extra
    return np.array([limit] + counts)


def ragged(stream_key, count, total, limit, skew):
    if count == 2:
        one = jax.random.randint(stream_key, (), max(1, total - limit), min(limit, total - 1) + 1)
        return jnp.stack([one, total - one])
    tallies = jnp.asarray(split_up(count, total, limit, skew), jnp.int32)
    couples = (count - 1) // 2
    giver, receiver = tallies[1:1 + 2 * couples:2], tallies[2:2 + 2 * couples:2]
    margin = jnp.minimum(giver - 1, limit - receiver)
    moved = jax.random.randint(jax.random.fold_in(stream_key, 1), (couples,), 0, 1 << 20) % (margin + 1)
    tallies = tallies.at[1:1 + 2 * couples:2].set(giver - moved).at[2:2 + 2 * couples:2].set(receiver + moved)
    return tallies[jax.random.permutation(jax.random.fold_in(stream_key, 2), count)]


def shared_out(own_key, own, number, rows, amount, top, reach, slope):
    order = jax.random.permutation(own_key, amount)
    crowded, ordinary = portions_of(amount, rows * top, reach, slope, True), portions_of(amount, rows * top, reach, slope, False)
    places = jnp.arange(amount)

    def named(sizes, rotation):
        used = int((sizes > 0).sum())
        fixed = max(1, used // 4)
        moved = fixed + (places - fixed + rotation * (used - fixed)) % max(1, amount - fixed)
        return jnp.zeros((amount,), jnp.int32).at[order[jnp.where(places < fixed, places, moved)]].set(jnp.asarray(sizes, jnp.int32))

    sizes = jnp.where(number % 4 == 0, named(crowded, number // 4), named(ordinary, number - number // 4 - 1))
    mixed = jax.random.permutation(jax.random.fold_in(own, 3), amount)
    donor, sink = mixed[0:amount // 2 * 2:2], mixed[1:amount // 2 * 2:2]
    slack = jnp.minimum(sizes[donor] - 1, reach - sizes[sink]) // 2
    slack = jnp.where((donor == order[0]) | (sink == order[0]) | (sizes[sink] == 0), 0, jnp.maximum(slack, 0))
    moved = jax.random.randint(jax.random.fold_in(own, 4), (amount // 2,), 0, 1 << 20) % (slack + 1)
    sizes = sizes.at[donor].add(-moved).at[sink].add(moved)
    labels = jnp.searchsorted(jnp.cumsum(sizes), jnp.arange(rows * top), side="right").astype(jnp.int32)
    table = labels.reshape(top, rows).T
    table = table[jax.random.permutation(jax.random.fold_in(own, 1), rows)]
    rotation = jax.random.randint(jax.random.fold_in(own, 2), (rows, 1), 0, top)
    return jnp.take_along_axis(table, (jnp.arange(top)[None, :] + rotation) % top, axis=1)


def portions_of(amount, total, bound, skew, full):
    loads = [(1 << 20) // math.isqrt(rank ** skew) + 1 for rank in range(1, amount + 1)]
    largest = bound if full else min(bound, max(-(-total // amount), total * loads[0] // sum(loads)))
    least = 1 if total - largest >= amount - 1 else 0
    given, surplus = [largest] + [least] * (amount - 1), total - largest - least * (amount - 1)
    while surplus > 0:
        candidates = [i for i in range(1, amount) if given[i] < largest] or [i for i in range(1, amount) if given[i] < bound]
        pool, budget = sum([loads[i] for i in candidates]), surplus
        for i in candidates:
            more = min(bound - given[i], max(1, budget * loads[i] // pool), surplus)
            given[i] = given[i] + more
            surplus = surplus - more
    return np.array(given)


def bell_draw(own_key, dims, scale, most, cuts=(), kind=jnp.bfloat16):
    loudness = shard_levels(own_key, dims, cuts, -0.22, 0.18) if cuts else 1.0
    result = jax.random.normal(own_key, dims, jnp.float32) * scale * loudness
    return jnp.minimum(jnp.maximum(result, -most), most).astype(kind)


def setup_inputs(seed: int = 0) -> dict:
    streams_of = jax.random.split(jax.random.key(seed), 20)
    inputs = bell_draw(streams_of[0], (MB, TOKENS, D), 1.0, 6.0, ((1, 16),), jnp.float32)
    cotangent = bell_draw(streams_of[1], (MB, TOKENS, D), 1.0, 6.0, ((1, 16),), jnp.float32)
    prev_logits = bell_draw(streams_of[2], (N_SECTION, MB, TOKENS, CHOICES), 0.5, 3.0, ((0, 2), (2, 16)), jnp.float32)
    lengths = jax.vmap(lambda own: ragged(own, SEQS + 1, SEQ_ROWS, SEQ_MOST, 2))(jax.random.split(streams_of[3], MB * N_EXPERT)).reshape((MB, N_EXPERT, SEQS + 1)).astype(jnp.int32)
    routes_keys = jax.random.split(jax.random.fold_in(streams_of[4], 1), N_SECTION * MB * TOKENS // TOK_DEV)
    routes_turns = jax.random.permutation(jax.random.fold_in(streams_of[4], 3), N_SECTION * MB * TOKENS // TOK_DEV)
    routes = jax.vmap(lambda own, number: shared_out(jax.random.fold_in(streams_of[4], 2), own, number, TOK_DEV, CHOICES, 2, ROUTE_MOST, 1))(routes_keys, routes_turns).reshape((N_SECTION, MB, TOKENS, 2))
    slot_order = jax.vmap(lambda own: jax.random.permutation(own, TOK_DEV))(jax.random.split(streams_of[5], N_SECTION * MB * (N_EXPERT * N_TENSOR))).reshape((N_SECTION, MB, N_EXPERT * N_TENSOR, TOK_DEV)).astype(jnp.int32)
    norm_gain1 = jnp.clip(1.0 + 0.1 * jax.random.normal(streams_of[6], (N_SECTION, D), jnp.float32), 0.5, 1.5)
    w_query = bell_draw(streams_of[7], (N_SECTION, D, D), D ** -0.5, 0.21875, ((0, 2), (2, 2)))
    w_key = bell_draw(streams_of[8], (N_SECTION, D, D), D ** -0.5, 0.21875, ((0, 2), (2, 2)))
    w_value = bell_draw(streams_of[9], (N_SECTION, D, D), D ** -0.5, 0.21875, ((0, 2), (2, 2)))
    w_out = bell_draw(streams_of[10], (N_SECTION, D, D), (D // 8) ** -0.5, 0.625, ((0, 2), (1, 2)))
    norm_gain2 = jnp.clip(1.0 + 0.1 * jax.random.normal(streams_of[11], (N_SECTION, D), jnp.float32), 0.5, 1.5)
    router = bell_draw(streams_of[12], (N_SECTION, D, CHOICES), (4 * D) ** -0.5, 0.109375, ((0, 2),), jnp.float32)
    router_residual = bell_draw(streams_of[13], (N_SECTION, CHOICES, CHOICES), CHOICES ** -0.5, 1.75, ((0, 2),), jnp.float32)
    const_gate = bell_draw(streams_of[14], (N_SECTION, 2, D), D ** -0.5, 0.21875, ((0, 2),), jnp.float32)
    const_value = bell_draw(streams_of[15], (N_SECTION, 2, D), 1.0, 5.0, ((0, 2),), jnp.float32)
    expert_gate = bell_draw(streams_of[16], (N_SECTION, EXPERTS, D, FF), D ** -0.5, 0.21875, ((0, 2), (1, 8), (3, 2)))
    expert_up = bell_draw(streams_of[17], (N_SECTION, EXPERTS, D, FF), D ** -0.5, 0.21875, ((0, 2), (1, 8), (3, 2)))
    expert_down = bell_draw(streams_of[18], (N_SECTION, EXPERTS, FF, D), FF ** -0.5, 0.125, ((0, 2), (1, 8), (2, 2)))
    return {"inputs": inputs, "cotangent": cotangent, "prev_logits": prev_logits, "lengths": lengths, "routes": routes, "slot_order": slot_order, "norm_gain1": norm_gain1, "w_query": w_query, "w_key": w_key, "w_value": w_value, "w_out": w_out, "norm_gain2": norm_gain2, "router": router, "router_residual": router_residual, "const_gate": const_gate, "const_value": const_value, "expert_gate": expert_gate, "expert_up": expert_up, "expert_down": expert_down}


@jax.custom_vjp
def low(v):
    return lax.optimization_barrier(v.astype(jnp.bfloat16)).astype(jnp.float32)

@jax.custom_vjp
def low_back(v):
    return v

def low_keep(v):
    return (low(v), None)

def low_pass(kept, grad):
    return (grad,)

def back_keep(v):
    return (v, None)

def back_low(kept, grad):
    return (low(grad),)
low.defvjp(low_keep, low_pass)
low_back.defvjp(back_keep, back_low)
epsilon = 1e-06
highest = lax.Precision.HIGHEST

def matmul(left, right):
    return jnp.dot(left, right, precision=highest)

def normed(values, gain):
    return values * lax.rsqrt(lax.optimization_barrier(jnp.mean(values * values, axis=-1, keepdims=True)) + epsilon) * gain

def layout(lengths_row, row_count):
    seq_ends = jnp.cumsum(lengths_row).astype(jnp.int32)
    row_index = jnp.arange(row_count, dtype=jnp.int32)
    passed = row_index[:, None] >= seq_ends[None, :SEQS]
    segment = lax.optimization_barrier(jnp.sum(passed.astype(jnp.int32), axis=1)).astype(jnp.int32)
    seq_start = lax.optimization_barrier(jnp.sum(jnp.where(passed, lengths_row[None, :SEQS], 0), axis=1)).astype(jnp.int32)
    same_seq = segment[:, None] == segment[None, :]
    causal = row_index[None, :] <= row_index[:, None]
    own_rows = (segment[:, None] < SEQS) | (row_index[None, :] == row_index[:, None])
    return ((row_index - seq_start).astype(jnp.int32), same_seq & causal & own_rows)

def rotary(values, position):
    half_width = values.shape[-1] // 2
    frequency = 10000.0 ** (-2.0 * jnp.arange(half_width, dtype=jnp.float32) / values.shape[-1])
    angles = position.astype(jnp.float32)[:, None] * frequency[None, :]
    cosine = jnp.cos(angles)[:, None, :]
    sine_part = jnp.sin(angles)[:, None, :]
    leading = values[..., :half_width]
    trailing = values[..., half_width:]
    return jnp.concatenate([leading * cosine - trailing * sine_part, trailing * cosine + leading * sine_part], axis=-1)

def attend(item, w_query, w_key, w_value, w_out):
    block_rows, position, allowed = item
    row_count = block_rows.shape[0]
    query_rot = low(rotary(low_back(matmul(block_rows, w_query)).reshape(row_count, HEADS, HEAD_DIM), position))
    key_rot = low(rotary(low_back(matmul(block_rows, w_key)).reshape(row_count, HEADS, HEAD_DIM), position))
    values = low(low_back(matmul(block_rows, w_value))).reshape(row_count, HEADS, HEAD_DIM)
    scores = jnp.einsum('qhd,khd->hqk', query_rot, key_rot, precision=highest) * HEAD_DIM ** (-0.5)
    scores = low_back(jnp.where(allowed[None], scores, -1e+30))
    shifted = jnp.exp(scores - lax.optimization_barrier(jnp.max(scores, axis=-1, keepdims=True)))
    probabilities = shifted / lax.optimization_barrier(jnp.sum(shifted, axis=-1, keepdims=True))
    mixed = low(low_back(jnp.einsum('hqk,khd->qhd', low(probabilities), values, precision=highest)))
    return low_back(matmul(mixed.reshape(row_count, D), w_out))

def expert_block(item):
    slot_rows, gate_matrix, up_matrix, down_matrix = item
    gate_value = low_back(matmul(slot_rows, gate_matrix))
    up_value = low_back(matmul(slot_rows, up_matrix))
    hidden = low(gate_value * jax.nn.sigmoid(gate_value) * up_value)
    return low(low_back(matmul(hidden, down_matrix)))

def slot_table(route_rows, order_rows):
    devices = N_EXPERT * N_TENSOR
    per_device = route_rows.reshape(devices, TOK_DEV, 2)

    def counted(item):
        device_routes, device_order = item
        before = (device_order[None, :] < device_order[:, None]).astype(jnp.float32)
        hit_count = lax.optimization_barrier(jnp.sum((device_routes[:, :, None] == jnp.arange(CHOICES, dtype=jnp.int32)[None, None, :]).astype(jnp.float32), axis=1))
        earlier = matmul(before, hit_count)
        return jnp.take_along_axis(earlier, device_routes, axis=1).astype(jnp.int32)
    slot_rank = lax.map(counted, (per_device, order_rows))
    device_rank = jnp.arange(devices, dtype=jnp.int32)[:, None, None]
    kept_mask = (per_device < EXPERTS) & (slot_rank < CAP)
    destination = jnp.where(kept_mask, per_device * (devices * CAP) + device_rank * CAP + slot_rank, EXPERTS * devices * CAP)
    return (destination.reshape(TOKENS, 2).astype(jnp.int32), kept_mask.reshape(TOKENS, 2).astype(jnp.float32))

def layer(block_input, section_params, prev_rows, route_rows, position, allowed, destination, kept_mask):
    gain_one, w_query, w_key, w_value, w_out, gain_two, router, router_residual, const_gate, const_value, expert_gate, expert_up, expert_down = section_params
    normed_one = low(normed(block_input, gain_one))
    attention_fn = jax.checkpoint(partial(attend, w_query=w_query, w_key=w_key, w_value=w_value, w_out=w_out))
    attended = lax.map(attention_fn, (normed_one.reshape(N_EXPERT, SEQ_ROWS, D), position, allowed))
    hidden_state = block_input + attended.reshape(TOKENS, D)
    normed_two = low(normed(hidden_state, gain_two))
    logits = matmul(normed_two, router) + matmul(prev_rows, router_residual)
    onehot = (route_rows[:, :, None] == jnp.arange(CHOICES, dtype=jnp.int32)[None, None, :]).astype(jnp.float32)
    picked = lax.optimization_barrier(jnp.sum(logits[:, None, :] * onehot, axis=2))
    shifted = jnp.exp(picked - lax.optimization_barrier(jnp.max(picked, axis=1, keepdims=True)))
    gates = shifted / lax.optimization_barrier(jnp.sum(shifted, axis=1, keepdims=True))
    flat_dest = destination.reshape(-1)
    spread = normed_two[:, None, :] * kept_mask[:, :, None]
    slots_total = EXPERTS * N_EXPERT * N_TENSOR * CAP
    buffer = jnp.zeros((slots_total + 1, D), jnp.float32).at[flat_dest].add(spread.reshape(-1, D))
    sent = low_back(buffer[:slots_total]).reshape(EXPERTS, N_EXPERT * N_TENSOR * CAP, D)
    returned = lax.map(jax.checkpoint(expert_block), (sent, expert_gate, expert_up, expert_down))
    returned = jnp.concatenate([returned.reshape(slots_total, D), jnp.zeros((1, D), jnp.float32)], axis=0)
    expert_out = returned[flat_dest].reshape(TOKENS, 2, D) * kept_mask[:, :, None]
    mix_rate = jax.nn.sigmoid(matmul(normed_two, const_gate.T))
    mix_out = mix_rate[:, :, None] * normed_two[:, None, :] + (1.0 - mix_rate)[:, :, None] * const_value[None, :, :]
    branch = expert_out + onehot[:, :, EXPERTS + 1, None] * normed_two[:, None, :]
    branch = branch + onehot[:, :, EXPERTS + 2, None] * mix_out[:, None, 0, :] + onehot[:, :, EXPERTS + 3, None] * mix_out[:, None, 1, :]
    return hidden_state + lax.optimization_barrier(jnp.sum(gates[:, :, None] * branch, axis=1))

def reference(inputs, cotangent, prev_logits, lengths, routes, slot_order, norm_gain1, w_query, w_key, w_value, w_out, norm_gain2, router, router_residual, const_gate, const_value, expert_gate, expert_up, expert_down):
    stacked = (norm_gain1, w_query, w_key, w_value, w_out, norm_gain2, router, router_residual, const_gate, const_value, expert_gate, expert_up, expert_down)
    params = [tuple((array[section_rank].astype(jnp.float32) for array in stacked)) for section_rank in range(N_SECTION)]
    totals = [tuple((jnp.zeros_like(array) for array in section_params)) for section_params in params]
    outputs = [[] for section_rank in range(N_SECTION)]
    in_grads = [[None] * MB for section_rank in range(N_SECTION)]
    prev_grads = [[None] * MB for section_rank in range(N_SECTION)]
    for micro_batch in range(MB):
        position, allowed = lax.map(partial(layout, row_count=SEQ_ROWS), lengths[micro_batch])
        carried = inputs[micro_batch].astype(jnp.float32)
        pullers = []
        for section_rank in range(N_SECTION):
            route_rows = routes[section_rank, micro_batch]
            destination, kept_mask = slot_table(route_rows, slot_order[section_rank, micro_batch])
            forward_fn = partial(layer, route_rows=route_rows, position=position, allowed=allowed, destination=destination, kept_mask=kept_mask)
            carried, puller = jax.vjp(forward_fn, carried, params[section_rank], prev_logits[section_rank, micro_batch].astype(jnp.float32))
            outputs[section_rank].append(carried)
            pullers.append(puller)
        flowing = cotangent[micro_batch].astype(jnp.float32)
        for section_rank in reversed(range(N_SECTION)):
            flowing, section_grads, prev_grad = pullers[section_rank](flowing)
            totals[section_rank] = tuple((total_part + grad_part for total_part, grad_part in zip(totals[section_rank], section_grads)))
            in_grads[section_rank][micro_batch] = flowing
            prev_grads[section_rank][micro_batch] = prev_grad
    layer_outputs = jnp.stack([jnp.stack(section_list) for section_list in outputs])
    input_grads = jnp.stack([jnp.stack(section_list) for section_list in in_grads])
    logit_grads = jnp.stack([jnp.stack(section_list) for section_list in prev_grads])
    merged = [jnp.stack([totals[section_rank][which] for section_rank in range(N_SECTION)]) for which in range(len(stacked))]
    return (layer_outputs, input_grads, logit_grads, merged[0], merged[1], merged[2], merged[3], merged[4], merged[5], merged[6], merged[7], merged[8], merged[9], merged[10], merged[11], merged[12])
```

```python
import functools
import types

import jax
import jax.numpy as jnp
import numpy as np
from jax import lax
from jax.experimental import pallas as pl
from jax.experimental.pallas import tpu as pltpu
from jax.sharding import PartitionSpec as P

HEAD_DIM = 64
LANES = 128
EPSILON = 1e-06
MESH = pl.DeviceIdType.MESH
f32, bf16, i32 = jnp.float32, jnp.bfloat16, jnp.int32

P_NORM, P_OUT, P_ROWS, P_PART, P_GROWS, P_GPART, P_DA, P_DX = range(8)


def dot(left, right):
    return jnp.dot(left, right, preferred_element_type=f32)


def dot_nt(left, right):
    return lax.dot_general(left, right, (((1,), (1,)), ((), ())), preferred_element_type=f32)


def dot_tn(left, right):
    return lax.dot_general(left, right, (((0,), (0,)), ((), ())), preferred_element_type=f32)


def wide(values):
    return values.astype(f32)


def halves(values):
    upper = values.astype(bf16)
    return upper, (values - wide(upper)).astype(bf16)


def dot3(how, left, right):
    left_hi, left_lo = halves(left)
    right_hi, right_lo = halves(right)
    return how(left_hi, right_hi) + (how(left_hi, right_lo) + how(left_lo, right_hi))


def inverse_rms(values):
    return lax.rsqrt(jnp.mean(values * values, axis=-1, keepdims=True) + EPSILON)


def iota(shape, dim):
    return lax.broadcasted_iota(i32, shape, dim)


def flag(condition):
    return wide(condition.astype(i32))


def half_lanes(width):
    return (iota((1, width), 1) % HEAD_DIM) < HEAD_DIM // 2


def turned(values, cosine, sine):
    quarter = HEAD_DIM // 2
    other = jnp.where(
        half_lanes(LANES),
        -pltpu.roll(values, LANES - quarter, 1),
        pltpu.roll(values, quarter, 1),
    )
    return values * cosine + other * sine


def turned_back(values, cosine, sine):
    quarter = HEAD_DIM // 2
    other = jnp.where(
        half_lanes(LANES),
        pltpu.roll(values, LANES - quarter, 1),
        -pltpu.roll(values, quarter, 1),
    )
    return values * cosine + other * sine


def chain_kernel(cfg, names, *refs):
    r = types.SimpleNamespace(**dict(zip(names, refs, strict=True)))
    owned, rows, experts, cap, cap_pad = cfg.owned, cfg.rows, cfg.experts, cfg.cap, cfg.cap_pad
    choices, slots, tiles, tile_rows = cfg.choices, cfg.slots, cfg.tiles, cfg.tile_rows
    per_tile, micro, sections, seqs = cfg.per_tile, cfg.micro, cfg.sections, cfg.seqs
    pairs, chunk = cfg.heads // 2, cfg.chunk
    scale = HEAD_DIM ** (-0.5)
    sec, me, core = (lax.axis_index(a) for a in ("section", "expert", "tensor"))
    other = 1 - core
    own_rows = pl.ds(pl.multiple_of(core * owned, owned), owned)
    other_rows = pl.ds(pl.multiple_of(other * owned, owned), owned)
    is_first, is_last = sec == 0, sec == sections - 1

    def pair(kind, m, j, source, target):
        return pltpu.make_async_remote_copy(
            src_ref=source,
            dst_ref=target,
            send_sem=r.pair_send.at[kind, m, j],
            recv_sem=r.pair_recv.at[kind, m, j],
            device_id={"tensor": other},
            device_id_type=MESH,
        )

    def hop(kind, m, source, target, section):
        return pltpu.make_async_remote_copy(
            src_ref=source,
            dst_ref=target,
            send_sem=r.hop_send.at[kind, m],
            recv_sem=r.hop_recv.at[kind, m],
            device_id={"section": section},
            device_id_type=MESH,
        )

    def slot_rows(index):
        return pl.ds(pl.multiple_of(index * cap_pad, cap_pad), cap_pad)

    def tile_of(j):
        return pl.ds(pl.multiple_of(j * tile_rows, tile_rows), tile_rows)

    def exchange(kind, m, peer, landed, source, target):
        return pltpu.make_async_remote_copy(
            src_ref=source.at[slot_rows(peer)],
            dst_ref=target.at[slot_rows(landed)],
            send_sem=r.a2a_send.at[kind, m, peer],
            recv_sem=r.a2a_recv.at[kind, m, landed],
            device_id={"expert": peer},
            device_id_type=MESH,
        )

    def send_all(kind, m, source, target):
        def step(k, carry):
            exchange(kind, m, lax.rem(me + k, experts), me, source, target).start()
            return carry

        lax.fori_loop(1, experts, step, 0)

    def wait_sent(kind, m, source, target):
        def step(k, carry):
            exchange(kind, m, lax.rem(me + k, experts), me, source, target).wait_send()
            return carry

        lax.fori_loop(1, experts, step, 0)

    def wait_landed(kind, m, landed, source, target):
        exchange(kind, m, landed, landed, source, target).wait_recv()

    def save(index, m, source, target):
        return pltpu.make_async_copy(source, target.at[m], r.local.at[index, m])

    barrier = pltpu.get_barrier_semaphore()

    def greet(k, carry):
        pl.semaphore_signal(
            barrier, inc=1, device_id={"expert": lax.rem(me + k, experts)}, device_id_type=MESH
        )
        return carry

    lax.fori_loop(1, experts, greet, 0)
    pl.semaphore_signal(barrier, inc=1, device_id={"tensor": other}, device_id_type=MESH)

    @pl.when(sec > 0)
    def _():
        pl.semaphore_signal(barrier, inc=1, device_id={"section": sec - 1}, device_id_type=MESH)

    @pl.when(sec < sections - 1)
    def _():
        pl.semaphore_signal(barrier, inc=1, device_id={"section": sec + 1}, device_id_type=MESH)

    for m in range(micro):

        @pl.when(is_first)
        def _():
            save_in = pltpu.make_async_copy(r.inputs.at[m], r.x.at[m], r.local.at[0, m])
            save_in.start()

    weights = [
        pltpu.make_async_copy(source, target, r.fetch.at[k])
        for k, (source, target) in enumerate(
            ((r.gate, r.gate_v), (r.up, r.up_v), (r.down, r.down_v))
        )
    ]
    for copy in weights:
        copy.start()
    beside = (sec > 0).astype(i32) + (sec < sections - 1).astype(i32)
    pl.semaphore_wait(barrier, experts + beside)

    def seq_bias(m):
        row = iota((rows, 1), 0)
        start = jnp.zeros((rows, 1), i32)
        end = r.lengths[m, 0]
        for k in range(seqs):
            start = jnp.where(row >= end, row if k == seqs - 1 else end, start)
            end = end + r.lengths[m, min(k + 1, seqs)]
        for c in range(rows // chunk):
            piece = slice(c * chunk, (c + 1) * chunk)
            key = iota((chunk, rows), 1)
            seen = (key <= row[piece]) & (key >= start[piece])
            r.bias[piece, :] = jnp.where(seen, 0.0, -1e30)

    def routing(m):
        lane = iota((owned, LANES), 1)
        lane_t = iota((LANES, owned), 0)
        col = [r.route_col[m, :, k : k + 1] for k in range(2)]
        row = [r.route_row[m, k : k + 1, :] for k in range(2)]
        order_row, order_col = r.order_row[m], r.order_col[m]
        hot = [wide((lane == col[k]).astype(i32)) for k in range(2)]
        hot_t = [wide((lane_t == row[k]).astype(i32)) for k in range(2)]
        before = wide((order_row < order_col).astype(i32)).astype(bf16)
        before_t = wide((order_col < order_row).astype(i32)).astype(bf16)
        earlier = dot(before, (hot[0] + hot[1]).astype(bf16))
        earlier_t = dot((hot_t[0] + hot_t[1]).astype(bf16), before_t)
        for k in range(2):
            slot = jnp.sum(earlier * hot[k], axis=1, keepdims=True).astype(i32)
            slot_t = jnp.sum(earlier_t * hot_t[k], axis=0, keepdims=True).astype(i32)
            place = jnp.where((col[k] < experts) & (slot < cap), col[k] * cap_pad + slot, -1)
            place_t = jnp.where((row[k] < experts) & (slot_t < cap), row[k] * cap_pad + slot_t, -1)
            r.place_col[m, :, k : k + 1] = place
            r.place_row[m, k : k + 1, :] = place_t

    def spread(m, k):
        return flag(iota((owned, slots), 1) == r.place_col[m, :, k : k + 1]).astype(bf16)

    def spread_t(m, k):
        return flag(iota((slots, owned), 0) == r.place_row[m, k : k + 1, :]).astype(bf16)

    def choice_flags(m):
        col = [r.route_col[m, :, k : k + 1] for k in range(2)]
        copies = [wide((col[k] == experts + 1).astype(i32)) for k in range(2)]
        consts = [
            [wide((col[k] == experts + 2 + c).astype(i32)) for c in range(2)] for k in range(2)
        ]
        return col, copies, consts

    def unpack_gates(m):
        pack = r.gates[m]
        return [pack[:, k : k + 1] for k in range(2)], [pack[:, 2 + k : 3 + k] for k in range(2)]

    def through_expert(m, kind_in, kind_out, pair_in, pair_out, outgoing, arrived, target, kept, compute):
        mine = arrived.at[core]
        theirs = arrived.at[other]

        def arrive(j, carry):
            def one(k, inner):
                source = j * per_tile + k

                @pl.when(source != me)
                def _():
                    wait_landed(kind_in, m, source, outgoing, mine)

                return inner

            lax.fori_loop(0, per_tile, one, 0)
            pair(pair_in, m, j, mine.at[tile_of(j)], mine.at[tile_of(j)]).start()
            return carry

        lax.fori_loop(0, tiles, arrive, 0)
        passes = kind_in // 2

        def keep(half, tile, j):
            return pltpu.make_async_copy(
                arrived.at[half, tile], kept.at[m, half, tile], r.keep.at[passes, m, half, j]
            )

        def work(j, carry):
            tile = tile_of(j)
            keep(core, tile, j).start()
            r.partial[tile, :] = compute(core, tile, 0, j)
            pair(pair_in, m, j, theirs.at[tile], theirs.at[tile]).wait_recv()
            keep(other, tile, j).start()
            r.part_out[tile, :] = compute(other, tile, 1, j).astype(bf16)
            keep(other, tile, j).wait()
            pair(pair_out, m, j, r.part_out.at[tile], r.part_in.at[tile]).start()
            return carry

        lax.fori_loop(0, tiles, work, 0)

        def read(j, carry):
            tile = tile_of(j)
            pair(pair_in, m, j, mine.at[tile], mine.at[tile]).wait_send()
            keep(core, tile, j).wait()
            return carry

        lax.fori_loop(0, tiles, read, 0)

        def finish(j, carry):
            tile = tile_of(j)
            pair(pair_out, m, j, r.part_out.at[tile], r.part_in.at[tile]).wait_recv()
            r.result[tile, :] = (r.partial[tile, :] + wide(r.part_in[tile, :])).astype(bf16)

            def one(k, inner):
                source = j * per_tile + k

                @pl.when(source != me)
                def _():
                    exchange(kind_out, m, source, me, r.result, target).start()

                @pl.when(source == me)
                def _():
                    target[slot_rows(me), :] = r.result[slot_rows(me), :]

                return inner

            lax.fori_loop(0, per_tile, one, 0)
            return carry

        lax.fori_loop(0, tiles, finish, 0)

        def done(j, carry):
            tile = tile_of(j)
            pair(pair_out, m, j, r.part_out.at[tile], r.part_in.at[tile]).wait_send()
            return carry

        lax.fori_loop(0, tiles, done, 0)
        wait_sent(kind_in, m, outgoing, mine)

    def wait_back(m, kind_out, target):

        def one(k, carry):
            wait_landed(kind_out, m, lax.rem(me + k, experts), r.result, target)
            return carry

        lax.fori_loop(1, experts, one, 0)
        wait_sent(kind_out, m, r.result, target)

    def forward(m, carry):
        @pl.when(is_first)
        def _():
            pltpu.make_async_copy(r.inputs.at[m], r.x.at[m], r.local.at[0, m]).wait()

        @pl.when(sec > 0)
        def _():
            hop(0, m, r.hop_out, r.hop_in.at[0, m], sec - 1).wait_recv()
            r.x[m] = wide(r.hop_in[0, m])

        x = r.x[m]
        r.norm[m, own_rows, :] = (x * inverse_rms(x) * r.gain1[...]).astype(bf16)
        pair(P_NORM, m, 0, r.norm.at[m, own_rows], r.norm.at[m, own_rows]).start()
        routing(m)
        seq_bias(m)
        pair(P_NORM, m, 0, r.norm.at[m, other_rows], r.norm.at[m, other_rows]).wait_recv()
        save(1, m, r.norm.at[m], r.h_norm).start()

        normed = r.norm[m]
        for stash, weight in ((r.q, r.w_query), (r.k, r.w_key)):
            flat = dot(normed, weight[...])
            for p in range(pairs):
                lanes = slice(p * LANES, (p + 1) * LANES)
                stash[m, :, lanes] = turned(flat[:, lanes], r.cosine[...], r.sine[...]).astype(bf16)
        r.v[m] = dot(normed, r.w_value[...]).astype(bf16)

        r.logsum[m] = jnp.zeros((rows, LANES), f32)
        lane = iota((1, LANES), 1)

        def head_pair(p, inner):
            lanes = pl.ds(pl.multiple_of(p * LANES, LANES), LANES)
            q2, k2, v2 = r.q[m, :, lanes], r.k[m, :, lanes], r.v[m, :, lanes]
            for half in range(2):
                keep = wide(((lane // HEAD_DIM) == half).astype(i32)).astype(bf16)
                km, vm = k2 * keep, v2 * keep
                for c in range(rows // chunk):
                    piece, reach = slice(c * chunk, (c + 1) * chunk), (c + 1) * chunk
                    scores = dot_nt(q2[piece], km[:reach]) * scale + r.bias[piece, :reach]
                    peak = jnp.max(scores, axis=-1, keepdims=True)
                    shifted = jnp.exp(scores - peak)
                    total = jnp.sum(shifted, axis=-1, keepdims=True)
                    probs = (shifted * (1.0 / total)).astype(bf16)
                    mixed = dot(probs, vm[:reach])
                    if half == 0:
                        r.mix[piece, :] = mixed
                    else:
                        r.o[m, piece, lanes] = (r.mix[piece, :] + mixed).astype(bf16)
                    r.logsum[m, piece, :] = jnp.where(
                        lane == 2 * p + half, peak + jnp.log(total), r.logsum[m, piece, :]
                    )
            return inner

        lax.fori_loop(0, pairs, head_pair, 0)
        save(2, m, r.o.at[m], r.h_o).start()

        r.half_out[...] = dot(r.o[m, other_rows, :], r.w_out[...]).astype(bf16)
        pair(P_OUT, m, 0, r.half_out, r.half_in.at[0, m]).start()
        summed = x + dot(r.o[m, own_rows, :], r.w_out[...])
        pair(P_OUT, m, 0, r.half_out, r.half_in.at[0, m]).wait_recv()
        hidden = summed + wide(r.half_in[0, m])
        r.h[m] = hidden
        normed2 = (hidden * inverse_rms(hidden) * r.gain2[...]).astype(bf16)
        r.norm2[m] = normed2

        into = r.arrived
        both = spread_t(m, 0) + spread_t(m, 1)
        r.outgoing[...] = dot(both, normed2).astype(bf16)
        send_all(0, m, r.outgoing, into.at[core])
        r.arrived[core, slot_rows(me), :] = r.outgoing[slot_rows(me), :]

        mixer_hi, mixer_lo = halves(r.mixer[...])
        logits = dot_nt(normed2, mixer_hi) + dot_nt(normed2, mixer_lo)
        logits = logits + dot3(dot, r.prev[m], r.residual[...])
        col, copies, consts = choice_flags(m)
        wide_lane = iota((owned, LANES), 1)
        picked = [
            jnp.sum(jnp.where(wide_lane == col[k], logits, 0.0), axis=1, keepdims=True)
            for k in range(2)
        ]
        gate = [jax.nn.sigmoid(picked[0] - picked[1]), jax.nn.sigmoid(picked[1] - picked[0])]
        rate = [jax.nn.sigmoid(logits[:, choices + c : choices + c + 1]) for c in range(2)]
        pack = jnp.zeros((owned, LANES), f32)
        for k, value in enumerate(gate + rate):
            pack = jnp.where(wide_lane == k, value, pack)
        r.gates[m] = pack

        @pl.when(m == 0)
        def _():
            for copy in weights:
                copy.wait()

        def compute(half, tile, slot, j):
            block = r.arrived[half, tile, :]
            place = pl.ds(pl.multiple_of(half * slots + tile.start, tile_rows), tile_rows)
            value = dot(block, r.gate_v[...])
            upper = dot(block, r.up_v[...])
            sig = jax.nn.sigmoid(value)
            active = value * sig
            inside = (active * upper).astype(bf16)
            r.by_up[place, :] = active.astype(bf16)
            r.by_gate[place, :] = (upper * sig * (1.0 + value * (1.0 - sig))).astype(bf16)

            def ring(at):
                rows_of = pl.ds(pl.multiple_of(half * slots + at * tile_rows, tile_rows), tile_rows)
                return pltpu.make_async_copy(
                    r.inside.at[slot], r.h_inside.at[m, rows_of], r.ring.at[slot, m, at]
                )

            @pl.when(j > 0)
            def _():
                ring(j - 1).wait()

            r.inside[slot] = inside
            ring(j).start()

            @pl.when(j == tiles - 1)
            def _():
                ring(j).wait()

            return dot(inside, r.down_v[...])

        through_expert(m, 0, 1, P_ROWS, P_PART, r.outgoing, into, r.back.at[m], r.h_rows, compute)
        stored = [
            save(5, m, r.by_up, r.h_up),
            save(6, m, r.by_gate, r.h_gate),
        ]
        for copy in stored:
            copy.start()
        wait_back(m, 1, r.back.at[m])

        apart = [dot(spread(m, k), r.back[m]) for k in range(2)]
        out = r.h[m] + gate[0] * apart[0] + gate[1] * apart[1]
        own = gate[0] * copies[0] + gate[1] * copies[1]
        for c in range(2):
            on = gate[0] * consts[0][c] + gate[1] * consts[1][c]
            own = own + on * rate[c]
            out = out + (on * (1.0 - rate[c])) * r.const_value[c : c + 1, :]
        out = out + own * wide(r.norm2[m])
        r.stage[...] = out
        save(3, m, r.stage, r.layer_out).start()

        @pl.when(sec < sections - 1)
        def _():
            copy = hop(0, m, r.hop_out, r.hop_in.at[0, m], sec + 1)
            r.hop_out[...] = out.astype(bf16)
            copy.start()
            copy.wait_send()

        pair(P_NORM, m, 0, r.norm.at[m, own_rows], r.norm.at[m, own_rows]).wait_send()
        pair(P_OUT, m, 0, r.half_out, r.half_in.at[0, m]).wait_send()
        save(3, m, r.stage, r.layer_out).wait()
        save(1, m, r.norm.at[m], r.h_norm).wait()
        save(2, m, r.o.at[m], r.h_o).wait()
        for copy in stored:
            copy.wait()
        return carry

    lax.fori_loop(0, micro, forward, 0)

    r.mixer_grad[...] = jnp.zeros_like(r.mixer_grad)
    r.residual_grad[...] = jnp.zeros_like(r.residual_grad)
    r.rows_grad[...] = jnp.zeros_like(r.rows_grad)

    def backward(m, carry):
        fetched = [
            pltpu.make_async_copy(r.h_up.at[m], r.by_up, r.local.at[7, m]),
            pltpu.make_async_copy(r.h_gate.at[m], r.by_gate, r.local.at[8, m]),
        ]
        for copy in fetched:
            copy.start()

        @pl.when(is_last)
        def _():
            copy = pltpu.make_async_copy(r.cotangent.at[m], r.dz, r.local.at[9, m])
            copy.start()
            copy.wait()

        @pl.when(sec < sections - 1)
        def _():
            hop(1, m, r.hop_out, r.hop_in.at[1, m], sec + 1).wait_recv()
            r.dz[...] = wide(r.hop_in[1, m])

        dz = r.dz[...]
        gate, rate = unpack_gates(m)
        into = r.arrived
        leaving = [dot(spread_t(m, k), (gate[k] * dz).astype(bf16)) for k in range(2)]
        r.outgoing[...] = (leaving[0] + leaving[1]).astype(bf16)
        send_all(2, m, r.outgoing, into.at[core])
        r.arrived[core, slot_rows(me), :] = r.outgoing[slot_rows(me), :]

        col, copies, consts = choice_flags(m)
        normed2 = r.norm2[m]
        dz_norm = jnp.sum(dz * wide(normed2), axis=1, keepdims=True)
        dz_const = [
            jnp.sum(dz * r.const_value[c : c + 1, :], axis=1, keepdims=True) for c in range(2)
        ]
        apart = [dot(spread(m, k), r.back[m]) for k in range(2)]
        dgate = []
        for k in range(2):
            value = jnp.sum(dz * apart[k], axis=1, keepdims=True)
            value = value + copies[k] * dz_norm
            for c in range(2):
                value = value + consts[k][c] * (rate[c] * dz_norm + (1.0 - rate[c]) * dz_const[c])
            dgate.append(value)
        coupled = gate[0] * gate[1] * (dgate[0] - dgate[1])
        lane = iota((owned, LANES), 1)
        dlogits = jnp.where(lane == col[0], coupled, jnp.where(lane == col[1], -coupled, 0.0))
        own = gate[0] * copies[0] + gate[1] * copies[1]
        for c in range(2):
            on = gate[0] * consts[0][c] + gate[1] * consts[1][c]
            own = own + on * rate[c]
            dmix = on * (dz_norm - dz_const[c]) * rate[c] * (1.0 - rate[c])
            dlogits = dlogits + jnp.where(lane == choices + c, dmix, 0.0)
            r.rows_grad[c : c + 1, :] += jnp.sum((on * (1.0 - rate[c])) * dz, axis=0, keepdims=True)
        dlogits_hi, dlogits_lo = halves(dlogits)
        r.mixer_grad[...] += dot_tn(dlogits_hi, normed2) + dot_tn(dlogits_lo, normed2)
        r.residual_grad[...] += dot3(dot_tn, r.prev[m], dlogits)
        r.logit_grad[m] = dot3(dot_nt, dlogits, r.residual[...])
        r.dnorm[...] = dot3(dot, dlogits, r.mixer[...]) + own * dz
        seq_bias(m)
        for copy in fetched:
            copy.wait()

        def compute(half, tile, slot, j):
            block = r.arrived[half, tile, :]
            place = pl.ds(pl.multiple_of(half * slots + tile.start, tile_rows), tile_rows)
            dinside = dot_nt(block, r.down_v[...])
            dvalue = (dinside * wide(r.by_gate[place, :])).astype(bf16)
            dupper = (dinside * wide(r.by_up[place, :])).astype(bf16)
            r.by_gate[place, :] = dvalue
            r.by_up[place, :] = dupper
            return dot_nt(dvalue, r.gate_v[...]) + dot_nt(dupper, r.up_v[...])

        through_expert(m, 2, 3, P_GROWS, P_GPART, r.outgoing, into, r.grad_back, r.h_grads, compute)
        stored = [
            save(11, m, r.by_up, r.h_up),
            save(12, m, r.by_gate, r.h_gate),
        ]
        for copy in stored:
            copy.start()
        wait_back(m, 3, r.grad_back)

        both = spread(m, 0) + spread(m, 1)
        dnorm = r.dnorm[...] + dot(both, r.grad_back[...])
        hidden = r.h[m]
        root = inverse_rms(hidden)
        scaled = dnorm * r.gain2[...]
        pull = root * root * root * jnp.mean(hidden * scaled, axis=-1, keepdims=True)
        dhidden = dz + root * scaled - hidden * pull
        r.rows_grad[3:4, :] += jnp.sum(dnorm * hidden * root, axis=0, keepdims=True)
        r.dh[...] = dhidden
        r.da[own_rows, :] = dhidden.astype(bf16)
        pair(P_DA, m, 0, r.da.at[own_rows], r.da.at[own_rows]).start()
        pair(P_DA, m, 0, r.da.at[other_rows], r.da.at[other_rows]).wait_recv()
        save_da = save(13, m, r.da, r.h_da)
        save_da.start()
        r.do[...] = dot_nt(r.da[...], r.w_out[...]).astype(bf16)

        head_lane = iota((1, LANES), 1)

        def head_pair(p, inner):
            lanes = pl.ds(pl.multiple_of(p * LANES, LANES), LANES)
            q2, k2, v2 = r.q[m, :, lanes], r.k[m, :, lanes], r.v[m, :, lanes]
            do2 = r.do[:, lanes]
            for half in range(2):
                keep = wide(((head_lane // HEAD_DIM) == half).astype(i32)).astype(bf16)
                km, vm, qm, dom = k2 * keep, v2 * keep, q2 * keep, do2 * keep
                for c in range(rows // chunk):
                    piece, reach = slice(c * chunk, (c + 1) * chunk), (c + 1) * chunk
                    scores = dot_nt(q2[piece], km[:reach]) * scale + r.bias[piece, :reach]
                    total = jnp.sum(
                        jnp.where(head_lane == 2 * p + half, r.logsum[m, piece, :], 0.0),
                        axis=1,
                        keepdims=True,
                    )
                    probs = jnp.exp(scores - total)
                    dprobs = dot_nt(do2[piece], vm[:reach])
                    meant = jnp.sum(dprobs * probs, axis=-1, keepdims=True)
                    dscores = (probs * (dprobs - meant)).astype(bf16)
                    dq = dot(dscores, km[:reach])
                    dk = dot_tn(dscores, qm[piece])
                    dv = dot_tn(probs.astype(bf16), dom[piece])
                    if half == 0:
                        r.mix[piece, :] = dq
                    else:
                        r.mix[piece, :] += dq
                    if half == 0 and c == 0:
                        r.mix_k[...] = jnp.zeros_like(r.mix_k)
                        r.mix_v[...] = jnp.zeros_like(r.mix_v)
                    r.mix_k[:reach, :] += dk
                    r.mix_v[:reach, :] += dv
            r.dq[:, lanes] = (turned_back(r.mix[...], r.cosine[...], r.sine[...]) * scale).astype(bf16)
            r.dk[:, lanes] = (turned_back(r.mix_k[...], r.cosine[...], r.sine[...]) * scale).astype(bf16)
            r.dv[:, lanes] = r.mix_v[...].astype(bf16)
            return inner

        lax.fori_loop(0, pairs, head_pair, 0)
        more = [save(14, m, r.dq, r.h_dq), save(15, m, r.dk, r.h_dk), save(16, m, r.dv, r.h_dv)]
        for copy in more:
            copy.start()

        def dnormed(piece):
            return (
                dot_nt(r.dq[piece, :], r.w_query[...])
                + dot_nt(r.dk[piece, :], r.w_key[...])
                + dot_nt(r.dv[piece, :], r.w_value[...])
            )

        r.half_out[...] = dnormed(other_rows).astype(bf16)
        pair(P_DX, m, 0, r.half_out, r.half_in.at[1, m]).start()
        kept = dnormed(own_rows)
        pair(P_DX, m, 0, r.half_out, r.half_in.at[1, m]).wait_recv()
        dnorm1 = kept + wide(r.half_in[1, m])
        x = r.x[m]
        root1 = inverse_rms(x)
        scaled1 = dnorm1 * r.gain1[...]
        pull1 = root1 * root1 * root1 * jnp.mean(x * scaled1, axis=-1, keepdims=True)
        dx = r.dh[...] + root1 * scaled1 - x * pull1
        r.stage[...] = dx
        save(4, m, r.stage, r.input_grad).start()

        @pl.when(sec > 0)
        def _():
            copy = hop(1, m, r.hop_out, r.hop_in.at[1, m], sec - 1)
            r.hop_out[...] = dx.astype(bf16)
            copy.start()
            copy.wait_send()

        r.rows_grad[2:3, :] += jnp.sum(dnorm1 * x * root1, axis=0, keepdims=True)
        pair(P_DA, m, 0, r.da.at[own_rows], r.da.at[own_rows]).wait_send()
        pair(P_DX, m, 0, r.half_out, r.half_in.at[1, m]).wait_send()
        save(4, m, r.stage, r.input_grad).wait()
        save_da.wait()
        for copy in stored + more:
            copy.wait()
        return carry

    lax.fori_loop(0, micro, backward, 0)


def run_chain(cfg, ins):
    vmem, anywhere = pl.BlockSpec(memory_space=pltpu.VMEM), pl.BlockSpec(memory_space=pl.ANY)
    smem = pl.BlockSpec(memory_space=pltpu.SMEM)
    far = {"inputs", "cotangent", "gate", "up", "down"}
    micro, owned, rows, width, inner = cfg.micro, cfg.owned, cfg.rows, cfg.width, cfg.inner
    heads_width, slots = cfg.heads * HEAD_DIM, cfg.slots
    shape = jax.ShapeDtypeStruct
    outs = dict(
        logit_grad=shape((micro, owned, LANES), f32),
        mixer_grad=shape((LANES, width), f32),
        residual_grad=shape((LANES, LANES), f32),
        rows_grad=shape((8, width), f32),
    )
    hbm_outs = dict(
        layer_out=shape((micro, owned, width), f32),
        input_grad=shape((micro, owned, width), f32),
        h_rows=shape((micro, 2, slots, width), bf16),
        h_grads=shape((micro, 2, slots, width), bf16),
        h_inside=shape((micro, 2 * slots, inner), bf16),
        h_up=shape((micro, 2 * slots, inner), bf16),
        h_gate=shape((micro, 2 * slots, inner), bf16),
        h_norm=shape((micro, rows, width), bf16),
        h_da=shape((micro, rows, width), bf16),
        h_o=shape((micro, rows, heads_width), bf16),
        h_dq=shape((micro, rows, heads_width), bf16),
        h_dk=shape((micro, rows, heads_width), bf16),
        h_dv=shape((micro, rows, heads_width), bf16),
    )
    dma = pltpu.SemaphoreType.DMA
    scratch = dict(
        gate_v=pltpu.VMEM((width, inner), bf16),
        up_v=pltpu.VMEM((width, inner), bf16),
        down_v=pltpu.VMEM((inner, width), bf16),
        x=pltpu.VMEM((micro, owned, width), f32),
        h=pltpu.VMEM((micro, owned, width), f32),
        norm=pltpu.VMEM((micro, rows, width), bf16),
        norm2=pltpu.VMEM((micro, owned, width), bf16),
        q=pltpu.VMEM((micro, rows, heads_width), bf16),
        k=pltpu.VMEM((micro, rows, heads_width), bf16),
        v=pltpu.VMEM((micro, rows, heads_width), bf16),
        o=pltpu.VMEM((micro, rows, heads_width), bf16),
        logsum=pltpu.VMEM((micro, rows, LANES), f32),
        gates=pltpu.VMEM((micro, owned, LANES), f32),
        place_col=pltpu.VMEM((micro, owned, 2), i32),
        place_row=pltpu.VMEM((micro, 2, owned), i32),
        bias=pltpu.VMEM((rows, rows), f32),
        arrived=pltpu.VMEM((2, slots, width), bf16),
        part_in=pltpu.VMEM((slots, width), bf16),
        back=pltpu.VMEM((micro, slots, width), bf16),
        half_in=pltpu.VMEM((2, micro, owned, width), bf16),
        hop_in=pltpu.VMEM((2, micro, owned, width), bf16),
        grad_back=pltpu.VMEM((slots, width), bf16),
        outgoing=pltpu.VMEM((slots, width), bf16),
        part_out=pltpu.VMEM((slots, width), bf16),
        result=pltpu.VMEM((slots, width), bf16),
        partial=pltpu.VMEM((slots, width), f32),
        half_out=pltpu.VMEM((owned, width), bf16),
        hop_out=pltpu.VMEM((owned, width), bf16),
        inside=pltpu.VMEM((2, cfg.tile_rows, inner), bf16),
        by_up=pltpu.VMEM((2 * slots, inner), bf16),
        by_gate=pltpu.VMEM((2 * slots, inner), bf16),
        dz=pltpu.VMEM((owned, width), f32),
        stage=pltpu.VMEM((owned, width), f32),
        dh=pltpu.VMEM((owned, width), f32),
        dnorm=pltpu.VMEM((owned, width), f32),
        da=pltpu.VMEM((rows, width), bf16),
        do=pltpu.VMEM((rows, heads_width), bf16),
        dq=pltpu.VMEM((rows, heads_width), bf16),
        dk=pltpu.VMEM((rows, heads_width), bf16),
        dv=pltpu.VMEM((rows, heads_width), bf16),
        mix=pltpu.VMEM((rows, LANES), f32),
        mix_k=pltpu.VMEM((rows, LANES), f32),
        mix_v=pltpu.VMEM((rows, LANES), f32),
        pair_send=dma((8, micro, cfg.tiles)),
        pair_recv=dma((8, micro, cfg.tiles)),
        hop_send=dma((2, micro)),
        hop_recv=dma((2, micro)),
        a2a_send=dma((4, micro, cfg.experts)),
        a2a_recv=dma((4, micro, cfg.experts)),
        local=dma((17, micro)),
        keep=dma((2, micro, 2, cfg.tiles)),
        ring=dma((2, micro, cfg.tiles)),
        fetch=dma((3,)),
    )
    names = [*ins, *outs, *hbm_outs, *scratch]
    flops = 2 * micro * (2 * slots * width * inner * 6 + rows * width * heads_width * 10)
    results = pl.pallas_call(
        functools.partial(chain_kernel, cfg, names),
        out_shape=[*outs.values(), *hbm_outs.values()],
        in_specs=[
            smem if name == "lengths" else anywhere if name in far else vmem for name in ins
        ],
        out_specs=[vmem] * len(outs) + [anywhere] * len(hbm_outs),
        scratch_shapes=[*scratch.values()],
        compiler_params=pltpu.CompilerParams(
            collective_id=0, has_side_effects=True, vmem_limit_bytes=60 * 2**20
        ),
        cost_estimate=pl.CostEstimate(flops=flops, bytes_accessed=50_000_000, transcendentals=0),
    )(*ins.values())
    return types.SimpleNamespace(**dict(zip([*outs, *hbm_outs], results, strict=True)))


def tail_kernel(cfg, names, *refs):
    r = types.SimpleNamespace(**dict(zip(names, refs, strict=True)))
    experts, width, pad = cfg.experts, cfg.width, cfg.small_pad
    side = width // 2
    outer = experts // 2
    me, core = lax.axis_index("expert"), lax.axis_index("tensor")
    mine_out, mine_in = me // 2, lax.rem(me, 2)
    beside = me + 1 - 2 * mine_in
    pieces = len(cfg.piece_rows)
    starts = [sum(cfg.piece_rows[:c]) * experts for c in range(pieces)]

    def peer_of(k):
        place = lax.rem(mine_out + k, outer)
        return place, place * 2 + mine_in

    barrier = pltpu.get_barrier_semaphore()
    pl.semaphore_signal(barrier, inc=1, device_id={"tensor": 1 - core}, device_id_type=MESH)
    pl.semaphore_signal(barrier, inc=1, device_id={"expert": beside}, device_id_type=MESH)

    def greet(k, carry):
        pl.semaphore_signal(barrier, inc=1, device_id={"expert": peer_of(k)[1]}, device_id_type=MESH)
        return carry

    lax.fori_loop(1, outer, greet, 0)

    loads = [
        pltpu.make_async_copy(source, target, r.fetch.at[k])
        for k, (source, target) in enumerate(
            (
                (r.h_rows, r.rows_v),
                (r.h_gate, r.gate_v),
                (r.h_up, r.up_v),
                (r.h_grads, r.grads_v),
                (r.h_inside, r.gate_v),
            )
        )
    ]
    for copy in loads[:4]:
        copy.start()

    r.pack[...] = jnp.zeros_like(r.pack)
    r.pack[:pad, :] = r.mixer_grad[:pad, :side]
    r.pack[pad : 2 * pad, :] = r.mixer_grad[:pad, side:]
    r.pack[2 * pad : 2 * pad + 8, :] = r.rows_grad[:, :side]
    r.pack[2 * pad + 8 : 2 * pad + 16, :] = r.rows_grad[:, side:]
    r.pack[2 * pad + 16 : 3 * pad + 16, :LANES] = r.residual_grad[:pad, :]
    r.pack_out[...] = r.pack[...].astype(bf16)
    pl.semaphore_wait(barrier, outer + 1)
    pack_copy = pltpu.make_async_remote_copy(
        src_ref=r.pack_out,
        dst_ref=r.pack_in,
        send_sem=r.pack_sem.at[0],
        recv_sem=r.pack_sem.at[1],
        device_id={"tensor": 1 - core},
        device_id_type=MESH,
    )
    pack_copy.start()

    def span(start, index, size):
        return pl.ds(pl.multiple_of(start + index * size, 16), size)

    def over_x(stage, c, source, target, from_rows, to_rows):
        return pltpu.make_async_remote_copy(
            src_ref=source.at[from_rows],
            dst_ref=target.at[to_rows],
            send_sem=r.x_send.at[stage, c],
            recv_sem=r.x_recv.at[stage, c],
            device_id={"expert": beside},
            device_id_type=MESH,
        )

    def over_z(stage, c, place, landed, peer, source, target):
        return pltpu.make_async_remote_copy(
            src_ref=source,
            dst_ref=target,
            send_sem=r.z_send.at[stage, c, place],
            recv_sem=r.z_recv.at[stage, c, landed],
            device_id={"expert": peer},
            device_id_type=MESH,
        )

    def half_of(c, which):
        return span(starts[c], which, outer * cfg.piece_rows[c])

    def landing(c):
        return pl.ds(starts[c] // 2, outer * cfg.piece_rows[c])

    def scatter_x(c):
        return over_x(0, c, r.sent, r.x_in, half_of(c, 1 - mine_in), landing(c))

    def gather_x(c, which):
        return over_x(1, c, r.summed, r.summed, half_of(c, which), half_of(c, which))

    def scatter_z(c, place, landed, peer):
        size = cfg.piece_rows[c]
        return over_z(
            0,
            c,
            place,
            landed,
            peer,
            r.z_out.at[span(starts[c] // 2, place, size)],
            r.z_in.at[landed, pl.ds(starts[c] // experts, size)],
        )

    def final(c, place):
        return span(starts[c], mine_in * outer + place, cfg.piece_rows[c])

    def gather_z(c, place, landed, peer):
        rows = final(c, landed)
        return over_z(1, c, place, landed, peer, r.summed.at[rows], r.summed.at[rows])

    def weight_grad(left, right):
        return dot_tn(left.reshape(-1, left.shape[-1]), right.reshape(-1, right.shape[-1]))

    products = ((r.h_norm, r.h_dq), (r.h_norm, r.h_dk), (r.h_norm, r.h_dv), (r.h_da, r.h_o))
    for c in range(pieces):
        rows = pl.ds(starts[c], experts * cfg.piece_rows[c])
        if c < 4:
            left, right = products[c]
            value = weight_grad(left[...], right[...])
            if value.shape[0] != experts * cfg.piece_rows[c]:
                r.sent[rows, :] = jnp.zeros((experts * cfg.piece_rows[c], side), bf16)
            r.sent[pl.ds(starts[c], value.shape[0]), :] = value.astype(bf16)
        else:
            pack_copy.wait()
            r.sent[rows, :] = (r.pack[...] + wide(r.pack_in[...])).astype(bf16)
        scatter_x(c).start()

    rows_all = cfg.micro * 2 * cfg.slots
    tile = 256
    steps = []
    for left, right, target in (
        (r.rows_v, r.gate_v, r.gate_grad),
        (r.rows_v, r.up_v, r.up_grad),
        (r.gate_v, r.grads_v, r.down_grad),
    ):
        for t in range(left.shape[-1] // tile):
            needs = ((0, 1), (0, 2), (3, 4))[len(steps) // (width // tile) if target is not r.down_grad else 2]
            steps.append((left, right, target, t, needs))

    loaded = set()
    flying = [None, None]

    def expert_step(index):
        left, right, target, t, needs = steps[index]
        if index == width // tile:
            loads[4].start()
        for k in needs:
            if k not in loaded:
                loads[k].wait()
                loaded.add(k)
        slot = index % 2
        if flying[slot] is not None:
            flying[slot].wait()
        wide_out = right.shape[-1]
        a = left[..., t * tile : (t + 1) * tile].reshape(rows_all, tile)
        r.stage[slot, :, :wide_out] = dot_tn(a, right[...].reshape(rows_all, wide_out))
        copy = pltpu.make_async_copy(
            r.stage.at[slot, :, pl.ds(0, wide_out)],
            target.at[pl.ds(t * tile, tile)],
            r.step_sem.at[index],
        )
        copy.start()
        flying[slot] = copy

    done = 0
    for c in range(pieces):
        upto = len(steps) * (c + 1) // pieces
        while done < upto:
            expert_step(done)
            done += 1
        scatter_x(c).wait_recv()
        rows = landing(c)
        r.z_out[rows, :] = (wide(r.sent[half_of(c, mine_in), :]) + wide(r.x_in[rows, :])).astype(bf16)

        def out_z(k, carry, c=c):
            place, peer = peer_of(k)
            scatter_z(c, place, mine_out, peer).start()
            return carry

        lax.fori_loop(1, outer, out_z, 0)

    for c in range(pieces):
        size = cfg.piece_rows[c]

        def add_z(k, total, c=c, size=size):
            place, peer = peer_of(k)
            scatter_z(c, place, place, peer).wait_recv()
            return total + wide(r.z_in[place, pl.ds(starts[c] // experts, size), :])

        total = lax.fori_loop(1, outer, add_z, wide(r.z_out[span(starts[c] // 2, mine_out, size), :]))
        r.summed[final(c, mine_out), :] = total.astype(bf16)

        def back_z(k, carry, c=c):
            place, peer = peer_of(k)
            gather_z(c, place, mine_out, peer).start()
            return carry

        lax.fori_loop(1, outer, back_z, 0)

    for c in range(pieces):

        def wait_z(k, carry, c=c):
            place, peer = peer_of(k)
            gather_z(c, place, place, peer).wait_recv()
            return carry

        lax.fori_loop(1, outer, wait_z, 0)
        gather_x(c, mine_in).start()
    for c in range(pieces):
        gather_x(c, 1 - mine_in).wait_recv()
    for c in range(pieces):
        scatter_x(c).wait_send()
        gather_x(c, mine_in).wait_send()

        def sent_z(k, carry, c=c):
            place, peer = peer_of(k)
            scatter_z(c, place, mine_out, peer).wait_send()
            gather_z(c, place, mine_out, peer).wait_send()
            return carry

        lax.fori_loop(1, outer, sent_z, 0)
    for copy in flying:
        copy.wait()


def run_tail(cfg, got):
    vmem, anywhere = pl.BlockSpec(memory_space=pltpu.VMEM), pl.BlockSpec(memory_space=pl.ANY)
    micro, width, inner, slots, experts = cfg.micro, cfg.width, cfg.inner, cfg.slots, cfg.experts
    side, outer = width // 2, experts // 2
    piece = -(-width // (16 * experts)) * 16
    small = -(-(3 * cfg.small_pad + 16) // (16 * experts)) * 16
    cfg.piece_rows = [piece] * 4 + [small]
    total = sum(cfg.piece_rows) * experts
    near = dict(
        h_norm=got.h_norm,
        h_da=got.h_da,
        h_o=got.h_o,
        h_dq=got.h_dq,
        h_dk=got.h_dk,
        h_dv=got.h_dv,
        mixer_grad=got.mixer_grad,
        residual_grad=got.residual_grad,
        rows_grad=got.rows_grad,
    )
    far = dict(
        h_rows=got.h_rows,
        h_grads=got.h_grads,
        h_inside=got.h_inside,
        h_up=got.h_up,
        h_gate=got.h_gate,
    )
    shape, dma = jax.ShapeDtypeStruct, pltpu.SemaphoreType.DMA
    outs = dict(
        summed=shape((total, side), bf16),
        gate_grad=shape((width, inner), f32),
        up_grad=shape((width, inner), f32),
        down_grad=shape((inner, width), f32),
    )
    scratch = dict(
        rows_v=pltpu.VMEM((micro, 2, slots, width), bf16),
        grads_v=pltpu.VMEM((micro, 2, slots, width), bf16),
        up_v=pltpu.VMEM((micro, 2 * slots, inner), bf16),
        gate_v=pltpu.VMEM((micro, 2 * slots, inner), bf16),
        sent=pltpu.VMEM((total, side), bf16),
        x_in=pltpu.VMEM((total // 2, side), bf16),
        z_out=pltpu.VMEM((total // 2, side), bf16),
        z_in=pltpu.VMEM((outer, total // experts, side), bf16),
        pack=pltpu.VMEM((small * experts, side), f32),
        pack_out=pltpu.VMEM((small * experts, side), bf16),
        pack_in=pltpu.VMEM((small * experts, side), bf16),
        stage=pltpu.VMEM((2, 256, max(inner, width)), f32),
        fetch=dma((5,)),
        step_sem=dma(((2 * width + inner) // 256,)),
        pack_sem=dma((2,)),
        x_send=dma((2, 5)),
        x_recv=dma((2, 5)),
        z_send=dma((2, 5, outer)),
        z_recv=dma((2, 5, outer)),
    )
    names = [*near, *far, *outs, *scratch]
    results = pl.pallas_call(
        functools.partial(tail_kernel, cfg, names),
        out_shape=[*outs.values()],
        in_specs=[vmem] * len(near) + [anywhere] * len(far),
        out_specs=[vmem] + [anywhere] * 3,
        scratch_shapes=[*scratch.values()],
        compiler_params=pltpu.CompilerParams(
            collective_id=1, has_side_effects=True, vmem_limit_bytes=60 * 2**20
        ),
        cost_estimate=pl.CostEstimate(
            flops=12 * micro * slots * width * inner, bytes_accessed=40_000_000, transcendentals=0
        ),
    )(*near.values(), *far.values())
    return types.SimpleNamespace(
        **dict(zip(outs, results, strict=True)), pad_rows=piece * experts
    )


def rope_tables(rows):
    half_width = HEAD_DIM // 2
    frequency = 10000.0 ** (-2.0 * np.arange(half_width, dtype=np.float64) / HEAD_DIM)
    angles = np.arange(rows, dtype=np.float64)[:, None] * frequency[None, :]
    angles = np.tile(angles, (1, LANES // half_width))
    return np.cos(angles).astype(np.float32), np.sin(angles).astype(np.float32)


def local(
    inputs,
    cotangent,
    prev_logits,
    lengths,
    routes,
    slot_order,
    norm_gain1,
    w_query,
    w_key,
    w_value,
    w_out,
    norm_gain2,
    router,
    router_residual,
    const_gate,
    const_value,
    expert_gate,
    expert_up,
    expert_down,
):
    micro, owned, width = inputs.shape
    tensors, peers = lax.axis_size("tensor"), lax.axis_size("expert")
    choices = router.shape[2]
    experts = choices - 4
    assert experts == peers and tensors == 2
    cap = 9 * 2 * owned // (8 * choices) + 1
    cap_pad = -(-cap // 16) * 16
    per_tile = max(d for d in range(1, peers + 1) if peers % d == 0 and d * cap_pad <= 256)
    cfg = types.SimpleNamespace(
        micro=micro,
        owned=owned,
        width=width,
        rows=owned * tensors,
        inner=expert_gate.shape[3],
        heads=w_query.shape[2] // HEAD_DIM,
        experts=experts,
        choices=choices,
        cap=cap,
        cap_pad=cap_pad,
        slots=peers * cap_pad,
        per_tile=per_tile,
        tiles=peers // per_tile,
        tile_rows=per_tile * cap_pad,
        sections=lax.axis_size("section"),
        seqs=lengths.shape[2] - 1,
        chunk=owned,
        small_pad=-(-(choices + 2) // 16) * 16,
    )
    cosine, sine = rope_tables(cfg.rows)
    mixer = jnp.concatenate(
        [router[0].T, const_gate[0], jnp.zeros((LANES - choices - 2, width), f32)], axis=0
    )
    lane_pad = LANES - choices
    ins = dict(
        lengths=lengths[:, 0],
        inputs=inputs,
        cotangent=cotangent,
        prev=jnp.pad(prev_logits[0], ((0, 0), (0, 0), (0, lane_pad))),
        route_col=routes[0],
        route_row=jnp.swapaxes(routes[0], 1, 2),
        order_row=slot_order[0],
        order_col=jnp.swapaxes(slot_order[0], 1, 2),
        gain1=norm_gain1,
        gain2=norm_gain2,
        w_query=w_query[0],
        w_key=w_key[0],
        w_value=w_value[0],
        w_out=w_out[0],
        mixer=mixer,
        residual=jnp.pad(router_residual[0], ((0, lane_pad), (0, lane_pad))),
        const_value=const_value[0],
        cosine=jnp.asarray(cosine),
        sine=jnp.asarray(sine),
        gate=expert_gate[0, 0],
        up=expert_up[0, 0],
        down=expert_down[0, 0],
    )
    got = run_chain(cfg, ins)

    tail = run_tail(cfg, got)
    query_grad, key_grad, value_grad, out_grad = (
        wide(tail.summed[c * tail.pad_rows : c * tail.pad_rows + width]) for c in range(4)
    )
    small = wide(tail.summed[4 * tail.pad_rows :])
    pad = cfg.small_pad
    mixer_grad = jnp.concatenate([small[:pad], small[pad : 2 * pad]], axis=1)
    rows_grad = jnp.concatenate([small[2 * pad : 2 * pad + 8], small[2 * pad + 8 : 2 * pad + 16]], axis=1)
    residual_grad = small[2 * pad + 16 : 3 * pad + 16, :LANES]
    return (
        got.layer_out[None],
        got.input_grad[None],
        got.logit_grad[None, :, :, :choices],
        rows_grad[None, 2],
        query_grad[None],
        key_grad[None],
        value_grad[None],
        out_grad.T[None],
        rows_grad[None, 3],
        mixer_grad[:choices].T[None],
        residual_grad[None, :choices, :choices],
        mixer_grad[None, choices : choices + 2],
        rows_grad[None, :2],
        tail.gate_grad[None, None],
        tail.up_grad[None, None],
        tail.down_grad[None, None],
    )


def solution(mesh):
    tokens = ("expert", "tensor")
    in_specs = (
        P(None, tokens, None),
        P(None, tokens, None),
        P("section", None, tokens, None),
        P(None, "expert", None),
        P("section", None, tokens, None),
        P("section", None, tokens, None),
        P("section", None),
        P("section", None, "tensor"),
        P("section", None, "tensor"),
        P("section", None, "tensor"),
        P("section", "tensor", None),
        P("section", None),
        P("section", None, None),
        P("section", None, None),
        P("section", None, None),
        P("section", None, None),
        P("section", "expert", None, "tensor"),
        P("section", "expert", None, "tensor"),
        P("section", "expert", "tensor", None),
    )
    out_specs = (
        P("section", None, tokens, None),
        P("section", None, tokens, None),
        P("section", None, tokens, None),
        P("section", None),
        P("section", None, "tensor"),
        P("section", None, "tensor"),
        P("section", None, "tensor"),
        P("section", "tensor", None),
        P("section", None),
        P("section", None, None),
        P("section", None, None),
        P("section", None, None),
        P("section", None, None),
        P("section", "expert", None, "tensor"),
        P("section", "expert", None, "tensor"),
        P("section", "expert", "tensor", None),
    )
    return jax.shard_map(local, mesh=mesh, in_specs=in_specs, out_specs=out_specs, check_vma=False)
```

```python
import functools
import types

import jax
import jax.numpy as jnp
import numpy as np
from jax import lax
from jax.experimental import pallas as pl
from jax.experimental.pallas import tpu as pltpu
from jax.sharding import PartitionSpec as P

HEAD_DIM = 64
LANES = 128
EPSILON = 1e-06
MESH = pl.DeviceIdType.MESH
f32, bf16, i32 = jnp.float32, jnp.bfloat16, jnp.int32

P_NORM, P_OUT, P_ROWS, P_PART, P_GROWS, P_GPART, P_DA, P_DX = range(8)


def dot(left, right):
    return jnp.dot(left, right, preferred_element_type=f32)


def dot_nt(left, right):
    return lax.dot_general(left, right, (((1,), (1,)), ((), ())), preferred_element_type=f32)


def dot_tn(left, right):
    return lax.dot_general(left, right, (((0,), (0,)), ((), ())), preferred_element_type=f32)


def wide(values):
    return values.astype(f32)


def halves(values):
    upper = values.astype(bf16)
    return upper, (values - wide(upper)).astype(bf16)


def dot3(how, left, right):
    left_hi, left_lo = halves(left)
    right_hi, right_lo = halves(right)
    return how(left_hi, right_hi) + (how(left_hi, right_lo) + how(left_lo, right_hi))


def inverse_rms(values):
    return lax.rsqrt(jnp.mean(values * values, axis=-1, keepdims=True) + EPSILON)


def iota(shape, dim):
    return lax.broadcasted_iota(i32, shape, dim)


def flag(condition):
    return wide(condition.astype(i32))


def half_lanes(width):
    return (iota((1, width), 1) % HEAD_DIM) < HEAD_DIM // 2


def turned(values, cosine, sine):
    quarter = HEAD_DIM // 2
    other = jnp.where(
        half_lanes(LANES),
        -pltpu.roll(values, LANES - quarter, 1),
        pltpu.roll(values, quarter, 1),
    )
    return values * cosine + other * sine


def turned_back(values, cosine, sine):
    quarter = HEAD_DIM // 2
    other = jnp.where(
        half_lanes(LANES),
        pltpu.roll(values, LANES - quarter, 1),
        -pltpu.roll(values, quarter, 1),
    )
    return values * cosine + other * sine


def chain_kernel(cfg, names, *refs):
    r = types.SimpleNamespace(**dict(zip(names, refs, strict=True)))
    owned, rows, experts, cap, slots = cfg.owned, cfg.rows, cfg.experts, cfg.cap, cfg.slots
    choices, micro, sections, seqs = cfg.choices, cfg.micro, cfg.sections, cfg.seqs
    pairs, chunk = cfg.heads // 2, cfg.chunk
    scale = HEAD_DIM ** (-0.5)
    sec, me, core = (lax.axis_index(a) for a in ("section", "expert", "tensor"))
    other = 1 - core
    own_rows = pl.ds(pl.multiple_of(core * owned, owned), owned)
    other_rows = pl.ds(pl.multiple_of(other * owned, owned), owned)
    is_first, is_last = sec == 0, sec == sections - 1

    def pair(kind, m, j, source, target):
        return pltpu.make_async_remote_copy(
            src_ref=source,
            dst_ref=target,
            send_sem=r.pair_send.at[kind, m, j],
            recv_sem=r.pair_recv.at[kind, m, j],
            device_id={"tensor": other},
            device_id_type=MESH,
        )

    def hop(kind, m, source, target, section):
        return pltpu.make_async_remote_copy(
            src_ref=source,
            dst_ref=target,
            send_sem=r.hop_send.at[kind, m],
            recv_sem=r.hop_recv.at[kind, m],
            device_id={"section": section},
            device_id_type=MESH,
        )

    main, rem, half_rows, rem_rows = cfg.main, cfg.rem, cfg.half_rows, cfg.rem_rows
    rem_start = experts * main
    group = experts // 2
    my_group, in_group = me // group, lax.rem(me, group)
    group_of = (my_group, 1 - my_group)

    def slot_rows(index):
        return pl.ds(pl.multiple_of(index * main, main), main)

    def group_rows(g, offset=0):
        return pl.ds(pl.multiple_of(offset + group_of[g] * half_rows, 16), half_rows)

    def last_rows(offset=0):
        return pl.ds(pl.multiple_of(offset + rem_start, 16), rem_rows)

    def get(ref, g, offset=0, cols=slice(None)):
        value = ref[group_rows(g, offset), cols]
        if g == 1 and rem:
            value = jnp.concatenate([value, ref[last_rows(offset), cols]], axis=0)
        return value

    def put(ref, g, value, offset=0, cols=slice(None)):
        ref[group_rows(g, offset), cols] = value[:half_rows]
        if g == 1 and rem:
            ref[last_rows(offset), cols] = value[half_rows:]

    pieces = -(-half_rows // 256)
    hidden_cols = [
        slice(k * cfg.inner // pieces, (k + 1) * cfg.inner // pieces) for k in range(pieces)
    ]

    def parts(g):
        return [group_rows(g)] + ([last_rows()] if g == 1 and rem else [])

    def peers_in(g, act):
        def step(k, carry):
            act(group_of[g] * group + lax.rem(in_group + k, group))
            return carry

        lax.fori_loop(1 - g, group, step, 0)

    def exchange(kind, m, peer, landed, source, target):
        return pltpu.make_async_remote_copy(
            src_ref=source.at[slot_rows(peer)],
            dst_ref=target.at[slot_rows(landed)],
            send_sem=r.a2a_send.at[kind, m, peer],
            recv_sem=r.a2a_recv.at[kind, m, landed],
            device_id={"expert": peer},
            device_id_type=MESH,
        )

    def exchange_rem(kind, m, peer, landed, source, target):
        return pltpu.make_async_remote_copy(
            src_ref=source.at[peer],
            dst_ref=target.at[landed],
            send_sem=r.rem_send.at[kind, m, peer],
            recv_sem=r.rem_recv.at[kind, m, landed],
            device_id={"expert": peer},
            device_id_type=MESH,
        )

    def lay_rem(ref, value):
        for k in range(rem):
            ref[:, k, :] = value[k * experts : (k + 1) * experts]

    def read_rem(ref):
        value = [ref[:, k, :] for k in range(rem)]
        rest = rem_rows - rem * experts
        if rest:
            value.append(jnp.zeros((rest, cfg.width), f32))
        return jnp.concatenate(value, axis=0).astype(bf16)

    def send_slots(kind, m, value):
        r.outgoing[...] = value[:rem_start].astype(bf16)
        mine = r.arrived.at[core]
        for g in (1, 0):
            peers_in(g, lambda p: exchange(kind, m, p, me, r.outgoing, mine).start())
        if rem:
            lay_rem(r.rem_out, value[rem_start:])
            for g in (1, 0):
                peers_in(g, lambda p: exchange_rem(kind, m, p, me, r.rem_out, r.rem_in).start())
            r.rem_in[pl.ds(me, 1)] = r.rem_out[pl.ds(me, 1)]
        r.arrived[core, slot_rows(me), :] = r.outgoing[slot_rows(me), :]

    def save(index, m, source, target):
        return pltpu.make_async_copy(source, target.at[m], r.local.at[index, m])

    grad_back = r.inside.at[pl.ds(0, slots), pl.ds(0, cfg.width)]
    back_hop = min(1, sections - 2)
    stage = r.partial.at[pl.ds(0, owned)]

    barrier = pltpu.get_barrier_semaphore()

    def greet(k, carry):
        pl.semaphore_signal(
            barrier, inc=1, device_id={"expert": lax.rem(me + k, experts)}, device_id_type=MESH
        )
        return carry

    lax.fori_loop(1, experts, greet, 0)
    pl.semaphore_signal(barrier, inc=1, device_id={"tensor": other}, device_id_type=MESH)

    @pl.when(sec > 0)
    def _():
        pl.semaphore_signal(barrier, inc=1, device_id={"section": sec - 1}, device_id_type=MESH)

    @pl.when(sec < sections - 1)
    def _():
        pl.semaphore_signal(barrier, inc=1, device_id={"section": sec + 1}, device_id_type=MESH)

    for m in range(micro):

        @pl.when(is_first)
        def _():
            save_in = pltpu.make_async_copy(r.inputs.at[m], r.x.at[m], r.local.at[0, m])
            save_in.start()

    weights = [
        pltpu.make_async_copy(source, target, r.fetch.at[k])
        for k, (source, target) in enumerate(
            ((r.gate, r.gate_v), (r.up, r.up_v), (r.down, r.down_v))
        )
    ]
    for copy in weights:
        copy.start()
    beside = (sec > 0).astype(i32) + (sec < sections - 1).astype(i32)
    pl.semaphore_wait(barrier, experts + beside)

    def seq_bias(m):
        row = iota((rows, 1), 0)
        start = jnp.zeros((rows, 1), i32)
        end = r.lengths[m, 0]
        for k in range(seqs):
            start = jnp.where(row >= end, row if k == seqs - 1 else end, start)
            end = end + r.lengths[m, min(k + 1, seqs)]
        for c in range(rows // chunk):
            piece = slice(c * chunk, (c + 1) * chunk)
            key = iota((chunk, rows), 1)
            seen = (key <= row[piece]) & (key >= start[piece])
            r.bias[piece, :] = jnp.where(seen, 0.0, -1e30).astype(bf16)

    def routing(m):
        lane = iota((owned, LANES), 1)
        lane_t = iota((LANES, owned), 0)
        col = [r.route_col[m, :, k : k + 1] for k in range(2)]
        row = [r.route_row[m, k : k + 1, :] for k in range(2)]
        order_row, order_col = r.order_row[m], r.order_col[m]
        hot = [wide((lane == col[k]).astype(i32)) for k in range(2)]
        hot_t = [wide((lane_t == row[k]).astype(i32)) for k in range(2)]
        before = wide((order_row < order_col).astype(i32)).astype(bf16)
        before_t = wide((order_col < order_row).astype(i32)).astype(bf16)
        earlier = dot(before, (hot[0] + hot[1]).astype(bf16))
        earlier_t = dot((hot_t[0] + hot_t[1]).astype(bf16), before_t)
        for k in range(2):
            slot = jnp.sum(earlier * hot[k], axis=1, keepdims=True).astype(i32)
            slot_t = jnp.sum(earlier_t * hot_t[k], axis=0, keepdims=True).astype(i32)

            def placed(choice, at):
                first = choice * main + at
                late = rem_start + (at - main) * experts + choice
                kept = (choice < experts) & (at < cap)
                return jnp.where(kept, jnp.where(at < main, first, late), -1)

            place, place_t = placed(col[k], slot), placed(row[k], slot_t)
            r.place_col[m, :, k : k + 1] = place
            r.place_row[m, k : k + 1, :] = place_t

    def spread(m, k):
        return flag(iota((owned, slots), 1) == r.place_col[m, :, k : k + 1]).astype(bf16)

    def spread_t(m, k):
        return flag(iota((slots, owned), 0) == r.place_row[m, k : k + 1, :]).astype(bf16)

    def choice_flags(m):
        col = [r.route_col[m, :, k : k + 1] for k in range(2)]
        copies = [wide((col[k] == experts + 1).astype(i32)) for k in range(2)]
        consts = [
            [wide((col[k] == experts + 2 + c).astype(i32)) for c in range(2)] for k in range(2)
        ]
        return col, copies, consts

    def unpack_gates(m):
        pack = r.gates[m]
        return [pack[:, k : k + 1] for k in range(2)], [pack[:, 2 + k : 3 + k] for k in range(2)]

    def through_expert(m, kind, pair_in, pair_out, target, kept, compute):
        mine, theirs = r.arrived.at[core], r.arrived.at[other]
        passes = kind // 2

        def keep(index, half, rows_of):
            return pltpu.make_async_copy(
                r.arrived.at[half, rows_of], kept.at[m, half, rows_of], r.keep.at[passes, m, index]
            )

        def forward_pair(g, which, side):
            return [
                pair(pair_in, m, g + k, side.at[rows_of], side.at[rows_of])
                for k, rows_of in enumerate(parts(g))
            ]

        def sums(g):
            return [
                pair(pair_out, m, g + k, r.part_out.at[rows_of], r.part_in.at[rows_of])
                for k, rows_of in enumerate(parts(g))
            ]

        everything = pl.ds(0, slots)
        for g in range(2):
            peers_in(g, lambda p: exchange(kind, m, p, p, r.outgoing, mine).wait_recv())
            if g == 1 and rem:
                for which in range(2):
                    peers_in(which, lambda p: exchange_rem(kind, m, p, p, r.rem_out, r.rem_in).wait_recv())
                r.arrived[core, last_rows(), :] = read_rem(r.rem_in)
            for copy in forward_pair(g, core, mine):
                copy.start()
            kept_mine = [keep(2 * g + k, core, rows_of) for k, rows_of in enumerate(parts(g))]
            for copy in kept_mine:
                copy.start()
            own = compute(core, g)
            put(r.partial, g, own)
            for copy in forward_pair(g, other, theirs):
                copy.wait_recv()
            if g == 1:
                kept_theirs = keep(1, other, everything)
                kept_theirs.start()
            put(r.part_out, g, compute(other, g).astype(bf16))
            if g == 1:
                kept_theirs.wait()
            for copy in sums(g):
                copy.start()
            for copy in sums(g):
                copy.wait_recv()
            value = get(r.partial, g) + wide(get(r.part_in, g))
            for copy in kept_mine:
                copy.wait()
            for copy in forward_pair(g, core, mine):
                copy.wait_send()
            put(r.result, g, value.astype(bf16))
            peers_in(g, lambda p: exchange(kind + 1, m, p, me, r.result, target).start())
            if g == 1 and rem:
                lay_rem(r.rem_result, value[half_rows:])
                for which in (1, 0):
                    peers_in(
                        which,
                        lambda p: exchange_rem(kind + 1, m, p, me, r.rem_result, r.rem_back).start(),
                    )
                r.rem_back[pl.ds(me, 1)] = r.rem_result[pl.ds(me, 1)]
        target[slot_rows(me), :] = r.result[slot_rows(me), :]
        for g in range(2):
            for copy in sums(g):
                copy.wait_send()
            peers_in(g, lambda p: exchange(kind, m, p, me, r.outgoing, mine).wait_send())
            if rem:
                peers_in(g, lambda p: exchange_rem(kind, m, p, me, r.rem_out, r.rem_in).wait_send())

    def wait_back(m, kind, target):
        for g in range(2):
            peers_in(g, lambda p: exchange(kind + 1, m, p, p, r.result, target).wait_recv())
            if rem:
                peers_in(g, lambda p: exchange_rem(kind + 1, m, p, p, r.rem_result, r.rem_back).wait_recv())
        if rem:
            target[last_rows(), :] = read_rem(r.rem_back)
        for g in range(2):
            peers_in(g, lambda p: exchange(kind + 1, m, p, me, r.result, target).wait_send())
            if rem:
                peers_in(g, lambda p: exchange_rem(kind + 1, m, p, me, r.rem_result, r.rem_back).wait_send())

    def forward(m, carry):
        @pl.when(is_first)
        def _():
            pltpu.make_async_copy(r.inputs.at[m], r.x.at[m], r.local.at[0, m]).wait()

        @pl.when(sec > 0)
        def _():
            hop(0, m, r.hop_out, r.hop_in.at[0, m], sec - 1).wait_recv()
            r.x[m] = wide(r.hop_in[0, m])

        x = r.x[m]
        r.norm[m, own_rows, :] = (x * inverse_rms(x) * r.gain1[...]).astype(bf16)
        pair(P_NORM, m, 0, r.norm.at[m, own_rows], r.norm.at[m, own_rows]).start()
        routing(m)
        seq_bias(m)
        pair(P_NORM, m, 0, r.norm.at[m, other_rows], r.norm.at[m, other_rows]).wait_recv()
        save(1, m, r.norm.at[m], r.h_norm).start()

        normed = r.norm[m]
        for stash, weight in ((r.q, r.w_query), (r.k, r.w_key)):
            flat = dot(normed, weight[...])
            for p in range(pairs):
                lanes = slice(p * LANES, (p + 1) * LANES)
                stash[m, :, lanes] = turned(flat[:, lanes], r.cosine[...], r.sine[...]).astype(bf16)
        r.v[m] = dot(normed, r.w_value[...]).astype(bf16)

        r.logsum[m] = jnp.zeros((rows, LANES), f32)
        lane = iota((1, LANES), 1)

        def head_pair(p, inner):
            lanes = pl.ds(pl.multiple_of(p * LANES, LANES), LANES)
            q2, k2, v2 = r.q[m, :, lanes], r.k[m, :, lanes], r.v[m, :, lanes]
            for half in range(2):
                keep = wide(((lane // HEAD_DIM) == half).astype(i32)).astype(bf16)
                km, vm = k2 * keep, v2 * keep
                for c in range(rows // chunk):
                    piece, reach = slice(c * chunk, (c + 1) * chunk), (c + 1) * chunk
                    scores = dot_nt(q2[piece], km[:reach]) * scale + wide(r.bias[piece, :reach])
                    peak = jnp.max(scores, axis=-1, keepdims=True)
                    shifted = jnp.exp(scores - peak)
                    total = jnp.sum(shifted, axis=-1, keepdims=True)
                    probs = (shifted * (1.0 / total)).astype(bf16)
                    mixed = dot(probs, vm[:reach])
                    if half == 0:
                        r.mix[piece, :] = mixed
                    else:
                        r.o[m, piece, lanes] = (r.mix[piece, :] + mixed).astype(bf16)
                    r.logsum[m, piece, :] = jnp.where(
                        lane == 2 * p + half, peak + jnp.log(total), r.logsum[m, piece, :]
                    )
            return inner

        lax.fori_loop(0, pairs, head_pair, 0)
        save(2, m, r.o.at[m], r.h_o).start()

        r.half_out[...] = dot(r.o[m, other_rows, :], r.w_out[...]).astype(bf16)
        pair(P_OUT, m, 0, r.half_out, r.half_in.at[0, m]).start()
        summed = x + dot(r.o[m, own_rows, :], r.w_out[...])
        pair(P_OUT, m, 0, r.half_out, r.half_in.at[0, m]).wait_recv()
        hidden = summed + wide(r.half_in[0, m])
        r.h[m] = hidden
        normed2 = (hidden * inverse_rms(hidden) * r.gain2[...]).astype(bf16)
        r.norm2[m] = normed2

        send_slots(0, m, dot(spread_t(m, 0) + spread_t(m, 1), normed2))

        mixer_hi, mixer_lo = halves(r.mixer[...])
        logits = dot_nt(normed2, mixer_hi) + dot_nt(normed2, mixer_lo)
        logits = logits + dot3(dot, r.prev[m], r.residual[...])
        col, copies, consts = choice_flags(m)
        wide_lane = iota((owned, LANES), 1)
        picked = [
            jnp.sum(jnp.where(wide_lane == col[k], logits, 0.0), axis=1, keepdims=True)
            for k in range(2)
        ]
        gate = [jax.nn.sigmoid(picked[0] - picked[1]), jax.nn.sigmoid(picked[1] - picked[0])]
        rate = [jax.nn.sigmoid(logits[:, choices + c : choices + c + 1]) for c in range(2)]
        pack = jnp.zeros((owned, LANES), f32)
        for k, value in enumerate(gate + rate):
            pack = jnp.where(wide_lane == k, value, pack)
        r.gates[m] = pack

        @pl.when(m == 0)
        def _():
            for copy in weights:
                copy.wait()

        def compute(half, g):
            block = get(r.arrived.at[half], g)
            offset = half * slots
            total = 0.0
            for cols in hidden_cols:
                value = dot(block, r.gate_v[:, cols])
                upper = dot(block, r.up_v[:, cols])
                sig = jax.nn.sigmoid(value)
                active = value * sig
                inside = (active * upper).astype(bf16)
                put(r.by_up, g, active.astype(bf16), offset, cols)
                slope = upper * sig * (1.0 + value * (1.0 - sig))
                put(r.by_gate, g, slope.astype(bf16), offset, cols)
                put(r.inside, g, inside, offset, cols)
                total = total + dot(inside, r.down_v[cols, :])
            return total

        through_expert(m, 0, P_ROWS, P_PART, r.back.at[m], r.h_rows, compute)
        stored = [
            save(10, m, r.inside, r.h_inside),
            save(5, m, r.by_up, r.h_up),
            save(6, m, r.by_gate, r.h_gate),
        ]
        for copy in stored:
            copy.start()
        wait_back(m, 0, r.back.at[m])

        apart = [dot(spread(m, k), r.back[m]) for k in range(2)]
        out = r.h[m] + gate[0] * apart[0] + gate[1] * apart[1]
        own = gate[0] * copies[0] + gate[1] * copies[1]
        for c in range(2):
            on = gate[0] * consts[0][c] + gate[1] * consts[1][c]
            own = own + on * rate[c]
            out = out + (on * (1.0 - rate[c])) * r.const_value[c : c + 1, :]
        out = out + own * wide(r.norm2[m])
        stage[...] = out
        save(3, m, stage, r.layer_out).start()

        @pl.when(sec < sections - 1)
        def _():
            copy = hop(0, m, r.hop_out, r.hop_in.at[0, m], sec + 1)
            r.hop_out[...] = out.astype(bf16)
            copy.start()
            copy.wait_send()

        pair(P_NORM, m, 0, r.norm.at[m, own_rows], r.norm.at[m, own_rows]).wait_send()
        pair(P_OUT, m, 0, r.half_out, r.half_in.at[0, m]).wait_send()
        save(3, m, stage, r.layer_out).wait()
        save(1, m, r.norm.at[m], r.h_norm).wait()
        save(2, m, r.o.at[m], r.h_o).wait()
        for copy in stored:
            copy.wait()
        return carry

    lax.fori_loop(0, micro, forward, 0)

    r.mixer_grad[...] = jnp.zeros_like(r.mixer_grad)
    r.residual_grad[...] = jnp.zeros_like(r.residual_grad)
    r.rows_grad[...] = jnp.zeros_like(r.rows_grad)

    def backward(m, carry):
        fetched = [
            pltpu.make_async_copy(r.h_up.at[m], r.by_up, r.local.at[7, m]),
            pltpu.make_async_copy(r.h_gate.at[m], r.by_gate, r.local.at[8, m]),
        ]
        for copy in fetched:
            copy.start()

        @pl.when(is_last)
        def _():
            copy = pltpu.make_async_copy(r.cotangent.at[m], r.dz, r.local.at[9, m])
            copy.start()
            copy.wait()

        @pl.when(sec < sections - 1)
        def _():
            hop(1, m, r.hop_out, r.hop_in.at[back_hop, m], sec + 1).wait_recv()
            r.dz[...] = wide(r.hop_in[back_hop, m])

        dz = r.dz[...]
        gate, rate = unpack_gates(m)
        leaving = [dot(spread_t(m, k), (gate[k] * dz).astype(bf16)) for k in range(2)]
        send_slots(2, m, leaving[0] + leaving[1])

        col, copies, consts = choice_flags(m)
        normed2 = r.norm2[m]
        dz_norm = jnp.sum(dz * wide(normed2), axis=1, keepdims=True)
        dz_const = [
            jnp.sum(dz * r.const_value[c : c + 1, :], axis=1, keepdims=True) for c in range(2)
        ]
        apart = [dot(spread(m, k), r.back[m]) for k in range(2)]
        dgate = []
        for k in range(2):
            value = jnp.sum(dz * apart[k], axis=1, keepdims=True)
            value = value + copies[k] * dz_norm
            for c in range(2):
                value = value + consts[k][c] * (rate[c] * dz_norm + (1.0 - rate[c]) * dz_const[c])
            dgate.append(value)
        coupled = gate[0] * gate[1] * (dgate[0] - dgate[1])
        lane = iota((owned, LANES), 1)
        dlogits = jnp.where(lane == col[0], coupled, jnp.where(lane == col[1], -coupled, 0.0))
        own = gate[0] * copies[0] + gate[1] * copies[1]
        for c in range(2):
            on = gate[0] * consts[0][c] + gate[1] * consts[1][c]
            own = own + on * rate[c]
            dmix = on * (dz_norm - dz_const[c]) * rate[c] * (1.0 - rate[c])
            dlogits = dlogits + jnp.where(lane == choices + c, dmix, 0.0)
            r.rows_grad[c : c + 1, :] += jnp.sum((on * (1.0 - rate[c])) * dz, axis=0, keepdims=True)
        dlogits_hi, dlogits_lo = halves(dlogits)
        r.mixer_grad[...] += dot_tn(dlogits_hi, normed2) + dot_tn(dlogits_lo, normed2)
        r.residual_grad[...] += dot3(dot_tn, r.prev[m], dlogits)
        r.logit_grad[m] = dot3(dot_nt, dlogits, r.residual[...])
        r.dnorm[...] = dot3(dot, dlogits, r.mixer[...]) + own * dz
        seq_bias(m)
        for copy in fetched:
            copy.wait()

        def compute(half, g):
            block = get(r.arrived.at[half], g)
            offset = half * slots
            total = 0.0
            for cols in hidden_cols:
                dinside = dot_nt(block, r.down_v[cols, :])
                dvalue = (dinside * wide(get(r.by_gate, g, offset, cols))).astype(bf16)
                dupper = (dinside * wide(get(r.by_up, g, offset, cols))).astype(bf16)
                put(r.by_gate, g, dvalue, offset, cols)
                put(r.by_up, g, dupper, offset, cols)
                total = total + dot_nt(dvalue, r.gate_v[:, cols]) + dot_nt(dupper, r.up_v[:, cols])
            return total

        through_expert(m, 2, P_GROWS, P_GPART, grad_back, r.h_grads, compute)
        stored = [
            save(11, m, r.by_up, r.h_up),
            save(12, m, r.by_gate, r.h_gate),
        ]
        for copy in stored:
            copy.start()
        wait_back(m, 2, grad_back)

        both = spread(m, 0) + spread(m, 1)
        dnorm = r.dnorm[...] + dot(both, grad_back[...])
        hidden = r.h[m]
        root = inverse_rms(hidden)
        scaled = dnorm * r.gain2[...]
        pull = root * root * root * jnp.mean(hidden * scaled, axis=-1, keepdims=True)
        dhidden = dz + root * scaled - hidden * pull
        r.rows_grad[3:4, :] += jnp.sum(dnorm * hidden * root, axis=0, keepdims=True)
        r.dh[...] = dhidden
        r.da[own_rows, :] = dhidden.astype(bf16)
        pair(P_DA, m, 0, r.da.at[own_rows], r.da.at[own_rows]).start()
        pair(P_DA, m, 0, r.da.at[other_rows], r.da.at[other_rows]).wait_recv()
        save_da = save(13, m, r.da, r.h_da)
        save_da.start()
        r.do[...] = dot_nt(r.da[...], r.w_out[...]).astype(bf16)

        head_lane = iota((1, LANES), 1)

        def head_pair(p, inner):
            lanes = pl.ds(pl.multiple_of(p * LANES, LANES), LANES)
            q2, k2, v2 = r.q[m, :, lanes], r.k[m, :, lanes], r.v[m, :, lanes]
            do2 = r.do[:, lanes]
            for half in range(2):
                keep = wide(((head_lane // HEAD_DIM) == half).astype(i32)).astype(bf16)
                km, vm, qm, dom = k2 * keep, v2 * keep, q2 * keep, do2 * keep
                for c in range(rows // chunk):
                    piece, reach = slice(c * chunk, (c + 1) * chunk), (c + 1) * chunk
                    scores = dot_nt(q2[piece], km[:reach]) * scale + wide(r.bias[piece, :reach])
                    total = jnp.sum(
                        jnp.where(head_lane == 2 * p + half, r.logsum[m, piece, :], 0.0),
                        axis=1,
                        keepdims=True,
                    )
                    probs = jnp.exp(scores - total)
                    dprobs = dot_nt(do2[piece], vm[:reach])
                    meant = jnp.sum(dprobs * probs, axis=-1, keepdims=True)
                    dscores = (probs * (dprobs - meant)).astype(bf16)
                    dq = dot(dscores, km[:reach])
                    dk = dot_tn(dscores, qm[piece])
                    dv = dot_tn(probs.astype(bf16), dom[piece])
                    if half == 0:
                        r.mix[piece, :] = dq
                    else:
                        r.mix[piece, :] += dq
                    if half == 0 and c == 0:
                        r.mix_k[...] = jnp.zeros_like(r.mix_k)
                        r.mix_v[...] = jnp.zeros_like(r.mix_v)
                    r.mix_k[:reach, :] += dk
                    r.mix_v[:reach, :] += dv
            r.dq[:, lanes] = (turned_back(r.mix[...], r.cosine[...], r.sine[...]) * scale).astype(bf16)
            r.dk[:, lanes] = (turned_back(r.mix_k[...], r.cosine[...], r.sine[...]) * scale).astype(bf16)
            r.dv[:, lanes] = r.mix_v[...].astype(bf16)
            return inner

        lax.fori_loop(0, pairs, head_pair, 0)
        more = [save(14, m, r.dq, r.h_dq), save(15, m, r.dk, r.h_dk), save(16, m, r.dv, r.h_dv)]
        for copy in more:
            copy.start()

        def dnormed(piece):
            return (
                dot_nt(r.dq[piece, :], r.w_query[...])
                + dot_nt(r.dk[piece, :], r.w_key[...])
                + dot_nt(r.dv[piece, :], r.w_value[...])
            )

        r.half_out[...] = dnormed(other_rows).astype(bf16)
        pair(P_DX, m, 0, r.half_out, r.half_in.at[1, m]).start()
        kept = dnormed(own_rows)
        pair(P_DX, m, 0, r.half_out, r.half_in.at[1, m]).wait_recv()
        dnorm1 = kept + wide(r.half_in[1, m])
        x = r.x[m]
        root1 = inverse_rms(x)
        scaled1 = dnorm1 * r.gain1[...]
        pull1 = root1 * root1 * root1 * jnp.mean(x * scaled1, axis=-1, keepdims=True)
        dx = r.dh[...] + root1 * scaled1 - x * pull1
        stage[...] = dx
        save(4, m, stage, r.input_grad).start()

        @pl.when(sec > 0)
        def _():
            copy = hop(1, m, r.hop_out, r.hop_in.at[back_hop, m], sec - 1)
            r.hop_out[...] = dx.astype(bf16)
            copy.start()
            copy.wait_send()

        r.rows_grad[2:3, :] += jnp.sum(dnorm1 * x * root1, axis=0, keepdims=True)
        pair(P_DA, m, 0, r.da.at[own_rows], r.da.at[own_rows]).wait_send()
        pair(P_DX, m, 0, r.half_out, r.half_in.at[1, m]).wait_send()
        save(4, m, stage, r.input_grad).wait()
        save_da.wait()
        for copy in stored + more:
            copy.wait()
        return carry

    lax.fori_loop(0, micro, backward, 0)


def run_chain(cfg, ins):
    vmem, anywhere = pl.BlockSpec(memory_space=pltpu.VMEM), pl.BlockSpec(memory_space=pl.ANY)
    smem = pl.BlockSpec(memory_space=pltpu.SMEM)
    far = {"inputs", "cotangent", "gate", "up", "down"}
    micro, owned, rows, width, inner = cfg.micro, cfg.owned, cfg.rows, cfg.width, cfg.inner
    heads_width, slots = cfg.heads * HEAD_DIM, cfg.slots
    shape = jax.ShapeDtypeStruct
    outs = dict(
        logit_grad=shape((micro, owned, LANES), f32),
        mixer_grad=shape((LANES, width), f32),
        residual_grad=shape((LANES, LANES), f32),
        rows_grad=shape((8, width), f32),
    )
    hbm_outs = dict(
        layer_out=shape((micro, owned, width), f32),
        input_grad=shape((micro, owned, width), f32),
        h_rows=shape((micro, 2, slots, width), bf16),
        h_grads=shape((micro, 2, slots, width), bf16),
        h_inside=shape((micro, 2 * slots, inner), bf16),
        h_up=shape((micro, 2 * slots, inner), bf16),
        h_gate=shape((micro, 2 * slots, inner), bf16),
        h_norm=shape((micro, rows, width), bf16),
        h_da=shape((micro, rows, width), bf16),
        h_o=shape((micro, rows, heads_width), bf16),
        h_dq=shape((micro, rows, heads_width), bf16),
        h_dk=shape((micro, rows, heads_width), bf16),
        h_dv=shape((micro, rows, heads_width), bf16),
    )
    dma = pltpu.SemaphoreType.DMA
    rem_scratch = {}
    if cfg.rem:
        last = pltpu.VMEM((cfg.experts, cfg.rem, width), f32)
        rem_sem = dma((4, micro, cfg.experts))
        rem_scratch = dict(
            rem_out=last, rem_in=last, rem_result=last, rem_back=last, rem_send=rem_sem, rem_recv=rem_sem
        )
    scratch = dict(
        gate_v=pltpu.VMEM((width, inner), bf16),
        up_v=pltpu.VMEM((width, inner), bf16),
        down_v=pltpu.VMEM((inner, width), bf16),
        x=pltpu.VMEM((micro, owned, width), f32),
        h=pltpu.VMEM((micro, owned, width), f32),
        norm=pltpu.VMEM((micro, rows, width), bf16),
        norm2=pltpu.VMEM((micro, owned, width), bf16),
        q=pltpu.VMEM((micro, rows, heads_width), bf16),
        k=pltpu.VMEM((micro, rows, heads_width), bf16),
        v=pltpu.VMEM((micro, rows, heads_width), bf16),
        o=pltpu.VMEM((micro, rows, heads_width), bf16),
        logsum=pltpu.VMEM((micro, rows, LANES), f32),
        gates=pltpu.VMEM((micro, owned, LANES), f32),
        place_col=pltpu.VMEM((micro, owned, 2), i32),
        place_row=pltpu.VMEM((micro, 2, owned), i32),
        bias=pltpu.VMEM((rows, rows), bf16),
        arrived=pltpu.VMEM((2, slots, width), bf16),
        part_in=pltpu.VMEM((slots, width), bf16),
        back=pltpu.VMEM((micro, slots, width), bf16),
        half_in=pltpu.VMEM((2, micro, owned, width), bf16),
        hop_in=pltpu.VMEM((min(2, cfg.sections - 1), micro, owned, width), bf16),
        outgoing=pltpu.VMEM((cfg.experts * cfg.main, width), bf16),
        part_out=pltpu.VMEM((slots, width), bf16),
        result=pltpu.VMEM((slots, width), bf16),
        partial=pltpu.VMEM((max(slots, owned), width), f32),
        half_out=pltpu.VMEM((owned, width), bf16),
        hop_out=pltpu.VMEM((owned, width), bf16),
        inside=pltpu.VMEM((2 * slots, inner), bf16),
        **rem_scratch,
        by_up=pltpu.VMEM((2 * slots, inner), bf16),
        by_gate=pltpu.VMEM((2 * slots, inner), bf16),
        dz=pltpu.VMEM((owned, width), f32),
        dh=pltpu.VMEM((owned, width), f32),
        dnorm=pltpu.VMEM((owned, width), f32),
        da=pltpu.VMEM((rows, width), bf16),
        do=pltpu.VMEM((rows, heads_width), bf16),
        dq=pltpu.VMEM((rows, heads_width), bf16),
        dk=pltpu.VMEM((rows, heads_width), bf16),
        dv=pltpu.VMEM((rows, heads_width), bf16),
        mix=pltpu.VMEM((rows, LANES), f32),
        mix_k=pltpu.VMEM((rows, LANES), f32),
        mix_v=pltpu.VMEM((rows, LANES), f32),
        pair_send=dma((8, micro, 3)),
        pair_recv=dma((8, micro, 3)),
        hop_send=dma((2, micro)),
        hop_recv=dma((2, micro)),
        a2a_send=dma((4, micro, cfg.experts)),
        a2a_recv=dma((4, micro, cfg.experts)),
        local=dma((17, micro)),
        keep=dma((2, micro, 4)),
        fetch=dma((3,)),
    )
    names = [*ins, *outs, *hbm_outs, *scratch]
    flops = 2 * micro * (2 * slots * width * inner * 6 + rows * width * heads_width * 10)
    results = pl.pallas_call(
        functools.partial(chain_kernel, cfg, names),
        out_shape=[*outs.values(), *hbm_outs.values()],
        in_specs=[
            smem if name == "lengths" else anywhere if name in far else vmem for name in ins
        ],
        out_specs=[vmem] * len(outs) + [anywhere] * len(hbm_outs),
        scratch_shapes=[*scratch.values()],
        compiler_params=pltpu.CompilerParams(
            collective_id=0, has_side_effects=True, vmem_limit_bytes=60 * 2**20
        ),
        cost_estimate=pl.CostEstimate(flops=flops, bytes_accessed=50_000_000, transcendentals=0),
    )(*ins.values())
    return types.SimpleNamespace(**dict(zip([*outs, *hbm_outs], results, strict=True)))


def tail_kernel(cfg, names, *refs):
    r = types.SimpleNamespace(**dict(zip(names, refs, strict=True)))
    experts, width, pad = cfg.experts, cfg.width, cfg.small_pad
    side = width // 2
    outer = experts // 2
    me, core = lax.axis_index("expert"), lax.axis_index("tensor")
    mine_out, mine_in = me // 2, lax.rem(me, 2)
    beside = me + 1 - 2 * mine_in
    pieces = len(cfg.piece_rows)
    starts = [sum(cfg.piece_rows[:c]) * experts for c in range(pieces)]

    def peer_of(k):
        place = lax.rem(mine_out + k, outer)
        return place, place * 2 + mine_in

    barrier = pltpu.get_barrier_semaphore()
    pl.semaphore_signal(barrier, inc=1, device_id={"tensor": 1 - core}, device_id_type=MESH)
    pl.semaphore_signal(barrier, inc=1, device_id={"expert": beside}, device_id_type=MESH)

    def greet(k, carry):
        pl.semaphore_signal(barrier, inc=1, device_id={"expert": peer_of(k)[1]}, device_id_type=MESH)
        return carry

    lax.fori_loop(1, outer, greet, 0)

    loads = [
        pltpu.make_async_copy(source, target, r.fetch.at[k])
        for k, (source, target) in enumerate(
            (
                (r.h_rows, r.rows_v),
                (r.h_gate, r.gate_v),
                (r.h_up, r.up_v),
                (r.h_grads, r.grads_v),
                (r.h_inside, r.gate_v),
            )
        )
    ]
    for copy in loads[:4]:
        copy.start()

    r.pack[...] = jnp.zeros_like(r.pack)
    r.pack[:pad, :] = r.mixer_grad[:pad, :side]
    r.pack[pad : 2 * pad, :] = r.mixer_grad[:pad, side:]
    r.pack[2 * pad : 2 * pad + 8, :] = r.rows_grad[:, :side]
    r.pack[2 * pad + 8 : 2 * pad + 16, :] = r.rows_grad[:, side:]
    r.pack[2 * pad + 16 : 3 * pad + 16, :LANES] = r.residual_grad[:pad, :]
    r.pack_out[...] = r.pack[...].astype(bf16)
    pl.semaphore_wait(barrier, outer + 1)
    pack_copy = pltpu.make_async_remote_copy(
        src_ref=r.pack_out,
        dst_ref=r.pack_in,
        send_sem=r.pack_sem.at[0],
        recv_sem=r.pack_sem.at[1],
        device_id={"tensor": 1 - core},
        device_id_type=MESH,
    )
    pack_copy.start()

    def span(start, index, size):
        return pl.ds(pl.multiple_of(start + index * size, 16), size)

    def over_x(stage, c, source, target, from_rows, to_rows):
        return pltpu.make_async_remote_copy(
            src_ref=source.at[from_rows],
            dst_ref=target.at[to_rows],
            send_sem=r.x_send.at[stage, c],
            recv_sem=r.x_recv.at[stage, c],
            device_id={"expert": beside},
            device_id_type=MESH,
        )

    def over_z(stage, c, place, landed, peer, source, target):
        return pltpu.make_async_remote_copy(
            src_ref=source,
            dst_ref=target,
            send_sem=r.z_send.at[stage, c, place],
            recv_sem=r.z_recv.at[stage, c, landed],
            device_id={"expert": peer},
            device_id_type=MESH,
        )

    def half_of(c, which):
        return span(starts[c], which, outer * cfg.piece_rows[c])

    def landing(c):
        return pl.ds(starts[c] // 2, outer * cfg.piece_rows[c])

    def scatter_x(c):
        return over_x(0, c, r.sent, r.x_in, half_of(c, 1 - mine_in), landing(c))

    def gather_x(c, which):
        return over_x(1, c, r.summed, r.summed, half_of(c, which), half_of(c, which))

    def scatter_z(c, place, landed, peer):
        size = cfg.piece_rows[c]
        return over_z(
            0,
            c,
            place,
            landed,
            peer,
            r.z_out.at[span(starts[c] // 2, place, size)],
            r.z_in.at[landed, pl.ds(starts[c] // experts, size)],
        )

    def final(c, place):
        return span(starts[c], mine_in * outer + place, cfg.piece_rows[c])

    def gather_z(c, place, landed, peer):
        rows = final(c, landed)
        return over_z(1, c, place, landed, peer, r.summed.at[rows], r.summed.at[rows])

    def weight_grad(left, right):
        return dot_tn(left.reshape(-1, left.shape[-1]), right.reshape(-1, right.shape[-1]))

    products = ((r.h_norm, r.h_dq), (r.h_norm, r.h_dk), (r.h_norm, r.h_dv), (r.h_da, r.h_o))
    for c in range(pieces):
        rows = pl.ds(starts[c], experts * cfg.piece_rows[c])
        if c < 4:
            left, right = products[c]
            value = weight_grad(left[...], right[...])
            if value.shape[0] != experts * cfg.piece_rows[c]:
                r.sent[rows, :] = jnp.zeros((experts * cfg.piece_rows[c], side), bf16)
            r.sent[pl.ds(starts[c], value.shape[0]), :] = value.astype(bf16)
        else:
            pack_copy.wait()
            r.sent[rows, :] = (r.pack[...] + wide(r.pack_in[...])).astype(bf16)
        scatter_x(c).start()

    rows_all = cfg.micro * 2 * cfg.slots
    tile = 256
    steps = []
    for left, right, target in (
        (r.rows_v, r.gate_v, r.gate_grad),
        (r.rows_v, r.up_v, r.up_grad),
        (r.gate_v, r.grads_v, r.down_grad),
    ):
        for t in range(left.shape[-1] // tile):
            needs = ((0, 1), (0, 2), (3, 4))[len(steps) // (width // tile) if target is not r.down_grad else 2]
            steps.append((left, right, target, t, needs))

    loaded = set()
    flying = [None, None]

    def expert_step(index):
        left, right, target, t, needs = steps[index]
        if index == width // tile:
            loads[4].start()
        for k in needs:
            if k not in loaded:
                loads[k].wait()
                loaded.add(k)
        slot = index % 2
        if flying[slot] is not None:
            flying[slot].wait()
        wide_out = right.shape[-1]
        a = left[..., t * tile : (t + 1) * tile].reshape(rows_all, tile)
        r.stage[slot, :, :wide_out] = dot_tn(a, right[...].reshape(rows_all, wide_out))
        copy = pltpu.make_async_copy(
            r.stage.at[slot, :, pl.ds(0, wide_out)],
            target.at[pl.ds(t * tile, tile)],
            r.step_sem.at[index],
        )
        copy.start()
        flying[slot] = copy

    done = 0
    for c in range(pieces):
        upto = len(steps) * (c + 1) // pieces
        while done < upto:
            expert_step(done)
            done += 1
        scatter_x(c).wait_recv()
        rows = landing(c)
        r.z_out[rows, :] = (wide(r.sent[half_of(c, mine_in), :]) + wide(r.x_in[rows, :])).astype(bf16)

        def out_z(k, carry, c=c):
            place, peer = peer_of(k)
            scatter_z(c, place, mine_out, peer).start()
            return carry

        lax.fori_loop(1, outer, out_z, 0)

    for c in range(pieces):
        size = cfg.piece_rows[c]

        def add_z(k, total, c=c, size=size):
            place, peer = peer_of(k)
            scatter_z(c, place, place, peer).wait_recv()
            return total + wide(r.z_in[place, pl.ds(starts[c] // experts, size), :])

        total = lax.fori_loop(1, outer, add_z, wide(r.z_out[span(starts[c] // 2, mine_out, size), :]))
        r.summed[final(c, mine_out), :] = total.astype(bf16)

        def back_z(k, carry, c=c):
            place, peer = peer_of(k)
            gather_z(c, place, mine_out, peer).start()
            return carry

        lax.fori_loop(1, outer, back_z, 0)

    for c in range(pieces):

        def wait_z(k, carry, c=c):
            place, peer = peer_of(k)
            gather_z(c, place, place, peer).wait_recv()
            return carry

        lax.fori_loop(1, outer, wait_z, 0)
        gather_x(c, mine_in).start()
    for c in range(pieces):
        gather_x(c, 1 - mine_in).wait_recv()
    for c in range(pieces):
        scatter_x(c).wait_send()
        gather_x(c, mine_in).wait_send()

        def sent_z(k, carry, c=c):
            place, peer = peer_of(k)
            scatter_z(c, place, mine_out, peer).wait_send()
            gather_z(c, place, mine_out, peer).wait_send()
            return carry

        lax.fori_loop(1, outer, sent_z, 0)
    for copy in flying:
        copy.wait()


def run_tail(cfg, got):
    vmem, anywhere = pl.BlockSpec(memory_space=pltpu.VMEM), pl.BlockSpec(memory_space=pl.ANY)
    micro, width, inner, slots, experts = cfg.micro, cfg.width, cfg.inner, cfg.slots, cfg.experts
    side, outer = width // 2, experts // 2
    piece = -(-width // (16 * experts)) * 16
    small = -(-(3 * cfg.small_pad + 16) // (16 * experts)) * 16
    cfg.piece_rows = [piece] * 4 + [small]
    total = sum(cfg.piece_rows) * experts
    near = dict(
        h_norm=got.h_norm,
        h_da=got.h_da,
        h_o=got.h_o,
        h_dq=got.h_dq,
        h_dk=got.h_dk,
        h_dv=got.h_dv,
        mixer_grad=got.mixer_grad,
        residual_grad=got.residual_grad,
        rows_grad=got.rows_grad,
    )
    far = dict(
        h_rows=got.h_rows,
        h_grads=got.h_grads,
        h_inside=got.h_inside,
        h_up=got.h_up,
        h_gate=got.h_gate,
    )
    shape, dma = jax.ShapeDtypeStruct, pltpu.SemaphoreType.DMA
    outs = dict(
        summed=shape((total, side), bf16),
        gate_grad=shape((width, inner), f32),
        up_grad=shape((width, inner), f32),
        down_grad=shape((inner, width), f32),
    )
    scratch = dict(
        rows_v=pltpu.VMEM((micro, 2, slots, width), bf16),
        grads_v=pltpu.VMEM((micro, 2, slots, width), bf16),
        up_v=pltpu.VMEM((micro, 2 * slots, inner), bf16),
        gate_v=pltpu.VMEM((micro, 2 * slots, inner), bf16),
        sent=pltpu.VMEM((total, side), bf16),
        x_in=pltpu.VMEM((total // 2, side), bf16),
        z_out=pltpu.VMEM((total // 2, side), bf16),
        z_in=pltpu.VMEM((outer, total // experts, side), bf16),
        pack=pltpu.VMEM((small * experts, side), f32),
        pack_out=pltpu.VMEM((small * experts, side), bf16),
        pack_in=pltpu.VMEM((small * experts, side), bf16),
        stage=pltpu.VMEM((2, 256, max(inner, width)), f32),
        fetch=dma((5,)),
        step_sem=dma(((2 * width + inner) // 256,)),
        pack_sem=dma((2,)),
        x_send=dma((2, 5)),
        x_recv=dma((2, 5)),
        z_send=dma((2, 5, outer)),
        z_recv=dma((2, 5, outer)),
    )
    names = [*near, *far, *outs, *scratch]
    results = pl.pallas_call(
        functools.partial(tail_kernel, cfg, names),
        out_shape=[*outs.values()],
        in_specs=[vmem] * len(near) + [anywhere] * len(far),
        out_specs=[vmem] + [anywhere] * 3,
        scratch_shapes=[*scratch.values()],
        compiler_params=pltpu.CompilerParams(
            collective_id=1, has_side_effects=True, vmem_limit_bytes=60 * 2**20
        ),
        cost_estimate=pl.CostEstimate(
            flops=12 * micro * slots * width * inner, bytes_accessed=40_000_000, transcendentals=0
        ),
    )(*near.values(), *far.values())
    return types.SimpleNamespace(
        **dict(zip(outs, results, strict=True)), pad_rows=piece * experts
    )


def rope_tables(rows):
    half_width = HEAD_DIM // 2
    frequency = 10000.0 ** (-2.0 * np.arange(half_width, dtype=np.float64) / HEAD_DIM)
    angles = np.arange(rows, dtype=np.float64)[:, None] * frequency[None, :]
    angles = np.tile(angles, (1, LANES // half_width))
    return np.cos(angles).astype(np.float32), np.sin(angles).astype(np.float32)


def local(
    inputs,
    cotangent,
    prev_logits,
    lengths,
    routes,
    slot_order,
    norm_gain1,
    w_query,
    w_key,
    w_value,
    w_out,
    norm_gain2,
    router,
    router_residual,
    const_gate,
    const_value,
    expert_gate,
    expert_up,
    expert_down,
):
    micro, owned, width = inputs.shape
    tensors, peers = lax.axis_size("tensor"), lax.axis_size("expert")
    choices = router.shape[2]
    experts = choices - 4
    assert experts == peers and tensors == 2
    cap = 9 * 2 * owned // (8 * choices) + 1
    main, rem = cap // 16 * 16, cap % 16
    if rem > 2 or not main:
        main, rem = main + (16 if rem else 0), 0
    rem_rows = -(-rem * peers // 16) * 16
    cfg = types.SimpleNamespace(
        micro=micro,
        owned=owned,
        width=width,
        rows=owned * tensors,
        inner=expert_gate.shape[3],
        heads=w_query.shape[2] // HEAD_DIM,
        experts=experts,
        choices=choices,
        cap=cap,
        main=main,
        rem=rem,
        rem_rows=rem_rows,
        half_rows=peers // 2 * main,
        slots=peers * main + rem_rows,
        sections=lax.axis_size("section"),
        seqs=lengths.shape[2] - 1,
        chunk=owned,
        small_pad=-(-(choices + 2) // 16) * 16,
    )
    cosine, sine = rope_tables(cfg.rows)
    mixer = jnp.concatenate(
        [router[0].T, const_gate[0], jnp.zeros((LANES - choices - 2, width), f32)], axis=0
    )
    lane_pad = LANES - choices
    ins = dict(
        lengths=lengths[:, 0],
        inputs=inputs,
        cotangent=cotangent,
        prev=jnp.pad(prev_logits[0], ((0, 0), (0, 0), (0, lane_pad))),
        route_col=routes[0],
        route_row=jnp.swapaxes(routes[0], 1, 2),
        order_row=slot_order[0],
        order_col=jnp.swapaxes(slot_order[0], 1, 2),
        gain1=norm_gain1,
        gain2=norm_gain2,
        w_query=w_query[0],
        w_key=w_key[0],
        w_value=w_value[0],
        w_out=w_out[0],
        mixer=mixer,
        residual=jnp.pad(router_residual[0], ((0, lane_pad), (0, lane_pad))),
        const_value=const_value[0],
        cosine=jnp.asarray(cosine),
        sine=jnp.asarray(sine),
        gate=expert_gate[0, 0],
        up=expert_up[0, 0],
        down=expert_down[0, 0],
    )
    got = run_chain(cfg, ins)

    tail = run_tail(cfg, got)
    query_grad, key_grad, value_grad, out_grad = (
        wide(tail.summed[c * tail.pad_rows : c * tail.pad_rows + width]) for c in range(4)
    )
    small = wide(tail.summed[4 * tail.pad_rows :])
    pad = cfg.small_pad
    mixer_grad = jnp.concatenate([small[:pad], small[pad : 2 * pad]], axis=1)
    rows_grad = jnp.concatenate([small[2 * pad : 2 * pad + 8], small[2 * pad + 8 : 2 * pad + 16]], axis=1)
    residual_grad = small[2 * pad + 16 : 3 * pad + 16, :LANES]
    return (
        got.layer_out[None],
        got.input_grad[None],
        got.logit_grad[None, :, :, :choices],
        rows_grad[None, 2],
        query_grad[None],
        key_grad[None],
        value_grad[None],
        out_grad.T[None],
        rows_grad[None, 3],
        mixer_grad[:choices].T[None],
        residual_grad[None, :choices, :choices],
        mixer_grad[None, choices : choices + 2],
        rows_grad[None, :2],
        tail.gate_grad[None, None],
        tail.up_grad[None, None],
        tail.down_grad[None, None],
    )


def solution(mesh):
    tokens = ("expert", "tensor")
    in_specs = (
        P(None, tokens, None),
        P(None, tokens, None),
        P("section", None, tokens, None),
        P(None, "expert", None),
        P("section", None, tokens, None),
        P("section", None, tokens, None),
        P("section", None),
        P("section", None, "tensor"),
        P("section", None, "tensor"),
        P("section", None, "tensor"),
        P("section", "tensor", None),
        P("section", None),
        P("section", None, None),
        P("section", None, None),
        P("section", None, None),
        P("section", None, None),
        P("section", "expert", None, "tensor"),
        P("section", "expert", None, "tensor"),
        P("section", "expert", "tensor", None),
    )
    out_specs = (
        P("section", None, tokens, None),
        P("section", None, tokens, None),
        P("section", None, tokens, None),
        P("section", None),
        P("section", None, "tensor"),
        P("section", None, "tensor"),
        P("section", None, "tensor"),
        P("section", "tensor", None),
        P("section", None),
        P("section", None, None),
        P("section", None, None),
        P("section", None, None),
        P("section", None, None),
        P("section", "expert", None, "tensor"),
        P("section", "expert", None, "tensor"),
        P("section", "expert", "tensor", None),
    )
    return jax.shard_map(local, mesh=mesh, in_specs=in_specs, out_specs=out_specs, check_vma=False)
```

```python
import functools
import types

import jax
import jax.numpy as jnp
import numpy as np
from jax import lax
from jax.experimental import pallas as pl
from jax.experimental.pallas import tpu as pltpu
from jax.sharding import PartitionSpec as P

HEAD_DIM = 64
LANES = 128
EPSILON = 1e-06
MESH = pl.DeviceIdType.MESH
f32, bf16, i32 = jnp.float32, jnp.bfloat16, jnp.int32

P_NORM, P_OUT, P_ROWS, P_PART, P_GROWS, P_GPART, P_DA, P_DX = range(8)


def dot(left, right):
    return jnp.dot(left, right, preferred_element_type=f32)


def dot_nt(left, right):
    return lax.dot_general(left, right, (((1,), (1,)), ((), ())), preferred_element_type=f32)


def dot_tn(left, right):
    return lax.dot_general(left, right, (((0,), (0,)), ((), ())), preferred_element_type=f32)


def wide(values):
    return values.astype(f32)


def halves(values):
    upper = values.astype(bf16)
    return upper, (values - wide(upper)).astype(bf16)


def dot3(how, left, right):
    left_hi, left_lo = halves(left)
    right_hi, right_lo = halves(right)
    return how(left_hi, right_hi) + (how(left_hi, right_lo) + how(left_lo, right_hi))


def inverse_rms(values):
    return lax.rsqrt(jnp.mean(values * values, axis=-1, keepdims=True) + EPSILON)


def iota(shape, dim):
    return lax.broadcasted_iota(i32, shape, dim)


def flag(condition):
    return wide(condition.astype(i32))


def half_lanes(width):
    return (iota((1, width), 1) % HEAD_DIM) < HEAD_DIM // 2


def turned(values, cosine, sine):
    quarter = HEAD_DIM // 2
    other = jnp.where(
        half_lanes(LANES),
        -pltpu.roll(values, LANES - quarter, 1),
        pltpu.roll(values, quarter, 1),
    )
    return values * cosine + other * sine


def turned_back(values, cosine, sine):
    quarter = HEAD_DIM // 2
    other = jnp.where(
        half_lanes(LANES),
        pltpu.roll(values, LANES - quarter, 1),
        -pltpu.roll(values, quarter, 1),
    )
    return values * cosine + other * sine


def chain_kernel(cfg, names, *refs):
    r = types.SimpleNamespace(**dict(zip(names, refs, strict=True)))
    owned, rows, experts, cap, slots = cfg.owned, cfg.rows, cfg.experts, cfg.cap, cfg.slots
    choices, micro, sections, seqs = cfg.choices, cfg.micro, cfg.sections, cfg.seqs
    pairs, chunk = cfg.heads // 2, cfg.chunk
    scale = HEAD_DIM ** (-0.5)
    sec, me, core = (lax.axis_index(a) for a in ("section", "expert", "tensor"))
    other = 1 - core
    own_rows = pl.ds(pl.multiple_of(core * owned, owned), owned)
    other_rows = pl.ds(pl.multiple_of(other * owned, owned), owned)
    is_first, is_last = sec == 0, sec == sections - 1

    deep = cfg.depth == micro

    def slot(m):
        return m if deep else 0

    def pair(kind, m, j, source, target):
        return pltpu.make_async_remote_copy(
            src_ref=source,
            dst_ref=target,
            send_sem=r.pair_send.at[kind, m, j],
            recv_sem=r.pair_recv.at[kind, m, j],
            device_id={"tensor": other},
            device_id_type=MESH,
        )

    def hop(kind, m, source, target, section):
        return pltpu.make_async_remote_copy(
            src_ref=source,
            dst_ref=target,
            send_sem=r.hop_send.at[kind, m],
            recv_sem=r.hop_recv.at[kind, m],
            device_id={"section": section},
            device_id_type=MESH,
        )

    main, rem, half_rows, rem_rows = cfg.main, cfg.rem, cfg.half_rows, cfg.rem_rows
    rem_start = experts * main
    group = experts // 2
    my_group, in_group = me // group, lax.rem(me, group)
    group_of = (my_group, 1 - my_group)

    def slot_rows(index):
        return pl.ds(pl.multiple_of(index * main, main), main)

    def group_rows(g, offset=0):
        return pl.ds(pl.multiple_of(offset + group_of[g] * half_rows, 16), half_rows)

    def last_rows(offset=0):
        return pl.ds(pl.multiple_of(offset + rem_start, 16), rem_rows)

    def get(ref, g, offset=0, cols=slice(None)):
        value = ref[group_rows(g, offset), cols]
        if g == 1 and rem:
            value = jnp.concatenate([value, ref[last_rows(offset), cols]], axis=0)
        return value

    def put(ref, g, value, offset=0, cols=slice(None)):
        ref[group_rows(g, offset), cols] = value[:half_rows]
        if g == 1 and rem:
            ref[last_rows(offset), cols] = value[half_rows:]

    pieces = -(-half_rows // 256)
    hidden_cols = [
        slice(k * cfg.inner // pieces, (k + 1) * cfg.inner // pieces) for k in range(pieces)
    ]

    def parts(g):
        return [group_rows(g)] + ([last_rows()] if g == 1 and rem else [])

    def peers_in(g, act):
        def step(k, carry):
            act(group_of[g] * group + lax.rem(in_group + k, group))
            return carry

        lax.fori_loop(1 - g, group, step, 0)

    def exchange(kind, m, peer, landed, source, target):
        return pltpu.make_async_remote_copy(
            src_ref=source.at[slot_rows(peer)],
            dst_ref=target.at[slot_rows(landed)],
            send_sem=r.a2a_send.at[kind, m, peer],
            recv_sem=r.a2a_recv.at[kind, m, landed],
            device_id={"expert": peer},
            device_id_type=MESH,
        )

    def exchange_rem(kind, m, peer, landed, source, target):
        return pltpu.make_async_remote_copy(
            src_ref=source.at[peer],
            dst_ref=target.at[landed],
            send_sem=r.rem_send.at[kind, m, peer],
            recv_sem=r.rem_recv.at[kind, m, landed],
            device_id={"expert": peer},
            device_id_type=MESH,
        )

    def lay_rem(ref, value):
        for k in range(rem):
            ref[:, k, :] = value[k * experts : (k + 1) * experts]

    def read_rem(ref):
        value = [ref[:, k, :] for k in range(rem)]
        rest = rem_rows - rem * experts
        if rest:
            value.append(jnp.zeros((rest, cfg.width), f32))
        return jnp.concatenate(value, axis=0).astype(bf16)

    def send_slots(kind, m, value):
        d = slot(m)
        outgoing, mine = r.outgoing.at[d], r.arrived.at[d, core]
        r.outgoing[d] = value[:rem_start].astype(bf16)
        for g in (1, 0):
            peers_in(g, lambda p: exchange(kind, m, p, me, outgoing, mine).start())
        if rem:
            rem_out, rem_in = r.rem_out.at[d], r.rem_in.at[d]
            lay_rem(rem_out, value[rem_start:])
            for g in (1, 0):
                peers_in(g, lambda p: exchange_rem(kind, m, p, me, rem_out, rem_in).start())
            rem_in[pl.ds(me, 1)] = rem_out[pl.ds(me, 1)]
        mine[slot_rows(me), :] = outgoing[slot_rows(me), :]

    def save(index, m, source, target):
        return pltpu.make_async_copy(source, target.at[m], r.local.at[index, m])

    def grad_back(m):
        return r.inside.at[slot(m), pl.ds(0, slots), pl.ds(0, cfg.width)]

    back_hop = min(1, sections - 2)
    def stage(m):
        return r.stage.at[m] if deep else r.partial.at[pl.ds(0, owned)]


    barrier = pltpu.get_barrier_semaphore()

    def greet(k, carry):
        pl.semaphore_signal(
            barrier, inc=1, device_id={"expert": lax.rem(me + k, experts)}, device_id_type=MESH
        )
        return carry

    lax.fori_loop(1, experts, greet, 0)
    pl.semaphore_signal(barrier, inc=1, device_id={"tensor": other}, device_id_type=MESH)

    @pl.when(sec > 0)
    def _():
        pl.semaphore_signal(barrier, inc=1, device_id={"section": sec - 1}, device_id_type=MESH)

    @pl.when(sec < sections - 1)
    def _():
        pl.semaphore_signal(barrier, inc=1, device_id={"section": sec + 1}, device_id_type=MESH)

    for m in range(micro):

        @pl.when(is_first)
        def _():
            pltpu.make_async_copy(r.inputs.at[m], r.x.at[m], r.local.at[0, m]).start()

        if deep:

            @pl.when(is_last)
            def _():
                pltpu.make_async_copy(r.cotangent.at[m], r.dz.at[m], r.local.at[9, m]).start()

    weights = [
        pltpu.make_async_copy(source, target, r.fetch.at[k])
        for k, (source, target) in enumerate(
            ((r.gate, r.gate_v), (r.up, r.up_v), (r.down, r.down_v))
        )
    ]
    for copy in weights:
        copy.start()
    beside = (sec > 0).astype(i32) + (sec < sections - 1).astype(i32)
    pl.semaphore_wait(barrier, experts + beside)

    def seq_bias(m):
        row = iota((rows, 1), 0)
        start = jnp.zeros((rows, 1), i32)
        end = r.lengths[m, 0]
        for k in range(seqs):
            start = jnp.where(row >= end, row if k == seqs - 1 else end, start)
            end = end + r.lengths[m, min(k + 1, seqs)]
        for c in range(rows // chunk):
            piece = slice(c * chunk, (c + 1) * chunk)
            key = iota((chunk, rows), 1)
            seen = (key <= row[piece]) & (key >= start[piece])
            r.bias[piece, :] = jnp.where(seen, 0.0, -1e30).astype(bf16)

    def routing(m):
        lane = iota((owned, LANES), 1)
        lane_t = iota((LANES, owned), 0)
        col = [r.route_col[m, :, k : k + 1] for k in range(2)]
        row = [r.route_row[m, k : k + 1, :] for k in range(2)]
        order_row, order_col = r.order_row[m], r.order_col[m]
        hot = [wide((lane == col[k]).astype(i32)) for k in range(2)]
        hot_t = [wide((lane_t == row[k]).astype(i32)) for k in range(2)]
        before = wide((order_row < order_col).astype(i32)).astype(bf16)
        before_t = wide((order_col < order_row).astype(i32)).astype(bf16)
        earlier = dot(before, (hot[0] + hot[1]).astype(bf16))
        earlier_t = dot((hot_t[0] + hot_t[1]).astype(bf16), before_t)
        for k in range(2):
            slot = jnp.sum(earlier * hot[k], axis=1, keepdims=True).astype(i32)
            slot_t = jnp.sum(earlier_t * hot_t[k], axis=0, keepdims=True).astype(i32)

            def placed(choice, at):
                first = choice * main + at
                late = rem_start + (at - main) * experts + choice
                kept = (choice < experts) & (at < cap)
                return jnp.where(kept, jnp.where(at < main, first, late), -1)

            place, place_t = placed(col[k], slot), placed(row[k], slot_t)
            r.place_col[m, :, k : k + 1] = place
            r.place_row[m, k : k + 1, :] = place_t

    def spread(m, k):
        return flag(iota((owned, slots), 1) == r.place_col[m, :, k : k + 1]).astype(bf16)

    def spread_t(m, k):
        return flag(iota((slots, owned), 0) == r.place_row[m, k : k + 1, :]).astype(bf16)

    def choice_flags(m):
        col = [r.route_col[m, :, k : k + 1] for k in range(2)]
        copies = [wide((col[k] == experts + 1).astype(i32)) for k in range(2)]
        consts = [
            [wide((col[k] == experts + 2 + c).astype(i32)) for c in range(2)] for k in range(2)
        ]
        return col, copies, consts

    def unpack_gates(m):
        pack = r.gates[m]
        return [pack[:, k : k + 1] for k in range(2)], [pack[:, 2 + k : 3 + k] for k in range(2)]

    def through_expert(m, kind, pair_in, pair_out, target, kept, compute):
        d = slot(m)
        arrived, outgoing, result = r.arrived.at[d], r.outgoing.at[d], r.result.at[d]
        mine, theirs = arrived.at[core], arrived.at[other]
        if rem:
            rem_out, rem_in = r.rem_out.at[d], r.rem_in.at[d]
            rem_result, rem_back = r.rem_result.at[d], r.rem_back.at[d]
        passes = kind // 2

        def keep(index, half, rows_of):
            return pltpu.make_async_copy(
                arrived.at[half, rows_of], kept.at[m, half, rows_of], r.keep.at[passes, m, index]
            )

        def forward_pair(g, which, side):
            return [
                pair(pair_in, m, g + k, side.at[rows_of], side.at[rows_of])
                for k, rows_of in enumerate(parts(g))
            ]

        def sums(g):
            return [
                pair(pair_out, m, g + k, r.part_out.at[rows_of], r.part_in.at[rows_of])
                for k, rows_of in enumerate(parts(g))
            ]

        everything = pl.ds(0, slots)
        for g in range(2):
            peers_in(g, lambda p: exchange(kind, m, p, p, outgoing, mine).wait_recv())
            if g == 1 and rem:
                for which in range(2):
                    peers_in(which, lambda p: exchange_rem(kind, m, p, p, rem_out, rem_in).wait_recv())
                arrived[core, last_rows(), :] = read_rem(rem_in)
            for copy in forward_pair(g, core, mine):
                copy.start()
            kept_mine = [keep(2 * g + k, core, rows_of) for k, rows_of in enumerate(parts(g))]
            for copy in kept_mine:
                copy.start()
            own = compute(core, g)
            put(r.partial, g, own)
            for copy in forward_pair(g, other, theirs):
                copy.wait_recv()
            if g == 1:
                kept_theirs = keep(1, other, everything)
                kept_theirs.start()
            put(r.part_out, g, compute(other, g).astype(bf16))
            if g == 1:
                kept_theirs.wait()
            for copy in sums(g):
                copy.start()
            for copy in sums(g):
                copy.wait_recv()
            value = get(r.partial, g) + wide(get(r.part_in, g))
            for copy in kept_mine:
                copy.wait()
            for copy in forward_pair(g, core, mine):
                copy.wait_send()
            put(result, g, value.astype(bf16))
            peers_in(g, lambda p: exchange(kind + 1, m, p, me, result, target).start())
            if g == 1 and rem:
                lay_rem(rem_result, value[half_rows:])
                for which in (1, 0):
                    peers_in(
                        which,
                        lambda p: exchange_rem(kind + 1, m, p, me, rem_result, rem_back).start(),
                    )
                rem_back[pl.ds(me, 1)] = rem_result[pl.ds(me, 1)]
        target[slot_rows(me), :] = result[slot_rows(me), :]
        for g in range(2):
            for copy in sums(g):
                copy.wait_send()
            peers_in(g, lambda p: exchange(kind, m, p, me, outgoing, mine).wait_send())
            if rem:
                peers_in(g, lambda p: exchange_rem(kind, m, p, me, rem_out, rem_in).wait_send())

    def wait_back(m, kind, target):
        result = r.result.at[slot(m)]
        if rem:
            rem_result, rem_back = r.rem_result.at[slot(m)], r.rem_back.at[slot(m)]
        for g in range(2):
            peers_in(g, lambda p: exchange(kind + 1, m, p, p, result, target).wait_recv())
            if rem:
                peers_in(g, lambda p: exchange_rem(kind + 1, m, p, p, rem_result, rem_back).wait_recv())
        if rem:
            target[last_rows(), :] = read_rem(rem_back)
        for g in range(2):
            peers_in(g, lambda p: exchange(kind + 1, m, p, me, result, target).wait_send())
            if rem:
                peers_in(g, lambda p: exchange_rem(kind + 1, m, p, me, rem_result, rem_back).wait_send())

    def attend(m):
        @pl.when(is_first)
        def _():
            pltpu.make_async_copy(r.inputs.at[m], r.x.at[m], r.local.at[0, m]).wait()

        @pl.when(sec > 0)
        def _():
            hop(0, m, r.hop_out.at[slot(m)], r.hop_in.at[0, m], sec - 1).wait_recv()
            r.x[m] = wide(r.hop_in[0, m])

        x = r.x[m]
        r.norm[m, own_rows, :] = (x * inverse_rms(x) * r.gain1[...]).astype(bf16)
        pair(P_NORM, m, 0, r.norm.at[m, own_rows], r.norm.at[m, own_rows]).start()
        routing(m)
        seq_bias(m)
        pair(P_NORM, m, 0, r.norm.at[m, other_rows], r.norm.at[m, other_rows]).wait_recv()
        save(1, m, r.norm.at[m], r.h_norm).start()

        normed = r.norm[m]
        for stash, weight in ((r.q, r.w_query), (r.k, r.w_key)):
            flat = dot(normed, weight[...])
            for p in range(pairs):
                lanes = slice(p * LANES, (p + 1) * LANES)
                stash[m, :, lanes] = turned(flat[:, lanes], r.cosine[...], r.sine[...]).astype(bf16)
        r.v[m] = dot(normed, r.w_value[...]).astype(bf16)

        r.logsum[m] = jnp.zeros((rows, LANES), f32)
        lane = iota((1, LANES), 1)

        def head_pair(p, inner):
            lanes = pl.ds(pl.multiple_of(p * LANES, LANES), LANES)
            q2, k2, v2 = r.q[m, :, lanes], r.k[m, :, lanes], r.v[m, :, lanes]
            for half in range(2):
                keep = wide(((lane // HEAD_DIM) == half).astype(i32)).astype(bf16)
                km, vm = k2 * keep, v2 * keep
                for c in range(rows // chunk):
                    piece, reach = slice(c * chunk, (c + 1) * chunk), (c + 1) * chunk
                    scores = dot_nt(q2[piece], km[:reach]) * scale + wide(r.bias[piece, :reach])
                    peak = jnp.max(scores, axis=-1, keepdims=True)
                    shifted = jnp.exp(scores - peak)
                    total = jnp.sum(shifted, axis=-1, keepdims=True)
                    probs = (shifted * (1.0 / total)).astype(bf16)
                    mixed = dot(probs, vm[:reach])
                    if half == 0:
                        r.mix[piece, :] = mixed
                    else:
                        r.o[m, piece, lanes] = (r.mix[piece, :] + mixed).astype(bf16)
                    r.logsum[m, piece, :] = jnp.where(
                        lane == 2 * p + half, peak + jnp.log(total), r.logsum[m, piece, :]
                    )
            return inner

        lax.fori_loop(0, pairs, head_pair, 0)
        save(2, m, r.o.at[m], r.h_o).start()

        r.half_out[...] = dot(r.o[m, other_rows, :], r.w_out[...]).astype(bf16)
        pair(P_OUT, m, 0, r.half_out, r.half_in.at[0, m]).start()
        summed = x + dot(r.o[m, own_rows, :], r.w_out[...])
        pair(P_OUT, m, 0, r.half_out, r.half_in.at[0, m]).wait_recv()
        hidden = summed + wide(r.half_in[0, m])
        r.h[m] = hidden
        normed2 = (hidden * inverse_rms(hidden) * r.gain2[...]).astype(bf16)
        r.norm2[m] = normed2

        send_slots(0, m, dot(spread_t(m, 0) + spread_t(m, 1), normed2))

        mixer_hi, mixer_lo = halves(r.mixer[...])
        logits = dot_nt(normed2, mixer_hi) + dot_nt(normed2, mixer_lo)
        logits = logits + dot3(dot, r.prev[m], r.residual[...])
        col, copies, consts = choice_flags(m)
        wide_lane = iota((owned, LANES), 1)
        picked = [
            jnp.sum(jnp.where(wide_lane == col[k], logits, 0.0), axis=1, keepdims=True)
            for k in range(2)
        ]
        gate = [jax.nn.sigmoid(picked[0] - picked[1]), jax.nn.sigmoid(picked[1] - picked[0])]
        rate = [jax.nn.sigmoid(logits[:, choices + c : choices + c + 1]) for c in range(2)]
        pack = jnp.zeros((owned, LANES), f32)
        for k, value in enumerate(gate + rate):
            pack = jnp.where(wide_lane == k, value, pack)
        r.gates[m] = pack
        pair(P_NORM, m, 0, r.norm.at[m, own_rows], r.norm.at[m, own_rows]).wait_send()
        pair(P_OUT, m, 0, r.half_out, r.half_in.at[0, m]).wait_send()

    def kept_forward(m):
        copies = [save(10, m, r.inside.at[slot(m)], r.h_inside)]
        if not deep:
            copies += [
                save(5, m, r.by_up.at[0], r.h_up),
                save(6, m, r.by_gate.at[0], r.h_gate),
            ]
        return copies

    def experts_forward(m):
        d = slot(m)
        by_up, by_gate, inside_of, arrived = r.by_up.at[d], r.by_gate.at[d], r.inside.at[d], r.arrived.at[d]

        @pl.when(m == 0)
        def _():
            for copy in weights:
                copy.wait()

        def compute(half, g):
            block = get(arrived.at[half], g)
            offset = half * slots
            total = 0.0
            for cols in hidden_cols:
                value = dot(block, r.gate_v[:, cols])
                upper = dot(block, r.up_v[:, cols])
                sig = jax.nn.sigmoid(value)
                active = value * sig
                inside = (active * upper).astype(bf16)
                put(by_up, g, active.astype(bf16), offset, cols)
                slope = upper * sig * (1.0 + value * (1.0 - sig))
                put(by_gate, g, slope.astype(bf16), offset, cols)
                put(inside_of, g, inside, offset, cols)
                total = total + dot(inside, r.down_v[cols, :])
            return total

        through_expert(m, 0, P_ROWS, P_PART, r.back.at[m], r.h_rows, compute)
        for copy in kept_forward(m):
            copy.start()

    def combine(m):
        gate, rate = unpack_gates(m)
        col, copies, consts = choice_flags(m)
        wait_back(m, 0, r.back.at[m])

        apart = [dot(spread(m, k), r.back[m]) for k in range(2)]
        out = r.h[m] + gate[0] * apart[0] + gate[1] * apart[1]
        own = gate[0] * copies[0] + gate[1] * copies[1]
        for c in range(2):
            on = gate[0] * consts[0][c] + gate[1] * consts[1][c]
            own = own + on * rate[c]
            out = out + (on * (1.0 - rate[c])) * r.const_value[c : c + 1, :]
        out = out + own * wide(r.norm2[m])
        stage(m)[...] = out
        save(3, m, stage(m), r.layer_out).start()

        @pl.when(sec < sections - 1)
        def _():
            r.hop_out[slot(m)] = out.astype(bf16)
            hop(0, m, r.hop_out.at[slot(m)], r.hop_in.at[0, m], sec + 1).start()

    def settle_forward(m):
        @pl.when(sec < sections - 1)
        def _():
            hop(0, m, r.hop_out.at[slot(m)], r.hop_in.at[0, m], sec + 1).wait_send()

        save(3, m, stage(m), r.layer_out).wait()
        save(1, m, r.norm.at[m], r.h_norm).wait()
        save(2, m, r.o.at[m], r.h_o).wait()
        for copy in kept_forward(m):
            copy.wait()

    def each(*phases):
        def run(chosen):
            def step(m, carry):
                for phase in chosen:
                    phase(m)
                return carry

            lax.fori_loop(0, micro, step, 0)

        for chosen in [[phase] for phase in phases] if deep else [phases]:
            run(chosen)

    each(attend, experts_forward, combine, settle_forward)

    r.mixer_grad[...] = jnp.zeros_like(r.mixer_grad)
    r.residual_grad[...] = jnp.zeros_like(r.residual_grad)
    r.rows_grad[...] = jnp.zeros_like(r.rows_grad)

    def fetched(m):
        return [
            pltpu.make_async_copy(r.h_up.at[m], r.by_up.at[0], r.local.at[7, m]),
            pltpu.make_async_copy(r.h_gate.at[m], r.by_gate.at[0], r.local.at[8, m]),
        ]

    def grad_start(m):
        d = slot(m)
        if not deep:
            for copy in fetched(m):
                copy.start()

        @pl.when(is_last)
        def _():
            copy = pltpu.make_async_copy(r.cotangent.at[m], r.dz.at[d], r.local.at[9, m])
            if not deep:
                copy.start()
            copy.wait()

        @pl.when(sec < sections - 1)
        def _():
            hop(1, m, r.hop_out.at[d], r.hop_in.at[back_hop, m], sec + 1).wait_recv()
            r.dz[d] = wide(r.hop_in[back_hop, m])

        dz = r.dz[d]
        gate, rate = unpack_gates(m)
        leaving = [dot(spread_t(m, k), (gate[k] * dz).astype(bf16)) for k in range(2)]
        send_slots(2, m, leaving[0] + leaving[1])

        col, copies, consts = choice_flags(m)
        normed2 = r.norm2[m]
        dz_norm = jnp.sum(dz * wide(normed2), axis=1, keepdims=True)
        dz_const = [
            jnp.sum(dz * r.const_value[c : c + 1, :], axis=1, keepdims=True) for c in range(2)
        ]
        apart = [dot(spread(m, k), r.back[m]) for k in range(2)]
        dgate = []
        for k in range(2):
            value = jnp.sum(dz * apart[k], axis=1, keepdims=True)
            value = value + copies[k] * dz_norm
            for c in range(2):
                value = value + consts[k][c] * (rate[c] * dz_norm + (1.0 - rate[c]) * dz_const[c])
            dgate.append(value)
        coupled = gate[0] * gate[1] * (dgate[0] - dgate[1])
        lane = iota((owned, LANES), 1)
        dlogits = jnp.where(lane == col[0], coupled, jnp.where(lane == col[1], -coupled, 0.0))
        own = gate[0] * copies[0] + gate[1] * copies[1]
        for c in range(2):
            on = gate[0] * consts[0][c] + gate[1] * consts[1][c]
            own = own + on * rate[c]
            dmix = on * (dz_norm - dz_const[c]) * rate[c] * (1.0 - rate[c])
            dlogits = dlogits + jnp.where(lane == choices + c, dmix, 0.0)
            r.rows_grad[c : c + 1, :] += jnp.sum((on * (1.0 - rate[c])) * dz, axis=0, keepdims=True)
        dlogits_hi, dlogits_lo = halves(dlogits)
        r.mixer_grad[...] += dot_tn(dlogits_hi, normed2) + dot_tn(dlogits_lo, normed2)
        r.residual_grad[...] += dot3(dot_tn, r.prev[m], dlogits)
        r.logit_grad[m] = dot3(dot_nt, dlogits, r.residual[...])
        r.dnorm[d] = dot3(dot, dlogits, r.mixer[...]) + own * dz

    def kept_backward(m):
        return [
            save(11, m, r.by_up.at[slot(m)], r.h_up),
            save(12, m, r.by_gate.at[slot(m)], r.h_gate),
        ]

    def experts_backward(m):
        d = slot(m)
        by_up, by_gate, arrived = r.by_up.at[d], r.by_gate.at[d], r.arrived.at[d]
        if not deep:
            for copy in fetched(m):
                copy.wait()

        def compute(half, g):
            block = get(arrived.at[half], g)
            offset = half * slots
            total = 0.0
            for cols in hidden_cols:
                dinside = dot_nt(block, r.down_v[cols, :])
                dvalue = (dinside * wide(get(by_gate, g, offset, cols))).astype(bf16)
                dupper = (dinside * wide(get(by_up, g, offset, cols))).astype(bf16)
                put(by_gate, g, dvalue, offset, cols)
                put(by_up, g, dupper, offset, cols)
                total = total + dot_nt(dvalue, r.gate_v[:, cols]) + dot_nt(dupper, r.up_v[:, cols])
            return total

        through_expert(m, 2, P_GROWS, P_GPART, grad_back(m), r.h_grads, compute)
        for copy in kept_backward(m):
            copy.start()

    def grad_finish(m):
        d = slot(m)
        seq_bias(m)
        wait_back(m, 2, grad_back(m))

        both = spread(m, 0) + spread(m, 1)
        dnorm = r.dnorm[d] + dot(both, grad_back(m)[...])
        hidden = r.h[m]
        root = inverse_rms(hidden)
        scaled = dnorm * r.gain2[...]
        pull = root * root * root * jnp.mean(hidden * scaled, axis=-1, keepdims=True)
        dhidden = r.dz[d] + root * scaled - hidden * pull
        r.rows_grad[3:4, :] += jnp.sum(dnorm * hidden * root, axis=0, keepdims=True)
        r.dh[...] = dhidden
        r.da[own_rows, :] = dhidden.astype(bf16)
        pair(P_DA, m, 0, r.da.at[own_rows], r.da.at[own_rows]).start()
        pair(P_DA, m, 0, r.da.at[other_rows], r.da.at[other_rows]).wait_recv()
        save_da = save(13, m, r.da, r.h_da)
        save_da.start()
        r.do[...] = dot_nt(r.da[...], r.w_out[...]).astype(bf16)

        head_lane = iota((1, LANES), 1)

        def head_pair(p, inner):
            lanes = pl.ds(pl.multiple_of(p * LANES, LANES), LANES)
            q2, k2, v2 = r.q[m, :, lanes], r.k[m, :, lanes], r.v[m, :, lanes]
            do2 = r.do[:, lanes]
            for half in range(2):
                keep = wide(((head_lane // HEAD_DIM) == half).astype(i32)).astype(bf16)
                km, vm, qm, dom = k2 * keep, v2 * keep, q2 * keep, do2 * keep
                for c in range(rows // chunk):
                    piece, reach = slice(c * chunk, (c + 1) * chunk), (c + 1) * chunk
                    scores = dot_nt(q2[piece], km[:reach]) * scale + wide(r.bias[piece, :reach])
                    total = jnp.sum(
                        jnp.where(head_lane == 2 * p + half, r.logsum[m, piece, :], 0.0),
                        axis=1,
                        keepdims=True,
                    )
                    probs = jnp.exp(scores - total)
                    dprobs = dot_nt(do2[piece], vm[:reach])
                    meant = jnp.sum(dprobs * probs, axis=-1, keepdims=True)
                    dscores = (probs * (dprobs - meant)).astype(bf16)
                    dq = dot(dscores, km[:reach])
                    dk = dot_tn(dscores, qm[piece])
                    dv = dot_tn(probs.astype(bf16), dom[piece])
                    if half == 0:
                        r.mix[piece, :] = dq
                    else:
                        r.mix[piece, :] += dq
                    if half == 0 and c == 0:
                        r.mix_k[...] = jnp.zeros_like(r.mix_k)
                        r.mix_v[...] = jnp.zeros_like(r.mix_v)
                    r.mix_k[:reach, :] += dk
                    r.mix_v[:reach, :] += dv
            r.dq[:, lanes] = (turned_back(r.mix[...], r.cosine[...], r.sine[...]) * scale).astype(bf16)
            r.dk[:, lanes] = (turned_back(r.mix_k[...], r.cosine[...], r.sine[...]) * scale).astype(bf16)
            r.dv[:, lanes] = r.mix_v[...].astype(bf16)
            return inner

        lax.fori_loop(0, pairs, head_pair, 0)
        more = [save(14, m, r.dq, r.h_dq), save(15, m, r.dk, r.h_dk), save(16, m, r.dv, r.h_dv)]
        for copy in more:
            copy.start()

        def dnormed(piece):
            return (
                dot_nt(r.dq[piece, :], r.w_query[...])
                + dot_nt(r.dk[piece, :], r.w_key[...])
                + dot_nt(r.dv[piece, :], r.w_value[...])
            )

        save_da.wait()
        r.half_out[...] = dnormed(other_rows).astype(bf16)
        pair(P_DX, m, 0, r.half_out, r.half_in.at[1, m]).start()
        kept = dnormed(own_rows)
        pair(P_DX, m, 0, r.half_out, r.half_in.at[1, m]).wait_recv()
        dnorm1 = kept + wide(r.half_in[1, m])
        x = r.x[m]
        root1 = inverse_rms(x)
        scaled1 = dnorm1 * r.gain1[...]
        pull1 = root1 * root1 * root1 * jnp.mean(x * scaled1, axis=-1, keepdims=True)
        dx = r.dh[...] + root1 * scaled1 - x * pull1
        stage(m)[...] = dx
        save(4, m, stage(m), r.input_grad).start()

        @pl.when(sec > 0)
        def _():
            r.hop_out[d] = dx.astype(bf16)
            hop(1, m, r.hop_out.at[d], r.hop_in.at[back_hop, m], sec - 1).start()

        r.rows_grad[2:3, :] += jnp.sum(dnorm1 * x * root1, axis=0, keepdims=True)
        pair(P_DA, m, 0, r.da.at[own_rows], r.da.at[own_rows]).wait_send()
        pair(P_DX, m, 0, r.half_out, r.half_in.at[1, m]).wait_send()
        for copy in more:
            copy.wait()

    def settle_backward(m):
        @pl.when(sec > 0)
        def _():
            hop(1, m, r.hop_out.at[slot(m)], r.hop_in.at[back_hop, m], sec - 1).wait_send()

        save(4, m, stage(m), r.input_grad).wait()
        for copy in kept_backward(m):
            copy.wait()

    each(grad_start, experts_backward, grad_finish, settle_backward)


def run_chain(cfg, ins):
    vmem, anywhere = pl.BlockSpec(memory_space=pltpu.VMEM), pl.BlockSpec(memory_space=pl.ANY)
    smem = pl.BlockSpec(memory_space=pltpu.SMEM)
    far = {"inputs", "cotangent", "gate", "up", "down"}
    micro, owned, rows, width, inner = cfg.micro, cfg.owned, cfg.rows, cfg.width, cfg.inner
    heads_width, slots = cfg.heads * HEAD_DIM, cfg.slots
    shape = jax.ShapeDtypeStruct
    outs = dict(
        logit_grad=shape((micro, owned, LANES), f32),
        mixer_grad=shape((LANES, width), f32),
        residual_grad=shape((LANES, LANES), f32),
        rows_grad=shape((8, width), f32),
    )
    hbm_outs = dict(
        layer_out=shape((micro, owned, width), f32),
        input_grad=shape((micro, owned, width), f32),
        h_rows=shape((micro, 2, slots, width), bf16),
        h_grads=shape((micro, 2, slots, width), bf16),
        h_inside=shape((micro, 2 * slots, inner), bf16),
        h_up=shape((micro, 2 * slots, inner), bf16),
        h_gate=shape((micro, 2 * slots, inner), bf16),
        h_norm=shape((micro, rows, width), bf16),
        h_da=shape((micro, rows, width), bf16),
        h_o=shape((micro, rows, heads_width), bf16),
        h_dq=shape((micro, rows, heads_width), bf16),
        h_dk=shape((micro, rows, heads_width), bf16),
        h_dv=shape((micro, rows, heads_width), bf16),
    )
    dma = pltpu.SemaphoreType.DMA
    depth = cfg.depth
    rem_scratch = {}
    if depth == micro:
        rem_scratch = dict(stage=pltpu.VMEM((micro, owned, width), f32))
    if cfg.rem:
        last = pltpu.VMEM((depth, cfg.experts, cfg.rem, width), f32)
        rem_sem = dma((4, micro, cfg.experts))
        rem_scratch |= dict(
            rem_out=last, rem_in=last, rem_result=last, rem_back=last, rem_send=rem_sem, rem_recv=rem_sem
        )
    scratch = dict(
        gate_v=pltpu.VMEM((width, inner), bf16),
        up_v=pltpu.VMEM((width, inner), bf16),
        down_v=pltpu.VMEM((inner, width), bf16),
        x=pltpu.VMEM((micro, owned, width), f32),
        h=pltpu.VMEM((micro, owned, width), f32),
        norm=pltpu.VMEM((micro, rows, width), bf16),
        norm2=pltpu.VMEM((micro, owned, width), bf16),
        q=pltpu.VMEM((micro, rows, heads_width), bf16),
        k=pltpu.VMEM((micro, rows, heads_width), bf16),
        v=pltpu.VMEM((micro, rows, heads_width), bf16),
        o=pltpu.VMEM((micro, rows, heads_width), bf16),
        logsum=pltpu.VMEM((micro, rows, LANES), f32),
        gates=pltpu.VMEM((micro, owned, LANES), f32),
        place_col=pltpu.VMEM((micro, owned, 2), i32),
        place_row=pltpu.VMEM((micro, 2, owned), i32),
        bias=pltpu.VMEM((rows, rows), bf16),
        arrived=pltpu.VMEM((depth, 2, slots, width), bf16),
        part_in=pltpu.VMEM((slots, width), bf16),
        back=pltpu.VMEM((micro, slots, width), bf16),
        half_in=pltpu.VMEM((2, micro, owned, width), bf16),
        hop_in=pltpu.VMEM((min(2, cfg.sections - 1), micro, owned, width), bf16),
        outgoing=pltpu.VMEM((depth, cfg.experts * cfg.main, width), bf16),
        part_out=pltpu.VMEM((slots, width), bf16),
        result=pltpu.VMEM((depth, slots, width), bf16),
        partial=pltpu.VMEM((max(slots, owned), width), f32),
        half_out=pltpu.VMEM((owned, width), bf16),
        hop_out=pltpu.VMEM((depth, owned, width), bf16),
        inside=pltpu.VMEM((depth, 2 * slots, inner), bf16),
        **rem_scratch,
        by_up=pltpu.VMEM((depth, 2 * slots, inner), bf16),
        by_gate=pltpu.VMEM((depth, 2 * slots, inner), bf16),
        dz=pltpu.VMEM((depth, owned, width), f32),
        dh=pltpu.VMEM((owned, width), f32),
        dnorm=pltpu.VMEM((depth, owned, width), f32),
        da=pltpu.VMEM((rows, width), bf16),
        do=pltpu.VMEM((rows, heads_width), bf16),
        dq=pltpu.VMEM((rows, heads_width), bf16),
        dk=pltpu.VMEM((rows, heads_width), bf16),
        dv=pltpu.VMEM((rows, heads_width), bf16),
        mix=pltpu.VMEM((rows, LANES), f32),
        mix_k=pltpu.VMEM((rows, LANES), f32),
        mix_v=pltpu.VMEM((rows, LANES), f32),
        pair_send=dma((8, micro, 3)),
        pair_recv=dma((8, micro, 3)),
        hop_send=dma((2, micro)),
        hop_recv=dma((2, micro)),
        a2a_send=dma((4, micro, cfg.experts)),
        a2a_recv=dma((4, micro, cfg.experts)),
        local=dma((17, micro)),
        keep=dma((2, micro, 4)),
        fetch=dma((3,)),
    )
    names = [*ins, *outs, *hbm_outs, *scratch]
    flops = 2 * micro * (2 * slots * width * inner * 6 + rows * width * heads_width * 10)
    results = pl.pallas_call(
        functools.partial(chain_kernel, cfg, names),
        out_shape=[*outs.values(), *hbm_outs.values()],
        in_specs=[
            smem if name == "lengths" else anywhere if name in far else vmem for name in ins
        ],
        out_specs=[vmem] * len(outs) + [anywhere] * len(hbm_outs),
        scratch_shapes=[*scratch.values()],
        compiler_params=pltpu.CompilerParams(
            collective_id=0, has_side_effects=True, vmem_limit_bytes=60 * 2**20
        ),
        cost_estimate=pl.CostEstimate(flops=flops, bytes_accessed=50_000_000, transcendentals=0),
    )(*ins.values())
    return types.SimpleNamespace(**dict(zip([*outs, *hbm_outs], results, strict=True)))


def tail_kernel(cfg, names, *refs):
    r = types.SimpleNamespace(**dict(zip(names, refs, strict=True)))
    experts, width, pad = cfg.experts, cfg.width, cfg.small_pad
    side = width // 2
    outer = experts // 2
    me, core = lax.axis_index("expert"), lax.axis_index("tensor")
    mine_out, mine_in = me // 2, lax.rem(me, 2)
    beside = me + 1 - 2 * mine_in
    pieces = len(cfg.piece_rows)
    starts = [sum(cfg.piece_rows[:c]) * experts for c in range(pieces)]

    def peer_of(k):
        place = lax.rem(mine_out + k, outer)
        return place, place * 2 + mine_in

    barrier = pltpu.get_barrier_semaphore()
    pl.semaphore_signal(barrier, inc=1, device_id={"tensor": 1 - core}, device_id_type=MESH)
    pl.semaphore_signal(barrier, inc=1, device_id={"expert": beside}, device_id_type=MESH)

    def greet(k, carry):
        pl.semaphore_signal(barrier, inc=1, device_id={"expert": peer_of(k)[1]}, device_id_type=MESH)
        return carry

    lax.fori_loop(1, outer, greet, 0)

    loads = [
        pltpu.make_async_copy(source, target, r.fetch.at[k])
        for k, (source, target) in enumerate(
            (
                (r.h_rows, r.rows_v),
                (r.h_gate, r.gate_v),
                (r.h_up, r.up_v),
                (r.h_grads, r.grads_v),
                (r.h_inside, r.gate_v),
            )
        )
    ]
    for copy in loads[:4]:
        copy.start()

    r.pack[...] = jnp.zeros_like(r.pack)
    r.pack[:pad, :] = r.mixer_grad[:pad, :side]
    r.pack[pad : 2 * pad, :] = r.mixer_grad[:pad, side:]
    r.pack[2 * pad : 2 * pad + 8, :] = r.rows_grad[:, :side]
    r.pack[2 * pad + 8 : 2 * pad + 16, :] = r.rows_grad[:, side:]
    r.pack[2 * pad + 16 : 3 * pad + 16, :LANES] = r.residual_grad[:pad, :]
    r.pack_out[...] = r.pack[...].astype(bf16)
    pl.semaphore_wait(barrier, outer + 1)
    pack_copy = pltpu.make_async_remote_copy(
        src_ref=r.pack_out,
        dst_ref=r.pack_in,
        send_sem=r.pack_sem.at[0],
        recv_sem=r.pack_sem.at[1],
        device_id={"tensor": 1 - core},
        device_id_type=MESH,
    )
    pack_copy.start()

    def span(start, index, size):
        return pl.ds(pl.multiple_of(start + index * size, 16), size)

    def over_x(stage, c, source, target, from_rows, to_rows):
        return pltpu.make_async_remote_copy(
            src_ref=source.at[from_rows],
            dst_ref=target.at[to_rows],
            send_sem=r.x_send.at[stage, c],
            recv_sem=r.x_recv.at[stage, c],
            device_id={"expert": beside},
            device_id_type=MESH,
        )

    def over_z(stage, c, place, landed, peer, source, target):
        return pltpu.make_async_remote_copy(
            src_ref=source,
            dst_ref=target,
            send_sem=r.z_send.at[stage, c, place],
            recv_sem=r.z_recv.at[stage, c, landed],
            device_id={"expert": peer},
            device_id_type=MESH,
        )

    def half_of(c, which):
        return span(starts[c], which, outer * cfg.piece_rows[c])

    def landing(c):
        return pl.ds(starts[c] // 2, outer * cfg.piece_rows[c])

    def scatter_x(c):
        return over_x(0, c, r.sent, r.x_in, half_of(c, 1 - mine_in), landing(c))

    def gather_x(c, which):
        return over_x(1, c, r.summed, r.summed, half_of(c, which), half_of(c, which))

    def scatter_z(c, place, landed, peer):
        size = cfg.piece_rows[c]
        return over_z(
            0,
            c,
            place,
            landed,
            peer,
            r.z_out.at[span(starts[c] // 2, place, size)],
            r.z_in.at[landed, pl.ds(starts[c] // experts, size)],
        )

    def final(c, place):
        return span(starts[c], mine_in * outer + place, cfg.piece_rows[c])

    def gather_z(c, place, landed, peer):
        rows = final(c, landed)
        return over_z(1, c, place, landed, peer, r.summed.at[rows], r.summed.at[rows])

    def weight_grad(left, right):
        return dot_tn(left.reshape(-1, left.shape[-1]), right.reshape(-1, right.shape[-1]))

    products = ((r.h_norm, r.h_dq), (r.h_norm, r.h_dk), (r.h_norm, r.h_dv), (r.h_da, r.h_o))
    for c in range(pieces):
        rows = pl.ds(starts[c], experts * cfg.piece_rows[c])
        if c < 4:
            left, right = products[c]
            value = weight_grad(left[...], right[...])
            if value.shape[0] != experts * cfg.piece_rows[c]:
                r.sent[rows, :] = jnp.zeros((experts * cfg.piece_rows[c], side), bf16)
            r.sent[pl.ds(starts[c], value.shape[0]), :] = value.astype(bf16)
        else:
            pack_copy.wait()
            r.sent[rows, :] = (r.pack[...] + wide(r.pack_in[...])).astype(bf16)
        scatter_x(c).start()

    rows_all = cfg.micro * 2 * cfg.slots
    tile = 256
    steps = []
    for left, right, target in (
        (r.rows_v, r.gate_v, r.gate_grad),
        (r.rows_v, r.up_v, r.up_grad),
        (r.gate_v, r.grads_v, r.down_grad),
    ):
        for t in range(left.shape[-1] // tile):
            needs = ((0, 1), (0, 2), (3, 4))[len(steps) // (width // tile) if target is not r.down_grad else 2]
            steps.append((left, right, target, t, needs))

    loaded = set()
    flying = [None, None]

    def expert_step(index):
        left, right, target, t, needs = steps[index]
        if index == width // tile:
            loads[4].start()
        for k in needs:
            if k not in loaded:
                loads[k].wait()
                loaded.add(k)
        slot = index % 2
        if flying[slot] is not None:
            flying[slot].wait()
        wide_out = right.shape[-1]
        a = left[..., t * tile : (t + 1) * tile].reshape(rows_all, tile)
        r.stage[slot, :, :wide_out] = dot_tn(a, right[...].reshape(rows_all, wide_out))
        copy = pltpu.make_async_copy(
            r.stage.at[slot, :, pl.ds(0, wide_out)],
            target.at[pl.ds(t * tile, tile)],
            r.step_sem.at[index],
        )
        copy.start()
        flying[slot] = copy

    done = 0
    for c in range(pieces):
        upto = len(steps) * (c + 1) // pieces
        while done < upto:
            expert_step(done)
            done += 1
        scatter_x(c).wait_recv()
        rows = landing(c)
        r.z_out[rows, :] = (wide(r.sent[half_of(c, mine_in), :]) + wide(r.x_in[rows, :])).astype(bf16)

        def out_z(k, carry, c=c):
            place, peer = peer_of(k)
            scatter_z(c, place, mine_out, peer).start()
            return carry

        lax.fori_loop(1, outer, out_z, 0)

    for c in range(pieces):
        size = cfg.piece_rows[c]

        def add_z(k, total, c=c, size=size):
            place, peer = peer_of(k)
            scatter_z(c, place, place, peer).wait_recv()
            return total + wide(r.z_in[place, pl.ds(starts[c] // experts, size), :])

        total = lax.fori_loop(1, outer, add_z, wide(r.z_out[span(starts[c] // 2, mine_out, size), :]))
        r.summed[final(c, mine_out), :] = total.astype(bf16)

        def back_z(k, carry, c=c):
            place, peer = peer_of(k)
            gather_z(c, place, mine_out, peer).start()
            return carry

        lax.fori_loop(1, outer, back_z, 0)

    for c in range(pieces):

        def wait_z(k, carry, c=c):
            place, peer = peer_of(k)
            gather_z(c, place, place, peer).wait_recv()
            return carry

        lax.fori_loop(1, outer, wait_z, 0)
        gather_x(c, mine_in).start()
    for c in range(pieces):
        gather_x(c, 1 - mine_in).wait_recv()
    for c in range(pieces):
        scatter_x(c).wait_send()
        gather_x(c, mine_in).wait_send()

        def sent_z(k, carry, c=c):
            place, peer = peer_of(k)
            scatter_z(c, place, mine_out, peer).wait_send()
            gather_z(c, place, mine_out, peer).wait_send()
            return carry

        lax.fori_loop(1, outer, sent_z, 0)
    for copy in flying:
        copy.wait()


def run_tail(cfg, got):
    vmem, anywhere = pl.BlockSpec(memory_space=pltpu.VMEM), pl.BlockSpec(memory_space=pl.ANY)
    micro, width, inner, slots, experts = cfg.micro, cfg.width, cfg.inner, cfg.slots, cfg.experts
    side, outer = width // 2, experts // 2
    piece = -(-width // (16 * experts)) * 16
    small = -(-(3 * cfg.small_pad + 16) // (16 * experts)) * 16
    cfg.piece_rows = [piece] * 4 + [small]
    total = sum(cfg.piece_rows) * experts
    near = dict(
        h_norm=got.h_norm,
        h_da=got.h_da,
        h_o=got.h_o,
        h_dq=got.h_dq,
        h_dk=got.h_dk,
        h_dv=got.h_dv,
        mixer_grad=got.mixer_grad,
        residual_grad=got.residual_grad,
        rows_grad=got.rows_grad,
    )
    far = dict(
        h_rows=got.h_rows,
        h_grads=got.h_grads,
        h_inside=got.h_inside,
        h_up=got.h_up,
        h_gate=got.h_gate,
    )
    shape, dma = jax.ShapeDtypeStruct, pltpu.SemaphoreType.DMA
    outs = dict(
        summed=shape((total, side), bf16),
        gate_grad=shape((width, inner), f32),
        up_grad=shape((width, inner), f32),
        down_grad=shape((inner, width), f32),
    )
    scratch = dict(
        rows_v=pltpu.VMEM((micro, 2, slots, width), bf16),
        grads_v=pltpu.VMEM((micro, 2, slots, width), bf16),
        up_v=pltpu.VMEM((micro, 2 * slots, inner), bf16),
        gate_v=pltpu.VMEM((micro, 2 * slots, inner), bf16),
        sent=pltpu.VMEM((total, side), bf16),
        x_in=pltpu.VMEM((total // 2, side), bf16),
        z_out=pltpu.VMEM((total // 2, side), bf16),
        z_in=pltpu.VMEM((outer, total // experts, side), bf16),
        pack=pltpu.VMEM((small * experts, side), f32),
        pack_out=pltpu.VMEM((small * experts, side), bf16),
        pack_in=pltpu.VMEM((small * experts, side), bf16),
        stage=pltpu.VMEM((2, 256, max(inner, width)), f32),
        fetch=dma((5,)),
        step_sem=dma(((2 * width + inner) // 256,)),
        pack_sem=dma((2,)),
        x_send=dma((2, 5)),
        x_recv=dma((2, 5)),
        z_send=dma((2, 5, outer)),
        z_recv=dma((2, 5, outer)),
    )
    names = [*near, *far, *outs, *scratch]
    results = pl.pallas_call(
        functools.partial(tail_kernel, cfg, names),
        out_shape=[*outs.values()],
        in_specs=[vmem] * len(near) + [anywhere] * len(far),
        out_specs=[vmem] + [anywhere] * 3,
        scratch_shapes=[*scratch.values()],
        compiler_params=pltpu.CompilerParams(
            collective_id=1, has_side_effects=True, vmem_limit_bytes=60 * 2**20
        ),
        cost_estimate=pl.CostEstimate(
            flops=12 * micro * slots * width * inner, bytes_accessed=40_000_000, transcendentals=0
        ),
    )(*near.values(), *far.values())
    return types.SimpleNamespace(
        **dict(zip(outs, results, strict=True)), pad_rows=piece * experts
    )


def rope_tables(rows):
    half_width = HEAD_DIM // 2
    frequency = 10000.0 ** (-2.0 * np.arange(half_width, dtype=np.float64) / HEAD_DIM)
    angles = np.arange(rows, dtype=np.float64)[:, None] * frequency[None, :]
    angles = np.tile(angles, (1, LANES // half_width))
    return np.cos(angles).astype(np.float32), np.sin(angles).astype(np.float32)


def local(
    inputs,
    cotangent,
    prev_logits,
    lengths,
    routes,
    slot_order,
    norm_gain1,
    w_query,
    w_key,
    w_value,
    w_out,
    norm_gain2,
    router,
    router_residual,
    const_gate,
    const_value,
    expert_gate,
    expert_up,
    expert_down,
):
    micro, owned, width = inputs.shape
    tensors, peers = lax.axis_size("tensor"), lax.axis_size("expert")
    choices = router.shape[2]
    experts = choices - 4
    assert experts == peers and tensors == 2
    cap = 9 * 2 * owned // (8 * choices) + 1
    main, rem = cap // 16 * 16, cap % 16
    if rem > 2 or not main:
        main, rem = main + (16 if rem else 0), 0
    rem_rows = -(-rem * peers // 16) * 16
    cfg = types.SimpleNamespace(
        micro=micro,
        owned=owned,
        width=width,
        rows=owned * tensors,
        inner=expert_gate.shape[3],
        heads=w_query.shape[2] // HEAD_DIM,
        experts=experts,
        choices=choices,
        cap=cap,
        main=main,
        rem=rem,
        rem_rows=rem_rows,
        half_rows=peers // 2 * main,
        slots=peers * main + rem_rows,
        depth=micro if peers * main <= 512 else 1,
        sections=lax.axis_size("section"),
        seqs=lengths.shape[2] - 1,
        chunk=owned,
        small_pad=-(-(choices + 2) // 16) * 16,
    )
    cosine, sine = rope_tables(cfg.rows)
    mixer = jnp.concatenate(
        [router[0].T, const_gate[0], jnp.zeros((LANES - choices - 2, width), f32)], axis=0
    )
    lane_pad = LANES - choices
    ins = dict(
        lengths=lengths[:, 0],
        inputs=inputs,
        cotangent=cotangent,
        prev=jnp.pad(prev_logits[0], ((0, 0), (0, 0), (0, lane_pad))),
        route_col=routes[0],
        route_row=jnp.swapaxes(routes[0], 1, 2),
        order_row=slot_order[0],
        order_col=jnp.swapaxes(slot_order[0], 1, 2),
        gain1=norm_gain1,
        gain2=norm_gain2,
        w_query=w_query[0],
        w_key=w_key[0],
        w_value=w_value[0],
        w_out=w_out[0],
        mixer=mixer,
        residual=jnp.pad(router_residual[0], ((0, lane_pad), (0, lane_pad))),
        const_value=const_value[0],
        cosine=jnp.asarray(cosine),
        sine=jnp.asarray(sine),
        gate=expert_gate[0, 0],
        up=expert_up[0, 0],
        down=expert_down[0, 0],
    )
    got = run_chain(cfg, ins)

    tail = run_tail(cfg, got)
    query_grad, key_grad, value_grad, out_grad = (
        wide(tail.summed[c * tail.pad_rows : c * tail.pad_rows + width]) for c in range(4)
    )
    small = wide(tail.summed[4 * tail.pad_rows :])
    pad = cfg.small_pad
    mixer_grad = jnp.concatenate([small[:pad], small[pad : 2 * pad]], axis=1)
    rows_grad = jnp.concatenate([small[2 * pad : 2 * pad + 8], small[2 * pad + 8 : 2 * pad + 16]], axis=1)
    residual_grad = small[2 * pad + 16 : 3 * pad + 16, :LANES]
    return (
        got.layer_out[None],
        got.input_grad[None],
        got.logit_grad[None, :, :, :choices],
        rows_grad[None, 2],
        query_grad[None],
        key_grad[None],
        value_grad[None],
        out_grad.T[None],
        rows_grad[None, 3],
        mixer_grad[:choices].T[None],
        residual_grad[None, :choices, :choices],
        mixer_grad[None, choices : choices + 2],
        rows_grad[None, :2],
        tail.gate_grad[None, None],
        tail.up_grad[None, None],
        tail.down_grad[None, None],
    )


def solution(mesh):
    tokens = ("expert", "tensor")
    in_specs = (
        P(None, tokens, None),
        P(None, tokens, None),
        P("section", None, tokens, None),
        P(None, "expert", None),
        P("section", None, tokens, None),
        P("section", None, tokens, None),
        P("section", None),
        P("section", None, "tensor"),
        P("section", None, "tensor"),
        P("section", None, "tensor"),
        P("section", "tensor", None),
        P("section", None),
        P("section", None, None),
        P("section", None, None),
        P("section", None, None),
        P("section", None, None),
        P("section", "expert", None, "tensor"),
        P("section", "expert", None, "tensor"),
        P("section", "expert", "tensor", None),
    )
    out_specs = (
        P("section", None, tokens, None),
        P("section", None, tokens, None),
        P("section", None, tokens, None),
        P("section", None),
        P("section", None, "tensor"),
        P("section", None, "tensor"),
        P("section", None, "tensor"),
        P("section", "tensor", None),
        P("section", None),
        P("section", None, None),
        P("section", None, None),
        P("section", None, None),
        P("section", None, None),
        P("section", "expert", None, "tensor"),
        P("section", "expert", None, "tensor"),
        P("section", "expert", "tensor", None),
    )
    return jax.shard_map(local, mesh=mesh, in_specs=in_specs, out_specs=out_specs, check_vma=False)
```

```python
import functools
import types

import jax
import jax.numpy as jnp
import numpy as np
from jax import lax
from jax.experimental import pallas as pl
from jax.experimental.pallas import tpu as pltpu
from jax.sharding import PartitionSpec as P

HEAD_DIM = 64
LANES = 128
EPSILON = 1e-06
MESH = pl.DeviceIdType.MESH
f32, bf16, i32 = jnp.float32, jnp.bfloat16, jnp.int32

P_NORM, P_OUT, P_ROWS, P_PART, P_GROWS, P_GPART, P_DA, P_DX = range(8)


def dot(left, right):
    return jnp.dot(left, right, preferred_element_type=f32)


def dot_nt(left, right):
    return lax.dot_general(left, right, (((1,), (1,)), ((), ())), preferred_element_type=f32)


def dot_tn(left, right):
    return lax.dot_general(left, right, (((0,), (0,)), ((), ())), preferred_element_type=f32)


def wide(values):
    return values.astype(f32)


def halves(values):
    upper = values.astype(bf16)
    return upper, (values - wide(upper)).astype(bf16)


def dot3(how, left, right):
    left_hi, left_lo = halves(left)
    right_hi, right_lo = halves(right)
    return how(left_hi, right_hi) + (how(left_hi, right_lo) + how(left_lo, right_hi))


def inverse_rms(values):
    return lax.rsqrt(jnp.mean(values * values, axis=-1, keepdims=True) + EPSILON)


def iota(shape, dim):
    return lax.broadcasted_iota(i32, shape, dim)


def flag(condition):
    return wide(condition.astype(i32))


def half_lanes(width):
    return (iota((1, width), 1) % HEAD_DIM) < HEAD_DIM // 2


def turned(values, cosine, sine):
    quarter = HEAD_DIM // 2
    other = jnp.where(
        half_lanes(LANES),
        -pltpu.roll(values, LANES - quarter, 1),
        pltpu.roll(values, quarter, 1),
    )
    return values * cosine + other * sine


def turned_back(values, cosine, sine):
    quarter = HEAD_DIM // 2
    other = jnp.where(
        half_lanes(LANES),
        pltpu.roll(values, LANES - quarter, 1),
        -pltpu.roll(values, quarter, 1),
    )
    return values * cosine + other * sine


def chain_kernel(cfg, names, *refs):
    r = types.SimpleNamespace(**dict(zip(names, refs, strict=True)))
    owned, rows, experts, cap, slots = cfg.owned, cfg.rows, cfg.experts, cfg.cap, cfg.slots
    choices, micro, sections, seqs = cfg.choices, cfg.micro, cfg.sections, cfg.seqs
    pairs, chunk = cfg.heads // 2, cfg.chunk
    scale = HEAD_DIM ** (-0.5)
    sec, me, core = (lax.axis_index(a) for a in ("section", "expert", "tensor"))
    other = 1 - core
    own_rows = pl.ds(pl.multiple_of(core * owned, owned), owned)
    other_rows = pl.ds(pl.multiple_of(other * owned, owned), owned)
    is_first, is_last = sec == 0, sec == sections - 1

    deep = cfg.depth == micro

    def slot(m):
        return m if deep else 0

    def pair(kind, m, j, source, target):
        return pltpu.make_async_remote_copy(
            src_ref=source,
            dst_ref=target,
            send_sem=r.pair_send.at[kind, m, j],
            recv_sem=r.pair_recv.at[kind, m, j],
            device_id={"tensor": other},
            device_id_type=MESH,
        )

    def hop(kind, m, source, target, section):
        return pltpu.make_async_remote_copy(
            src_ref=source,
            dst_ref=target,
            send_sem=r.hop_send.at[kind, m],
            recv_sem=r.hop_recv.at[kind, m],
            device_id={"section": section},
            device_id_type=MESH,
        )

    main, rem, half_rows, rem_rows = cfg.main, cfg.rem, cfg.half_rows, cfg.rem_rows
    rem_start = experts * main
    group = experts // 2
    my_group, in_group = me // group, lax.rem(me, group)
    group_of = (my_group, 1 - my_group)

    def slot_rows(index):
        return pl.ds(pl.multiple_of(index * main, main), main)

    def group_rows(g, offset=0):
        return pl.ds(pl.multiple_of(offset + group_of[g] * half_rows, 16), half_rows)

    def last_rows(offset=0):
        return pl.ds(pl.multiple_of(offset + rem_start, 16), rem_rows)

    def get(ref, g, offset=0, cols=slice(None)):
        value = ref[group_rows(g, offset), cols]
        if g == 1 and rem:
            value = jnp.concatenate([value, ref[last_rows(offset), cols]], axis=0)
        return value

    def put(ref, g, value, offset=0, cols=slice(None)):
        ref[group_rows(g, offset), cols] = value[:half_rows]
        if g == 1 and rem:
            ref[last_rows(offset), cols] = value[half_rows:]

    pieces = -(-half_rows // 256)
    hidden_cols = [
        slice(k * cfg.inner // pieces, (k + 1) * cfg.inner // pieces) for k in range(pieces)
    ]

    def parts(g):
        return [group_rows(g)] + ([last_rows()] if g == 1 and rem else [])

    def peers_in(g, act):
        def step(k, carry):
            act(group_of[g] * group + lax.rem(in_group + k, group))
            return carry

        lax.fori_loop(1 - g, group, step, 0)

    def exchange(kind, m, peer, landed, source, target):
        return pltpu.make_async_remote_copy(
            src_ref=source.at[slot_rows(peer)],
            dst_ref=target.at[slot_rows(landed)],
            send_sem=r.a2a_send.at[kind, m, peer],
            recv_sem=r.a2a_recv.at[kind, m, landed],
            device_id={"expert": peer},
            device_id_type=MESH,
        )

    def exchange_rem(kind, m, peer, landed, source, target):
        return pltpu.make_async_remote_copy(
            src_ref=source.at[peer],
            dst_ref=target.at[landed],
            send_sem=r.rem_send.at[kind, m, peer],
            recv_sem=r.rem_recv.at[kind, m, landed],
            device_id={"expert": peer},
            device_id_type=MESH,
        )

    def lay_rem(ref, value):
        for k in range(rem):
            ref[:, k, :] = value[k * experts : (k + 1) * experts]

    def read_rem(ref):
        value = [ref[:, k, :] for k in range(rem)]
        rest = rem_rows - rem * experts
        if rest:
            value.append(jnp.zeros((rest, cfg.width), f32))
        return jnp.concatenate(value, axis=0).astype(bf16)

    def send_slots(kind, m, value):
        d = slot(m)
        outgoing, mine = r.outgoing.at[d], r.arrived.at[d, core]
        r.outgoing[d] = value[:rem_start].astype(bf16)
        for g in (1, 0):
            peers_in(g, lambda p: exchange(kind, m, p, me, outgoing, mine).start())
        if rem:
            rem_out, rem_in = r.rem_out.at[d], r.rem_in.at[d]
            lay_rem(rem_out, value[rem_start:])
            for g in (1, 0):
                peers_in(g, lambda p: exchange_rem(kind, m, p, me, rem_out, rem_in).start())
            rem_in[pl.ds(me, 1)] = rem_out[pl.ds(me, 1)]
        mine[slot_rows(me), :] = outgoing[slot_rows(me), :]

    def save(index, m, source, target):
        return pltpu.make_async_copy(source, target.at[m], r.local.at[index, m])

    def grad_back(m):
        return r.inside.at[slot(m), pl.ds(0, slots), pl.ds(0, cfg.width)]

    back_hop = min(1, sections - 2)
    def stage(m):
        return r.stage.at[m] if deep else r.partial.at[pl.ds(0, owned)]


    barrier = pltpu.get_barrier_semaphore()

    def greet(k, carry):
        pl.semaphore_signal(
            barrier, inc=1, device_id={"expert": lax.rem(me + k, experts)}, device_id_type=MESH
        )
        return carry

    lax.fori_loop(1, experts, greet, 0)
    pl.semaphore_signal(barrier, inc=1, device_id={"tensor": other}, device_id_type=MESH)

    @pl.when(sec > 0)
    def _():
        pl.semaphore_signal(barrier, inc=1, device_id={"section": sec - 1}, device_id_type=MESH)

    @pl.when(sec < sections - 1)
    def _():
        pl.semaphore_signal(barrier, inc=1, device_id={"section": sec + 1}, device_id_type=MESH)

    for m in range(micro):

        @pl.when(is_first)
        def _():
            pltpu.make_async_copy(r.inputs.at[m], r.x.at[m], r.local.at[0, m]).start()

        if deep:

            @pl.when(is_last)
            def _():
                pltpu.make_async_copy(r.cotangent.at[m], r.dz.at[m], r.local.at[9, m]).start()

    weights = [
        pltpu.make_async_copy(source, target, r.fetch.at[k])
        for k, (source, target) in enumerate(
            ((r.gate, r.gate_v), (r.up, r.up_v), (r.down, r.down_v))
        )
    ]
    for copy in weights:
        copy.start()
    beside = (sec > 0).astype(i32) + (sec < sections - 1).astype(i32)
    pl.semaphore_wait(barrier, experts + beside)

    r.mixer[...] = jnp.zeros_like(r.mixer)
    r.mixer[:choices, :] = r.router_in[...]
    r.mixer[choices : choices + 2, :] = r.const_gate[...]
    r.residual[...] = jnp.zeros_like(r.residual)
    r.residual[:choices, :choices] = r.residual_in[...]
    r.prev_t[...] = jnp.zeros_like(r.prev_t)
    for m in range(micro):
        r.prev_t[m, :choices, :] = r.prev_in[:, m, :]
        table = jnp.concatenate(
            [r.route_row[m], r.order_row[m], jnp.zeros((13, owned), i32)], axis=0
        )
        unit = flag(iota((owned, owned), 0) == iota((owned, owned), 1)).astype(bf16)
        r.cols[m] = dot_nt(unit, wide(table).astype(bf16)).astype(i32)

    def seq_bias(m):
        row = iota((rows, 1), 0)
        start = jnp.zeros((rows, 1), i32)
        end = r.lengths[m, 0]
        for k in range(seqs):
            start = jnp.where(row >= end, row if k == seqs - 1 else end, start)
            end = end + r.lengths[m, min(k + 1, seqs)]
        for c in range(rows // chunk):
            piece = slice(c * chunk, (c + 1) * chunk)
            key = iota((chunk, rows), 1)
            seen = (key <= row[piece]) & (key >= start[piece])
            r.bias[piece, :] = jnp.where(seen, 0.0, -1e30).astype(bf16)

    def routing(m):
        lane = iota((owned, LANES), 1)
        lane_t = iota((LANES, owned), 0)
        col = [r.cols[m, :, k : k + 1] for k in range(2)]
        row = [r.route_row[m, k : k + 1, :] for k in range(2)]
        order_row, order_col = r.order_row[m], r.cols[m, :, 2:3]
        hot = [wide((lane == col[k]).astype(i32)) for k in range(2)]
        hot_t = [wide((lane_t == row[k]).astype(i32)) for k in range(2)]
        before = wide((order_row < order_col).astype(i32)).astype(bf16)
        before_t = wide((order_col < order_row).astype(i32)).astype(bf16)
        earlier = dot(before, (hot[0] + hot[1]).astype(bf16))
        earlier_t = dot((hot_t[0] + hot_t[1]).astype(bf16), before_t)
        for k in range(2):
            slot = jnp.sum(earlier * hot[k], axis=1, keepdims=True).astype(i32)
            slot_t = jnp.sum(earlier_t * hot_t[k], axis=0, keepdims=True).astype(i32)

            def placed(choice, at):
                first = choice * main + at
                late = rem_start + (at - main) * experts + choice
                kept = (choice < experts) & (at < cap)
                return jnp.where(kept, jnp.where(at < main, first, late), -1)

            place, place_t = placed(col[k], slot), placed(row[k], slot_t)
            r.place_col[m, :, k : k + 1] = place
            r.place_row[m, k : k + 1, :] = place_t

    def spread(m, k):
        return flag(iota((owned, slots), 1) == r.place_col[m, :, k : k + 1]).astype(bf16)

    def spread_t(m, k):
        return flag(iota((slots, owned), 0) == r.place_row[m, k : k + 1, :]).astype(bf16)

    def choice_flags(m):
        col = [r.cols[m, :, k : k + 1] for k in range(2)]
        copies = [wide((col[k] == experts + 1).astype(i32)) for k in range(2)]
        consts = [
            [wide((col[k] == experts + 2 + c).astype(i32)) for c in range(2)] for k in range(2)
        ]
        return col, copies, consts

    def unpack_gates(m):
        pack = r.gates[m]
        return [pack[:, k : k + 1] for k in range(2)], [pack[:, 2 + k : 3 + k] for k in range(2)]

    def through_expert(m, kind, pair_in, pair_out, target, kept, compute):
        d = slot(m)
        arrived, outgoing, result = r.arrived.at[d], r.outgoing.at[d], r.result.at[d]
        mine, theirs = arrived.at[core], arrived.at[other]
        if rem:
            rem_out, rem_in = r.rem_out.at[d], r.rem_in.at[d]
            rem_result, rem_back = r.rem_result.at[d], r.rem_back.at[d]
        passes = kind // 2

        def keep(index, half, rows_of):
            return pltpu.make_async_copy(
                arrived.at[half, rows_of], kept.at[m, half, rows_of], r.keep.at[passes, m, index]
            )

        def forward_pair(g, which, side):
            return [
                pair(pair_in, m, g + k, side.at[rows_of], side.at[rows_of])
                for k, rows_of in enumerate(parts(g))
            ]

        def sums(g):
            return [
                pair(pair_out, m, g + k, r.part_out.at[rows_of], r.part_in.at[rows_of])
                for k, rows_of in enumerate(parts(g))
            ]

        everything = pl.ds(0, slots)

        def kept_mine(g):
            return [keep(2 * g + k, core, rows_of) for k, rows_of in enumerate(parts(g))]

        def arrive(g):
            peers_in(g, lambda p: exchange(kind, m, p, p, outgoing, mine).wait_recv())
            if g == 1 and rem:
                for which in range(2):
                    peers_in(which, lambda p: exchange_rem(kind, m, p, p, rem_out, rem_in).wait_recv())
                mine[last_rows(), :] = read_rem(rem_in)
            for copy in forward_pair(g, core, mine):
                copy.start()
            for copy in kept_mine(g):
                copy.start()

        def work(g):
            put(r.partial, g, compute(core, g))
            for copy in forward_pair(g, other, theirs):
                copy.wait_recv()
            if g == 1:
                keep(1, other, everything).start()
            put(r.part_out, g, compute(other, g).astype(bf16))
            if g == 1:
                keep(1, other, everything).wait()
            for copy in sums(g):
                copy.start()

        def finish(g):
            for copy in sums(g):
                copy.wait_recv()
            value = get(r.partial, g) + wide(get(r.part_in, g))
            for copy in kept_mine(g):
                copy.wait()
            for copy in forward_pair(g, core, mine):
                copy.wait_send()
            put(result, g, value.astype(bf16))
            peers_in(g, lambda p: exchange(kind + 1, m, p, me, result, target).start())
            if g == 1 and rem:
                lay_rem(rem_result, value[half_rows:])
                for which in (1, 0):
                    peers_in(
                        which,
                        lambda p: exchange_rem(kind + 1, m, p, me, rem_result, rem_back).start(),
                    )
                rem_back[pl.ds(me, 1)] = rem_result[pl.ds(me, 1)]

        arrive(0)
        work(0)
        arrive(1)
        finish(0)
        work(1)
        finish(1)
        target[slot_rows(me), :] = result[slot_rows(me), :]
        for g in range(2):
            for copy in sums(g):
                copy.wait_send()
            peers_in(g, lambda p: exchange(kind, m, p, me, outgoing, mine).wait_send())
            if rem:
                peers_in(g, lambda p: exchange_rem(kind, m, p, me, rem_out, rem_in).wait_send())

    def wait_back(m, kind, target):
        result = r.result.at[slot(m)]
        if rem:
            rem_result, rem_back = r.rem_result.at[slot(m)], r.rem_back.at[slot(m)]
        for g in range(2):
            peers_in(g, lambda p: exchange(kind + 1, m, p, p, result, target).wait_recv())
            if rem:
                peers_in(g, lambda p: exchange_rem(kind + 1, m, p, p, rem_result, rem_back).wait_recv())
        if rem:
            target[last_rows(), :] = read_rem(rem_back)
        for g in range(2):
            peers_in(g, lambda p: exchange(kind + 1, m, p, me, result, target).wait_send())
            if rem:
                peers_in(g, lambda p: exchange_rem(kind + 1, m, p, me, rem_result, rem_back).wait_send())

    def attend(m):
        @pl.when(is_first)
        def _():
            pltpu.make_async_copy(r.inputs.at[m], r.x.at[m], r.local.at[0, m]).wait()

        @pl.when(sec > 0)
        def _():
            hop(0, m, r.hop_out.at[slot(m)], r.hop_in.at[0, m], sec - 1).wait_recv()
            r.x[m] = wide(r.hop_in[0, m])

        x = r.x[m]
        r.norm[m, own_rows, :] = (x * inverse_rms(x) * r.gain1[...]).astype(bf16)
        pair(P_NORM, m, 0, r.norm.at[m, own_rows], r.norm.at[m, own_rows]).start()
        routing(m)
        seq_bias(m)

        def project(some):
            normed = r.norm[m, some, :]
            cosine, sine = r.cosine[some, :], r.sine[some, :]
            for stash, weight in ((r.q, r.w_query), (r.k, r.w_key)):
                flat = dot(normed, weight[...])
                for p in range(pairs):
                    lanes = slice(p * LANES, (p + 1) * LANES)
                    stash[m, some, lanes] = turned(flat[:, lanes], cosine, sine).astype(bf16)
            r.v[m, some, :] = dot(normed, r.w_value[...]).astype(bf16)

        project(own_rows)
        pair(P_NORM, m, 0, r.norm.at[m, other_rows], r.norm.at[m, other_rows]).wait_recv()
        save(1, m, r.norm.at[m], r.h_norm).start()
        project(other_rows)

        r.logsum[m] = jnp.zeros((rows, LANES), f32)
        lane = iota((1, LANES), 1)

        def head_pair(p, inner):
            lanes = pl.ds(pl.multiple_of(p * LANES, LANES), LANES)
            q2, k2, v2 = r.q[m, :, lanes], r.k[m, :, lanes], r.v[m, :, lanes]
            for half in range(2):
                keep = wide(((lane // HEAD_DIM) == half).astype(i32)).astype(bf16)
                km, vm = k2 * keep, v2 * keep
                for c in range(rows // chunk):
                    piece, reach = slice(c * chunk, (c + 1) * chunk), (c + 1) * chunk
                    scores = dot_nt(q2[piece], km[:reach]) * scale + wide(r.bias[piece, :reach])
                    peak = jnp.max(scores, axis=-1, keepdims=True)
                    shifted = jnp.exp(scores - peak)
                    total = jnp.sum(shifted, axis=-1, keepdims=True)
                    probs = (shifted * (1.0 / total)).astype(bf16)
                    mixed = dot(probs, vm[:reach])
                    if half == 0:
                        r.mix[piece, :] = mixed
                    else:
                        r.o[m, piece, lanes] = (r.mix[piece, :] + mixed).astype(bf16)
                    r.logsum[m, piece, :] = jnp.where(
                        lane == 2 * p + half, peak + jnp.log(total), r.logsum[m, piece, :]
                    )
            return inner

        lax.fori_loop(0, pairs, head_pair, 0)
        save(2, m, r.o.at[m], r.h_o).start()

    def attend_send(m):
        r.half_out[...] = dot(r.o[m, other_rows, :], r.w_out[...]).astype(bf16)
        pair(P_OUT, m, 0, r.half_out, r.half_in.at[0, m]).start()
        summed = r.x[m] + dot(r.o[m, own_rows, :], r.w_out[...])
        pair(P_OUT, m, 0, r.half_out, r.half_in.at[0, m]).wait_recv()
        hidden = summed + wide(r.half_in[0, m])
        r.h[m] = hidden
        normed2 = (hidden * inverse_rms(hidden) * r.gain2[...]).astype(bf16)
        r.norm2[m] = normed2

        send_slots(0, m, dot(spread_t(m, 0) + spread_t(m, 1), normed2))

        mixer_hi, mixer_lo = halves(r.mixer[...])
        logits = dot_nt(normed2, mixer_hi) + dot_nt(normed2, mixer_lo)
        logits = logits + dot3(dot_tn, r.prev_t[m], r.residual[...])
        col, copies, consts = choice_flags(m)
        wide_lane = iota((owned, LANES), 1)
        picked = [
            jnp.sum(jnp.where(wide_lane == col[k], logits, 0.0), axis=1, keepdims=True)
            for k in range(2)
        ]
        gate = [jax.nn.sigmoid(picked[0] - picked[1]), jax.nn.sigmoid(picked[1] - picked[0])]
        rate = [jax.nn.sigmoid(logits[:, choices + c : choices + c + 1]) for c in range(2)]
        pack = jnp.zeros((owned, LANES), f32)
        for k, value in enumerate(gate + rate):
            pack = jnp.where(wide_lane == k, value, pack)
        r.gates[m] = pack
        pair(P_NORM, m, 0, r.norm.at[m, own_rows], r.norm.at[m, own_rows]).wait_send()
        pair(P_OUT, m, 0, r.half_out, r.half_in.at[0, m]).wait_send()

    def kept_forward(m):
        copies = [save(10, m, r.inside.at[slot(m)], r.h_inside)]
        if not deep:
            copies += [
                save(5, m, r.by_up.at[0], r.h_up),
                save(6, m, r.by_gate.at[0], r.h_gate),
            ]
        return copies

    def experts_forward(m):
        d = slot(m)
        by_up, by_gate, inside_of, arrived = r.by_up.at[d], r.by_gate.at[d], r.inside.at[d], r.arrived.at[d]

        @pl.when(m == 0)
        def _():
            for copy in weights:
                copy.wait()

        def compute(half, g):
            block = get(arrived.at[half], g)
            offset = half * slots
            total = 0.0
            for cols in hidden_cols:
                value = dot(block, r.gate_v[:, cols])
                upper = dot(block, r.up_v[:, cols])
                sig = jax.nn.sigmoid(value)
                active = value * sig
                inside = (active * upper).astype(bf16)
                put(by_up, g, active.astype(bf16), offset, cols)
                slope = upper * sig * (1.0 + value * (1.0 - sig))
                put(by_gate, g, slope.astype(bf16), offset, cols)
                put(inside_of, g, inside, offset, cols)
                total = total + dot(inside, r.down_v[cols, :])
            return total

        through_expert(m, 0, P_ROWS, P_PART, r.back.at[m], r.h_rows, compute)
        for copy in kept_forward(m):
            copy.start()

    def combine(m):
        gate, rate = unpack_gates(m)
        col, copies, consts = choice_flags(m)
        wait_back(m, 0, r.back.at[m])

        apart = [dot(spread(m, k), r.back[m]) for k in range(2)]
        out = r.h[m] + gate[0] * apart[0] + gate[1] * apart[1]
        own = gate[0] * copies[0] + gate[1] * copies[1]
        for c in range(2):
            on = gate[0] * consts[0][c] + gate[1] * consts[1][c]
            own = own + on * rate[c]
            out = out + (on * (1.0 - rate[c])) * r.const_value[c : c + 1, :]
        out = out + own * wide(r.norm2[m])
        stage(m)[...] = out
        save(3, m, stage(m), r.layer_out).start()

        @pl.when(sec < sections - 1)
        def _():
            r.hop_out[slot(m)] = out.astype(bf16)
            hop(0, m, r.hop_out.at[slot(m)], r.hop_in.at[0, m], sec + 1).start()

    def settle_forward(m):
        @pl.when(sec < sections - 1)
        def _():
            hop(0, m, r.hop_out.at[slot(m)], r.hop_in.at[0, m], sec + 1).wait_send()

        save(3, m, stage(m), r.layer_out).wait()
        save(1, m, r.norm.at[m], r.h_norm).wait()
        save(2, m, r.o.at[m], r.h_o).wait()
        for copy in kept_forward(m):
            copy.wait()

    r.mixer_grad[...] = jnp.zeros_like(r.mixer_grad)
    r.residual_grad[...] = jnp.zeros_like(r.residual_grad)
    r.rows_grad[...] = jnp.zeros_like(r.rows_grad)

    def fetched(m):
        return [
            pltpu.make_async_copy(r.h_up.at[m], r.by_up.at[0], r.local.at[7, m]),
            pltpu.make_async_copy(r.h_gate.at[m], r.by_gate.at[0], r.local.at[8, m]),
        ]

    def grad_start(m):
        d = slot(m)
        if deep:
            settle_forward(m)
        else:
            for copy in fetched(m):
                copy.start()

        @pl.when(is_last)
        def _():
            copy = pltpu.make_async_copy(r.cotangent.at[m], r.dz.at[d], r.local.at[9, m])
            if not deep:
                copy.start()
            copy.wait()

        @pl.when(sec < sections - 1)
        def _():
            hop(1, m, r.hop_out.at[d], r.hop_in.at[back_hop, m], sec + 1).wait_recv()
            r.dz[d] = wide(r.hop_in[back_hop, m])

        dz = r.dz[d]
        gate, rate = unpack_gates(m)
        leaving = [dot(spread_t(m, k), (gate[k] * dz).astype(bf16)) for k in range(2)]
        send_slots(2, m, leaving[0] + leaving[1])

        col, copies, consts = choice_flags(m)
        normed2 = r.norm2[m]
        dz_norm = jnp.sum(dz * wide(normed2), axis=1, keepdims=True)
        dz_const = [
            jnp.sum(dz * r.const_value[c : c + 1, :], axis=1, keepdims=True) for c in range(2)
        ]
        apart = [dot(spread(m, k), r.back[m]) for k in range(2)]
        dgate = []
        for k in range(2):
            value = jnp.sum(dz * apart[k], axis=1, keepdims=True)
            value = value + copies[k] * dz_norm
            for c in range(2):
                value = value + consts[k][c] * (rate[c] * dz_norm + (1.0 - rate[c]) * dz_const[c])
            dgate.append(value)
        coupled = gate[0] * gate[1] * (dgate[0] - dgate[1])
        lane = iota((owned, LANES), 1)
        dlogits = jnp.where(lane == col[0], coupled, jnp.where(lane == col[1], -coupled, 0.0))
        own = gate[0] * copies[0] + gate[1] * copies[1]
        for c in range(2):
            on = gate[0] * consts[0][c] + gate[1] * consts[1][c]
            own = own + on * rate[c]
            dmix = on * (dz_norm - dz_const[c]) * rate[c] * (1.0 - rate[c])
            dlogits = dlogits + jnp.where(lane == choices + c, dmix, 0.0)
            r.rows_grad[c : c + 1, :] += jnp.sum((on * (1.0 - rate[c])) * dz, axis=0, keepdims=True)
        dlogits_hi, dlogits_lo = halves(dlogits)
        r.mixer_grad[...] += dot_tn(dlogits_hi, normed2) + dot_tn(dlogits_lo, normed2)
        r.residual_grad[...] += dot3(dot, r.prev_t[m], dlogits)
        r.logit_grad[m] = dot3(dot_nt, dlogits, r.residual[...])
        r.dnorm[d] = dot3(dot, dlogits, r.mixer[...]) + own * dz

    def kept_backward(m):
        return [
            save(11, m, r.by_up.at[slot(m)], r.h_up),
            save(12, m, r.by_gate.at[slot(m)], r.h_gate),
        ]

    def experts_backward(m):
        d = slot(m)
        by_up, by_gate, arrived = r.by_up.at[d], r.by_gate.at[d], r.arrived.at[d]
        if not deep:
            for copy in fetched(m):
                copy.wait()

        def compute(half, g):
            block = get(arrived.at[half], g)
            offset = half * slots
            total = 0.0
            for cols in hidden_cols:
                dinside = dot_nt(block, r.down_v[cols, :])
                dvalue = (dinside * wide(get(by_gate, g, offset, cols))).astype(bf16)
                dupper = (dinside * wide(get(by_up, g, offset, cols))).astype(bf16)
                put(by_gate, g, dvalue, offset, cols)
                put(by_up, g, dupper, offset, cols)
                total = total + dot_nt(dvalue, r.gate_v[:, cols]) + dot_nt(dupper, r.up_v[:, cols])
            return total

        through_expert(m, 2, P_GROWS, P_GPART, grad_back(m), r.h_grads, compute)
        for copy in kept_backward(m):
            copy.start()

    def grad_attend(m):
        d = slot(m)
        wait_back(m, 2, grad_back(m))

        both = spread(m, 0) + spread(m, 1)
        dnorm = r.dnorm[d] + dot(both, grad_back(m)[...])
        hidden = r.h[m]
        root = inverse_rms(hidden)
        scaled = dnorm * r.gain2[...]
        pull = root * root * root * jnp.mean(hidden * scaled, axis=-1, keepdims=True)
        dhidden = r.dz[d] + root * scaled - hidden * pull
        r.rows_grad[3:4, :] += jnp.sum(dnorm * hidden * root, axis=0, keepdims=True)
        r.dh[...] = dhidden
        r.da[own_rows, :] = dhidden.astype(bf16)
        pair(P_DA, m, 0, r.da.at[own_rows], r.da.at[own_rows]).start()
        seq_bias(m)
        r.do[own_rows, :] = dot_nt(r.da[own_rows, :], r.w_out[...]).astype(bf16)
        pair(P_DA, m, 0, r.da.at[other_rows], r.da.at[other_rows]).wait_recv()
        save(13, m, r.da, r.h_da).start()
        r.do[other_rows, :] = dot_nt(r.da[other_rows, :], r.w_out[...]).astype(bf16)

        head_lane = iota((1, LANES), 1)

        def head_pair(p, inner):
            lanes = pl.ds(pl.multiple_of(p * LANES, LANES), LANES)
            q2, k2, v2 = r.q[m, :, lanes], r.k[m, :, lanes], r.v[m, :, lanes]
            do2 = r.do[:, lanes]
            for half in range(2):
                keep = wide(((head_lane // HEAD_DIM) == half).astype(i32)).astype(bf16)
                km, vm, qm, dom = k2 * keep, v2 * keep, q2 * keep, do2 * keep
                for c in range(rows // chunk):
                    piece, reach = slice(c * chunk, (c + 1) * chunk), (c + 1) * chunk
                    scores = dot_nt(q2[piece], km[:reach]) * scale + wide(r.bias[piece, :reach])
                    total = jnp.sum(
                        jnp.where(head_lane == 2 * p + half, r.logsum[m, piece, :], 0.0),
                        axis=1,
                        keepdims=True,
                    )
                    probs = jnp.exp(scores - total)
                    dprobs = dot_nt(do2[piece], vm[:reach])
                    meant = jnp.sum(dprobs * probs, axis=-1, keepdims=True)
                    dscores = (probs * (dprobs - meant)).astype(bf16)
                    dq = dot(dscores, km[:reach])
                    dk = dot_tn(dscores, qm[piece])
                    dv = dot_tn(probs.astype(bf16), dom[piece])
                    if half == 0:
                        r.mix[piece, :] = dq
                    else:
                        r.mix[piece, :] += dq
                    if half == 0 and c == 0:
                        r.mix_k[...] = jnp.zeros_like(r.mix_k)
                        r.mix_v[...] = jnp.zeros_like(r.mix_v)
                    r.mix_k[:reach, :] += dk
                    r.mix_v[:reach, :] += dv
            r.dq[:, lanes] = (turned_back(r.mix[...], r.cosine[...], r.sine[...]) * scale).astype(bf16)
            r.dk[:, lanes] = (turned_back(r.mix_k[...], r.cosine[...], r.sine[...]) * scale).astype(bf16)
            r.dv[:, lanes] = r.mix_v[...].astype(bf16)
            return inner

        lax.fori_loop(0, pairs, head_pair, 0)
        for copy in kept_heads(m):
            copy.start()

    def kept_heads(m):
        return [save(14, m, r.dq, r.h_dq), save(15, m, r.dk, r.h_dk), save(16, m, r.dv, r.h_dv)]

    def grad_finish(m):
        d = slot(m)

        def dnormed(piece):
            return (
                dot_nt(r.dq[piece, :], r.w_query[...])
                + dot_nt(r.dk[piece, :], r.w_key[...])
                + dot_nt(r.dv[piece, :], r.w_value[...])
            )

        save(13, m, r.da, r.h_da).wait()
        r.half_out[...] = dnormed(other_rows).astype(bf16)
        pair(P_DX, m, 0, r.half_out, r.half_in.at[1, m]).start()
        kept = dnormed(own_rows)
        pair(P_DX, m, 0, r.half_out, r.half_in.at[1, m]).wait_recv()
        dnorm1 = kept + wide(r.half_in[1, m])
        x = r.x[m]
        root1 = inverse_rms(x)
        scaled1 = dnorm1 * r.gain1[...]
        pull1 = root1 * root1 * root1 * jnp.mean(x * scaled1, axis=-1, keepdims=True)
        dx = r.dh[...] + root1 * scaled1 - x * pull1
        stage(m)[...] = dx
        save(4, m, stage(m), r.input_grad).start()

        @pl.when(sec > 0)
        def _():
            r.hop_out[d] = dx.astype(bf16)
            hop(1, m, r.hop_out.at[d], r.hop_in.at[back_hop, m], sec - 1).start()

        r.rows_grad[2:3, :] += jnp.sum(dnorm1 * x * root1, axis=0, keepdims=True)
        pair(P_DA, m, 0, r.da.at[own_rows], r.da.at[own_rows]).wait_send()
        pair(P_DX, m, 0, r.half_out, r.half_in.at[1, m]).wait_send()
        for copy in kept_heads(m):
            copy.wait()

    def settle_backward(m):
        @pl.when(sec > 0)
        def _():
            hop(1, m, r.hop_out.at[slot(m)], r.hop_in.at[back_hop, m], sec - 1).wait_send()

        save(4, m, stage(m), r.input_grad).wait()
        for copy in kept_backward(m):
            copy.wait()

    if deep:
        def all_of(*phases):
            def step(m, carry):
                for phase in phases:
                    phase(m)
                return carry

            lax.fori_loop(0, micro, step, 0)

        def turn(m):
            combine(m)

            @pl.when(is_last)
            def _():
                grad_start(m)

        def start_rest(m):
            @pl.when(sec < sections - 1)
            def _():
                grad_start(m)

        all_of(attend, attend_send)
        all_of(experts_forward)
        all_of(turn)
        all_of(start_rest)
        all_of(experts_backward)
        all_of(grad_attend, grad_finish)
        for m in range(micro):
            settle_backward(m)
    else:

        def there(m, carry):
            for phase in (attend, attend_send, experts_forward, combine, settle_forward):
                phase(m)
            return carry

        def back_again(m, carry):
            for phase in (grad_start, experts_backward, grad_attend, grad_finish, settle_backward):
                phase(m)
            return carry

        lax.fori_loop(0, micro, there, 0)
        lax.fori_loop(0, micro, back_again, 0)


def run_chain(cfg, ins):
    vmem, anywhere = pl.BlockSpec(memory_space=pltpu.VMEM), pl.BlockSpec(memory_space=pl.ANY)
    smem = pl.BlockSpec(memory_space=pltpu.SMEM)
    far = {"inputs", "cotangent", "gate", "up", "down"}
    micro, owned, rows, width, inner = cfg.micro, cfg.owned, cfg.rows, cfg.width, cfg.inner
    heads_width, slots = cfg.heads * HEAD_DIM, cfg.slots
    shape = jax.ShapeDtypeStruct
    outs = dict(
        logit_grad=shape((micro, owned, LANES), f32),
        mixer_grad=shape((LANES, width), f32),
        residual_grad=shape((LANES, LANES), f32),
        rows_grad=shape((8, width), f32),
    )
    hbm_outs = dict(
        layer_out=shape((micro, owned, width), f32),
        input_grad=shape((micro, owned, width), f32),
        h_rows=shape((micro, 2, slots, width), bf16),
        h_grads=shape((micro, 2, slots, width), bf16),
        h_inside=shape((micro, 2 * slots, inner), bf16),
        h_up=shape((micro, 2 * slots, inner), bf16),
        h_gate=shape((micro, 2 * slots, inner), bf16),
        h_norm=shape((micro, rows, width), bf16),
        h_da=shape((micro, rows, width), bf16),
        h_o=shape((micro, rows, heads_width), bf16),
        h_dq=shape((micro, rows, heads_width), bf16),
        h_dk=shape((micro, rows, heads_width), bf16),
        h_dv=shape((micro, rows, heads_width), bf16),
    )
    dma = pltpu.SemaphoreType.DMA
    depth = cfg.depth
    rem_scratch = {}
    if depth == micro:
        rem_scratch = dict(stage=pltpu.VMEM((micro, owned, width), f32))
    if cfg.rem:
        last = pltpu.VMEM((depth, cfg.experts, cfg.rem, width), f32)
        rem_sem = dma((4, micro, cfg.experts))
        rem_scratch |= dict(
            rem_out=last, rem_in=last, rem_result=last, rem_back=last, rem_send=rem_sem, rem_recv=rem_sem
        )
    scratch = dict(
        gate_v=pltpu.VMEM((width, inner), bf16),
        up_v=pltpu.VMEM((width, inner), bf16),
        down_v=pltpu.VMEM((inner, width), bf16),
        x=pltpu.VMEM((micro, owned, width), f32),
        h=pltpu.VMEM((micro, owned, width), f32),
        norm=pltpu.VMEM((micro, rows, width), bf16),
        norm2=pltpu.VMEM((micro, owned, width), bf16),
        q=pltpu.VMEM((micro, rows, heads_width), bf16),
        k=pltpu.VMEM((micro, rows, heads_width), bf16),
        v=pltpu.VMEM((micro, rows, heads_width), bf16),
        o=pltpu.VMEM((micro, rows, heads_width), bf16),
        logsum=pltpu.VMEM((micro, rows, LANES), f32),
        mixer=pltpu.VMEM((LANES, width), f32),
        residual=pltpu.VMEM((LANES, LANES), f32),
        prev_t=pltpu.VMEM((micro, LANES, owned), f32),
        cols=pltpu.VMEM((micro, owned, 16), i32),
        gates=pltpu.VMEM((micro, owned, LANES), f32),
        place_col=pltpu.VMEM((micro, owned, 2), i32),
        place_row=pltpu.VMEM((micro, 2, owned), i32),
        bias=pltpu.VMEM((rows, rows), bf16),
        arrived=pltpu.VMEM((depth, 2, slots, width), bf16),
        part_in=pltpu.VMEM((slots, width), bf16),
        back=pltpu.VMEM((micro, slots, width), bf16),
        half_in=pltpu.VMEM((2, micro, owned, width), bf16),
        hop_in=pltpu.VMEM((min(2, cfg.sections - 1), micro, owned, width), bf16),
        outgoing=pltpu.VMEM((depth, cfg.experts * cfg.main, width), bf16),
        part_out=pltpu.VMEM((slots, width), bf16),
        result=pltpu.VMEM((depth, slots, width), bf16),
        partial=pltpu.VMEM((max(slots, owned), width), f32),
        half_out=pltpu.VMEM((owned, width), bf16),
        hop_out=pltpu.VMEM((depth, owned, width), bf16),
        inside=pltpu.VMEM((depth, 2 * slots, inner), bf16),
        **rem_scratch,
        by_up=pltpu.VMEM((depth, 2 * slots, inner), bf16),
        by_gate=pltpu.VMEM((depth, 2 * slots, inner), bf16),
        dz=pltpu.VMEM((depth, owned, width), f32),
        dh=pltpu.VMEM((owned, width), f32),
        dnorm=pltpu.VMEM((depth, owned, width), f32),
        da=pltpu.VMEM((rows, width), bf16),
        do=pltpu.VMEM((rows, heads_width), bf16),
        dq=pltpu.VMEM((rows, heads_width), bf16),
        dk=pltpu.VMEM((rows, heads_width), bf16),
        dv=pltpu.VMEM((rows, heads_width), bf16),
        mix=pltpu.VMEM((rows, LANES), f32),
        mix_k=pltpu.VMEM((rows, LANES), f32),
        mix_v=pltpu.VMEM((rows, LANES), f32),
        pair_send=dma((8, micro, 3)),
        pair_recv=dma((8, micro, 3)),
        hop_send=dma((2, micro)),
        hop_recv=dma((2, micro)),
        a2a_send=dma((4, micro, cfg.experts)),
        a2a_recv=dma((4, micro, cfg.experts)),
        local=dma((17, micro)),
        keep=dma((2, micro, 4)),
        fetch=dma((3,)),
    )
    names = [*ins, *outs, *hbm_outs, *scratch]
    flops = 2 * micro * (2 * slots * width * inner * 6 + rows * width * heads_width * 10)
    results = pl.pallas_call(
        functools.partial(chain_kernel, cfg, names),
        out_shape=[*outs.values(), *hbm_outs.values()],
        in_specs=[
            smem if name == "lengths" else anywhere if name in far else vmem for name in ins
        ],
        out_specs=[vmem] * len(outs) + [anywhere] * len(hbm_outs),
        scratch_shapes=[*scratch.values()],
        compiler_params=pltpu.CompilerParams(
            collective_id=0, has_side_effects=True, vmem_limit_bytes=60 * 2**20
        ),
        cost_estimate=pl.CostEstimate(flops=flops, bytes_accessed=50_000_000, transcendentals=0),
    )(*ins.values())
    return types.SimpleNamespace(**dict(zip([*outs, *hbm_outs], results, strict=True)))


def tail_kernel(cfg, names, *refs):
    r = types.SimpleNamespace(**dict(zip(names, refs, strict=True)))
    experts, width, pad = cfg.experts, cfg.width, cfg.small_pad
    side = width // 2
    outer = experts // 2
    me, core = lax.axis_index("expert"), lax.axis_index("tensor")
    mine_out, mine_in = me // 2, lax.rem(me, 2)
    beside = me + 1 - 2 * mine_in
    pieces = len(cfg.piece_rows)
    starts = [sum(cfg.piece_rows[:c]) * experts for c in range(pieces)]

    def peer_of(k):
        place = lax.rem(mine_out + k, outer)
        return place, place * 2 + mine_in

    barrier = pltpu.get_barrier_semaphore()
    pl.semaphore_signal(barrier, inc=1, device_id={"tensor": 1 - core}, device_id_type=MESH)
    pl.semaphore_signal(barrier, inc=1, device_id={"expert": beside}, device_id_type=MESH)

    def greet(k, carry):
        pl.semaphore_signal(barrier, inc=1, device_id={"expert": peer_of(k)[1]}, device_id_type=MESH)
        return carry

    lax.fori_loop(1, outer, greet, 0)

    loads = [
        pltpu.make_async_copy(source, target, r.fetch.at[k])
        for k, (source, target) in enumerate(
            (
                (r.h_rows, r.rows_v),
                (r.h_gate, r.gate_v),
                (r.h_up, r.up_v),
                (r.h_grads, r.grads_v),
                (r.h_inside, r.gate_v),
            )
        )
    ]
    for copy in loads[:4]:
        copy.start()

    r.pack[...] = jnp.zeros_like(r.pack)
    r.pack[:pad, :] = r.mixer_grad[:pad, :side]
    r.pack[pad : 2 * pad, :] = r.mixer_grad[:pad, side:]
    r.pack[2 * pad : 2 * pad + 8, :] = r.rows_grad[:, :side]
    r.pack[2 * pad + 8 : 2 * pad + 16, :] = r.rows_grad[:, side:]
    r.pack[2 * pad + 16 : 3 * pad + 16, :LANES] = r.residual_grad[:pad, :]
    r.pack_out[...] = r.pack[...].astype(bf16)
    pl.semaphore_wait(barrier, outer + 1)
    pack_copy = pltpu.make_async_remote_copy(
        src_ref=r.pack_out,
        dst_ref=r.pack_in,
        send_sem=r.pack_sem.at[0],
        recv_sem=r.pack_sem.at[1],
        device_id={"tensor": 1 - core},
        device_id_type=MESH,
    )
    pack_copy.start()

    def span(start, index, size):
        return pl.ds(pl.multiple_of(start + index * size, 16), size)

    def over_x(stage, c, source, target, from_rows, to_rows):
        return pltpu.make_async_remote_copy(
            src_ref=source.at[from_rows],
            dst_ref=target.at[to_rows],
            send_sem=r.x_send.at[stage, c],
            recv_sem=r.x_recv.at[stage, c],
            device_id={"expert": beside},
            device_id_type=MESH,
        )

    def over_z(stage, c, place, landed, peer, source, target):
        return pltpu.make_async_remote_copy(
            src_ref=source,
            dst_ref=target,
            send_sem=r.z_send.at[stage, c, place],
            recv_sem=r.z_recv.at[stage, c, landed],
            device_id={"expert": peer},
            device_id_type=MESH,
        )

    def half_of(c, which):
        return span(starts[c], which, outer * cfg.piece_rows[c])

    def landing(c):
        return pl.ds(starts[c] // 2, outer * cfg.piece_rows[c])

    def scatter_x(c):
        return over_x(0, c, r.sent, r.x_in, half_of(c, 1 - mine_in), landing(c))

    def gather_x(c, which):
        return over_x(1, c, r.summed, r.summed, half_of(c, which), half_of(c, which))

    def scatter_z(c, place, landed, peer):
        size = cfg.piece_rows[c]
        return over_z(
            0,
            c,
            place,
            landed,
            peer,
            r.z_out.at[span(starts[c] // 2, place, size)],
            r.z_in.at[landed, pl.ds(starts[c] // experts, size)],
        )

    def final(c, place):
        return span(starts[c], mine_in * outer + place, cfg.piece_rows[c])

    def gather_z(c, place, landed, peer):
        rows = final(c, landed)
        return over_z(1, c, place, landed, peer, r.summed.at[rows], r.summed.at[rows])

    def weight_grad(left, right):
        return dot_tn(left.reshape(-1, left.shape[-1]), right.reshape(-1, right.shape[-1]))

    products = ((r.h_norm, r.h_dq), (r.h_norm, r.h_dk), (r.h_norm, r.h_dv), (r.h_da, r.h_o))
    for c in range(pieces):
        rows = pl.ds(starts[c], experts * cfg.piece_rows[c])
        if c < 4:
            left, right = products[c]
            value = weight_grad(left[...], right[...])
            if value.shape[0] != experts * cfg.piece_rows[c]:
                r.sent[rows, :] = jnp.zeros((experts * cfg.piece_rows[c], side), bf16)
            r.sent[pl.ds(starts[c], value.shape[0]), :] = value.astype(bf16)
        else:
            pack_copy.wait()
            r.sent[rows, :] = (r.pack[...] + wide(r.pack_in[...])).astype(bf16)
        scatter_x(c).start()

    rows_all = cfg.micro * 2 * cfg.slots
    tile = 256
    steps = []
    for left, right, target in (
        (r.rows_v, r.gate_v, r.gate_grad),
        (r.rows_v, r.up_v, r.up_grad),
        (r.gate_v, r.grads_v, r.down_grad),
    ):
        for t in range(left.shape[-1] // tile):
            needs = ((0, 1), (0, 2), (3, 4))[len(steps) // (width // tile) if target is not r.down_grad else 2]
            steps.append((left, right, target, t, needs))

    loaded = set()
    flying = [None, None]

    def expert_step(index):
        left, right, target, t, needs = steps[index]
        if index == width // tile:
            loads[4].start()
        for k in needs:
            if k not in loaded:
                loads[k].wait()
                loaded.add(k)
        slot = index % 2
        if flying[slot] is not None:
            flying[slot].wait()
        wide_out = right.shape[-1]
        a = left[..., t * tile : (t + 1) * tile].reshape(rows_all, tile)
        r.stage[slot, :, :wide_out] = dot_tn(a, right[...].reshape(rows_all, wide_out)).astype(bf16)
        copy = pltpu.make_async_copy(
            r.stage.at[slot, :, pl.ds(0, wide_out)],
            target.at[pl.ds(t * tile, tile)],
            r.step_sem.at[index],
        )
        copy.start()
        flying[slot] = copy

    done = 0
    for c in range(pieces):
        upto = len(steps) * (c + 1) // pieces
        while done < upto:
            expert_step(done)
            done += 1
        scatter_x(c).wait_recv()
        rows = landing(c)
        r.z_out[rows, :] = (wide(r.sent[half_of(c, mine_in), :]) + wide(r.x_in[rows, :])).astype(bf16)

        def out_z(k, carry, c=c):
            place, peer = peer_of(k)
            scatter_z(c, place, mine_out, peer).start()
            return carry

        lax.fori_loop(1, outer, out_z, 0)

    for c in range(pieces):
        size = cfg.piece_rows[c]

        def add_z(k, total, c=c, size=size):
            place, peer = peer_of(k)
            scatter_z(c, place, place, peer).wait_recv()
            return total + wide(r.z_in[place, pl.ds(starts[c] // experts, size), :])

        total = lax.fori_loop(1, outer, add_z, wide(r.z_out[span(starts[c] // 2, mine_out, size), :]))
        r.summed[final(c, mine_out), :] = total.astype(bf16)

        def back_z(k, carry, c=c):
            place, peer = peer_of(k)
            gather_z(c, place, mine_out, peer).start()
            return carry

        lax.fori_loop(1, outer, back_z, 0)

    for c in range(pieces):

        def wait_z(k, carry, c=c):
            place, peer = peer_of(k)
            gather_z(c, place, place, peer).wait_recv()
            return carry

        lax.fori_loop(1, outer, wait_z, 0)
        gather_x(c, mine_in).start()
    for c in range(pieces):
        gather_x(c, 1 - mine_in).wait_recv()
    for c in range(pieces):
        scatter_x(c).wait_send()
        gather_x(c, mine_in).wait_send()

        def sent_z(k, carry, c=c):
            place, peer = peer_of(k)
            scatter_z(c, place, mine_out, peer).wait_send()
            gather_z(c, place, mine_out, peer).wait_send()
            return carry

        lax.fori_loop(1, outer, sent_z, 0)
    for copy in flying:
        copy.wait()


def run_tail(cfg, got):
    vmem, anywhere = pl.BlockSpec(memory_space=pltpu.VMEM), pl.BlockSpec(memory_space=pl.ANY)
    micro, width, inner, slots, experts = cfg.micro, cfg.width, cfg.inner, cfg.slots, cfg.experts
    side, outer = width // 2, experts // 2
    piece = -(-width // (16 * experts)) * 16
    small = -(-(3 * cfg.small_pad + 16) // (16 * experts)) * 16
    cfg.piece_rows = [piece] * 4 + [small]
    total = sum(cfg.piece_rows) * experts
    near = dict(
        h_norm=got.h_norm,
        h_da=got.h_da,
        h_o=got.h_o,
        h_dq=got.h_dq,
        h_dk=got.h_dk,
        h_dv=got.h_dv,
        mixer_grad=got.mixer_grad,
        residual_grad=got.residual_grad,
        rows_grad=got.rows_grad,
    )
    far = dict(
        h_rows=got.h_rows,
        h_grads=got.h_grads,
        h_inside=got.h_inside,
        h_up=got.h_up,
        h_gate=got.h_gate,
    )
    shape, dma = jax.ShapeDtypeStruct, pltpu.SemaphoreType.DMA
    outs = dict(
        summed=shape((total, side), bf16),
        gate_grad=shape((width, inner), bf16),
        up_grad=shape((width, inner), bf16),
        down_grad=shape((inner, width), bf16),
    )
    scratch = dict(
        rows_v=pltpu.VMEM((micro, 2, slots, width), bf16),
        grads_v=pltpu.VMEM((micro, 2, slots, width), bf16),
        up_v=pltpu.VMEM((micro, 2 * slots, inner), bf16),
        gate_v=pltpu.VMEM((micro, 2 * slots, inner), bf16),
        sent=pltpu.VMEM((total, side), bf16),
        x_in=pltpu.VMEM((total // 2, side), bf16),
        z_out=pltpu.VMEM((total // 2, side), bf16),
        z_in=pltpu.VMEM((outer, total // experts, side), bf16),
        pack=pltpu.VMEM((small * experts, side), f32),
        pack_out=pltpu.VMEM((small * experts, side), bf16),
        pack_in=pltpu.VMEM((small * experts, side), bf16),
        stage=pltpu.VMEM((2, 256, max(inner, width)), bf16),
        fetch=dma((5,)),
        step_sem=dma(((2 * width + inner) // 256,)),
        pack_sem=dma((2,)),
        x_send=dma((2, 5)),
        x_recv=dma((2, 5)),
        z_send=dma((2, 5, outer)),
        z_recv=dma((2, 5, outer)),
    )
    names = [*near, *far, *outs, *scratch]
    results = pl.pallas_call(
        functools.partial(tail_kernel, cfg, names),
        out_shape=[*outs.values()],
        in_specs=[vmem] * len(near) + [anywhere] * len(far),
        out_specs=[vmem] + [anywhere] * 3,
        scratch_shapes=[*scratch.values()],
        compiler_params=pltpu.CompilerParams(
            collective_id=1, has_side_effects=True, vmem_limit_bytes=60 * 2**20
        ),
        cost_estimate=pl.CostEstimate(
            flops=12 * micro * slots * width * inner, bytes_accessed=40_000_000, transcendentals=0
        ),
    )(*near.values(), *far.values())
    return types.SimpleNamespace(
        **dict(zip(outs, results, strict=True)), pad_rows=piece * experts
    )


def rope_tables(rows):
    half_width = HEAD_DIM // 2
    frequency = 10000.0 ** (-2.0 * np.arange(half_width, dtype=np.float64) / HEAD_DIM)
    angles = np.arange(rows, dtype=np.float64)[:, None] * frequency[None, :]
    angles = np.tile(angles, (1, LANES // half_width))
    return np.cos(angles).astype(np.float32), np.sin(angles).astype(np.float32)


def local(
    inputs,
    cotangent,
    prev_logits,
    lengths,
    routes,
    slot_order,
    norm_gain1,
    w_query,
    w_key,
    w_value,
    w_out,
    norm_gain2,
    router,
    router_residual,
    const_gate,
    const_value,
    expert_gate,
    expert_up,
    expert_down,
):
    micro, owned, width = inputs.shape
    tensors, peers = lax.axis_size("tensor"), lax.axis_size("expert")
    choices = router.shape[2]
    experts = choices - 4
    assert experts == peers and tensors == 2
    cap = 9 * 2 * owned // (8 * choices) + 1
    main, rem = cap // 16 * 16, cap % 16
    if rem > 2 or not main:
        main, rem = main + (16 if rem else 0), 0
    rem_rows = -(-rem * peers // 16) * 16
    cfg = types.SimpleNamespace(
        micro=micro,
        owned=owned,
        width=width,
        rows=owned * tensors,
        inner=expert_gate.shape[3],
        heads=w_query.shape[2] // HEAD_DIM,
        experts=experts,
        choices=choices,
        cap=cap,
        main=main,
        rem=rem,
        rem_rows=rem_rows,
        half_rows=peers // 2 * main,
        slots=peers * main + rem_rows,
        depth=micro if peers * main <= 512 else 1,
        sections=lax.axis_size("section"),
        seqs=lengths.shape[2] - 1,
        chunk=owned,
        small_pad=-(-(choices + 2) // 16) * 16,
    )
    cosine, sine = rope_tables(cfg.rows)
    ins = dict(
        lengths=lengths[:, 0],
        inputs=inputs,
        cotangent=cotangent,
        prev_in=jnp.transpose(prev_logits[0], (2, 0, 1)),
        route_row=jnp.swapaxes(routes[0], 1, 2),
        order_row=slot_order[0],
        gain1=norm_gain1,
        gain2=norm_gain2,
        w_query=w_query[0],
        w_key=w_key[0],
        w_value=w_value[0],
        w_out=w_out[0],
        router_in=router[0].T,
        const_gate=const_gate[0],
        residual_in=router_residual[0],
        const_value=const_value[0],
        cosine=jnp.asarray(cosine),
        sine=jnp.asarray(sine),
        gate=expert_gate[0, 0],
        up=expert_up[0, 0],
        down=expert_down[0, 0],
    )
    got = run_chain(cfg, ins)

    tail = run_tail(cfg, got)
    query_grad, key_grad, value_grad, out_grad = (
        wide(tail.summed[c * tail.pad_rows : c * tail.pad_rows + width]) for c in range(4)
    )
    small = wide(tail.summed[4 * tail.pad_rows :])
    pad = cfg.small_pad
    mixer_grad = jnp.concatenate([small[:pad], small[pad : 2 * pad]], axis=1)
    rows_grad = jnp.concatenate([small[2 * pad : 2 * pad + 8], small[2 * pad + 8 : 2 * pad + 16]], axis=1)
    residual_grad = small[2 * pad + 16 : 3 * pad + 16, :LANES]
    return (
        got.layer_out[None],
        got.input_grad[None],
        got.logit_grad[None, :, :, :choices],
        rows_grad[None, 2],
        query_grad[None],
        key_grad[None],
        value_grad[None],
        out_grad.T[None],
        rows_grad[None, 3],
        mixer_grad[:choices].T[None],
        residual_grad[None, :choices, :choices],
        mixer_grad[None, choices : choices + 2],
        rows_grad[None, :2],
        wide(tail.gate_grad)[None, None],
        wide(tail.up_grad)[None, None],
        wide(tail.down_grad)[None, None],
    )


def solution(mesh):
    tokens = ("expert", "tensor")
    in_specs = (
        P(None, tokens, None),
        P(None, tokens, None),
        P("section", None, tokens, None),
        P(None, "expert", None),
        P("section", None, tokens, None),
        P("section", None, tokens, None),
        P("section", None),
        P("section", None, "tensor"),
        P("section", None, "tensor"),
        P("section", None, "tensor"),
        P("section", "tensor", None),
        P("section", None),
        P("section", None, None),
        P("section", None, None),
        P("section", None, None),
        P("section", None, None),
        P("section", "expert", None, "tensor"),
        P("section", "expert", None, "tensor"),
        P("section", "expert", "tensor", None),
    )
    out_specs = (
        P("section", None, tokens, None),
        P("section", None, tokens, None),
        P("section", None, tokens, None),
        P("section", None),
        P("section", None, "tensor"),
        P("section", None, "tensor"),
        P("section", None, "tensor"),
        P("section", "tensor", None),
        P("section", None),
        P("section", None, None),
        P("section", None, None),
        P("section", None, None),
        P("section", None, None),
        P("section", "expert", None, "tensor"),
        P("section", "expert", None, "tensor"),
        P("section", "expert", "tensor", None),
    )
    return jax.shard_map(local, mesh=mesh, in_specs=in_specs, out_specs=out_specs, check_vma=False)
```

```python
import functools
import types

import jax
import jax.numpy as jnp
import numpy as np
from jax import lax
from jax.experimental import pallas as pl
from jax.experimental.pallas import tpu as pltpu
from jax.sharding import PartitionSpec as P

HEAD_DIM = 64
LANES = 128
EPSILON = 1e-06
MESH = pl.DeviceIdType.MESH
f32, bf16, i32 = jnp.float32, jnp.bfloat16, jnp.int32

P_NORM, P_OUT, P_ROWS, P_PART, P_GROWS, P_GPART, P_DA, P_DX = range(8)


def dot(left, right):
    return jnp.dot(left, right, preferred_element_type=f32)


def dot_nt(left, right):
    return lax.dot_general(left, right, (((1,), (1,)), ((), ())), preferred_element_type=f32)


def dot_tn(left, right):
    return lax.dot_general(left, right, (((0,), (0,)), ((), ())), preferred_element_type=f32)


def wide(values):
    return values.astype(f32)


def halves(values):
    upper = values.astype(bf16)
    return upper, (values - wide(upper)).astype(bf16)


def dot3(how, left, right):
    left_hi, left_lo = halves(left)
    right_hi, right_lo = halves(right)
    return how(left_hi, right_hi) + (how(left_hi, right_lo) + how(left_lo, right_hi))


def inverse_rms(values):
    return lax.rsqrt(jnp.mean(values * values, axis=-1, keepdims=True) + EPSILON)


def iota(shape, dim):
    return lax.broadcasted_iota(i32, shape, dim)


def flag(condition):
    return wide(condition.astype(i32))


def half_lanes(width):
    return (iota((1, width), 1) % HEAD_DIM) < HEAD_DIM // 2


def turned(values, cosine, sine):
    quarter = HEAD_DIM // 2
    other = jnp.where(
        half_lanes(LANES),
        -pltpu.roll(values, LANES - quarter, 1),
        pltpu.roll(values, quarter, 1),
    )
    return values * cosine + other * sine


def turned_back(values, cosine, sine):
    quarter = HEAD_DIM // 2
    other = jnp.where(
        half_lanes(LANES),
        pltpu.roll(values, LANES - quarter, 1),
        -pltpu.roll(values, quarter, 1),
    )
    return values * cosine + other * sine


def chain_kernel(cfg, names, *refs):
    r = types.SimpleNamespace(**dict(zip(names, refs, strict=True)))
    owned, rows, experts, cap, slots = cfg.owned, cfg.rows, cfg.experts, cfg.cap, cfg.slots
    choices, micro, sections, seqs = cfg.choices, cfg.micro, cfg.sections, cfg.seqs
    pairs, chunk = cfg.heads // 2, cfg.chunk
    scale = HEAD_DIM ** (-0.5)
    sec, me, core = (lax.axis_index(a) for a in ("section", "expert", "tensor"))
    other = 1 - core
    own_rows = pl.ds(pl.multiple_of(core * owned, owned), owned)
    other_rows = pl.ds(pl.multiple_of(other * owned, owned), owned)
    is_first, is_last = sec == 0, sec == sections - 1

    deep = cfg.depth == micro

    def slot(m):
        return m if deep else 0

    def pair(kind, m, j, source, target):
        return pltpu.make_async_remote_copy(
            src_ref=source,
            dst_ref=target,
            send_sem=r.pair_send.at[kind, m, j],
            recv_sem=r.pair_recv.at[kind, m, j],
            device_id={"tensor": other},
            device_id_type=MESH,
        )

    def hop(kind, m, source, target, section):
        return pltpu.make_async_remote_copy(
            src_ref=source,
            dst_ref=target,
            send_sem=r.hop_send.at[kind, m],
            recv_sem=r.hop_recv.at[kind, m],
            device_id={"section": section},
            device_id_type=MESH,
        )

    main, rem, half_rows, rem_rows = cfg.main, cfg.rem, cfg.half_rows, cfg.rem_rows
    rem_start = experts * main
    group = experts // 2
    my_group, in_group = me // group, lax.rem(me, group)
    group_of = (my_group, 1 - my_group)

    def slot_rows(index):
        return pl.ds(pl.multiple_of(index * main, main), main)

    def group_rows(g, offset=0):
        return pl.ds(pl.multiple_of(offset + group_of[g] * half_rows, 16), half_rows)

    def last_rows(offset=0):
        return pl.ds(pl.multiple_of(offset + rem_start, 16), rem_rows)

    def get(ref, g, offset=0, cols=slice(None)):
        value = ref[group_rows(g, offset), cols]
        if g == 1 and rem:
            value = jnp.concatenate([value, ref[last_rows(offset), cols]], axis=0)
        return value

    def put(ref, g, value, offset=0, cols=slice(None)):
        ref[group_rows(g, offset), cols] = value[:half_rows]
        if g == 1 and rem:
            ref[last_rows(offset), cols] = value[half_rows:]

    pieces = -(-half_rows // 256)
    hidden_cols = [
        slice(k * cfg.inner // pieces, (k + 1) * cfg.inner // pieces) for k in range(pieces)
    ]

    def parts(g):
        return [group_rows(g)] + ([last_rows()] if g == 1 and rem else [])

    def peers_in(g, act):
        def step(k, carry):
            act(group_of[g] * group + lax.rem(in_group + k, group))
            return carry

        lax.fori_loop(1 - g, group, step, 0)

    def exchange(kind, m, peer, landed, source, target):
        return pltpu.make_async_remote_copy(
            src_ref=source.at[slot_rows(peer)],
            dst_ref=target.at[slot_rows(landed)],
            send_sem=r.a2a_send.at[kind, m, peer],
            recv_sem=r.a2a_recv.at[kind, m, landed],
            device_id={"expert": peer},
            device_id_type=MESH,
        )

    def exchange_rem(kind, m, peer, landed, source, target):
        return pltpu.make_async_remote_copy(
            src_ref=source.at[peer],
            dst_ref=target.at[landed],
            send_sem=r.rem_send.at[kind, m, peer],
            recv_sem=r.rem_recv.at[kind, m, landed],
            device_id={"expert": peer},
            device_id_type=MESH,
        )

    outer = experts // 2
    mirrored = outer - 1 - me // 2

    def to_relay(kind, m, peer, source):
        place = lax.rem(peer, 2)
        return pltpu.make_async_remote_copy(
            src_ref=source.at[slot_rows(peer)],
            dst_ref=r.relay.at[kind, m, place],
            send_sem=r.a2a_send.at[kind, m, peer],
            recv_sem=r.relay_recv.at[kind, m, place],
            device_id={"section": 1 - sec},
            device_id_type=MESH,
        )

    def relay_copy(kind, m, place):
        target = (r.arrived.at[m, core], r.back.at[m], r.arrived.at[m, core], grad_back(m))[kind]
        return pltpu.make_async_remote_copy(
            src_ref=r.relay.at[kind, m, place],
            dst_ref=target.at[slot_rows(me)],
            send_sem=r.relay_send.at[kind, m, place],
            recv_sem=r.a2a_recv.at[kind, m, me],
            device_id={"section": 1 - sec, "expert": mirrored * 2 + place},
            device_id_type=MESH,
        )

    def relay(kind, m):
        for place in range(2):
            pltpu.make_async_remote_copy(
                src_ref=r.relay.at[kind, m, place],
                dst_ref=r.relay.at[kind, m, place],
                send_sem=r.relay_send.at[kind, m, place],
                recv_sem=r.relay_recv.at[kind, m, place],
                device_id={"section": 1 - sec},
                device_id_type=MESH,
            ).wait_recv()
            relay_copy(kind, m, place).start()

    def relays_for_first():
        return [(k, m) for k in range(2) for m in range(micro) if (k, m) != (1, micro - 1)]

    def send_block(kind, m, peer, source, target):
        if not cfg.relay:
            exchange(kind, m, peer, me, source, target).start()
            return
        aside = peer // 2 == mirrored
        if kind == 1:
            aside = aside & ((sec > 0) | (m < micro - 1))

        @pl.when(aside)
        def _():
            to_relay(kind, m, peer, source).start()

        @pl.when(jnp.logical_not(aside))
        def _():
            exchange(kind, m, peer, me, source, target).start()

    def lay_rem(ref, value):
        for k in range(rem):
            ref[:, k, :] = value[k * experts : (k + 1) * experts]

    def read_rem(ref):
        value = [ref[:, k, :] for k in range(rem)]
        rest = rem_rows - rem * experts
        if rest:
            value.append(jnp.zeros((rest, cfg.width), f32))
        return jnp.concatenate(value, axis=0).astype(bf16)

    def send_slots(kind, m, value):
        d = slot(m)
        outgoing, mine = r.outgoing.at[d], r.arrived.at[d, core]
        r.outgoing[d] = value[:rem_start].astype(bf16)
        for g in (1, 0):
            peers_in(g, lambda p: send_block(kind, m, p, outgoing, mine))
        if rem:
            rem_out, rem_in = r.rem_out.at[d], r.rem_in.at[d]
            lay_rem(rem_out, value[rem_start:])
            for g in (1, 0):
                peers_in(g, lambda p: exchange_rem(kind, m, p, me, rem_out, rem_in).start())
            rem_in[pl.ds(me, 1)] = rem_out[pl.ds(me, 1)]
        mine[slot_rows(me), :] = outgoing[slot_rows(me), :]

    def save(index, m, source, target):
        return pltpu.make_async_copy(source, target.at[m], r.local.at[index, m])

    def grad_back(m):
        return r.inside.at[slot(m), pl.ds(0, slots), pl.ds(0, cfg.width)]

    back_hop = min(1, sections - 2)
    def stage(m):
        return r.stage.at[m] if deep else r.partial.at[pl.ds(0, owned)]


    barrier = pltpu.get_barrier_semaphore()

    def greet(k, carry):
        pl.semaphore_signal(
            barrier, inc=1, device_id={"expert": lax.rem(me + k, experts)}, device_id_type=MESH
        )
        return carry

    lax.fori_loop(1, experts, greet, 0)
    pl.semaphore_signal(barrier, inc=1, device_id={"tensor": other}, device_id_type=MESH)

    @pl.when(sec > 0)
    def _():
        pl.semaphore_signal(barrier, inc=1, device_id={"section": sec - 1}, device_id_type=MESH)

    @pl.when(sec < sections - 1)
    def _():
        pl.semaphore_signal(barrier, inc=1, device_id={"section": sec + 1}, device_id_type=MESH)

    for m in range(micro):

        @pl.when(is_first)
        def _():
            pltpu.make_async_copy(r.inputs.at[m], r.x.at[m], r.local.at[0, m]).start()

        if deep:

            @pl.when(is_last)
            def _():
                pltpu.make_async_copy(r.cotangent.at[m], r.dz.at[m], r.local.at[9, m]).start()

    weights = [
        pltpu.make_async_copy(source, target, r.fetch.at[k])
        for k, (source, target) in enumerate(
            ((r.gate, r.gate_v), (r.up, r.up_v), (r.down, r.down_v))
        )
    ]
    for copy in weights:
        copy.start()
    if cfg.relay:
        for place in range(2):
            pl.semaphore_signal(
                barrier,
                inc=1,
                device_id={"section": 1 - sec, "expert": mirrored * 2 + place},
                device_id_type=MESH,
            )
    beside = (sec > 0).astype(i32) + (sec < sections - 1).astype(i32)
    pl.semaphore_wait(barrier, experts + beside + (2 if cfg.relay else 0))

    r.mixer[...] = jnp.zeros_like(r.mixer)
    r.mixer[:choices, :] = r.router_in[...]
    r.mixer[choices : choices + 2, :] = r.const_gate[...]
    r.residual[...] = jnp.zeros_like(r.residual)
    r.residual[:choices, :choices] = r.residual_in[...]
    r.prev_t[...] = jnp.zeros_like(r.prev_t)
    for m in range(micro):
        r.prev_t[m, :choices, :] = r.prev_in[:, m, :]
        table = jnp.concatenate(
            [r.route_row[m], r.order_row[m], jnp.zeros((13, owned), i32)], axis=0
        )
        unit = flag(iota((owned, owned), 0) == iota((owned, owned), 1)).astype(bf16)
        r.cols[m] = dot_nt(unit, wide(table).astype(bf16)).astype(i32)

    def seq_bias(m):
        row = iota((rows, 1), 0)
        start = jnp.zeros((rows, 1), i32)
        end = r.lengths[m, 0]
        for k in range(seqs):
            start = jnp.where(row >= end, row if k == seqs - 1 else end, start)
            end = end + r.lengths[m, min(k + 1, seqs)]
        for c in range(rows // chunk):
            piece = slice(c * chunk, (c + 1) * chunk)
            key = iota((chunk, rows), 1)
            seen = (key <= row[piece]) & (key >= start[piece])
            r.bias[piece, :] = jnp.where(seen, 0.0, -1e30).astype(bf16)

    def routing(m):
        lane = iota((owned, LANES), 1)
        lane_t = iota((LANES, owned), 0)
        col = [r.cols[m, :, k : k + 1] for k in range(2)]
        row = [r.route_row[m, k : k + 1, :] for k in range(2)]
        order_row, order_col = r.order_row[m], r.cols[m, :, 2:3]
        hot = [wide((lane == col[k]).astype(i32)) for k in range(2)]
        hot_t = [wide((lane_t == row[k]).astype(i32)) for k in range(2)]
        before = wide((order_row < order_col).astype(i32)).astype(bf16)
        before_t = wide((order_col < order_row).astype(i32)).astype(bf16)
        earlier = dot(before, (hot[0] + hot[1]).astype(bf16))
        earlier_t = dot((hot_t[0] + hot_t[1]).astype(bf16), before_t)
        for k in range(2):
            slot = jnp.sum(earlier * hot[k], axis=1, keepdims=True).astype(i32)
            slot_t = jnp.sum(earlier_t * hot_t[k], axis=0, keepdims=True).astype(i32)

            def placed(choice, at):
                first = choice * main + at
                late = rem_start + (at - main) * experts + choice
                kept = (choice < experts) & (at < cap)
                return jnp.where(kept, jnp.where(at < main, first, late), -1)

            place, place_t = placed(col[k], slot), placed(row[k], slot_t)
            r.place_col[m, :, k : k + 1] = place
            r.place_row[m, k : k + 1, :] = place_t

    def spread(m, k):
        return flag(iota((owned, slots), 1) == r.place_col[m, :, k : k + 1]).astype(bf16)

    def spread_t(m, k):
        return flag(iota((slots, owned), 0) == r.place_row[m, k : k + 1, :]).astype(bf16)

    def choice_flags(m):
        col = [r.cols[m, :, k : k + 1] for k in range(2)]
        copies = [wide((col[k] == experts + 1).astype(i32)) for k in range(2)]
        consts = [
            [wide((col[k] == experts + 2 + c).astype(i32)) for c in range(2)] for k in range(2)
        ]
        return col, copies, consts

    def unpack_gates(m):
        pack = r.gates[m]
        return [pack[:, k : k + 1] for k in range(2)], [pack[:, 2 + k : 3 + k] for k in range(2)]

    def through_expert(m, kind, pair_in, pair_out, target, kept, compute):
        d = slot(m)
        arrived, outgoing, result = r.arrived.at[d], r.outgoing.at[d], r.result.at[d]
        mine, theirs = arrived.at[core], arrived.at[other]
        if rem:
            rem_out, rem_in = r.rem_out.at[d], r.rem_in.at[d]
            rem_result, rem_back = r.rem_result.at[d], r.rem_back.at[d]
        passes = kind // 2

        def keep(index, half, rows_of):
            return pltpu.make_async_copy(
                arrived.at[half, rows_of], kept.at[m, half, rows_of], r.keep.at[passes, m, index]
            )

        def forward_pair(g, which, side):
            return [
                pair(pair_in, m, g + k, side.at[rows_of], side.at[rows_of])
                for k, rows_of in enumerate(parts(g))
            ]

        def sums(g):
            return [
                pair(pair_out, m, g + k, r.part_out.at[rows_of], r.part_in.at[rows_of])
                for k, rows_of in enumerate(parts(g))
            ]

        everything = pl.ds(0, slots)

        def kept_mine(g):
            return [keep(2 * g + k, core, rows_of) for k, rows_of in enumerate(parts(g))]

        def arrive(g):
            peers_in(g, lambda p: exchange(kind, m, p, p, outgoing, mine).wait_recv())
            if g == 1 and rem:
                for which in range(2):
                    peers_in(which, lambda p: exchange_rem(kind, m, p, p, rem_out, rem_in).wait_recv())
                mine[last_rows(), :] = read_rem(rem_in)
            for copy in forward_pair(g, core, mine):
                copy.start()
            for copy in kept_mine(g):
                copy.start()

        def work(g):
            put(r.partial, g, compute(core, g))
            for copy in forward_pair(g, other, theirs):
                copy.wait_recv()
            if g == 1:
                keep(1, other, everything).start()
            put(r.part_out, g, compute(other, g).astype(bf16))
            if g == 1:
                keep(1, other, everything).wait()
            for copy in sums(g):
                copy.start()

        def finish(g):
            for copy in sums(g):
                copy.wait_recv()
            value = get(r.partial, g) + wide(get(r.part_in, g))
            for copy in kept_mine(g):
                copy.wait()
            for copy in forward_pair(g, core, mine):
                copy.wait_send()
            put(result, g, value.astype(bf16))
            peers_in(g, lambda p: send_block(kind + 1, m, p, result, target))
            if g == 1 and rem:
                lay_rem(rem_result, value[half_rows:])
                for which in (1, 0):
                    peers_in(
                        which,
                        lambda p: exchange_rem(kind + 1, m, p, me, rem_result, rem_back).start(),
                    )
                rem_back[pl.ds(me, 1)] = rem_result[pl.ds(me, 1)]

        arrive(0)
        work(0)
        arrive(1)
        finish(0)
        work(1)
        finish(1)
        target[slot_rows(me), :] = result[slot_rows(me), :]
        for g in range(2):
            for copy in sums(g):
                copy.wait_send()
            peers_in(g, lambda p: exchange(kind, m, p, me, outgoing, mine).wait_send())
            if rem:
                peers_in(g, lambda p: exchange_rem(kind, m, p, me, rem_out, rem_in).wait_send())

    def wait_back(m, kind, target):
        result = r.result.at[slot(m)]
        if rem:
            rem_result, rem_back = r.rem_result.at[slot(m)], r.rem_back.at[slot(m)]
        for g in range(2):
            peers_in(g, lambda p: exchange(kind + 1, m, p, p, result, target).wait_recv())
            if rem:
                peers_in(g, lambda p: exchange_rem(kind + 1, m, p, p, rem_result, rem_back).wait_recv())
        if rem:
            target[last_rows(), :] = read_rem(rem_back)
        for g in range(2):
            peers_in(g, lambda p: exchange(kind + 1, m, p, me, result, target).wait_send())
            if rem:
                peers_in(g, lambda p: exchange_rem(kind + 1, m, p, me, rem_result, rem_back).wait_send())

    def attend(m):
        @pl.when(is_first)
        def _():
            pltpu.make_async_copy(r.inputs.at[m], r.x.at[m], r.local.at[0, m]).wait()

        @pl.when(sec > 0)
        def _():
            hop(0, m, r.hop_out.at[slot(m)], r.hop_in.at[0, m], sec - 1).wait_recv()
            r.x[m] = wide(r.hop_in[0, m])

        x = r.x[m]
        r.norm[m, own_rows, :] = (x * inverse_rms(x) * r.gain1[...]).astype(bf16)
        pair(P_NORM, m, 0, r.norm.at[m, own_rows], r.norm.at[m, own_rows]).start()
        routing(m)
        seq_bias(m)

        def project(some):
            normed = r.norm[m, some, :]
            cosine, sine = r.cosine[some, :], r.sine[some, :]
            for stash, weight in ((r.q, r.w_query), (r.k, r.w_key)):
                flat = dot(normed, weight[...])
                for p in range(pairs):
                    lanes = slice(p * LANES, (p + 1) * LANES)
                    stash[m, some, lanes] = turned(flat[:, lanes], cosine, sine).astype(bf16)
            r.v[m, some, :] = dot(normed, r.w_value[...]).astype(bf16)

        project(own_rows)
        pair(P_NORM, m, 0, r.norm.at[m, other_rows], r.norm.at[m, other_rows]).wait_recv()
        save(1, m, r.norm.at[m], r.h_norm).start()
        project(other_rows)

        r.logsum[m] = jnp.zeros((rows, LANES), f32)
        lane = iota((1, LANES), 1)

        def head_pair(p, inner):
            lanes = pl.ds(pl.multiple_of(p * LANES, LANES), LANES)
            q2, k2, v2 = r.q[m, :, lanes], r.k[m, :, lanes], r.v[m, :, lanes]
            for half in range(2):
                keep = wide(((lane // HEAD_DIM) == half).astype(i32)).astype(bf16)
                km, vm = k2 * keep, v2 * keep
                for c in range(rows // chunk):
                    piece, reach = slice(c * chunk, (c + 1) * chunk), (c + 1) * chunk
                    scores = dot_nt(q2[piece], km[:reach]) * scale + wide(r.bias[piece, :reach])
                    peak = jnp.max(scores, axis=-1, keepdims=True)
                    shifted = jnp.exp(scores - peak)
                    total = jnp.sum(shifted, axis=-1, keepdims=True)
                    probs = (shifted * (1.0 / total)).astype(bf16)
                    mixed = dot(probs, vm[:reach])
                    if half == 0:
                        r.mix[piece, :] = mixed
                    else:
                        r.o[m, piece, lanes] = (r.mix[piece, :] + mixed).astype(bf16)
                    r.logsum[m, piece, :] = jnp.where(
                        lane == 2 * p + half, peak + jnp.log(total), r.logsum[m, piece, :]
                    )
            return inner

        lax.fori_loop(0, pairs, head_pair, 0)
        save(2, m, r.o.at[m], r.h_o).start()

    def attend_send(m):
        r.half_out[...] = dot(r.o[m, other_rows, :], r.w_out[...]).astype(bf16)
        pair(P_OUT, m, 0, r.half_out, r.half_in.at[0, m]).start()
        summed = r.x[m] + dot(r.o[m, own_rows, :], r.w_out[...])
        pair(P_OUT, m, 0, r.half_out, r.half_in.at[0, m]).wait_recv()
        hidden = summed + wide(r.half_in[0, m])
        r.h[m] = hidden
        normed2 = (hidden * inverse_rms(hidden) * r.gain2[...]).astype(bf16)
        r.norm2[m] = normed2

        send_slots(0, m, dot(spread_t(m, 0) + spread_t(m, 1), normed2))

        mixer_hi, mixer_lo = halves(r.mixer[...])
        logits = dot_nt(normed2, mixer_hi) + dot_nt(normed2, mixer_lo)
        logits = logits + dot3(dot_tn, r.prev_t[m], r.residual[...])
        col, copies, consts = choice_flags(m)
        wide_lane = iota((owned, LANES), 1)
        picked = [
            jnp.sum(jnp.where(wide_lane == col[k], logits, 0.0), axis=1, keepdims=True)
            for k in range(2)
        ]
        gate = [jax.nn.sigmoid(picked[0] - picked[1]), jax.nn.sigmoid(picked[1] - picked[0])]
        rate = [jax.nn.sigmoid(logits[:, choices + c : choices + c + 1]) for c in range(2)]
        pack = jnp.zeros((owned, LANES), f32)
        for k, value in enumerate(gate + rate):
            pack = jnp.where(wide_lane == k, value, pack)
        r.gates[m] = pack
        pair(P_NORM, m, 0, r.norm.at[m, own_rows], r.norm.at[m, own_rows]).wait_send()
        pair(P_OUT, m, 0, r.half_out, r.half_in.at[0, m]).wait_send()

    def kept_forward(m):
        copies = [save(10, m, r.inside.at[slot(m)], r.h_inside)]
        if not deep:
            copies += [
                save(5, m, r.by_up.at[0], r.h_up),
                save(6, m, r.by_gate.at[0], r.h_gate),
            ]
        return copies

    def experts_forward(m):
        d = slot(m)
        by_up, by_gate, inside_of, arrived = r.by_up.at[d], r.by_gate.at[d], r.inside.at[d], r.arrived.at[d]

        @pl.when(m == 0)
        def _():
            for copy in weights:
                copy.wait()

        def compute(half, g):
            block = get(arrived.at[half], g)
            offset = half * slots
            total = 0.0
            for cols in hidden_cols:
                value = dot(block, r.gate_v[:, cols])
                upper = dot(block, r.up_v[:, cols])
                sig = jax.nn.sigmoid(value)
                active = value * sig
                inside = (active * upper).astype(bf16)
                put(by_up, g, active.astype(bf16), offset, cols)
                slope = upper * sig * (1.0 + value * (1.0 - sig))
                put(by_gate, g, slope.astype(bf16), offset, cols)
                put(inside_of, g, inside, offset, cols)
                total = total + dot(inside, r.down_v[cols, :])
            return total

        through_expert(m, 0, P_ROWS, P_PART, r.back.at[m], r.h_rows, compute)
        for copy in kept_forward(m):
            copy.start()

    def combine(m):
        gate, rate = unpack_gates(m)
        col, copies, consts = choice_flags(m)
        wait_back(m, 0, r.back.at[m])

        apart = [dot(spread(m, k), r.back[m]) for k in range(2)]
        out = r.h[m] + gate[0] * apart[0] + gate[1] * apart[1]
        own = gate[0] * copies[0] + gate[1] * copies[1]
        for c in range(2):
            on = gate[0] * consts[0][c] + gate[1] * consts[1][c]
            own = own + on * rate[c]
            out = out + (on * (1.0 - rate[c])) * r.const_value[c : c + 1, :]
        out = out + own * wide(r.norm2[m])
        stage(m)[...] = out
        save(3, m, stage(m), r.layer_out).start()

        @pl.when(sec < sections - 1)
        def _():
            r.hop_out[slot(m)] = out.astype(bf16)
            hop(0, m, r.hop_out.at[slot(m)], r.hop_in.at[0, m], sec + 1).start()

    def settle_forward(m):
        @pl.when(sec < sections - 1)
        def _():
            hop(0, m, r.hop_out.at[slot(m)], r.hop_in.at[0, m], sec + 1).wait_send()

        save(3, m, stage(m), r.layer_out).wait()
        save(1, m, r.norm.at[m], r.h_norm).wait()
        save(2, m, r.o.at[m], r.h_o).wait()
        for copy in kept_forward(m):
            copy.wait()

    r.mixer_grad[...] = jnp.zeros_like(r.mixer_grad)
    r.residual_grad[...] = jnp.zeros_like(r.residual_grad)
    r.rows_grad[...] = jnp.zeros_like(r.rows_grad)

    def fetched(m):
        return [
            pltpu.make_async_copy(r.h_up.at[m], r.by_up.at[0], r.local.at[7, m]),
            pltpu.make_async_copy(r.h_gate.at[m], r.by_gate.at[0], r.local.at[8, m]),
        ]

    def grad_start(m):
        d = slot(m)
        if deep:
            settle_forward(m)
        else:
            for copy in fetched(m):
                copy.start()

        @pl.when(is_last)
        def _():
            copy = pltpu.make_async_copy(r.cotangent.at[m], r.dz.at[d], r.local.at[9, m])
            if not deep:
                copy.start()
            copy.wait()

        @pl.when(sec < sections - 1)
        def _():
            hop(1, m, r.hop_out.at[d], r.hop_in.at[back_hop, m], sec + 1).wait_recv()
            r.dz[d] = wide(r.hop_in[back_hop, m])

        dz = r.dz[d]
        gate, rate = unpack_gates(m)
        leaving = [dot(spread_t(m, k), (gate[k] * dz).astype(bf16)) for k in range(2)]
        send_slots(2, m, leaving[0] + leaving[1])

        col, copies, consts = choice_flags(m)
        normed2 = r.norm2[m]
        dz_norm = jnp.sum(dz * wide(normed2), axis=1, keepdims=True)
        dz_const = [
            jnp.sum(dz * r.const_value[c : c + 1, :], axis=1, keepdims=True) for c in range(2)
        ]
        apart = [dot(spread(m, k), r.back[m]) for k in range(2)]
        dgate = []
        for k in range(2):
            value = jnp.sum(dz * apart[k], axis=1, keepdims=True)
            value = value + copies[k] * dz_norm
            for c in range(2):
                value = value + consts[k][c] * (rate[c] * dz_norm + (1.0 - rate[c]) * dz_const[c])
            dgate.append(value)
        coupled = gate[0] * gate[1] * (dgate[0] - dgate[1])
        lane = iota((owned, LANES), 1)
        dlogits = jnp.where(lane == col[0], coupled, jnp.where(lane == col[1], -coupled, 0.0))
        own = gate[0] * copies[0] + gate[1] * copies[1]
        for c in range(2):
            on = gate[0] * consts[0][c] + gate[1] * consts[1][c]
            own = own + on * rate[c]
            dmix = on * (dz_norm - dz_const[c]) * rate[c] * (1.0 - rate[c])
            dlogits = dlogits + jnp.where(lane == choices + c, dmix, 0.0)
            r.rows_grad[c : c + 1, :] += jnp.sum((on * (1.0 - rate[c])) * dz, axis=0, keepdims=True)
        dlogits_hi, dlogits_lo = halves(dlogits)
        r.mixer_grad[...] += dot_tn(dlogits_hi, normed2) + dot_tn(dlogits_lo, normed2)
        r.residual_grad[...] += dot3(dot, r.prev_t[m], dlogits)
        r.logit_grad[m] = dot3(dot_nt, dlogits, r.residual[...])
        r.dnorm[d] = dot3(dot, dlogits, r.mixer[...]) + own * dz

    def kept_backward(m):
        return [
            save(11, m, r.by_up.at[slot(m)], r.h_up),
            save(12, m, r.by_gate.at[slot(m)], r.h_gate),
        ]

    def experts_backward(m):
        d = slot(m)
        by_up, by_gate, arrived = r.by_up.at[d], r.by_gate.at[d], r.arrived.at[d]
        if not deep:
            for copy in fetched(m):
                copy.wait()

        def compute(half, g):
            block = get(arrived.at[half], g)
            offset = half * slots
            total = 0.0
            for cols in hidden_cols:
                dinside = dot_nt(block, r.down_v[cols, :])
                dvalue = (dinside * wide(get(by_gate, g, offset, cols))).astype(bf16)
                dupper = (dinside * wide(get(by_up, g, offset, cols))).astype(bf16)
                put(by_gate, g, dvalue, offset, cols)
                put(by_up, g, dupper, offset, cols)
                total = total + dot_nt(dvalue, r.gate_v[:, cols]) + dot_nt(dupper, r.up_v[:, cols])
            return total

        through_expert(m, 2, P_GROWS, P_GPART, grad_back(m), r.h_grads, compute)
        for copy in kept_backward(m):
            copy.start()

    def grad_attend(m):
        d = slot(m)
        wait_back(m, 2, grad_back(m))

        both = spread(m, 0) + spread(m, 1)
        dnorm = r.dnorm[d] + dot(both, grad_back(m)[...])
        hidden = r.h[m]
        root = inverse_rms(hidden)
        scaled = dnorm * r.gain2[...]
        pull = root * root * root * jnp.mean(hidden * scaled, axis=-1, keepdims=True)
        dhidden = r.dz[d] + root * scaled - hidden * pull
        r.rows_grad[3:4, :] += jnp.sum(dnorm * hidden * root, axis=0, keepdims=True)
        r.dh[...] = dhidden
        r.da[own_rows, :] = dhidden.astype(bf16)
        pair(P_DA, m, 0, r.da.at[own_rows], r.da.at[own_rows]).start()
        seq_bias(m)
        r.do[own_rows, :] = dot_nt(r.da[own_rows, :], r.w_out[...]).astype(bf16)
        pair(P_DA, m, 0, r.da.at[other_rows], r.da.at[other_rows]).wait_recv()
        save(13, m, r.da, r.h_da).start()
        r.do[other_rows, :] = dot_nt(r.da[other_rows, :], r.w_out[...]).astype(bf16)

        head_lane = iota((1, LANES), 1)

        def head_pair(p, inner):
            lanes = pl.ds(pl.multiple_of(p * LANES, LANES), LANES)
            q2, k2, v2 = r.q[m, :, lanes], r.k[m, :, lanes], r.v[m, :, lanes]
            do2 = r.do[:, lanes]
            for half in range(2):
                keep = wide(((head_lane // HEAD_DIM) == half).astype(i32)).astype(bf16)
                km, vm, qm, dom = k2 * keep, v2 * keep, q2 * keep, do2 * keep
                for c in range(rows // chunk):
                    piece, reach = slice(c * chunk, (c + 1) * chunk), (c + 1) * chunk
                    scores = dot_nt(q2[piece], km[:reach]) * scale + wide(r.bias[piece, :reach])
                    total = jnp.sum(
                        jnp.where(head_lane == 2 * p + half, r.logsum[m, piece, :], 0.0),
                        axis=1,
                        keepdims=True,
                    )
                    probs = jnp.exp(scores - total)
                    dprobs = dot_nt(do2[piece], vm[:reach])
                    meant = jnp.sum(dprobs * probs, axis=-1, keepdims=True)
                    dscores = (probs * (dprobs - meant)).astype(bf16)
                    dq = dot(dscores, km[:reach])
                    dk = dot_tn(dscores, qm[piece])
                    dv = dot_tn(probs.astype(bf16), dom[piece])
                    if half == 0:
                        r.mix[piece, :] = dq
                    else:
                        r.mix[piece, :] += dq
                    if half == 0 and c == 0:
                        r.mix_k[...] = jnp.zeros_like(r.mix_k)
                        r.mix_v[...] = jnp.zeros_like(r.mix_v)
                    r.mix_k[:reach, :] += dk
                    r.mix_v[:reach, :] += dv
            r.dq[:, lanes] = (turned_back(r.mix[...], r.cosine[...], r.sine[...]) * scale).astype(bf16)
            r.dk[:, lanes] = (turned_back(r.mix_k[...], r.cosine[...], r.sine[...]) * scale).astype(bf16)
            r.dv[:, lanes] = r.mix_v[...].astype(bf16)
            return inner

        lax.fori_loop(0, pairs, head_pair, 0)
        for copy in kept_heads(m):
            copy.start()

    def kept_heads(m):
        return [save(14, m, r.dq, r.h_dq), save(15, m, r.dk, r.h_dk), save(16, m, r.dv, r.h_dv)]

    def grad_finish(m):
        d = slot(m)

        def dnormed(piece):
            return (
                dot_nt(r.dq[piece, :], r.w_query[...])
                + dot_nt(r.dk[piece, :], r.w_key[...])
                + dot_nt(r.dv[piece, :], r.w_value[...])
            )

        save(13, m, r.da, r.h_da).wait()
        r.half_out[...] = dnormed(other_rows).astype(bf16)
        pair(P_DX, m, 0, r.half_out, r.half_in.at[1, m]).start()
        kept = dnormed(own_rows)
        pair(P_DX, m, 0, r.half_out, r.half_in.at[1, m]).wait_recv()
        dnorm1 = kept + wide(r.half_in[1, m])
        x = r.x[m]
        root1 = inverse_rms(x)
        scaled1 = dnorm1 * r.gain1[...]
        pull1 = root1 * root1 * root1 * jnp.mean(x * scaled1, axis=-1, keepdims=True)
        dx = r.dh[...] + root1 * scaled1 - x * pull1
        stage(m)[...] = dx
        save(4, m, stage(m), r.input_grad).start()

        @pl.when(sec > 0)
        def _():
            r.hop_out[d] = dx.astype(bf16)
            hop(1, m, r.hop_out.at[d], r.hop_in.at[back_hop, m], sec - 1).start()

        r.rows_grad[2:3, :] += jnp.sum(dnorm1 * x * root1, axis=0, keepdims=True)
        pair(P_DA, m, 0, r.da.at[own_rows], r.da.at[own_rows]).wait_send()
        pair(P_DX, m, 0, r.half_out, r.half_in.at[1, m]).wait_send()
        for copy in kept_heads(m):
            copy.wait()

    def settle_backward(m):
        @pl.when(sec > 0)
        def _():
            hop(1, m, r.hop_out.at[slot(m)], r.hop_in.at[back_hop, m], sec - 1).wait_send()

        save(4, m, stage(m), r.input_grad).wait()
        for copy in kept_backward(m):
            copy.wait()

    if deep:
        def all_of(*phases):
            def step(m, carry):
                for phase in phases:
                    phase(m)
                return carry

            lax.fori_loop(0, micro, step, 0)

        def turn(m):
            combine(m)

            @pl.when(is_last)
            def _():
                grad_start(m)

        def start_rest(m):
            @pl.when(sec < sections - 1)
            def _():
                grad_start(m)

        every = [(k, m) for k in range(4) for m in range(micro)]
        if cfg.relay:

            @pl.when(is_last)
            def _():
                for k, m in relays_for_first():
                    relay(k, m)

        all_of(attend, attend_send)
        all_of(experts_forward)
        all_of(turn)
        if cfg.relay:

            @pl.when(is_first)
            def _():
                for k, m in every:
                    relay(k, m)

        all_of(start_rest)
        all_of(experts_backward)
        all_of(grad_attend, grad_finish)
        if cfg.relay:

            @pl.when(is_last)
            def _():
                for k, m in every:
                    if k >= 2:
                        relay(k, m)
                for k, m in relays_for_first() + [(k, m) for k, m in every if k >= 2]:
                    for place in range(2):
                        relay_copy(k, m, place).wait_send()

            @pl.when(is_first)
            def _():
                for k, m in every:
                    for place in range(2):
                        relay_copy(k, m, place).wait_send()

        for m in range(micro):
            settle_backward(m)
    else:

        def there(m, carry):
            for phase in (attend, attend_send, experts_forward, combine, settle_forward):
                phase(m)
            return carry

        def back_again(m, carry):
            for phase in (grad_start, experts_backward, grad_attend, grad_finish, settle_backward):
                phase(m)
            return carry

        lax.fori_loop(0, micro, there, 0)
        lax.fori_loop(0, micro, back_again, 0)


def run_chain(cfg, ins):
    vmem, anywhere = pl.BlockSpec(memory_space=pltpu.VMEM), pl.BlockSpec(memory_space=pl.ANY)
    smem = pl.BlockSpec(memory_space=pltpu.SMEM)
    far = {"inputs", "cotangent", "gate", "up", "down"}
    micro, owned, rows, width, inner = cfg.micro, cfg.owned, cfg.rows, cfg.width, cfg.inner
    heads_width, slots = cfg.heads * HEAD_DIM, cfg.slots
    shape = jax.ShapeDtypeStruct
    outs = dict(
        logit_grad=shape((micro, owned, LANES), f32),
        mixer_grad=shape((LANES, width), f32),
        residual_grad=shape((LANES, LANES), f32),
        rows_grad=shape((8, width), f32),
    )
    hbm_outs = dict(
        layer_out=shape((micro, owned, width), f32),
        input_grad=shape((micro, owned, width), f32),
        h_rows=shape((micro, 2, slots, width), bf16),
        h_grads=shape((micro, 2, slots, width), bf16),
        h_inside=shape((micro, 2 * slots, inner), bf16),
        h_up=shape((micro, 2 * slots, inner), bf16),
        h_gate=shape((micro, 2 * slots, inner), bf16),
        h_norm=shape((micro, rows, width), bf16),
        h_da=shape((micro, rows, width), bf16),
        h_o=shape((micro, rows, heads_width), bf16),
        h_dq=shape((micro, rows, heads_width), bf16),
        h_dk=shape((micro, rows, heads_width), bf16),
        h_dv=shape((micro, rows, heads_width), bf16),
    )
    dma = pltpu.SemaphoreType.DMA
    depth = cfg.depth
    rem_scratch = {}
    if depth == micro:
        rem_scratch = dict(stage=pltpu.VMEM((micro, owned, width), f32))
    if cfg.rem:
        last = pltpu.VMEM((depth, cfg.experts, cfg.rem, width), f32)
        rem_sem = dma((4, micro, cfg.experts))
        rem_scratch |= dict(
            rem_out=last, rem_in=last, rem_result=last, rem_back=last, rem_send=rem_sem, rem_recv=rem_sem
        )
    if cfg.relay:
        relay_sem = dma((4, micro, 2))
        rem_scratch |= dict(
            relay=pltpu.VMEM((4, micro, 2, cfg.main, width), bf16),
            relay_send=relay_sem,
            relay_recv=relay_sem,
        )
    scratch = dict(
        gate_v=pltpu.VMEM((width, inner), bf16),
        up_v=pltpu.VMEM((width, inner), bf16),
        down_v=pltpu.VMEM((inner, width), bf16),
        x=pltpu.VMEM((micro, owned, width), f32),
        h=pltpu.VMEM((micro, owned, width), f32),
        norm=pltpu.VMEM((micro, rows, width), bf16),
        norm2=pltpu.VMEM((micro, owned, width), bf16),
        q=pltpu.VMEM((micro, rows, heads_width), bf16),
        k=pltpu.VMEM((micro, rows, heads_width), bf16),
        v=pltpu.VMEM((micro, rows, heads_width), bf16),
        o=pltpu.VMEM((micro, rows, heads_width), bf16),
        logsum=pltpu.VMEM((micro, rows, LANES), f32),
        mixer=pltpu.VMEM((LANES, width), f32),
        residual=pltpu.VMEM((LANES, LANES), f32),
        prev_t=pltpu.VMEM((micro, LANES, owned), f32),
        cols=pltpu.VMEM((micro, owned, 16), i32),
        gates=pltpu.VMEM((micro, owned, LANES), f32),
        place_col=pltpu.VMEM((micro, owned, 2), i32),
        place_row=pltpu.VMEM((micro, 2, owned), i32),
        bias=pltpu.VMEM((rows, rows), bf16),
        arrived=pltpu.VMEM((depth, 2, slots, width), bf16),
        part_in=pltpu.VMEM((slots, width), bf16),
        back=pltpu.VMEM((micro, slots, width), bf16),
        half_in=pltpu.VMEM((2, micro, owned, width), bf16),
        hop_in=pltpu.VMEM((min(2, cfg.sections - 1), micro, owned, width), bf16),
        outgoing=pltpu.VMEM((depth, cfg.experts * cfg.main, width), bf16),
        part_out=pltpu.VMEM((slots, width), bf16),
        result=pltpu.VMEM((depth, slots, width), bf16),
        partial=pltpu.VMEM((max(slots, owned), width), f32),
        half_out=pltpu.VMEM((owned, width), bf16),
        hop_out=pltpu.VMEM((depth, owned, width), bf16),
        inside=pltpu.VMEM((depth, 2 * slots, inner), bf16),
        **rem_scratch,
        by_up=pltpu.VMEM((depth, 2 * slots, inner), bf16),
        by_gate=pltpu.VMEM((depth, 2 * slots, inner), bf16),
        dz=pltpu.VMEM((depth, owned, width), f32),
        dh=pltpu.VMEM((owned, width), f32),
        dnorm=pltpu.VMEM((depth, owned, width), f32),
        da=pltpu.VMEM((rows, width), bf16),
        do=pltpu.VMEM((rows, heads_width), bf16),
        dq=pltpu.VMEM((rows, heads_width), bf16),
        dk=pltpu.VMEM((rows, heads_width), bf16),
        dv=pltpu.VMEM((rows, heads_width), bf16),
        mix=pltpu.VMEM((rows, LANES), f32),
        mix_k=pltpu.VMEM((rows, LANES), f32),
        mix_v=pltpu.VMEM((rows, LANES), f32),
        pair_send=dma((8, micro, 3)),
        pair_recv=dma((8, micro, 3)),
        hop_send=dma((2, micro)),
        hop_recv=dma((2, micro)),
        a2a_send=dma((4, micro, cfg.experts)),
        a2a_recv=dma((4, micro, cfg.experts)),
        local=dma((17, micro)),
        keep=dma((2, micro, 4)),
        fetch=dma((3,)),
    )
    names = [*ins, *outs, *hbm_outs, *scratch]
    flops = 2 * micro * (2 * slots * width * inner * 6 + rows * width * heads_width * 10)
    results = pl.pallas_call(
        functools.partial(chain_kernel, cfg, names),
        out_shape=[*outs.values(), *hbm_outs.values()],
        in_specs=[
            smem if name == "lengths" else anywhere if name in far else vmem for name in ins
        ],
        out_specs=[vmem] * len(outs) + [anywhere] * len(hbm_outs),
        scratch_shapes=[*scratch.values()],
        compiler_params=pltpu.CompilerParams(
            collective_id=0, has_side_effects=True, vmem_limit_bytes=60 * 2**20
        ),
        cost_estimate=pl.CostEstimate(flops=flops, bytes_accessed=50_000_000, transcendentals=0),
    )(*ins.values())
    return types.SimpleNamespace(**dict(zip([*outs, *hbm_outs], results, strict=True)))


def tail_kernel(cfg, names, *refs):
    r = types.SimpleNamespace(**dict(zip(names, refs, strict=True)))
    experts, width, pad = cfg.experts, cfg.width, cfg.small_pad
    side = width // 2
    outer = experts // 2
    me, core = lax.axis_index("expert"), lax.axis_index("tensor")
    mine_out, mine_in = me // 2, lax.rem(me, 2)
    beside = me + 1 - 2 * mine_in
    pieces = len(cfg.piece_rows)
    starts = [sum(cfg.piece_rows[:c]) * experts for c in range(pieces)]

    def peer_of(k):
        place = lax.rem(mine_out + k, outer)
        return place, place * 2 + mine_in

    barrier = pltpu.get_barrier_semaphore()
    pl.semaphore_signal(barrier, inc=1, device_id={"tensor": 1 - core}, device_id_type=MESH)
    pl.semaphore_signal(barrier, inc=1, device_id={"expert": beside}, device_id_type=MESH)

    def greet(k, carry):
        pl.semaphore_signal(barrier, inc=1, device_id={"expert": peer_of(k)[1]}, device_id_type=MESH)
        return carry

    lax.fori_loop(1, outer, greet, 0)

    loads = [
        pltpu.make_async_copy(source, target, r.fetch.at[k])
        for k, (source, target) in enumerate(
            (
                (r.h_rows, r.rows_v),
                (r.h_gate, r.gate_v),
                (r.h_up, r.up_v),
                (r.h_grads, r.grads_v),
                (r.h_inside, r.gate_v),
            )
        )
    ]
    for copy in loads[:4]:
        copy.start()

    r.pack[...] = jnp.zeros_like(r.pack)
    r.pack[:pad, :] = r.mixer_grad[:pad, :side]
    r.pack[pad : 2 * pad, :] = r.mixer_grad[:pad, side:]
    r.pack[2 * pad : 2 * pad + 8, :] = r.rows_grad[:, :side]
    r.pack[2 * pad + 8 : 2 * pad + 16, :] = r.rows_grad[:, side:]
    r.pack[2 * pad + 16 : 3 * pad + 16, :LANES] = r.residual_grad[:pad, :]
    r.pack_out[...] = r.pack[...].astype(bf16)
    pl.semaphore_wait(barrier, outer + 1)
    pack_copy = pltpu.make_async_remote_copy(
        src_ref=r.pack_out,
        dst_ref=r.pack_in,
        send_sem=r.pack_sem.at[0],
        recv_sem=r.pack_sem.at[1],
        device_id={"tensor": 1 - core},
        device_id_type=MESH,
    )
    pack_copy.start()

    def span(start, index, size):
        return pl.ds(pl.multiple_of(start + index * size, 16), size)

    def over_x(stage, c, source, target, from_rows, to_rows):
        return pltpu.make_async_remote_copy(
            src_ref=source.at[from_rows],
            dst_ref=target.at[to_rows],
            send_sem=r.x_send.at[stage, c],
            recv_sem=r.x_recv.at[stage, c],
            device_id={"expert": beside},
            device_id_type=MESH,
        )

    def over_z(stage, c, place, landed, peer, source, target):
        return pltpu.make_async_remote_copy(
            src_ref=source,
            dst_ref=target,
            send_sem=r.z_send.at[stage, c, place],
            recv_sem=r.z_recv.at[stage, c, landed],
            device_id={"expert": peer},
            device_id_type=MESH,
        )

    def half_of(c, which):
        return span(starts[c], which, outer * cfg.piece_rows[c])

    def landing(c):
        return pl.ds(starts[c] // 2, outer * cfg.piece_rows[c])

    def scatter_x(c):
        return over_x(0, c, r.sent, r.x_in, half_of(c, 1 - mine_in), landing(c))

    def gather_x(c, which):
        return over_x(1, c, r.summed, r.summed, half_of(c, which), half_of(c, which))

    def scatter_z(c, place, landed, peer):
        size = cfg.piece_rows[c]
        return over_z(
            0,
            c,
            place,
            landed,
            peer,
            r.z_out.at[span(starts[c] // 2, place, size)],
            r.z_in.at[landed, pl.ds(starts[c] // experts, size)],
        )

    def final(c, place):
        return span(starts[c], mine_in * outer + place, cfg.piece_rows[c])

    def gather_z(c, place, landed, peer):
        rows = final(c, landed)
        return over_z(1, c, place, landed, peer, r.summed.at[rows], r.summed.at[rows])

    def weight_grad(left, right):
        return dot_tn(left.reshape(-1, left.shape[-1]), right.reshape(-1, right.shape[-1]))

    products = ((r.h_norm, r.h_dq), (r.h_norm, r.h_dk), (r.h_norm, r.h_dv), (r.h_da, r.h_o))
    for c in range(pieces):
        rows = pl.ds(starts[c], experts * cfg.piece_rows[c])
        if c < 4:
            left, right = products[c]
            value = weight_grad(left[...], right[...])
            if value.shape[0] != experts * cfg.piece_rows[c]:
                r.sent[rows, :] = jnp.zeros((experts * cfg.piece_rows[c], side), bf16)
            r.sent[pl.ds(starts[c], value.shape[0]), :] = value.astype(bf16)
        else:
            pack_copy.wait()
            r.sent[rows, :] = (r.pack[...] + wide(r.pack_in[...])).astype(bf16)
        scatter_x(c).start()

    rows_all = cfg.micro * 2 * cfg.slots
    tile = 256
    steps = []
    for left, right, target in (
        (r.rows_v, r.gate_v, r.gate_grad),
        (r.rows_v, r.up_v, r.up_grad),
        (r.gate_v, r.grads_v, r.down_grad),
    ):
        for t in range(left.shape[-1] // tile):
            needs = ((0, 1), (0, 2), (3, 4))[len(steps) // (width // tile) if target is not r.down_grad else 2]
            steps.append((left, right, target, t, needs))

    loaded = set()
    flying = [None, None]

    def expert_step(index):
        left, right, target, t, needs = steps[index]
        if index == width // tile:
            loads[4].start()
        for k in needs:
            if k not in loaded:
                loads[k].wait()
                loaded.add(k)
        slot = index % 2
        if flying[slot] is not None:
            flying[slot].wait()
        wide_out = right.shape[-1]
        a = left[..., t * tile : (t + 1) * tile].reshape(rows_all, tile)
        r.stage[slot, :, :wide_out] = dot_tn(a, right[...].reshape(rows_all, wide_out)).astype(bf16)
        copy = pltpu.make_async_copy(
            r.stage.at[slot, :, pl.ds(0, wide_out)],
            target.at[pl.ds(t * tile, tile)],
            r.step_sem.at[index],
        )
        copy.start()
        flying[slot] = copy

    done = 0
    for c in range(pieces):
        upto = len(steps) * (c + 1) // pieces
        while done < upto:
            expert_step(done)
            done += 1
        scatter_x(c).wait_recv()
        rows = landing(c)
        r.z_out[rows, :] = (wide(r.sent[half_of(c, mine_in), :]) + wide(r.x_in[rows, :])).astype(bf16)

        def out_z(k, carry, c=c):
            place, peer = peer_of(k)
            scatter_z(c, place, mine_out, peer).start()
            return carry

        lax.fori_loop(1, outer, out_z, 0)

    for c in range(pieces):
        size = cfg.piece_rows[c]

        def add_z(k, total, c=c, size=size):
            place, peer = peer_of(k)
            scatter_z(c, place, place, peer).wait_recv()
            return total + wide(r.z_in[place, pl.ds(starts[c] // experts, size), :])

        total = lax.fori_loop(1, outer, add_z, wide(r.z_out[span(starts[c] // 2, mine_out, size), :]))
        r.summed[final(c, mine_out), :] = total.astype(bf16)

        def back_z(k, carry, c=c):
            place, peer = peer_of(k)
            gather_z(c, place, mine_out, peer).start()
            return carry

        lax.fori_loop(1, outer, back_z, 0)

    for c in range(pieces):

        def wait_z(k, carry, c=c):
            place, peer = peer_of(k)
            gather_z(c, place, place, peer).wait_recv()
            return carry

        lax.fori_loop(1, outer, wait_z, 0)
        gather_x(c, mine_in).start()
    for c in range(pieces):
        gather_x(c, 1 - mine_in).wait_recv()
    for c in range(pieces):
        scatter_x(c).wait_send()
        gather_x(c, mine_in).wait_send()

        def sent_z(k, carry, c=c):
            place, peer = peer_of(k)
            scatter_z(c, place, mine_out, peer).wait_send()
            gather_z(c, place, mine_out, peer).wait_send()
            return carry

        lax.fori_loop(1, outer, sent_z, 0)
    for copy in flying:
        copy.wait()


def run_tail(cfg, got):
    vmem, anywhere = pl.BlockSpec(memory_space=pltpu.VMEM), pl.BlockSpec(memory_space=pl.ANY)
    micro, width, inner, slots, experts = cfg.micro, cfg.width, cfg.inner, cfg.slots, cfg.experts
    side, outer = width // 2, experts // 2
    piece = -(-width // (16 * experts)) * 16
    small = -(-(3 * cfg.small_pad + 16) // (16 * experts)) * 16
    cfg.piece_rows = [piece] * 4 + [small]
    total = sum(cfg.piece_rows) * experts
    near = dict(
        h_norm=got.h_norm,
        h_da=got.h_da,
        h_o=got.h_o,
        h_dq=got.h_dq,
        h_dk=got.h_dk,
        h_dv=got.h_dv,
        mixer_grad=got.mixer_grad,
        residual_grad=got.residual_grad,
        rows_grad=got.rows_grad,
    )
    far = dict(
        h_rows=got.h_rows,
        h_grads=got.h_grads,
        h_inside=got.h_inside,
        h_up=got.h_up,
        h_gate=got.h_gate,
    )
    shape, dma = jax.ShapeDtypeStruct, pltpu.SemaphoreType.DMA
    outs = dict(
        summed=shape((total, side), bf16),
        gate_grad=shape((width, inner), bf16),
        up_grad=shape((width, inner), bf16),
        down_grad=shape((inner, width), bf16),
    )
    scratch = dict(
        rows_v=pltpu.VMEM((micro, 2, slots, width), bf16),
        grads_v=pltpu.VMEM((micro, 2, slots, width), bf16),
        up_v=pltpu.VMEM((micro, 2 * slots, inner), bf16),
        gate_v=pltpu.VMEM((micro, 2 * slots, inner), bf16),
        sent=pltpu.VMEM((total, side), bf16),
        x_in=pltpu.VMEM((total // 2, side), bf16),
        z_out=pltpu.VMEM((total // 2, side), bf16),
        z_in=pltpu.VMEM((outer, total // experts, side), bf16),
        pack=pltpu.VMEM((small * experts, side), f32),
        pack_out=pltpu.VMEM((small * experts, side), bf16),
        pack_in=pltpu.VMEM((small * experts, side), bf16),
        stage=pltpu.VMEM((2, 256, max(inner, width)), bf16),
        fetch=dma((5,)),
        step_sem=dma(((2 * width + inner) // 256,)),
        pack_sem=dma((2,)),
        x_send=dma((2, 5)),
        x_recv=dma((2, 5)),
        z_send=dma((2, 5, outer)),
        z_recv=dma((2, 5, outer)),
    )
    names = [*near, *far, *outs, *scratch]
    results = pl.pallas_call(
        functools.partial(tail_kernel, cfg, names),
        out_shape=[*outs.values()],
        in_specs=[vmem] * len(near) + [anywhere] * len(far),
        out_specs=[vmem] + [anywhere] * 3,
        scratch_shapes=[*scratch.values()],
        compiler_params=pltpu.CompilerParams(
            collective_id=1, has_side_effects=True, vmem_limit_bytes=60 * 2**20
        ),
        cost_estimate=pl.CostEstimate(
            flops=12 * micro * slots * width * inner, bytes_accessed=40_000_000, transcendentals=0
        ),
    )(*near.values(), *far.values())
    return types.SimpleNamespace(
        **dict(zip(outs, results, strict=True)), pad_rows=piece * experts
    )


def rope_tables(rows):
    half_width = HEAD_DIM // 2
    frequency = 10000.0 ** (-2.0 * np.arange(half_width, dtype=np.float64) / HEAD_DIM)
    angles = np.arange(rows, dtype=np.float64)[:, None] * frequency[None, :]
    angles = np.tile(angles, (1, LANES // half_width))
    return np.cos(angles).astype(np.float32), np.sin(angles).astype(np.float32)


def local(
    inputs,
    cotangent,
    prev_logits,
    lengths,
    routes,
    slot_order,
    norm_gain1,
    w_query,
    w_key,
    w_value,
    w_out,
    norm_gain2,
    router,
    router_residual,
    const_gate,
    const_value,
    expert_gate,
    expert_up,
    expert_down,
):
    micro, owned, width = inputs.shape
    tensors, peers = lax.axis_size("tensor"), lax.axis_size("expert")
    choices = router.shape[2]
    experts = choices - 4
    assert experts == peers and tensors == 2
    cap = 9 * 2 * owned // (8 * choices) + 1
    main, rem = cap // 16 * 16, cap % 16
    if rem > 2 or not main:
        main, rem = main + (16 if rem else 0), 0
    rem_rows = -(-rem * peers // 16) * 16
    cfg = types.SimpleNamespace(
        micro=micro,
        owned=owned,
        width=width,
        rows=owned * tensors,
        inner=expert_gate.shape[3],
        heads=w_query.shape[2] // HEAD_DIM,
        experts=experts,
        choices=choices,
        cap=cap,
        main=main,
        rem=rem,
        rem_rows=rem_rows,
        half_rows=peers // 2 * main,
        slots=peers * main + rem_rows,
        depth=micro if peers * main <= 512 else 1,
        sections=lax.axis_size("section"),
        seqs=lengths.shape[2] - 1,
        chunk=owned,
        small_pad=-(-(choices + 2) // 16) * 16,
    )
    cfg.relay = cfg.depth == micro and cfg.sections == 2 and peers == 8
    cosine, sine = rope_tables(cfg.rows)
    ins = dict(
        lengths=lengths[:, 0],
        inputs=inputs,
        cotangent=cotangent,
        prev_in=jnp.transpose(prev_logits[0], (2, 0, 1)),
        route_row=jnp.swapaxes(routes[0], 1, 2),
        order_row=slot_order[0],
        gain1=norm_gain1,
        gain2=norm_gain2,
        w_query=w_query[0],
        w_key=w_key[0],
        w_value=w_value[0],
        w_out=w_out[0],
        router_in=router[0].T,
        const_gate=const_gate[0],
        residual_in=router_residual[0],
        const_value=const_value[0],
        cosine=jnp.asarray(cosine),
        sine=jnp.asarray(sine),
        gate=expert_gate[0, 0],
        up=expert_up[0, 0],
        down=expert_down[0, 0],
    )
    got = run_chain(cfg, ins)

    tail = run_tail(cfg, got)
    query_grad, key_grad, value_grad, out_grad = (
        wide(tail.summed[c * tail.pad_rows : c * tail.pad_rows + width]) for c in range(4)
    )
    small = wide(tail.summed[4 * tail.pad_rows :])
    pad = cfg.small_pad
    mixer_grad = jnp.concatenate([small[:pad], small[pad : 2 * pad]], axis=1)
    rows_grad = jnp.concatenate([small[2 * pad : 2 * pad + 8], small[2 * pad + 8 : 2 * pad + 16]], axis=1)
    residual_grad = small[2 * pad + 16 : 3 * pad + 16, :LANES]
    return (
        got.layer_out[None],
        got.input_grad[None],
        got.logit_grad[None, :, :, :choices],
        rows_grad[None, 2],
        query_grad[None],
        key_grad[None],
        value_grad[None],
        out_grad.T[None],
        rows_grad[None, 3],
        mixer_grad[:choices].T[None],
        residual_grad[None, :choices, :choices],
        mixer_grad[None, choices : choices + 2],
        rows_grad[None, :2],
        wide(tail.gate_grad)[None, None],
        wide(tail.up_grad)[None, None],
        wide(tail.down_grad)[None, None],
    )


def solution(mesh):
    tokens = ("expert", "tensor")
    in_specs = (
        P(None, tokens, None),
        P(None, tokens, None),
        P("section", None, tokens, None),
        P(None, "expert", None),
        P("section", None, tokens, None),
        P("section", None, tokens, None),
        P("section", None),
        P("section", None, "tensor"),
        P("section", None, "tensor"),
        P("section", None, "tensor"),
        P("section", "tensor", None),
        P("section", None),
        P("section", None, None),
        P("section", None, None),
        P("section", None, None),
        P("section", None, None),
        P("section", "expert", None, "tensor"),
        P("section", "expert", None, "tensor"),
        P("section", "expert", "tensor", None),
    )
    out_specs = (
        P("section", None, tokens, None),
        P("section", None, tokens, None),
        P("section", None, tokens, None),
        P("section", None),
        P("section", None, "tensor"),
        P("section", None, "tensor"),
        P("section", None, "tensor"),
        P("section", "tensor", None),
        P("section", None),
        P("section", None, None),
        P("section", None, None),
        P("section", None, None),
        P("section", None, None),
        P("section", "expert", None, "tensor"),
        P("section", "expert", None, "tensor"),
        P("section", "expert", "tensor", None),
    )
    return jax.shard_map(local, mesh=mesh, in_specs=in_specs, out_specs=out_specs, check_vma=False)
```

```python
import functools
import types

import jax
import jax.numpy as jnp
import numpy as np
from jax import lax
from jax.experimental import pallas as pl
from jax.experimental.pallas import tpu as pltpu
from jax.sharding import PartitionSpec as P

HEAD_DIM = 64
LANES = 128
EPSILON = 1e-06
MESH = pl.DeviceIdType.MESH
f32, bf16, i32 = jnp.float32, jnp.bfloat16, jnp.int32

P_NORM, P_OUT, P_ROWS, P_PART, P_GROWS, P_GPART, P_DA, P_DX = range(8)


def dot(left, right):
    return jnp.dot(left, right, preferred_element_type=f32)


def dot_nt(left, right):
    return lax.dot_general(left, right, (((1,), (1,)), ((), ())), preferred_element_type=f32)


def dot_tn(left, right):
    return lax.dot_general(left, right, (((0,), (0,)), ((), ())), preferred_element_type=f32)


def wide(values):
    return values.astype(f32)


def halves(values):
    upper = values.astype(bf16)
    return upper, (values - wide(upper)).astype(bf16)


def dot3(how, left, right):
    left_hi, left_lo = halves(left)
    right_hi, right_lo = halves(right)
    return how(left_hi, right_hi) + (how(left_hi, right_lo) + how(left_lo, right_hi))


def inverse_rms(values):
    return lax.rsqrt(jnp.mean(values * values, axis=-1, keepdims=True) + EPSILON)


def iota(shape, dim):
    return lax.broadcasted_iota(i32, shape, dim)


def flag(condition):
    return wide(condition.astype(i32))


def half_lanes(width):
    return (iota((1, width), 1) % HEAD_DIM) < HEAD_DIM // 2


def turned(values, cosine, sine):
    quarter = HEAD_DIM // 2
    other = jnp.where(
        half_lanes(LANES),
        -pltpu.roll(values, LANES - quarter, 1),
        pltpu.roll(values, quarter, 1),
    )
    return values * cosine + other * sine


def turned_back(values, cosine, sine):
    quarter = HEAD_DIM // 2
    other = jnp.where(
        half_lanes(LANES),
        pltpu.roll(values, LANES - quarter, 1),
        -pltpu.roll(values, quarter, 1),
    )
    return values * cosine + other * sine


def chain_kernel(cfg, names, *refs):
    r = types.SimpleNamespace(**dict(zip(names, refs, strict=True)))
    owned, rows, experts, cap, slots = cfg.owned, cfg.rows, cfg.experts, cfg.cap, cfg.slots
    choices, micro, sections, seqs = cfg.choices, cfg.micro, cfg.sections, cfg.seqs
    pairs, chunk = cfg.heads // 2, cfg.chunk
    scale = HEAD_DIM ** (-0.5)
    sec, me, core = (lax.axis_index(a) for a in ("section", "expert", "tensor"))
    other = 1 - core
    own_rows = pl.ds(pl.multiple_of(core * owned, owned), owned)
    other_rows = pl.ds(pl.multiple_of(other * owned, owned), owned)
    is_first, is_last = sec == 0, sec == sections - 1

    deep = cfg.depth == micro

    def slot(m):
        return m if deep else 0

    def pair(kind, m, j, source, target):
        return pltpu.make_async_remote_copy(
            src_ref=source,
            dst_ref=target,
            send_sem=r.pair_send.at[kind, m, j],
            recv_sem=r.pair_recv.at[kind, m, j],
            device_id={"tensor": other},
            device_id_type=MESH,
        )

    def hop(kind, m, source, target, section):
        return pltpu.make_async_remote_copy(
            src_ref=source,
            dst_ref=target,
            send_sem=r.hop_send.at[kind, m],
            recv_sem=r.hop_recv.at[kind, m],
            device_id={"section": section},
            device_id_type=MESH,
        )

    main, rem, half_rows, rem_rows = cfg.main, cfg.rem, cfg.half_rows, cfg.rem_rows
    rem_start = experts * main
    group = experts // 2
    my_group, in_group = me // group, lax.rem(me, group)
    group_of = (my_group, 1 - my_group)

    def slot_rows(index):
        return pl.ds(pl.multiple_of(index * main, main), main)

    def group_rows(g, offset=0):
        return pl.ds(pl.multiple_of(offset + group_of[g] * half_rows, 16), half_rows)

    def last_rows(offset=0):
        return pl.ds(pl.multiple_of(offset + rem_start, 16), rem_rows)

    def get(ref, g, offset=0, cols=slice(None)):
        value = ref[group_rows(g, offset), cols]
        if g == 1 and rem:
            value = jnp.concatenate([value, ref[last_rows(offset), cols]], axis=0)
        return value

    def put(ref, g, value, offset=0, cols=slice(None)):
        ref[group_rows(g, offset), cols] = value[:half_rows]
        if g == 1 and rem:
            ref[last_rows(offset), cols] = value[half_rows:]

    pieces = -(-half_rows // 256)
    hidden_cols = [
        slice(k * cfg.inner // pieces, (k + 1) * cfg.inner // pieces) for k in range(pieces)
    ]

    def parts(g):
        return [group_rows(g)] + ([last_rows()] if g == 1 and rem else [])

    def peers_in(g, act):
        def step(k, carry):
            act(group_of[g] * group + lax.rem(in_group + k, group))
            return carry

        lax.fori_loop(1 - g, group, step, 0)

    def exchange(kind, m, peer, landed, source, target):
        return pltpu.make_async_remote_copy(
            src_ref=source.at[slot_rows(peer)],
            dst_ref=target.at[slot_rows(landed)],
            send_sem=r.a2a_send.at[kind, m, peer],
            recv_sem=r.a2a_recv.at[kind, m, landed],
            device_id={"expert": peer},
            device_id_type=MESH,
        )

    def exchange_rem(kind, m, peer, landed, source, target):
        return pltpu.make_async_remote_copy(
            src_ref=source.at[peer],
            dst_ref=target.at[landed],
            send_sem=r.rem_send.at[kind, m, peer],
            recv_sem=r.rem_recv.at[kind, m, landed],
            device_id={"expert": peer},
            device_id_type=MESH,
        )

    outer = experts // 2
    mirrored = outer - 1 - me // 2

    def to_relay(kind, m, peer, source):
        place = lax.rem(peer, 2)
        return pltpu.make_async_remote_copy(
            src_ref=source.at[slot_rows(peer)],
            dst_ref=r.relay.at[kind, m, place],
            send_sem=r.a2a_send.at[kind, m, peer],
            recv_sem=r.relay_recv.at[kind, m, place],
            device_id={"section": 1 - sec},
            device_id_type=MESH,
        )

    def relay_copy(kind, m, place):
        target = (r.arrived.at[m, core], r.back.at[m], r.arrived.at[m, core], grad_back(m))[kind]
        return pltpu.make_async_remote_copy(
            src_ref=r.relay.at[kind, m, place],
            dst_ref=target.at[slot_rows(me)],
            send_sem=r.relay_send.at[kind, m, place],
            recv_sem=r.a2a_recv.at[kind, m, me],
            device_id={"section": 1 - sec, "expert": mirrored * 2 + place},
            device_id_type=MESH,
        )

    def relay(kind, m):
        for place in range(2):
            pltpu.make_async_remote_copy(
                src_ref=r.relay.at[kind, m, place],
                dst_ref=r.relay.at[kind, m, place],
                send_sem=r.relay_send.at[kind, m, place],
                recv_sem=r.relay_recv.at[kind, m, place],
                device_id={"section": 1 - sec},
                device_id_type=MESH,
            ).wait_recv()
            relay_copy(kind, m, place).start()

    def relays_for_first():
        return [(k, m) for k in range(2) for m in range(micro) if (k, m) != (1, micro - 1)]

    def send_block(kind, m, peer, source, target):
        if not cfg.relay:
            exchange(kind, m, peer, me, source, target).start()
            return
        aside = peer // 2 == mirrored
        if kind == 1:
            aside = aside & ((sec > 0) | (m < micro - 1))

        @pl.when(aside)
        def _():
            to_relay(kind, m, peer, source).start()

        @pl.when(jnp.logical_not(aside))
        def _():
            exchange(kind, m, peer, me, source, target).start()

    def lay_rem(ref, value):
        for k in range(rem):
            ref[:, k, :] = value[k * experts : (k + 1) * experts]

    def read_rem(ref):
        value = [ref[:, k, :] for k in range(rem)]
        rest = rem_rows - rem * experts
        if rest:
            value.append(jnp.zeros((rest, cfg.width), f32))
        return jnp.concatenate(value, axis=0).astype(bf16)

    def send_slots(kind, m, value):
        d = slot(m)
        outgoing, mine = r.outgoing.at[d], r.arrived.at[d, core]
        r.outgoing[d] = value[:rem_start].astype(bf16)
        for g in (1, 0):
            peers_in(g, lambda p: send_block(kind, m, p, outgoing, mine))
        if rem:
            rem_out, rem_in = r.rem_out.at[d], r.rem_in.at[d]
            lay_rem(rem_out, value[rem_start:])
            for g in (1, 0):
                peers_in(g, lambda p: exchange_rem(kind, m, p, me, rem_out, rem_in).start())
            rem_in[pl.ds(me, 1)] = rem_out[pl.ds(me, 1)]
        mine[slot_rows(me), :] = outgoing[slot_rows(me), :]

    def save(index, m, source, target):
        return pltpu.make_async_copy(source, target.at[m], r.local.at[index, m])

    def grad_back(m):
        return r.inside.at[slot(m), pl.ds(0, slots), pl.ds(0, cfg.width)]

    back_hop = min(1, sections - 2)
    def stage(m):
        return r.stage.at[m] if deep else r.partial.at[pl.ds(0, owned)]


    barrier = pltpu.get_barrier_semaphore()

    def greet(k, carry):
        pl.semaphore_signal(
            barrier, inc=1, device_id={"expert": lax.rem(me + k, experts)}, device_id_type=MESH
        )
        return carry

    lax.fori_loop(1, experts, greet, 0)
    pl.semaphore_signal(barrier, inc=1, device_id={"tensor": other}, device_id_type=MESH)

    @pl.when(sec > 0)
    def _():
        pl.semaphore_signal(barrier, inc=1, device_id={"section": sec - 1}, device_id_type=MESH)

    @pl.when(sec < sections - 1)
    def _():
        pl.semaphore_signal(barrier, inc=1, device_id={"section": sec + 1}, device_id_type=MESH)

    for m in range(micro):

        @pl.when(is_first)
        def _():
            pltpu.make_async_copy(r.inputs.at[m], r.x.at[m], r.local.at[0, m]).start()

        if deep:

            @pl.when(is_last)
            def _():
                pltpu.make_async_copy(r.cotangent.at[m], r.dz.at[m], r.local.at[9, m]).start()

    weights = [
        pltpu.make_async_copy(source, target, r.fetch.at[k])
        for k, (source, target) in enumerate(
            ((r.gate, r.gate_v), (r.up, r.up_v), (r.down, r.down_v))
        )
    ]
    for copy in weights:
        copy.start()
    if cfg.relay:
        for place in range(2):
            pl.semaphore_signal(
                barrier,
                inc=1,
                device_id={"section": 1 - sec, "expert": mirrored * 2 + place},
                device_id_type=MESH,
            )
    beside = (sec > 0).astype(i32) + (sec < sections - 1).astype(i32)
    pl.semaphore_wait(barrier, experts + beside + (2 if cfg.relay else 0))

    r.mixer[...] = jnp.zeros_like(r.mixer)
    r.mixer[:choices, :] = r.router_in[...]
    r.mixer[choices : choices + 2, :] = r.const_gate[...]
    r.residual[...] = jnp.zeros_like(r.residual)
    r.residual[:choices, :choices] = r.residual_in[...]
    r.prev_t[...] = jnp.zeros_like(r.prev_t)
    for m in range(micro):
        r.prev_t[m, :choices, :] = r.prev_in[:, m, :]
        table = jnp.concatenate(
            [r.route_row[m], r.order_row[m], jnp.zeros((13, owned), i32)], axis=0
        )
        unit = flag(iota((owned, owned), 0) == iota((owned, owned), 1)).astype(bf16)
        r.cols[m] = dot_nt(unit, wide(table).astype(bf16)).astype(i32)

    def seq_bias(m):
        row = iota((rows, 1), 0)
        start = jnp.zeros((rows, 1), i32)
        end = r.lengths[m, 0]
        for k in range(seqs):
            start = jnp.where(row >= end, row if k == seqs - 1 else end, start)
            end = end + r.lengths[m, min(k + 1, seqs)]
        for c in range(rows // chunk):
            piece = slice(c * chunk, (c + 1) * chunk)
            key = iota((chunk, rows), 1)
            seen = (key <= row[piece]) & (key >= start[piece])
            r.bias[piece, :] = jnp.where(seen, 0.0, -1e30).astype(r.bias.dtype)

    def routing(m):
        lane = iota((owned, LANES), 1)
        lane_t = iota((LANES, owned), 0)
        col = [r.cols[m, :, k : k + 1] for k in range(2)]
        row = [r.route_row[m, k : k + 1, :] for k in range(2)]
        order_row, order_col = r.order_row[m], r.cols[m, :, 2:3]
        hot = [wide((lane == col[k]).astype(i32)) for k in range(2)]
        hot_t = [wide((lane_t == row[k]).astype(i32)) for k in range(2)]
        before = wide((order_row < order_col).astype(i32)).astype(bf16)
        before_t = wide((order_col < order_row).astype(i32)).astype(bf16)
        earlier = dot(before, (hot[0] + hot[1]).astype(bf16))
        earlier_t = dot((hot_t[0] + hot_t[1]).astype(bf16), before_t)
        for k in range(2):
            slot = jnp.sum(earlier * hot[k], axis=1, keepdims=True).astype(i32)
            slot_t = jnp.sum(earlier_t * hot_t[k], axis=0, keepdims=True).astype(i32)

            def placed(choice, at):
                first = choice * main + at
                late = rem_start + (at - main) * experts + choice
                kept = (choice < experts) & (at < cap)
                return jnp.where(kept, jnp.where(at < main, first, late), -1)

            place, place_t = placed(col[k], slot), placed(row[k], slot_t)
            r.place_col[m, :, k : k + 1] = place
            r.place_row[m, k : k + 1, :] = place_t

    def spread(m, k):
        return flag(iota((owned, slots), 1) == r.place_col[m, :, k : k + 1]).astype(bf16)

    def spread_t(m, k):
        return flag(iota((slots, owned), 0) == r.place_row[m, k : k + 1, :]).astype(bf16)

    def choice_flags(m):
        col = [r.cols[m, :, k : k + 1] for k in range(2)]
        copies = [wide((col[k] == experts + 1).astype(i32)) for k in range(2)]
        consts = [
            [wide((col[k] == experts + 2 + c).astype(i32)) for c in range(2)] for k in range(2)
        ]
        return col, copies, consts

    def unpack_gates(m):
        pack = r.gates[m]
        return [pack[:, k : k + 1] for k in range(2)], [pack[:, 2 + k : 3 + k] for k in range(2)]

    def through_expert(m, kind, pair_in, pair_out, target, kept, compute):
        d = slot(m)
        arrived, outgoing, result = r.arrived.at[d], r.outgoing.at[d], r.result.at[d]
        mine, theirs = arrived.at[core], arrived.at[other]
        if rem:
            rem_out, rem_in = r.rem_out.at[d], r.rem_in.at[d]
            rem_result, rem_back = r.rem_result.at[d], r.rem_back.at[d]
        passes = kind // 2

        def keep(index, half, rows_of):
            return pltpu.make_async_copy(
                arrived.at[half, rows_of], kept.at[m, half, rows_of], r.keep.at[passes, m, index]
            )

        def forward_pair(g, which, side):
            return [
                pair(pair_in, m, g + k, side.at[rows_of], side.at[rows_of])
                for k, rows_of in enumerate(parts(g))
            ]

        def sums(g):
            return [
                pair(pair_out, m, g + k, r.part_out.at[rows_of], r.part_in.at[rows_of])
                for k, rows_of in enumerate(parts(g))
            ]

        everything = pl.ds(0, slots)

        def kept_mine(g):
            return [keep(2 * g + k, core, rows_of) for k, rows_of in enumerate(parts(g))]

        def arrive(g):
            peers_in(g, lambda p: exchange(kind, m, p, p, outgoing, mine).wait_recv())
            if g == 1 and rem:
                for which in range(2):
                    peers_in(which, lambda p: exchange_rem(kind, m, p, p, rem_out, rem_in).wait_recv())
                mine[last_rows(), :] = read_rem(rem_in)
            for copy in forward_pair(g, core, mine):
                copy.start()
            for copy in kept_mine(g):
                copy.start()

        def work(g):
            put(r.partial, g, compute(core, g))
            for copy in forward_pair(g, other, theirs):
                copy.wait_recv()
            if g == 1:
                keep(1, other, everything).start()
            put(r.part_out, g, compute(other, g).astype(bf16))
            if g == 1:
                keep(1, other, everything).wait()
            for copy in sums(g):
                copy.start()

        def finish(g):
            for copy in sums(g):
                copy.wait_recv()
            value = get(r.partial, g) + wide(get(r.part_in, g))
            for copy in kept_mine(g):
                copy.wait()
            for copy in forward_pair(g, core, mine):
                copy.wait_send()
            put(result, g, value.astype(bf16))
            peers_in(g, lambda p: send_block(kind + 1, m, p, result, target))
            if g == 1 and rem:
                lay_rem(rem_result, value[half_rows:])
                for which in (1, 0):
                    peers_in(
                        which,
                        lambda p: exchange_rem(kind + 1, m, p, me, rem_result, rem_back).start(),
                    )
                rem_back[pl.ds(me, 1)] = rem_result[pl.ds(me, 1)]

        arrive(0)
        work(0)
        arrive(1)
        finish(0)
        work(1)
        finish(1)
        target[slot_rows(me), :] = result[slot_rows(me), :]
        for g in range(2):
            for copy in sums(g):
                copy.wait_send()
            peers_in(g, lambda p: exchange(kind, m, p, me, outgoing, mine).wait_send())
            if rem:
                peers_in(g, lambda p: exchange_rem(kind, m, p, me, rem_out, rem_in).wait_send())

    def wait_back(m, kind, target):
        result = r.result.at[slot(m)]
        if rem:
            rem_result, rem_back = r.rem_result.at[slot(m)], r.rem_back.at[slot(m)]
        for g in range(2):
            peers_in(g, lambda p: exchange(kind + 1, m, p, p, result, target).wait_recv())
            if rem:
                peers_in(g, lambda p: exchange_rem(kind + 1, m, p, p, rem_result, rem_back).wait_recv())
        if rem:
            target[last_rows(), :] = read_rem(rem_back)
        for g in range(2):
            peers_in(g, lambda p: exchange(kind + 1, m, p, me, result, target).wait_send())
            if rem:
                peers_in(g, lambda p: exchange_rem(kind + 1, m, p, me, rem_result, rem_back).wait_send())

    def attend(m):
        @pl.when(is_first)
        def _():
            pltpu.make_async_copy(r.inputs.at[m], r.x.at[m], r.local.at[0, m]).wait()

        @pl.when(sec > 0)
        def _():
            hop(0, m, r.hop_out.at[slot(m)], r.hop_in.at[0, m], sec - 1).wait_recv()
            r.x[m] = wide(r.hop_in[0, m])

        x = r.x[m]
        r.norm[m, own_rows, :] = (x * inverse_rms(x) * r.gain1[...]).astype(bf16)
        pair(P_NORM, m, 0, r.norm.at[m, own_rows], r.norm.at[m, own_rows]).start()
        routing(m)
        seq_bias(m)

        def project(some):
            normed = r.norm[m, some, :]
            cosine, sine = r.cosine[some, :], r.sine[some, :]
            for stash, weight, factor in ((r.q, r.w_query, scale), (r.k, r.w_key, 1.0)):
                flat = dot(normed, weight[...]) * factor
                for p in range(pairs):
                    lanes = slice(p * LANES, (p + 1) * LANES)
                    stash[m, some, lanes] = turned(flat[:, lanes], cosine, sine).astype(bf16)
            r.v[m, some, :] = dot(normed, r.w_value[...]).astype(bf16)

        project(own_rows)
        pair(P_NORM, m, 0, r.norm.at[m, other_rows], r.norm.at[m, other_rows]).wait_recv()
        save(1, m, r.norm.at[m], r.h_norm).start()
        project(other_rows)

        r.logsum[m] = jnp.zeros((rows, LANES), f32)
        lane = iota((1, LANES), 1)

        def head_pair(p, inner):
            lanes = pl.ds(pl.multiple_of(p * LANES, LANES), LANES)
            q2, k2, v2 = r.q[m, :, lanes], r.k[m, :, lanes], r.v[m, :, lanes]
            for half in range(2):
                keep = wide(((lane // HEAD_DIM) == half).astype(i32)).astype(bf16)
                km, vm = k2 * keep, v2 * keep
                for c in range(rows // chunk):
                    piece, reach = slice(c * chunk, (c + 1) * chunk), (c + 1) * chunk
                    scores = dot_nt(q2[piece], km[:reach]) + wide(r.bias[piece, :reach])
                    peak = jnp.max(scores, axis=-1, keepdims=True)
                    shifted = jnp.exp(scores - peak)
                    total = jnp.sum(shifted, axis=-1, keepdims=True)
                    mixed = dot(shifted.astype(bf16), vm[:reach]) * (1.0 / total)
                    if half == 0:
                        r.mix[piece, :] = mixed
                    else:
                        r.o[m, piece, lanes] = (r.mix[piece, :] + mixed).astype(bf16)
                    r.logsum[m, piece, :] = jnp.where(
                        lane == 2 * p + half, peak + jnp.log(total), r.logsum[m, piece, :]
                    )
            return inner

        lax.fori_loop(0, pairs, head_pair, 0)
        save(2, m, r.o.at[m], r.h_o).start()

    def attend_send(m):
        r.half_out[...] = dot(r.o[m, other_rows, :], r.w_out[...]).astype(bf16)
        pair(P_OUT, m, 0, r.half_out, r.half_in.at[0, m]).start()
        summed = r.x[m] + dot(r.o[m, own_rows, :], r.w_out[...])
        pair(P_OUT, m, 0, r.half_out, r.half_in.at[0, m]).wait_recv()
        hidden = summed + wide(r.half_in[0, m])
        r.h[m] = hidden
        normed2 = (hidden * inverse_rms(hidden) * r.gain2[...]).astype(bf16)
        r.norm2[m] = normed2

        send_slots(0, m, dot(spread_t(m, 0) + spread_t(m, 1), normed2))

        mixer_hi, mixer_lo = halves(r.mixer[...])
        logits = dot_nt(normed2, mixer_hi) + dot_nt(normed2, mixer_lo)
        logits = logits + dot3(dot_tn, r.prev_t[m], r.residual[...])
        col, copies, consts = choice_flags(m)
        wide_lane = iota((owned, LANES), 1)
        picked = [
            jnp.sum(jnp.where(wide_lane == col[k], logits, 0.0), axis=1, keepdims=True)
            for k in range(2)
        ]
        gate = [jax.nn.sigmoid(picked[0] - picked[1]), jax.nn.sigmoid(picked[1] - picked[0])]
        rate = [jax.nn.sigmoid(logits[:, choices + c : choices + c + 1]) for c in range(2)]
        pack = jnp.zeros((owned, LANES), f32)
        for k, value in enumerate(gate + rate):
            pack = jnp.where(wide_lane == k, value, pack)
        r.gates[m] = pack
        pair(P_NORM, m, 0, r.norm.at[m, own_rows], r.norm.at[m, own_rows]).wait_send()
        pair(P_OUT, m, 0, r.half_out, r.half_in.at[0, m]).wait_send()

    def kept_forward(m):
        copies = [save(10, m, r.inside.at[slot(m)], r.h_inside)]
        if not deep:
            copies += [
                save(5, m, r.by_up.at[0], r.h_up),
                save(6, m, r.by_gate.at[0], r.h_gate),
            ]
        return copies

    def experts_forward(m):
        d = slot(m)
        by_up, by_gate, inside_of, arrived = r.by_up.at[d], r.by_gate.at[d], r.inside.at[d], r.arrived.at[d]

        @pl.when(m == 0)
        def _():
            for copy in weights:
                copy.wait()

        def compute(half, g):
            block = get(arrived.at[half], g)
            offset = half * slots
            total = 0.0
            for cols in hidden_cols:
                value = dot(block, r.gate_v[:, cols])
                upper = dot(block, r.up_v[:, cols])
                sig = jax.nn.sigmoid(value)
                active = value * sig
                inside = (active * upper).astype(bf16)
                put(by_up, g, active.astype(bf16), offset, cols)
                slope = upper * sig * (1.0 + value * (1.0 - sig))
                put(by_gate, g, slope.astype(bf16), offset, cols)
                put(inside_of, g, inside, offset, cols)
                total = total + dot(inside, r.down_v[cols, :])
            return total

        through_expert(m, 0, P_ROWS, P_PART, r.back.at[m], r.h_rows, compute)
        for copy in kept_forward(m):
            copy.start()

    def combine(m):
        gate, rate = unpack_gates(m)
        col, copies, consts = choice_flags(m)
        wait_back(m, 0, r.back.at[m])

        apart = [dot(spread(m, k), r.back[m]) for k in range(2)]
        out = r.h[m] + gate[0] * apart[0] + gate[1] * apart[1]
        own = gate[0] * copies[0] + gate[1] * copies[1]
        for c in range(2):
            on = gate[0] * consts[0][c] + gate[1] * consts[1][c]
            own = own + on * rate[c]
            out = out + (on * (1.0 - rate[c])) * r.const_value[c : c + 1, :]
        out = out + own * wide(r.norm2[m])
        stage(m)[...] = out
        save(3, m, stage(m), r.layer_out).start()

        @pl.when(sec < sections - 1)
        def _():
            r.hop_out[slot(m)] = out.astype(bf16)
            hop(0, m, r.hop_out.at[slot(m)], r.hop_in.at[0, m], sec + 1).start()

    def settle_forward(m):
        @pl.when(sec < sections - 1)
        def _():
            hop(0, m, r.hop_out.at[slot(m)], r.hop_in.at[0, m], sec + 1).wait_send()

        save(3, m, stage(m), r.layer_out).wait()
        save(1, m, r.norm.at[m], r.h_norm).wait()
        save(2, m, r.o.at[m], r.h_o).wait()
        for copy in kept_forward(m):
            copy.wait()

    r.mixer_grad[...] = jnp.zeros_like(r.mixer_grad)
    r.residual_grad[...] = jnp.zeros_like(r.residual_grad)
    r.rows_grad[...] = jnp.zeros_like(r.rows_grad)

    def fetched(m):
        return [
            pltpu.make_async_copy(r.h_up.at[m], r.by_up.at[0], r.local.at[7, m]),
            pltpu.make_async_copy(r.h_gate.at[m], r.by_gate.at[0], r.local.at[8, m]),
        ]

    def grad_start(m):
        d = slot(m)
        if deep:
            settle_forward(m)
        else:
            for copy in fetched(m):
                copy.start()

        @pl.when(is_last)
        def _():
            copy = pltpu.make_async_copy(r.cotangent.at[m], r.dz.at[d], r.local.at[9, m])
            if not deep:
                copy.start()
            copy.wait()

        @pl.when(sec < sections - 1)
        def _():
            hop(1, m, r.hop_out.at[d], r.hop_in.at[back_hop, m], sec + 1).wait_recv()
            r.dz[d] = wide(r.hop_in[back_hop, m])

        dz = r.dz[d]
        gate, rate = unpack_gates(m)
        leaving = [dot(spread_t(m, k), (gate[k] * dz).astype(bf16)) for k in range(2)]
        send_slots(2, m, leaving[0] + leaving[1])

        col, copies, consts = choice_flags(m)
        normed2 = r.norm2[m]
        dz_norm = jnp.sum(dz * wide(normed2), axis=1, keepdims=True)
        dz_const = [
            jnp.sum(dz * r.const_value[c : c + 1, :], axis=1, keepdims=True) for c in range(2)
        ]
        apart = [dot(spread(m, k), r.back[m]) for k in range(2)]
        dgate = []
        for k in range(2):
            value = jnp.sum(dz * apart[k], axis=1, keepdims=True)
            value = value + copies[k] * dz_norm
            for c in range(2):
                value = value + consts[k][c] * (rate[c] * dz_norm + (1.0 - rate[c]) * dz_const[c])
            dgate.append(value)
        coupled = gate[0] * gate[1] * (dgate[0] - dgate[1])
        lane = iota((owned, LANES), 1)
        dlogits = jnp.where(lane == col[0], coupled, jnp.where(lane == col[1], -coupled, 0.0))
        own = gate[0] * copies[0] + gate[1] * copies[1]
        for c in range(2):
            on = gate[0] * consts[0][c] + gate[1] * consts[1][c]
            own = own + on * rate[c]
            dmix = on * (dz_norm - dz_const[c]) * rate[c] * (1.0 - rate[c])
            dlogits = dlogits + jnp.where(lane == choices + c, dmix, 0.0)
            r.rows_grad[c : c + 1, :] += jnp.sum((on * (1.0 - rate[c])) * dz, axis=0, keepdims=True)
        dlogits_hi, dlogits_lo = halves(dlogits)
        r.mixer_grad[...] += dot_tn(dlogits_hi, normed2) + dot_tn(dlogits_lo, normed2)
        r.residual_grad[...] += dot3(dot, r.prev_t[m], dlogits)
        r.logit_grad[m] = dot3(dot_nt, dlogits, r.residual[...])
        r.dnorm[d] = dot3(dot, dlogits, r.mixer[...]) + own * dz

    def kept_backward(m):
        return [
            save(11, m, r.by_up.at[slot(m)], r.h_up),
            save(12, m, r.by_gate.at[slot(m)], r.h_gate),
        ]

    def experts_backward(m):
        d = slot(m)
        by_up, by_gate, arrived = r.by_up.at[d], r.by_gate.at[d], r.arrived.at[d]
        if not deep:
            for copy in fetched(m):
                copy.wait()

        def compute(half, g):
            block = get(arrived.at[half], g)
            offset = half * slots
            total = 0.0
            for cols in hidden_cols:
                dinside = dot_nt(block, r.down_v[cols, :])
                dvalue = (dinside * wide(get(by_gate, g, offset, cols))).astype(bf16)
                dupper = (dinside * wide(get(by_up, g, offset, cols))).astype(bf16)
                put(by_gate, g, dvalue, offset, cols)
                put(by_up, g, dupper, offset, cols)
                total = total + dot_nt(dvalue, r.gate_v[:, cols]) + dot_nt(dupper, r.up_v[:, cols])
            return total

        through_expert(m, 2, P_GROWS, P_GPART, grad_back(m), r.h_grads, compute)
        for copy in kept_backward(m):
            copy.start()

    def grad_attend(m):
        d = slot(m)
        wait_back(m, 2, grad_back(m))

        both = spread(m, 0) + spread(m, 1)
        dnorm = r.dnorm[d] + dot(both, grad_back(m)[...])
        hidden = r.h[m]
        root = inverse_rms(hidden)
        scaled = dnorm * r.gain2[...]
        pull = root * root * root * jnp.mean(hidden * scaled, axis=-1, keepdims=True)
        dhidden = r.dz[d] + root * scaled - hidden * pull
        r.rows_grad[3:4, :] += jnp.sum(dnorm * hidden * root, axis=0, keepdims=True)
        r.dh[...] = dhidden
        r.da[own_rows, :] = dhidden.astype(bf16)
        pair(P_DA, m, 0, r.da.at[own_rows], r.da.at[own_rows]).start()
        seq_bias(m)
        r.do[own_rows, :] = dot_nt(r.da[own_rows, :], r.w_out[...]).astype(bf16)
        pair(P_DA, m, 0, r.da.at[other_rows], r.da.at[other_rows]).wait_recv()
        save(13, m, r.da, r.h_da).start()
        r.do[other_rows, :] = dot_nt(r.da[other_rows, :], r.w_out[...]).astype(bf16)

        head_lane = iota((1, LANES), 1)

        def head_pair(p, inner):
            lanes = pl.ds(pl.multiple_of(p * LANES, LANES), LANES)
            q2, k2, v2 = r.q[m, :, lanes], r.k[m, :, lanes], r.v[m, :, lanes]
            do2 = r.do[:, lanes]
            for half in range(2):
                keep = wide(((head_lane // HEAD_DIM) == half).astype(i32)).astype(bf16)
                km, vm, qm, dom = k2 * keep, v2 * keep, q2 * keep, do2 * keep
                for c in range(rows // chunk):
                    piece, reach = slice(c * chunk, (c + 1) * chunk), (c + 1) * chunk
                    scores = dot_nt(q2[piece], km[:reach]) + wide(r.bias[piece, :reach])
                    total = jnp.sum(
                        jnp.where(head_lane == 2 * p + half, r.logsum[m, piece, :], 0.0),
                        axis=1,
                        keepdims=True,
                    )
                    probs = jnp.exp(scores - total)
                    dprobs = dot_nt(do2[piece], vm[:reach])
                    meant = jnp.sum(dprobs * probs, axis=-1, keepdims=True)
                    dscores = (probs * (dprobs - meant)).astype(bf16)
                    dq = dot(dscores, km[:reach])
                    dk = dot_tn(dscores, qm[piece])
                    dv = dot_tn(probs.astype(bf16), dom[piece])
                    if half == 0:
                        r.mix[piece, :] = dq
                    else:
                        r.mix[piece, :] += dq
                    if half == 0 and c == 0:
                        r.mix_k[...] = jnp.zeros_like(r.mix_k)
                        r.mix_v[...] = jnp.zeros_like(r.mix_v)
                    r.mix_k[:reach, :] += dk
                    r.mix_v[:reach, :] += dv
            r.dq[:, lanes] = (turned_back(r.mix[...], r.cosine[...], r.sine[...]) * scale).astype(bf16)
            r.dk[:, lanes] = turned_back(r.mix_k[...], r.cosine[...], r.sine[...]).astype(bf16)
            r.dv[:, lanes] = r.mix_v[...].astype(bf16)
            return inner

        lax.fori_loop(0, pairs, head_pair, 0)
        for copy in kept_heads(m):
            copy.start()

    def kept_heads(m):
        return [save(14, m, r.dq, r.h_dq), save(15, m, r.dk, r.h_dk), save(16, m, r.dv, r.h_dv)]

    def grad_finish(m):
        d = slot(m)

        def dnormed(piece):
            return (
                dot_nt(r.dq[piece, :], r.w_query[...])
                + dot_nt(r.dk[piece, :], r.w_key[...])
                + dot_nt(r.dv[piece, :], r.w_value[...])
            )

        save(13, m, r.da, r.h_da).wait()
        r.half_out[...] = dnormed(other_rows).astype(bf16)
        pair(P_DX, m, 0, r.half_out, r.half_in.at[1, m]).start()
        kept = dnormed(own_rows)
        pair(P_DX, m, 0, r.half_out, r.half_in.at[1, m]).wait_recv()
        dnorm1 = kept + wide(r.half_in[1, m])
        x = r.x[m]
        root1 = inverse_rms(x)
        scaled1 = dnorm1 * r.gain1[...]
        pull1 = root1 * root1 * root1 * jnp.mean(x * scaled1, axis=-1, keepdims=True)
        dx = r.dh[...] + root1 * scaled1 - x * pull1
        stage(m)[...] = dx
        save(4, m, stage(m), r.input_grad).start()

        @pl.when(sec > 0)
        def _():
            r.hop_out[d] = dx.astype(bf16)
            hop(1, m, r.hop_out.at[d], r.hop_in.at[back_hop, m], sec - 1).start()

        r.rows_grad[2:3, :] += jnp.sum(dnorm1 * x * root1, axis=0, keepdims=True)
        pair(P_DA, m, 0, r.da.at[own_rows], r.da.at[own_rows]).wait_send()
        pair(P_DX, m, 0, r.half_out, r.half_in.at[1, m]).wait_send()
        for copy in kept_heads(m):
            copy.wait()

    def settle_backward(m):
        @pl.when(sec > 0)
        def _():
            hop(1, m, r.hop_out.at[slot(m)], r.hop_in.at[back_hop, m], sec - 1).wait_send()

        save(4, m, stage(m), r.input_grad).wait()
        for copy in kept_backward(m):
            copy.wait()

    if deep:
        def all_of(*phases):
            def step(m, carry):
                for phase in phases:
                    phase(m)
                return carry

            lax.fori_loop(0, micro, step, 0)

        def turn(m):
            combine(m)

            @pl.when(is_last)
            def _():
                grad_start(m)

        def start_rest(m):
            @pl.when(sec < sections - 1)
            def _():
                grad_start(m)

        every = [(k, m) for k in range(4) for m in range(micro)]
        if cfg.relay:

            @pl.when(is_last)
            def _():
                for k, m in relays_for_first():
                    relay(k, m)

        all_of(attend, attend_send)
        all_of(experts_forward)
        all_of(turn)
        if cfg.relay:

            @pl.when(is_first)
            def _():
                for k, m in every:
                    relay(k, m)

        all_of(start_rest)
        all_of(experts_backward)
        all_of(grad_attend, grad_finish)
        if cfg.relay:

            @pl.when(is_last)
            def _():
                for k, m in every:
                    if k >= 2:
                        relay(k, m)
                for k, m in relays_for_first() + [(k, m) for k, m in every if k >= 2]:
                    for place in range(2):
                        relay_copy(k, m, place).wait_send()

            @pl.when(is_first)
            def _():
                for k, m in every:
                    for place in range(2):
                        relay_copy(k, m, place).wait_send()

        for m in range(micro):
            settle_backward(m)
    else:

        def there(m, carry):
            for phase in (attend, attend_send, experts_forward, combine, settle_forward):
                phase(m)
            return carry

        def back_again(m, carry):
            for phase in (grad_start, experts_backward, grad_attend, grad_finish, settle_backward):
                phase(m)
            return carry

        lax.fori_loop(0, micro, there, 0)
        lax.fori_loop(0, micro, back_again, 0)


def run_chain(cfg, ins):
    vmem, anywhere = pl.BlockSpec(memory_space=pltpu.VMEM), pl.BlockSpec(memory_space=pl.ANY)
    smem = pl.BlockSpec(memory_space=pltpu.SMEM)
    far = {"inputs", "cotangent", "gate", "up", "down"}
    micro, owned, rows, width, inner = cfg.micro, cfg.owned, cfg.rows, cfg.width, cfg.inner
    heads_width, slots = cfg.heads * HEAD_DIM, cfg.slots
    shape = jax.ShapeDtypeStruct
    outs = dict(
        logit_grad=shape((micro, owned, LANES), f32),
        mixer_grad=shape((LANES, width), f32),
        residual_grad=shape((LANES, LANES), f32),
        rows_grad=shape((8, width), f32),
    )
    hbm_outs = dict(
        layer_out=shape((micro, owned, width), f32),
        input_grad=shape((micro, owned, width), f32),
        h_rows=shape((micro, 2, slots, width), bf16),
        h_grads=shape((micro, 2, slots, width), bf16),
        h_inside=shape((micro, 2 * slots, inner), bf16),
        h_up=shape((micro, 2 * slots, inner), bf16),
        h_gate=shape((micro, 2 * slots, inner), bf16),
        h_norm=shape((micro, rows, width), bf16),
        h_da=shape((micro, rows, width), bf16),
        h_o=shape((micro, rows, heads_width), bf16),
        h_dq=shape((micro, rows, heads_width), bf16),
        h_dk=shape((micro, rows, heads_width), bf16),
        h_dv=shape((micro, rows, heads_width), bf16),
    )
    dma = pltpu.SemaphoreType.DMA
    depth = cfg.depth
    rem_scratch = {}
    if depth == micro:
        rem_scratch = dict(stage=pltpu.VMEM((micro, owned, width), f32))
    if cfg.rem:
        last = pltpu.VMEM((depth, cfg.experts, cfg.rem, width), f32)
        rem_sem = dma((4, micro, cfg.experts))
        rem_scratch |= dict(
            rem_out=last, rem_in=last, rem_result=last, rem_back=last, rem_send=rem_sem, rem_recv=rem_sem
        )
    if cfg.relay:
        relay_sem = dma((4, micro, 2))
        rem_scratch |= dict(
            relay=pltpu.VMEM((4, micro, 2, cfg.main, width), bf16),
            relay_send=relay_sem,
            relay_recv=relay_sem,
        )
    scratch = dict(
        gate_v=pltpu.VMEM((width, inner), bf16),
        up_v=pltpu.VMEM((width, inner), bf16),
        down_v=pltpu.VMEM((inner, width), bf16),
        x=pltpu.VMEM((micro, owned, width), f32),
        h=pltpu.VMEM((micro, owned, width), f32),
        norm=pltpu.VMEM((micro, rows, width), bf16),
        norm2=pltpu.VMEM((micro, owned, width), bf16),
        q=pltpu.VMEM((micro, rows, heads_width), bf16),
        k=pltpu.VMEM((micro, rows, heads_width), bf16),
        v=pltpu.VMEM((micro, rows, heads_width), bf16),
        o=pltpu.VMEM((micro, rows, heads_width), bf16),
        logsum=pltpu.VMEM((micro, rows, LANES), f32),
        mixer=pltpu.VMEM((LANES, width), f32),
        residual=pltpu.VMEM((LANES, LANES), f32),
        prev_t=pltpu.VMEM((micro, LANES, owned), f32),
        cols=pltpu.VMEM((micro, owned, 16), i32),
        gates=pltpu.VMEM((micro, owned, LANES), f32),
        place_col=pltpu.VMEM((micro, owned, 2), i32),
        place_row=pltpu.VMEM((micro, 2, owned), i32),
        bias=pltpu.VMEM((rows, rows), f32 if depth == micro else bf16),
        arrived=pltpu.VMEM((depth, 2, slots, width), bf16),
        part_in=pltpu.VMEM((slots, width), bf16),
        back=pltpu.VMEM((micro, slots, width), bf16),
        half_in=pltpu.VMEM((2, micro, owned, width), bf16),
        hop_in=pltpu.VMEM((min(2, cfg.sections - 1), micro, owned, width), bf16),
        outgoing=pltpu.VMEM((depth, cfg.experts * cfg.main, width), bf16),
        part_out=pltpu.VMEM((slots, width), bf16),
        result=pltpu.VMEM((depth, slots, width), bf16),
        partial=pltpu.VMEM((max(slots, owned), width), f32),
        half_out=pltpu.VMEM((owned, width), bf16),
        hop_out=pltpu.VMEM((depth, owned, width), bf16),
        inside=pltpu.VMEM((depth, 2 * slots, inner), bf16),
        **rem_scratch,
        by_up=pltpu.VMEM((depth, 2 * slots, inner), bf16),
        by_gate=pltpu.VMEM((depth, 2 * slots, inner), bf16),
        dz=pltpu.VMEM((depth, owned, width), f32),
        dh=pltpu.VMEM((owned, width), f32),
        dnorm=pltpu.VMEM((depth, owned, width), f32),
        da=pltpu.VMEM((rows, width), bf16),
        do=pltpu.VMEM((rows, heads_width), bf16),
        dq=pltpu.VMEM((rows, heads_width), bf16),
        dk=pltpu.VMEM((rows, heads_width), bf16),
        dv=pltpu.VMEM((rows, heads_width), bf16),
        mix=pltpu.VMEM((rows, LANES), f32),
        mix_k=pltpu.VMEM((rows, LANES), f32),
        mix_v=pltpu.VMEM((rows, LANES), f32),
        pair_send=dma((8, micro, 3)),
        pair_recv=dma((8, micro, 3)),
        hop_send=dma((2, micro)),
        hop_recv=dma((2, micro)),
        a2a_send=dma((4, micro, cfg.experts)),
        a2a_recv=dma((4, micro, cfg.experts)),
        local=dma((17, micro)),
        keep=dma((2, micro, 4)),
        fetch=dma((3,)),
    )
    names = [*ins, *outs, *hbm_outs, *scratch]
    flops = 2 * micro * (2 * slots * width * inner * 6 + rows * width * heads_width * 10)
    results = pl.pallas_call(
        functools.partial(chain_kernel, cfg, names),
        out_shape=[*outs.values(), *hbm_outs.values()],
        in_specs=[
            smem if name == "lengths" else anywhere if name in far else vmem for name in ins
        ],
        out_specs=[vmem] * len(outs) + [anywhere] * len(hbm_outs),
        scratch_shapes=[*scratch.values()],
        compiler_params=pltpu.CompilerParams(
            collective_id=0, has_side_effects=True, vmem_limit_bytes=60 * 2**20
        ),
        cost_estimate=pl.CostEstimate(flops=flops, bytes_accessed=50_000_000, transcendentals=0),
    )(*ins.values())
    return types.SimpleNamespace(**dict(zip([*outs, *hbm_outs], results, strict=True)))


def tail_kernel(cfg, names, *refs):
    r = types.SimpleNamespace(**dict(zip(names, refs, strict=True)))
    experts, width, pad = cfg.experts, cfg.width, cfg.small_pad
    side = width // 2
    outer = experts // 2
    me, core = lax.axis_index("expert"), lax.axis_index("tensor")
    mine_out, mine_in = me // 2, lax.rem(me, 2)
    beside = me + 1 - 2 * mine_in
    pieces = len(cfg.piece_rows)
    starts = [sum(cfg.piece_rows[:c]) * experts for c in range(pieces)]

    def peer_of(k):
        place = lax.rem(mine_out + k, outer)
        return place, place * 2 + mine_in

    barrier = pltpu.get_barrier_semaphore()
    pl.semaphore_signal(barrier, inc=1, device_id={"tensor": 1 - core}, device_id_type=MESH)
    pl.semaphore_signal(barrier, inc=1, device_id={"expert": beside}, device_id_type=MESH)

    def greet(k, carry):
        pl.semaphore_signal(barrier, inc=1, device_id={"expert": peer_of(k)[1]}, device_id_type=MESH)
        return carry

    lax.fori_loop(1, outer, greet, 0)

    loads = [
        pltpu.make_async_copy(source, target, r.fetch.at[k])
        for k, (source, target) in enumerate(
            (
                (r.h_rows, r.rows_v),
                (r.h_gate, r.gate_v),
                (r.h_up, r.up_v),
                (r.h_grads, r.grads_v),
                (r.h_inside, r.gate_v),
            )
        )
    ]
    for copy in loads[:4]:
        copy.start()

    r.pack[...] = jnp.zeros_like(r.pack)
    r.pack[:pad, :] = r.mixer_grad[:pad, :side]
    r.pack[pad : 2 * pad, :] = r.mixer_grad[:pad, side:]
    r.pack[2 * pad : 2 * pad + 8, :] = r.rows_grad[:, :side]
    r.pack[2 * pad + 8 : 2 * pad + 16, :] = r.rows_grad[:, side:]
    r.pack[2 * pad + 16 : 3 * pad + 16, :LANES] = r.residual_grad[:pad, :]
    r.pack_out[...] = r.pack[...].astype(bf16)
    pl.semaphore_wait(barrier, outer + 1)
    pack_copy = pltpu.make_async_remote_copy(
        src_ref=r.pack_out,
        dst_ref=r.pack_in,
        send_sem=r.pack_sem.at[0],
        recv_sem=r.pack_sem.at[1],
        device_id={"tensor": 1 - core},
        device_id_type=MESH,
    )
    pack_copy.start()

    def span(start, index, size):
        return pl.ds(pl.multiple_of(start + index * size, 16), size)

    def over_x(stage, c, source, target, from_rows, to_rows):
        return pltpu.make_async_remote_copy(
            src_ref=source.at[from_rows],
            dst_ref=target.at[to_rows],
            send_sem=r.x_send.at[stage, c],
            recv_sem=r.x_recv.at[stage, c],
            device_id={"expert": beside},
            device_id_type=MESH,
        )

    def over_z(stage, c, place, landed, peer, source, target):
        return pltpu.make_async_remote_copy(
            src_ref=source,
            dst_ref=target,
            send_sem=r.z_send.at[stage, c, place],
            recv_sem=r.z_recv.at[stage, c, landed],
            device_id={"expert": peer},
            device_id_type=MESH,
        )

    def half_of(c, which):
        return span(starts[c], which, outer * cfg.piece_rows[c])

    def landing(c):
        return pl.ds(starts[c] // 2, outer * cfg.piece_rows[c])

    def scatter_x(c):
        return over_x(0, c, r.sent, r.x_in, half_of(c, 1 - mine_in), landing(c))

    def gather_x(c, which):
        return over_x(1, c, r.summed, r.summed, half_of(c, which), half_of(c, which))

    def scatter_z(c, place, landed, peer):
        size = cfg.piece_rows[c]
        return over_z(
            0,
            c,
            place,
            landed,
            peer,
            r.z_out.at[span(starts[c] // 2, place, size)],
            r.z_in.at[landed, pl.ds(starts[c] // experts, size)],
        )

    def final(c, place):
        return span(starts[c], mine_in * outer + place, cfg.piece_rows[c])

    def gather_z(c, place, landed, peer):
        rows = final(c, landed)
        return over_z(1, c, place, landed, peer, r.summed.at[rows], r.summed.at[rows])

    def weight_grad(left, right):
        return dot_tn(left.reshape(-1, left.shape[-1]), right.reshape(-1, right.shape[-1]))

    products = ((r.h_da, r.h_o), (r.h_norm, r.h_dv), (r.h_norm, r.h_dk), (r.h_norm, r.h_dq))
    splits = cfg.splits

    def launch(c):
        rows = pl.ds(starts[c], experts * cfg.piece_rows[c])
        if c == pieces - 1:
            pack_copy.wait()
            r.sent[rows, :] = (r.pack[...] + wide(r.pack_in[...])).astype(bf16)
        elif c % splits == 0:
            left, right = products[c // splits]
            value = weight_grad(left[...], right[...])
            covered = splits * experts * cfg.piece_rows[c]
            if value.shape[0] != covered:
                r.sent[pl.ds(starts[c], covered), :] = jnp.zeros((covered, side), bf16)
            r.sent[pl.ds(starts[c], value.shape[0]), :] = value.astype(bf16)
        scatter_x(c).start()

    rows_all = cfg.micro * 2 * cfg.slots
    tile = 256
    steps = []
    for left, right, target in (
        (r.rows_v, r.gate_v, r.gate_grad),
        (r.rows_v, r.up_v, r.up_grad),
        (r.gate_v, r.grads_v, r.down_grad),
    ):
        for t in range(left.shape[-1] // tile):
            needs = ((0, 1), (0, 2), (3, 4))[len(steps) // (width // tile) if target is not r.down_grad else 2]
            steps.append((left, right, target, t, needs))

    loaded = set()
    flying = [None, None]

    def expert_step(index):
        left, right, target, t, needs = steps[index]
        if index == width // tile:
            loads[4].start()
        for k in needs:
            if k not in loaded:
                loads[k].wait()
                loaded.add(k)
        slot = index % 2
        if flying[slot] is not None:
            flying[slot].wait()
        wide_out = right.shape[-1]
        a = left[..., t * tile : (t + 1) * tile].reshape(rows_all, tile)
        r.stage[slot, :, :wide_out] = dot_tn(a, right[...].reshape(rows_all, wide_out)).astype(bf16)
        copy = pltpu.make_async_copy(
            r.stage.at[slot, :, pl.ds(0, wide_out)],
            target.at[pl.ds(t * tile, tile)],
            r.step_sem.at[index],
        )
        copy.start()
        flying[slot] = copy

    def reduce_x(c):
        scatter_x(c).wait_recv()
        rows = landing(c)
        r.z_out[rows, :] = (wide(r.sent[half_of(c, mine_in), :]) + wide(r.x_in[rows, :])).astype(bf16)

        def out_z(k, carry):
            place, peer = peer_of(k)
            scatter_z(c, place, mine_out, peer).start()
            return carry

        lax.fori_loop(1, outer, out_z, 0)

    def reduce_z(c):
        size = cfg.piece_rows[c]

        def add_z(k, total):
            place, peer = peer_of(k)
            scatter_z(c, place, place, peer).wait_recv()
            return total + wide(r.z_in[place, pl.ds(starts[c] // experts, size), :])

        total = lax.fori_loop(1, outer, add_z, wide(r.z_out[span(starts[c] // 2, mine_out, size), :]))
        r.summed[final(c, mine_out), :] = total.astype(bf16)

        def back_z(k, carry):
            place, peer = peer_of(k)
            gather_z(c, place, mine_out, peer).start()
            return carry

        lax.fori_loop(1, outer, back_z, 0)

    def spread_x(c):
        def wait_z(k, carry):
            place, peer = peer_of(k)
            gather_z(c, place, place, peer).wait_recv()
            return carry

        lax.fori_loop(1, outer, wait_z, 0)
        gather_x(c, mine_in).start()

    done = 0
    launch(0)
    launch(1)
    for k in range(pieces + 4):
        if k < pieces:
            reduce_x(k)
        if k + 2 < pieces:
            launch(k + 2)
        if 0 <= k - 2 < pieces:
            reduce_z(k - 2)
        if 0 <= k - 4 < pieces:
            spread_x(k - 4)
        while done < min(len(steps), len(steps) * (k + 1) // pieces):
            expert_step(done)
            done += 1
    for c in range(pieces):
        gather_x(c, 1 - mine_in).wait_recv()
    for c in range(pieces):
        scatter_x(c).wait_send()
        gather_x(c, mine_in).wait_send()

        def sent_z(k, carry, c=c):
            place, peer = peer_of(k)
            scatter_z(c, place, mine_out, peer).wait_send()
            gather_z(c, place, mine_out, peer).wait_send()
            return carry

        lax.fori_loop(1, outer, sent_z, 0)
    for copy in flying:
        copy.wait()


def run_tail(cfg, got):
    vmem, anywhere = pl.BlockSpec(memory_space=pltpu.VMEM), pl.BlockSpec(memory_space=pl.ANY)
    micro, width, inner, slots, experts = cfg.micro, cfg.width, cfg.inner, cfg.slots, cfg.experts
    side, outer = width // 2, experts // 2
    cfg.splits = 2 if width % (32 * experts) == 0 else 1
    piece = -(-width // (16 * cfg.splits * experts)) * 16
    small = -(-(3 * cfg.small_pad + 16) // (16 * experts)) * 16
    cfg.piece_rows = [piece] * (4 * cfg.splits) + [small]
    total = sum(cfg.piece_rows) * experts
    near = dict(
        h_norm=got.h_norm,
        h_da=got.h_da,
        h_o=got.h_o,
        h_dq=got.h_dq,
        h_dk=got.h_dk,
        h_dv=got.h_dv,
        mixer_grad=got.mixer_grad,
        residual_grad=got.residual_grad,
        rows_grad=got.rows_grad,
    )
    far = dict(
        h_rows=got.h_rows,
        h_grads=got.h_grads,
        h_inside=got.h_inside,
        h_up=got.h_up,
        h_gate=got.h_gate,
    )
    shape, dma = jax.ShapeDtypeStruct, pltpu.SemaphoreType.DMA
    outs = dict(
        summed=shape((total, side), bf16),
        gate_grad=shape((width, inner), bf16),
        up_grad=shape((width, inner), bf16),
        down_grad=shape((inner, width), bf16),
    )
    scratch = dict(
        rows_v=pltpu.VMEM((micro, 2, slots, width), bf16),
        grads_v=pltpu.VMEM((micro, 2, slots, width), bf16),
        up_v=pltpu.VMEM((micro, 2 * slots, inner), bf16),
        gate_v=pltpu.VMEM((micro, 2 * slots, inner), bf16),
        sent=pltpu.VMEM((total, side), bf16),
        x_in=pltpu.VMEM((total // 2, side), bf16),
        z_out=pltpu.VMEM((total // 2, side), bf16),
        z_in=pltpu.VMEM((outer, total // experts, side), bf16),
        pack=pltpu.VMEM((small * experts, side), f32),
        pack_out=pltpu.VMEM((small * experts, side), bf16),
        pack_in=pltpu.VMEM((small * experts, side), bf16),
        stage=pltpu.VMEM((2, 256, max(inner, width)), bf16),
        fetch=dma((5,)),
        step_sem=dma(((2 * width + inner) // 256,)),
        pack_sem=dma((2,)),
        x_send=dma((2, len(cfg.piece_rows))),
        x_recv=dma((2, len(cfg.piece_rows))),
        z_send=dma((2, len(cfg.piece_rows), outer)),
        z_recv=dma((2, len(cfg.piece_rows), outer)),
    )
    names = [*near, *far, *outs, *scratch]
    results = pl.pallas_call(
        functools.partial(tail_kernel, cfg, names),
        out_shape=[*outs.values()],
        in_specs=[vmem] * len(near) + [anywhere] * len(far),
        out_specs=[vmem] + [anywhere] * 3,
        scratch_shapes=[*scratch.values()],
        compiler_params=pltpu.CompilerParams(
            collective_id=1, has_side_effects=True, vmem_limit_bytes=60 * 2**20
        ),
        cost_estimate=pl.CostEstimate(
            flops=12 * micro * slots * width * inner, bytes_accessed=40_000_000, transcendentals=0
        ),
    )(*near.values(), *far.values())
    return types.SimpleNamespace(
        **dict(zip(outs, results, strict=True)), pad_rows=piece * cfg.splits * experts
    )


def rope_tables(rows):
    half_width = HEAD_DIM // 2
    frequency = 10000.0 ** (-2.0 * np.arange(half_width, dtype=np.float64) / HEAD_DIM)
    angles = np.arange(rows, dtype=np.float64)[:, None] * frequency[None, :]
    angles = np.tile(angles, (1, LANES // half_width))
    return np.cos(angles).astype(np.float32), np.sin(angles).astype(np.float32)


def local(
    inputs,
    cotangent,
    prev_logits,
    lengths,
    routes,
    slot_order,
    norm_gain1,
    w_query,
    w_key,
    w_value,
    w_out,
    norm_gain2,
    router,
    router_residual,
    const_gate,
    const_value,
    expert_gate,
    expert_up,
    expert_down,
):
    micro, owned, width = inputs.shape
    tensors, peers = lax.axis_size("tensor"), lax.axis_size("expert")
    choices = router.shape[2]
    experts = choices - 4
    assert experts == peers and tensors == 2
    cap = 9 * 2 * owned // (8 * choices) + 1
    main, rem = cap // 16 * 16, cap % 16
    if rem > 2 or not main:
        main, rem = main + (16 if rem else 0), 0
    rem_rows = -(-rem * peers // 16) * 16
    cfg = types.SimpleNamespace(
        micro=micro,
        owned=owned,
        width=width,
        rows=owned * tensors,
        inner=expert_gate.shape[3],
        heads=w_query.shape[2] // HEAD_DIM,
        experts=experts,
        choices=choices,
        cap=cap,
        main=main,
        rem=rem,
        rem_rows=rem_rows,
        half_rows=peers // 2 * main,
        slots=peers * main + rem_rows,
        depth=micro if peers * main <= 512 else 1,
        sections=lax.axis_size("section"),
        seqs=lengths.shape[2] - 1,
        chunk=owned,
        small_pad=-(-(choices + 2) // 16) * 16,
    )
    cfg.relay = cfg.depth == micro and cfg.sections == 2 and peers == 8
    cosine, sine = rope_tables(cfg.rows)
    ins = dict(
        lengths=lengths[:, 0],
        inputs=inputs,
        cotangent=cotangent,
        prev_in=jnp.transpose(prev_logits[0], (2, 0, 1)),
        route_row=jnp.swapaxes(routes[0], 1, 2),
        order_row=slot_order[0],
        gain1=norm_gain1,
        gain2=norm_gain2,
        w_query=w_query[0],
        w_key=w_key[0],
        w_value=w_value[0],
        w_out=w_out[0],
        router_in=router[0].T,
        const_gate=const_gate[0],
        residual_in=router_residual[0],
        const_value=const_value[0],
        cosine=jnp.asarray(cosine),
        sine=jnp.asarray(sine),
        gate=expert_gate[0, 0],
        up=expert_up[0, 0],
        down=expert_down[0, 0],
    )
    got = run_chain(cfg, ins)

    tail = run_tail(cfg, got)
    out_grad, value_grad, key_grad, query_grad = (
        wide(tail.summed[c * tail.pad_rows : c * tail.pad_rows + width]) for c in range(4)
    )
    small = wide(tail.summed[4 * tail.pad_rows :])
    pad = cfg.small_pad
    mixer_grad = jnp.concatenate([small[:pad], small[pad : 2 * pad]], axis=1)
    rows_grad = jnp.concatenate([small[2 * pad : 2 * pad + 8], small[2 * pad + 8 : 2 * pad + 16]], axis=1)
    residual_grad = small[2 * pad + 16 : 3 * pad + 16, :LANES]
    return (
        got.layer_out[None],
        got.input_grad[None],
        got.logit_grad[None, :, :, :choices],
        rows_grad[None, 2],
        query_grad[None],
        key_grad[None],
        value_grad[None],
        out_grad.T[None],
        rows_grad[None, 3],
        mixer_grad[:choices].T[None],
        residual_grad[None, :choices, :choices],
        mixer_grad[None, choices : choices + 2],
        rows_grad[None, :2],
        wide(tail.gate_grad)[None, None],
        wide(tail.up_grad)[None, None],
        wide(tail.down_grad)[None, None],
    )


def solution(mesh):
    tokens = ("expert", "tensor")
    in_specs = (
        P(None, tokens, None),
        P(None, tokens, None),
        P("section", None, tokens, None),
        P(None, "expert", None),
        P("section", None, tokens, None),
        P("section", None, tokens, None),
        P("section", None),
        P("section", None, "tensor"),
        P("section", None, "tensor"),
        P("section", None, "tensor"),
        P("section", "tensor", None),
        P("section", None),
        P("section", None, None),
        P("section", None, None),
        P("section", None, None),
        P("section", None, None),
        P("section", "expert", None, "tensor"),
        P("section", "expert", None, "tensor"),
        P("section", "expert", "tensor", None),
    )
    out_specs = (
        P("section", None, tokens, None),
        P("section", None, tokens, None),
        P("section", None, tokens, None),
        P("section", None),
        P("section", None, "tensor"),
        P("section", None, "tensor"),
        P("section", None, "tensor"),
        P("section", "tensor", None),
        P("section", None),
        P("section", None, None),
        P("section", None, None),
        P("section", None, None),
        P("section", None, None),
        P("section", "expert", None, "tensor"),
        P("section", "expert", None, "tensor"),
        P("section", "expert", "tensor", None),
    )
    return jax.shard_map(local, mesh=mesh, in_specs=in_specs, out_specs=out_specs, check_vma=False)
```

```python
import functools
import types

import jax
import jax.numpy as jnp
import numpy as np
from jax import lax
from jax.experimental import pallas as pl
from jax.experimental.pallas import tpu as pltpu
from jax.sharding import PartitionSpec as P

HEAD_DIM = 64
LANES = 128
EPSILON = 1e-06
MESH = pl.DeviceIdType.MESH
f32, bf16, i32 = jnp.float32, jnp.bfloat16, jnp.int32

P_NORM, P_OUT, P_ROWS, P_PART, P_GROWS, P_GPART, P_DA, P_DX = range(8)


def dot(left, right):
    return jnp.dot(left, right, preferred_element_type=f32)


def dot_nt(left, right):
    return lax.dot_general(left, right, (((1,), (1,)), ((), ())), preferred_element_type=f32)


def dot_tn(left, right):
    return lax.dot_general(left, right, (((0,), (0,)), ((), ())), preferred_element_type=f32)


def wide(values):
    return values.astype(f32)


def halves(values):
    upper = values.astype(bf16)
    return upper, (values - wide(upper)).astype(bf16)


def dot3(how, left, right):
    left_hi, left_lo = halves(left)
    right_hi, right_lo = halves(right)
    return how(left_hi, right_hi) + (how(left_hi, right_lo) + how(left_lo, right_hi))


def inverse_rms(values):
    return lax.rsqrt(jnp.mean(values * values, axis=-1, keepdims=True) + EPSILON)


def iota(shape, dim):
    return lax.broadcasted_iota(i32, shape, dim)


def flag(condition):
    return wide(condition.astype(i32))


def half_lanes(width):
    return (iota((1, width), 1) % HEAD_DIM) < HEAD_DIM // 2


def turned(values, cosine, sine):
    quarter = HEAD_DIM // 2
    other = jnp.where(
        half_lanes(LANES),
        -pltpu.roll(values, LANES - quarter, 1),
        pltpu.roll(values, quarter, 1),
    )
    return values * cosine + other * sine


def turned_back(values, cosine, sine):
    quarter = HEAD_DIM // 2
    other = jnp.where(
        half_lanes(LANES),
        pltpu.roll(values, LANES - quarter, 1),
        -pltpu.roll(values, quarter, 1),
    )
    return values * cosine + other * sine


def chain_kernel(cfg, names, *refs):
    r = types.SimpleNamespace(**dict(zip(names, refs, strict=True)))
    owned, rows, experts, cap, slots = cfg.owned, cfg.rows, cfg.experts, cfg.cap, cfg.slots
    choices, micro, sections, seqs = cfg.choices, cfg.micro, cfg.sections, cfg.seqs
    pairs, chunk = cfg.heads // 2, cfg.chunk
    scale = HEAD_DIM ** (-0.5)
    sec, me, core = (lax.axis_index(a) for a in ("section", "expert", "tensor"))
    other = 1 - core
    own_rows = pl.ds(pl.multiple_of(core * owned, owned), owned)
    other_rows = pl.ds(pl.multiple_of(other * owned, owned), owned)
    is_first, is_last = sec == 0, sec == sections - 1

    deep = cfg.depth == micro

    def slot(m):
        return m if deep else 0

    def pair(kind, m, j, source, target):
        return pltpu.make_async_remote_copy(
            src_ref=source,
            dst_ref=target,
            send_sem=r.pair_send.at[kind, m, j],
            recv_sem=r.pair_recv.at[kind, m, j],
            device_id={"tensor": other},
            device_id_type=MESH,
        )

    def hop(kind, m, source, target, section):
        return pltpu.make_async_remote_copy(
            src_ref=source,
            dst_ref=target,
            send_sem=r.hop_send.at[kind, m],
            recv_sem=r.hop_recv.at[kind, m],
            device_id={"section": section},
            device_id_type=MESH,
        )

    main, rem, half_rows, rem_rows = cfg.main, cfg.rem, cfg.half_rows, cfg.rem_rows
    rem_start = experts * main
    group = experts // 2
    my_group, in_group = me // group, lax.rem(me, group)
    group_of = (my_group, 1 - my_group)

    def slot_rows(index):
        return pl.ds(pl.multiple_of(index * main, main), main)

    def group_rows(g, offset=0):
        return pl.ds(pl.multiple_of(offset + group_of[g] * half_rows, 16), half_rows)

    def last_rows(offset=0):
        return pl.ds(pl.multiple_of(offset + rem_start, 16), rem_rows)

    def get(ref, g, offset=0, cols=slice(None)):
        value = ref[group_rows(g, offset), cols]
        if g == 1 and rem:
            value = jnp.concatenate([value, ref[last_rows(offset), cols]], axis=0)
        return value

    def put(ref, g, value, offset=0, cols=slice(None)):
        ref[group_rows(g, offset), cols] = value[:half_rows]
        if g == 1 and rem:
            ref[last_rows(offset), cols] = value[half_rows:]

    pieces = -(-half_rows // 256)
    hidden_cols = [
        slice(k * cfg.inner // pieces, (k + 1) * cfg.inner // pieces) for k in range(pieces)
    ]

    def parts(g):
        return [group_rows(g)] + ([last_rows()] if g == 1 and rem else [])

    def peers_in(g, act):
        def step(k, carry):
            act(group_of[g] * group + lax.rem(in_group + k, group))
            return carry

        lax.fori_loop(1 - g, group, step, 0)

    def exchange(kind, m, peer, landed, source, target):
        return pltpu.make_async_remote_copy(
            src_ref=source.at[slot_rows(peer)],
            dst_ref=target.at[slot_rows(landed)],
            send_sem=r.a2a_send.at[kind, m, peer],
            recv_sem=r.a2a_recv.at[kind, m, landed],
            device_id={"expert": peer},
            device_id_type=MESH,
        )

    def exchange_rem(kind, m, peer, landed, source, target):
        return pltpu.make_async_remote_copy(
            src_ref=source.at[peer],
            dst_ref=target.at[landed],
            send_sem=r.rem_send.at[kind, m, peer],
            recv_sem=r.rem_recv.at[kind, m, landed],
            device_id={"expert": peer},
            device_id_type=MESH,
        )

    outer = experts // 2
    mirrored = outer - 1 - me // 2

    def to_relay(kind, m, peer, source):
        place = lax.rem(peer, 2)
        return pltpu.make_async_remote_copy(
            src_ref=source.at[slot_rows(peer)],
            dst_ref=r.relay.at[kind, m, place],
            send_sem=r.a2a_send.at[kind, m, peer],
            recv_sem=r.relay_recv.at[kind, m, place],
            device_id={"section": 1 - sec},
            device_id_type=MESH,
        )

    def relay_copy(kind, m, place):
        target = (r.arrived.at[m, core], r.back.at[m], r.arrived.at[m, core], grad_back(m))[kind]
        return pltpu.make_async_remote_copy(
            src_ref=r.relay.at[kind, m, place],
            dst_ref=target.at[slot_rows(me)],
            send_sem=r.relay_send.at[kind, m, place],
            recv_sem=r.a2a_recv.at[kind, m, me],
            device_id={"section": 1 - sec, "expert": mirrored * 2 + place},
            device_id_type=MESH,
        )

    def relay(kind, m):
        for place in range(2):
            pltpu.make_async_remote_copy(
                src_ref=r.relay.at[kind, m, place],
                dst_ref=r.relay.at[kind, m, place],
                send_sem=r.relay_send.at[kind, m, place],
                recv_sem=r.relay_recv.at[kind, m, place],
                device_id={"section": 1 - sec},
                device_id_type=MESH,
            ).wait_recv()
            relay_copy(kind, m, place).start()

    def relays_for_first():
        return [(k, m) for k in range(2) for m in range(micro) if (k, m) != (1, micro - 1)]

    def send_block(kind, m, peer, source, target):
        if not cfg.relay:
            exchange(kind, m, peer, me, source, target).start()
            return
        aside = peer // 2 == mirrored
        if kind == 1:
            aside = aside & ((sec > 0) | (m < micro - 1))

        @pl.when(aside)
        def _():
            to_relay(kind, m, peer, source).start()

        @pl.when(jnp.logical_not(aside))
        def _():
            exchange(kind, m, peer, me, source, target).start()

    def lay_rem(ref, value):
        for k in range(rem):
            ref[:, k, :] = value[k * experts : (k + 1) * experts]

    def read_rem(ref):
        value = [ref[:, k, :] for k in range(rem)]
        rest = rem_rows - rem * experts
        if rest:
            value.append(jnp.zeros((rest, cfg.width), f32))
        return jnp.concatenate(value, axis=0).astype(bf16)

    def send_slots(kind, m, value):
        d = slot(m)
        outgoing, mine = r.outgoing.at[d], r.arrived.at[d, core]
        r.outgoing[d] = value[:rem_start].astype(bf16)
        for g in (1, 0):
            peers_in(g, lambda p: send_block(kind, m, p, outgoing, mine))
        if rem:
            rem_out, rem_in = r.rem_out.at[d], r.rem_in.at[d]
            lay_rem(rem_out, value[rem_start:])
            for g in (1, 0):
                peers_in(g, lambda p: exchange_rem(kind, m, p, me, rem_out, rem_in).start())
            rem_in[pl.ds(me, 1)] = rem_out[pl.ds(me, 1)]
        mine[slot_rows(me), :] = outgoing[slot_rows(me), :]

    def save(index, m, source, target):
        return pltpu.make_async_copy(source, target.at[m], r.local.at[index, m])

    def grad_back(m):
        return r.inside.at[slot(m), pl.ds(0, slots), pl.ds(0, cfg.width)]

    back_hop = min(1, sections - 2)
    def stage(m):
        return r.stage.at[m] if deep else r.partial.at[pl.ds(0, owned)]


    barrier = pltpu.get_barrier_semaphore()

    def greet(k, carry):
        pl.semaphore_signal(
            barrier, inc=1, device_id={"expert": lax.rem(me + k, experts)}, device_id_type=MESH
        )
        return carry

    lax.fori_loop(1, experts, greet, 0)
    pl.semaphore_signal(barrier, inc=1, device_id={"tensor": other}, device_id_type=MESH)

    @pl.when(sec > 0)
    def _():
        pl.semaphore_signal(barrier, inc=1, device_id={"section": sec - 1}, device_id_type=MESH)

    @pl.when(sec < sections - 1)
    def _():
        pl.semaphore_signal(barrier, inc=1, device_id={"section": sec + 1}, device_id_type=MESH)

    for m in range(micro):

        @pl.when(is_first)
        def _():
            pltpu.make_async_copy(r.inputs.at[m], r.x.at[m], r.local.at[0, m]).start()

        if deep:

            @pl.when(is_last)
            def _():
                pltpu.make_async_copy(r.cotangent.at[m], r.dz.at[m], r.local.at[9, m]).start()

    weights = [
        pltpu.make_async_copy(source, target, r.fetch.at[k])
        for k, (source, target) in enumerate(
            ((r.gate, r.gate_v), (r.up, r.up_v), (r.down, r.down_v))
        )
    ]
    for copy in weights:
        copy.start()
    if cfg.relay:
        for place in range(2):
            pl.semaphore_signal(
                barrier,
                inc=1,
                device_id={"section": 1 - sec, "expert": mirrored * 2 + place},
                device_id_type=MESH,
            )
    beside = (sec > 0).astype(i32) + (sec < sections - 1).astype(i32)

    r.mixer[...] = jnp.zeros_like(r.mixer)
    r.mixer[:choices, :] = r.router_in[...]
    r.mixer[choices : choices + 2, :] = r.const_gate[...]
    r.residual[...] = jnp.zeros_like(r.residual)
    r.residual[:choices, :choices] = r.residual_in[...]
    r.prev_t[...] = jnp.zeros_like(r.prev_t)
    for m in range(micro):
        r.prev_t[m, :choices, :] = r.prev_in[:, m, :]
        table = jnp.concatenate(
            [r.route_row[m], r.order_row[m], jnp.zeros((13, owned), i32)], axis=0
        )
        unit = flag(iota((owned, owned), 0) == iota((owned, owned), 1)).astype(bf16)
        r.cols[m] = dot_nt(unit, wide(table).astype(bf16)).astype(i32)

    def seq_bias(m):
        row = iota((rows, 1), 0)
        start = jnp.zeros((rows, 1), i32)
        end = r.lengths[m, 0]
        for k in range(seqs):
            start = jnp.where(row >= end, row if k == seqs - 1 else end, start)
            end = end + r.lengths[m, min(k + 1, seqs)]
        for c in range(rows // chunk):
            piece = slice(c * chunk, (c + 1) * chunk)
            key = iota((chunk, rows), 1)
            seen = (key <= row[piece]) & (key >= start[piece])
            r.bias[piece, :] = jnp.where(seen, 0.0, -1e30).astype(r.bias.dtype)

    def routing(m):
        lane = iota((owned, LANES), 1)
        lane_t = iota((LANES, owned), 0)
        col = [r.cols[m, :, k : k + 1] for k in range(2)]
        row = [r.route_row[m, k : k + 1, :] for k in range(2)]
        order_row, order_col = r.order_row[m], r.cols[m, :, 2:3]
        hot = [wide((lane == col[k]).astype(i32)) for k in range(2)]
        hot_t = [wide((lane_t == row[k]).astype(i32)) for k in range(2)]
        before = wide((order_row < order_col).astype(i32)).astype(bf16)
        before_t = wide((order_col < order_row).astype(i32)).astype(bf16)
        earlier = dot(before, (hot[0] + hot[1]).astype(bf16))
        earlier_t = dot((hot_t[0] + hot_t[1]).astype(bf16), before_t)
        for k in range(2):
            slot = jnp.sum(earlier * hot[k], axis=1, keepdims=True).astype(i32)
            slot_t = jnp.sum(earlier_t * hot_t[k], axis=0, keepdims=True).astype(i32)

            def placed(choice, at):
                first = choice * main + at
                late = rem_start + (at - main) * experts + choice
                kept = (choice < experts) & (at < cap)
                return jnp.where(kept, jnp.where(at < main, first, late), -1)

            place, place_t = placed(col[k], slot), placed(row[k], slot_t)
            r.place_col[m, :, k : k + 1] = place
            r.place_row[m, k : k + 1, :] = place_t

    def spread(m, k):
        return flag(iota((owned, slots), 1) == r.place_col[m, :, k : k + 1]).astype(bf16)

    def spread_t(m, k):
        return flag(iota((slots, owned), 0) == r.place_row[m, k : k + 1, :]).astype(bf16)

    def choice_flags(m):
        col = [r.cols[m, :, k : k + 1] for k in range(2)]
        copies = [wide((col[k] == experts + 1).astype(i32)) for k in range(2)]
        consts = [
            [wide((col[k] == experts + 2 + c).astype(i32)) for c in range(2)] for k in range(2)
        ]
        return col, copies, consts

    def unpack_gates(m):
        pack = r.gates[m]
        return [pack[:, k : k + 1] for k in range(2)], [pack[:, 2 + k : 3 + k] for k in range(2)]

    def through_expert(m, kind, pair_in, pair_out, target, kept, compute):
        d = slot(m)
        arrived, outgoing, result = r.arrived.at[d], r.outgoing.at[d], r.result.at[d]
        mine, theirs = arrived.at[core], arrived.at[other]
        if rem:
            rem_out, rem_in = r.rem_out.at[d], r.rem_in.at[d]
            rem_result, rem_back = r.rem_result.at[d], r.rem_back.at[d]
        passes = kind // 2

        def keep(index, half, rows_of):
            return pltpu.make_async_copy(
                arrived.at[half, rows_of], kept.at[m, half, rows_of], r.keep.at[passes, m, index]
            )

        def forward_pair(g, which, side):
            return [
                pair(pair_in, m, g + k, side.at[rows_of], side.at[rows_of])
                for k, rows_of in enumerate(parts(g))
            ]

        def sums(g):
            return [
                pair(pair_out, m, g + k, r.part_out.at[rows_of], r.part_in.at[rows_of])
                for k, rows_of in enumerate(parts(g))
            ]

        everything = pl.ds(0, slots)

        def kept_mine(g):
            return [keep(2 * g + k, core, rows_of) for k, rows_of in enumerate(parts(g))]

        def arrive(g):
            peers_in(g, lambda p: exchange(kind, m, p, p, outgoing, mine).wait_recv())
            if g == 1 and rem:
                for which in range(2):
                    peers_in(which, lambda p: exchange_rem(kind, m, p, p, rem_out, rem_in).wait_recv())
                mine[last_rows(), :] = read_rem(rem_in)
            for copy in forward_pair(g, core, mine):
                copy.start()
            for copy in kept_mine(g):
                copy.start()

        def work(g):
            put(r.partial, g, compute(core, g))
            for copy in forward_pair(g, other, theirs):
                copy.wait_recv()
            if g == 1:
                keep(1, other, everything).start()
            put(r.part_out, g, compute(other, g).astype(bf16))
            if g == 1:
                keep(1, other, everything).wait()
            for copy in sums(g):
                copy.start()

        def finish(g):
            for copy in sums(g):
                copy.wait_recv()
            value = get(r.partial, g) + wide(get(r.part_in, g))
            for copy in kept_mine(g):
                copy.wait()
            for copy in forward_pair(g, core, mine):
                copy.wait_send()
            put(result, g, value.astype(bf16))
            peers_in(g, lambda p: send_block(kind + 1, m, p, result, target))
            if g == 1 and rem:
                lay_rem(rem_result, value[half_rows:])
                for which in (1, 0):
                    peers_in(
                        which,
                        lambda p: exchange_rem(kind + 1, m, p, me, rem_result, rem_back).start(),
                    )
                rem_back[pl.ds(me, 1)] = rem_result[pl.ds(me, 1)]

        arrive(0)
        work(0)
        arrive(1)
        finish(0)
        work(1)
        finish(1)
        target[slot_rows(me), :] = result[slot_rows(me), :]
        for g in range(2):
            for copy in sums(g):
                copy.wait_send()
            peers_in(g, lambda p: exchange(kind, m, p, me, outgoing, mine).wait_send())
            if rem:
                peers_in(g, lambda p: exchange_rem(kind, m, p, me, rem_out, rem_in).wait_send())

    def wait_back(m, kind, target):
        result = r.result.at[slot(m)]
        if rem:
            rem_result, rem_back = r.rem_result.at[slot(m)], r.rem_back.at[slot(m)]
        for g in range(2):
            peers_in(g, lambda p: exchange(kind + 1, m, p, p, result, target).wait_recv())
            if rem:
                peers_in(g, lambda p: exchange_rem(kind + 1, m, p, p, rem_result, rem_back).wait_recv())
        if rem:
            target[last_rows(), :] = read_rem(rem_back)
        for g in range(2):
            peers_in(g, lambda p: exchange(kind + 1, m, p, me, result, target).wait_send())
            if rem:
                peers_in(g, lambda p: exchange_rem(kind + 1, m, p, me, rem_result, rem_back).wait_send())

    def attend(m):
        @pl.when(is_first)
        def _():
            pltpu.make_async_copy(r.inputs.at[m], r.x.at[m], r.local.at[0, m]).wait()

        @pl.when(sec > 0)
        def _():
            hop(0, m, r.hop_out.at[slot(m)], r.hop_in.at[0, m], sec - 1).wait_recv()
            r.x[m] = wide(r.hop_in[0, m])

        x = r.x[m]
        r.norm[m, own_rows, :] = (x * inverse_rms(x) * r.gain1[...]).astype(bf16)
        pair(P_NORM, m, 0, r.norm.at[m, own_rows], r.norm.at[m, own_rows]).start()
        routing(m)
        seq_bias(m)

        def project(some):
            normed = r.norm[m, some, :]
            cosine, sine = r.cosine[some, :], r.sine[some, :]
            for stash, weight, factor in ((r.q, r.w_query, scale), (r.k, r.w_key, 1.0)):
                flat = dot(normed, weight[...]) * factor
                for p in range(pairs):
                    lanes = slice(p * LANES, (p + 1) * LANES)
                    stash[m, some, lanes] = turned(flat[:, lanes], cosine, sine).astype(bf16)
            r.v[m, some, :] = dot(normed, r.w_value[...]).astype(bf16)

        project(own_rows)
        pair(P_NORM, m, 0, r.norm.at[m, other_rows], r.norm.at[m, other_rows]).wait_recv()
        save(1, m, r.norm.at[m], r.h_norm).start()
        project(other_rows)

        r.logsum[m] = jnp.zeros((rows, LANES), f32)
        lane = iota((1, LANES), 1)

        def head_pair(p, inner):
            lanes = pl.ds(pl.multiple_of(p * LANES, LANES), LANES)
            q2, k2, v2 = r.q[m, :, lanes], r.k[m, :, lanes], r.v[m, :, lanes]
            for half in range(2):
                keep = wide(((lane // HEAD_DIM) == half).astype(i32)).astype(bf16)
                km, vm = k2 * keep, v2 * keep
                for c in range(rows // chunk):
                    piece, reach = slice(c * chunk, (c + 1) * chunk), (c + 1) * chunk
                    scores = dot_nt(q2[piece], km[:reach]) + wide(r.bias[piece, :reach])
                    peak = jnp.max(scores, axis=-1, keepdims=True)
                    shifted = jnp.exp(scores - peak)
                    total = jnp.sum(shifted, axis=-1, keepdims=True)
                    mixed = dot(shifted.astype(bf16), vm[:reach]) * (1.0 / total)
                    if half == 0:
                        r.mix[piece, :] = mixed
                    else:
                        r.o[m, piece, lanes] = (r.mix[piece, :] + mixed).astype(bf16)
                    r.logsum[m, piece, :] = jnp.where(
                        lane == 2 * p + half, peak + jnp.log(total), r.logsum[m, piece, :]
                    )
            return inner

        lax.fori_loop(0, pairs, head_pair, 0, unroll=deep)
        save(2, m, r.o.at[m], r.h_o).start()

    def attend_send(m):
        r.half_out[...] = dot(r.o[m, other_rows, :], r.w_out[...]).astype(bf16)
        pair(P_OUT, m, 0, r.half_out, r.half_in.at[0, m]).start()
        summed = r.x[m] + dot(r.o[m, own_rows, :], r.w_out[...])
        pair(P_OUT, m, 0, r.half_out, r.half_in.at[0, m]).wait_recv()
        hidden = summed + wide(r.half_in[0, m])
        r.h[m] = hidden
        normed2 = (hidden * inverse_rms(hidden) * r.gain2[...]).astype(bf16)
        r.norm2[m] = normed2

        send_slots(0, m, dot(spread_t(m, 0) + spread_t(m, 1), normed2))

        mixer_hi, mixer_lo = halves(r.mixer[...])
        logits = dot_nt(normed2, mixer_hi) + dot_nt(normed2, mixer_lo)
        logits = logits + dot3(dot_tn, r.prev_t[m], r.residual[...])
        col, copies, consts = choice_flags(m)
        wide_lane = iota((owned, LANES), 1)
        picked = [
            jnp.sum(jnp.where(wide_lane == col[k], logits, 0.0), axis=1, keepdims=True)
            for k in range(2)
        ]
        gate = [jax.nn.sigmoid(picked[0] - picked[1]), jax.nn.sigmoid(picked[1] - picked[0])]
        rate = [jax.nn.sigmoid(logits[:, choices + c : choices + c + 1]) for c in range(2)]
        pack = jnp.zeros((owned, LANES), f32)
        for k, value in enumerate(gate + rate):
            pack = jnp.where(wide_lane == k, value, pack)
        r.gates[m] = pack
        pair(P_NORM, m, 0, r.norm.at[m, own_rows], r.norm.at[m, own_rows]).wait_send()
        pair(P_OUT, m, 0, r.half_out, r.half_in.at[0, m]).wait_send()

    def kept_forward(m):
        copies = [save(10, m, r.inside.at[slot(m)], r.h_inside)]
        if not deep:
            copies += [
                save(5, m, r.by_up.at[0], r.h_up),
                save(6, m, r.by_gate.at[0], r.h_gate),
            ]
        return copies

    def experts_forward(m):
        d = slot(m)
        by_up, by_gate, inside_of, arrived = r.by_up.at[d], r.by_gate.at[d], r.inside.at[d], r.arrived.at[d]

        @pl.when(m == 0)
        def _():
            for copy in weights:
                copy.wait()

        def compute(half, g):
            block = get(arrived.at[half], g)
            offset = half * slots
            total = 0.0
            for cols in hidden_cols:
                value = dot(block, r.gate_v[:, cols])
                upper = dot(block, r.up_v[:, cols])
                sig = jax.nn.sigmoid(value)
                active = value * sig
                inside = (active * upper).astype(bf16)
                put(by_up, g, active.astype(bf16), offset, cols)
                slope = upper * sig * (1.0 + value * (1.0 - sig))
                put(by_gate, g, slope.astype(bf16), offset, cols)
                put(inside_of, g, inside, offset, cols)
                total = total + dot(inside, r.down_v[cols, :])
            return total

        through_expert(m, 0, P_ROWS, P_PART, r.back.at[m], r.h_rows, compute)
        for copy in kept_forward(m):
            copy.start()

    def combine(m):
        gate, rate = unpack_gates(m)
        col, copies, consts = choice_flags(m)
        wait_back(m, 0, r.back.at[m])

        apart = [dot(spread(m, k), r.back[m]) for k in range(2)]
        out = r.h[m] + gate[0] * apart[0] + gate[1] * apart[1]
        own = gate[0] * copies[0] + gate[1] * copies[1]
        for c in range(2):
            on = gate[0] * consts[0][c] + gate[1] * consts[1][c]
            own = own + on * rate[c]
            out = out + (on * (1.0 - rate[c])) * r.const_value[c : c + 1, :]
        out = out + own * wide(r.norm2[m])
        stage(m)[...] = out
        save(3, m, stage(m), r.layer_out).start()

        @pl.when(sec < sections - 1)
        def _():
            r.hop_out[slot(m)] = out.astype(bf16)
            hop(0, m, r.hop_out.at[slot(m)], r.hop_in.at[0, m], sec + 1).start()

    def settle_forward(m):
        @pl.when(sec < sections - 1)
        def _():
            hop(0, m, r.hop_out.at[slot(m)], r.hop_in.at[0, m], sec + 1).wait_send()

        save(3, m, stage(m), r.layer_out).wait()
        save(1, m, r.norm.at[m], r.h_norm).wait()
        save(2, m, r.o.at[m], r.h_o).wait()
        for copy in kept_forward(m):
            copy.wait()

    r.mixer_grad[...] = jnp.zeros_like(r.mixer_grad)
    r.residual_grad[...] = jnp.zeros_like(r.residual_grad)
    r.rows_grad[...] = jnp.zeros_like(r.rows_grad)

    def fetched(m):
        return [
            pltpu.make_async_copy(r.h_up.at[m], r.by_up.at[0], r.local.at[7, m]),
            pltpu.make_async_copy(r.h_gate.at[m], r.by_gate.at[0], r.local.at[8, m]),
        ]

    def grad_start(m):
        d = slot(m)
        if deep:
            settle_forward(m)
        else:
            for copy in fetched(m):
                copy.start()

        @pl.when(is_last)
        def _():
            copy = pltpu.make_async_copy(r.cotangent.at[m], r.dz.at[d], r.local.at[9, m])
            if not deep:
                copy.start()
            copy.wait()

        @pl.when(sec < sections - 1)
        def _():
            hop(1, m, r.hop_out.at[d], r.hop_in.at[back_hop, m], sec + 1).wait_recv()
            r.dz[d] = wide(r.hop_in[back_hop, m])

        dz = r.dz[d]
        gate, rate = unpack_gates(m)
        leaving = [dot(spread_t(m, k), (gate[k] * dz).astype(bf16)) for k in range(2)]
        send_slots(2, m, leaving[0] + leaving[1])

        col, copies, consts = choice_flags(m)
        normed2 = r.norm2[m]
        dz_norm = jnp.sum(dz * wide(normed2), axis=1, keepdims=True)
        dz_const = [
            jnp.sum(dz * r.const_value[c : c + 1, :], axis=1, keepdims=True) for c in range(2)
        ]
        apart = [dot(spread(m, k), r.back[m]) for k in range(2)]
        dgate = []
        for k in range(2):
            value = jnp.sum(dz * apart[k], axis=1, keepdims=True)
            value = value + copies[k] * dz_norm
            for c in range(2):
                value = value + consts[k][c] * (rate[c] * dz_norm + (1.0 - rate[c]) * dz_const[c])
            dgate.append(value)
        coupled = gate[0] * gate[1] * (dgate[0] - dgate[1])
        lane = iota((owned, LANES), 1)
        dlogits = jnp.where(lane == col[0], coupled, jnp.where(lane == col[1], -coupled, 0.0))
        own = gate[0] * copies[0] + gate[1] * copies[1]
        for c in range(2):
            on = gate[0] * consts[0][c] + gate[1] * consts[1][c]
            own = own + on * rate[c]
            dmix = on * (dz_norm - dz_const[c]) * rate[c] * (1.0 - rate[c])
            dlogits = dlogits + jnp.where(lane == choices + c, dmix, 0.0)
            r.rows_grad[c : c + 1, :] += jnp.sum((on * (1.0 - rate[c])) * dz, axis=0, keepdims=True)
        dlogits_hi, dlogits_lo = halves(dlogits)
        r.mixer_grad[...] += dot_tn(dlogits_hi, normed2) + dot_tn(dlogits_lo, normed2)
        r.residual_grad[...] += dot3(dot, r.prev_t[m], dlogits)
        r.logit_grad[m] = dot3(dot_nt, dlogits, r.residual[...])
        r.dnorm[d] = dot3(dot, dlogits, r.mixer[...]) + own * dz

    def kept_backward(m):
        return [
            save(11, m, r.by_up.at[slot(m)], r.h_up),
            save(12, m, r.by_gate.at[slot(m)], r.h_gate),
        ]

    def experts_backward(m):
        d = slot(m)
        by_up, by_gate, arrived = r.by_up.at[d], r.by_gate.at[d], r.arrived.at[d]
        if not deep:
            for copy in fetched(m):
                copy.wait()

        def compute(half, g):
            block = get(arrived.at[half], g)
            offset = half * slots
            total = 0.0
            for cols in hidden_cols:
                dinside = dot_nt(block, r.down_v[cols, :])
                dvalue = (dinside * wide(get(by_gate, g, offset, cols))).astype(bf16)
                dupper = (dinside * wide(get(by_up, g, offset, cols))).astype(bf16)
                put(by_gate, g, dvalue, offset, cols)
                put(by_up, g, dupper, offset, cols)
                total = total + dot_nt(dvalue, r.gate_v[:, cols]) + dot_nt(dupper, r.up_v[:, cols])
            return total

        through_expert(m, 2, P_GROWS, P_GPART, grad_back(m), r.h_grads, compute)
        for copy in kept_backward(m):
            copy.start()

    def grad_attend(m):
        d = slot(m)
        wait_back(m, 2, grad_back(m))

        both = spread(m, 0) + spread(m, 1)
        dnorm = r.dnorm[d] + dot(both, grad_back(m)[...])
        hidden = r.h[m]
        root = inverse_rms(hidden)
        scaled = dnorm * r.gain2[...]
        pull = root * root * root * jnp.mean(hidden * scaled, axis=-1, keepdims=True)
        dhidden = r.dz[d] + root * scaled - hidden * pull
        r.rows_grad[3:4, :] += jnp.sum(dnorm * hidden * root, axis=0, keepdims=True)
        r.dh[...] = dhidden
        r.da[own_rows, :] = dhidden.astype(bf16)
        pair(P_DA, m, 0, r.da.at[own_rows], r.da.at[own_rows]).start()
        seq_bias(m)
        r.do[own_rows, :] = dot_nt(r.da[own_rows, :], r.w_out[...]).astype(bf16)
        pair(P_DA, m, 0, r.da.at[other_rows], r.da.at[other_rows]).wait_recv()
        save(13, m, r.da, r.h_da).start()
        r.do[other_rows, :] = dot_nt(r.da[other_rows, :], r.w_out[...]).astype(bf16)

        head_lane = iota((1, LANES), 1)

        def head_pair(p, inner):
            lanes = pl.ds(pl.multiple_of(p * LANES, LANES), LANES)
            q2, k2, v2 = r.q[m, :, lanes], r.k[m, :, lanes], r.v[m, :, lanes]
            do2 = r.do[:, lanes]
            for half in range(2):
                keep = wide(((head_lane // HEAD_DIM) == half).astype(i32)).astype(bf16)
                km, vm, qm, dom = k2 * keep, v2 * keep, q2 * keep, do2 * keep
                for c in range(rows // chunk):
                    piece, reach = slice(c * chunk, (c + 1) * chunk), (c + 1) * chunk
                    scores = dot_nt(q2[piece], km[:reach]) + wide(r.bias[piece, :reach])
                    total = jnp.sum(
                        jnp.where(head_lane == 2 * p + half, r.logsum[m, piece, :], 0.0),
                        axis=1,
                        keepdims=True,
                    )
                    probs = jnp.exp(scores - total)
                    dprobs = dot_nt(do2[piece], vm[:reach])
                    meant = jnp.sum(dprobs * probs, axis=-1, keepdims=True)
                    dscores = (probs * (dprobs - meant)).astype(bf16)
                    dq = dot(dscores, km[:reach])
                    dk = dot_tn(dscores, qm[piece])
                    dv = dot_tn(probs.astype(bf16), dom[piece])
                    if half == 0:
                        r.mix[piece, :] = dq
                    else:
                        r.mix[piece, :] += dq
                    if half == 0 and c == 0:
                        r.mix_k[:reach, :] = dk
                        r.mix_v[:reach, :] = dv
                        if reach < rows:
                            r.mix_k[reach:, :] = jnp.zeros((rows - reach, LANES), f32)
                            r.mix_v[reach:, :] = jnp.zeros((rows - reach, LANES), f32)
                    else:
                        r.mix_k[:reach, :] += dk
                        r.mix_v[:reach, :] += dv
            r.dq[:, lanes] = (turned_back(r.mix[...], r.cosine[...], r.sine[...]) * scale).astype(bf16)
            r.dk[:, lanes] = turned_back(r.mix_k[...], r.cosine[...], r.sine[...]).astype(bf16)
            r.dv[:, lanes] = r.mix_v[...].astype(bf16)
            return inner

        lax.fori_loop(0, pairs, head_pair, 0, unroll=deep)
        for copy in kept_heads(m):
            copy.start()

    def kept_heads(m):
        return [save(14, m, r.dq, r.h_dq), save(15, m, r.dk, r.h_dk), save(16, m, r.dv, r.h_dv)]

    def grad_finish(m):
        d = slot(m)

        def dnormed(piece):
            return (
                dot_nt(r.dq[piece, :], r.w_query[...])
                + dot_nt(r.dk[piece, :], r.w_key[...])
                + dot_nt(r.dv[piece, :], r.w_value[...])
            )

        save(13, m, r.da, r.h_da).wait()
        r.half_out[...] = dnormed(other_rows).astype(bf16)
        pair(P_DX, m, 0, r.half_out, r.half_in.at[1, m]).start()
        kept = dnormed(own_rows)
        pair(P_DX, m, 0, r.half_out, r.half_in.at[1, m]).wait_recv()
        dnorm1 = kept + wide(r.half_in[1, m])
        x = r.x[m]
        root1 = inverse_rms(x)
        scaled1 = dnorm1 * r.gain1[...]
        pull1 = root1 * root1 * root1 * jnp.mean(x * scaled1, axis=-1, keepdims=True)
        dx = r.dh[...] + root1 * scaled1 - x * pull1
        stage(m)[...] = dx
        save(4, m, stage(m), r.input_grad).start()

        @pl.when(sec > 0)
        def _():
            r.hop_out[d] = dx.astype(bf16)
            hop(1, m, r.hop_out.at[d], r.hop_in.at[back_hop, m], sec - 1).start()

        r.rows_grad[2:3, :] += jnp.sum(dnorm1 * x * root1, axis=0, keepdims=True)
        pair(P_DA, m, 0, r.da.at[own_rows], r.da.at[own_rows]).wait_send()
        pair(P_DX, m, 0, r.half_out, r.half_in.at[1, m]).wait_send()
        for copy in kept_heads(m):
            copy.wait()

    def settle_backward(m):
        @pl.when(sec > 0)
        def _():
            hop(1, m, r.hop_out.at[slot(m)], r.hop_in.at[back_hop, m], sec - 1).wait_send()

        save(4, m, stage(m), r.input_grad).wait()
        for copy in kept_backward(m):
            copy.wait()

    pl.semaphore_wait(barrier, experts + beside + (2 if cfg.relay else 0))

    if deep:
        def all_of(*phases):
            def step(m, carry):
                for phase in phases:
                    phase(m)
                return carry

            lax.fori_loop(0, micro, step, 0)

        def turn(m):
            combine(m)

            @pl.when(is_last)
            def _():
                grad_start(m)

        def start_rest(m):
            @pl.when(sec < sections - 1)
            def _():
                grad_start(m)

        every = [(k, m) for k in range(4) for m in range(micro)]
        if cfg.relay:

            @pl.when(is_last)
            def _():
                for k, m in relays_for_first():
                    relay(k, m)

        all_of(attend, attend_send)
        all_of(experts_forward)
        all_of(turn)
        if cfg.relay:

            @pl.when(is_first)
            def _():
                for k, m in every:
                    relay(k, m)

        all_of(start_rest)
        all_of(experts_backward)
        all_of(grad_attend, grad_finish)
        if cfg.relay:

            @pl.when(is_last)
            def _():
                for k, m in every:
                    if k >= 2:
                        relay(k, m)
                for k, m in relays_for_first() + [(k, m) for k, m in every if k >= 2]:
                    for place in range(2):
                        relay_copy(k, m, place).wait_send()

            @pl.when(is_first)
            def _():
                for k, m in every:
                    for place in range(2):
                        relay_copy(k, m, place).wait_send()

        for m in range(micro):
            settle_backward(m)
    else:

        def there(m, carry):
            for phase in (attend, attend_send, experts_forward, combine, settle_forward):
                phase(m)
            return carry

        def back_again(m, carry):
            for phase in (grad_start, experts_backward, grad_attend, grad_finish, settle_backward):
                phase(m)
            return carry

        lax.fori_loop(0, micro, there, 0)
        lax.fori_loop(0, micro, back_again, 0)


def run_chain(cfg, ins):
    vmem, anywhere = pl.BlockSpec(memory_space=pltpu.VMEM), pl.BlockSpec(memory_space=pl.ANY)
    smem = pl.BlockSpec(memory_space=pltpu.SMEM)
    far = {"inputs", "cotangent", "gate", "up", "down"}
    micro, owned, rows, width, inner = cfg.micro, cfg.owned, cfg.rows, cfg.width, cfg.inner
    heads_width, slots = cfg.heads * HEAD_DIM, cfg.slots
    shape = jax.ShapeDtypeStruct
    outs = dict(
        logit_grad=shape((micro, owned, LANES), f32),
        mixer_grad=shape((LANES, width), f32),
        residual_grad=shape((LANES, LANES), f32),
        rows_grad=shape((8, width), f32),
    )
    hbm_outs = dict(
        layer_out=shape((micro, owned, width), f32),
        input_grad=shape((micro, owned, width), f32),
        h_rows=shape((micro, 2, slots, width), bf16),
        h_grads=shape((micro, 2, slots, width), bf16),
        h_inside=shape((micro, 2 * slots, inner), bf16),
        h_up=shape((micro, 2 * slots, inner), bf16),
        h_gate=shape((micro, 2 * slots, inner), bf16),
        h_norm=shape((micro, rows, width), bf16),
        h_da=shape((micro, rows, width), bf16),
        h_o=shape((micro, rows, heads_width), bf16),
        h_dq=shape((micro, rows, heads_width), bf16),
        h_dk=shape((micro, rows, heads_width), bf16),
        h_dv=shape((micro, rows, heads_width), bf16),
    )
    dma = pltpu.SemaphoreType.DMA
    depth = cfg.depth
    rem_scratch = {}
    if depth == micro:
        rem_scratch = dict(stage=pltpu.VMEM((micro, owned, width), f32))
    if cfg.rem:
        last = pltpu.VMEM((depth, cfg.experts, cfg.rem, width), f32)
        rem_sem = dma((4, micro, cfg.experts))
        rem_scratch |= dict(
            rem_out=last, rem_in=last, rem_result=last, rem_back=last, rem_send=rem_sem, rem_recv=rem_sem
        )
    if cfg.relay:
        relay_sem = dma((4, micro, 2))
        rem_scratch |= dict(
            relay=pltpu.VMEM((4, micro, 2, cfg.main, width), bf16),
            relay_send=relay_sem,
            relay_recv=relay_sem,
        )
    scratch = dict(
        gate_v=pltpu.VMEM((width, inner), bf16),
        up_v=pltpu.VMEM((width, inner), bf16),
        down_v=pltpu.VMEM((inner, width), bf16),
        x=pltpu.VMEM((micro, owned, width), f32),
        h=pltpu.VMEM((micro, owned, width), f32),
        norm=pltpu.VMEM((micro, rows, width), bf16),
        norm2=pltpu.VMEM((micro, owned, width), bf16),
        q=pltpu.VMEM((micro, rows, heads_width), bf16),
        k=pltpu.VMEM((micro, rows, heads_width), bf16),
        v=pltpu.VMEM((micro, rows, heads_width), bf16),
        o=pltpu.VMEM((micro, rows, heads_width), bf16),
        logsum=pltpu.VMEM((micro, rows, LANES), f32),
        mixer=pltpu.VMEM((LANES, width), f32),
        residual=pltpu.VMEM((LANES, LANES), f32),
        prev_t=pltpu.VMEM((micro, LANES, owned), f32),
        cols=pltpu.VMEM((micro, owned, 16), i32),
        gates=pltpu.VMEM((micro, owned, LANES), f32),
        place_col=pltpu.VMEM((micro, owned, 2), i32),
        place_row=pltpu.VMEM((micro, 2, owned), i32),
        bias=pltpu.VMEM((rows, rows), f32 if depth == micro else bf16),
        arrived=pltpu.VMEM((depth, 2, slots, width), bf16),
        part_in=pltpu.VMEM((slots, width), bf16),
        back=pltpu.VMEM((micro, slots, width), bf16),
        half_in=pltpu.VMEM((2, micro, owned, width), bf16),
        hop_in=pltpu.VMEM((min(2, cfg.sections - 1), micro, owned, width), bf16),
        outgoing=pltpu.VMEM((depth, cfg.experts * cfg.main, width), bf16),
        part_out=pltpu.VMEM((slots, width), bf16),
        result=pltpu.VMEM((depth, slots, width), bf16),
        partial=pltpu.VMEM((max(slots, owned), width), f32),
        half_out=pltpu.VMEM((owned, width), bf16),
        hop_out=pltpu.VMEM((depth, owned, width), bf16),
        inside=pltpu.VMEM((depth, 2 * slots, inner), bf16),
        **rem_scratch,
        by_up=pltpu.VMEM((depth, 2 * slots, inner), bf16),
        by_gate=pltpu.VMEM((depth, 2 * slots, inner), bf16),
        dz=pltpu.VMEM((depth, owned, width), f32),
        dh=pltpu.VMEM((owned, width), f32),
        dnorm=pltpu.VMEM((depth, owned, width), f32),
        da=pltpu.VMEM((rows, width), bf16),
        do=pltpu.VMEM((rows, heads_width), bf16),
        dq=pltpu.VMEM((rows, heads_width), bf16),
        dk=pltpu.VMEM((rows, heads_width), bf16),
        dv=pltpu.VMEM((rows, heads_width), bf16),
        mix=pltpu.VMEM((rows, LANES), f32),
        mix_k=pltpu.VMEM((rows, LANES), f32),
        mix_v=pltpu.VMEM((rows, LANES), f32),
        pair_send=dma((8, micro, 3)),
        pair_recv=dma((8, micro, 3)),
        hop_send=dma((2, micro)),
        hop_recv=dma((2, micro)),
        a2a_send=dma((4, micro, cfg.experts)),
        a2a_recv=dma((4, micro, cfg.experts)),
        local=dma((17, micro)),
        keep=dma((2, micro, 4)),
        fetch=dma((3,)),
    )
    names = [*ins, *outs, *hbm_outs, *scratch]
    flops = 2 * micro * (2 * slots * width * inner * 6 + rows * width * heads_width * 10)
    results = pl.pallas_call(
        functools.partial(chain_kernel, cfg, names),
        out_shape=[*outs.values(), *hbm_outs.values()],
        in_specs=[
            smem if name == "lengths" else anywhere if name in far else vmem for name in ins
        ],
        out_specs=[vmem] * len(outs) + [anywhere] * len(hbm_outs),
        scratch_shapes=[*scratch.values()],
        compiler_params=pltpu.CompilerParams(
            collective_id=0, has_side_effects=True, vmem_limit_bytes=60 * 2**20
        ),
        cost_estimate=pl.CostEstimate(flops=flops, bytes_accessed=50_000_000, transcendentals=0),
    )(*ins.values())
    return types.SimpleNamespace(**dict(zip([*outs, *hbm_outs], results, strict=True)))


def tail_kernel(cfg, names, *refs):
    r = types.SimpleNamespace(**dict(zip(names, refs, strict=True)))
    experts, width, pad = cfg.experts, cfg.width, cfg.small_pad
    side = width // 2
    outer = experts // 2
    me, core = lax.axis_index("expert"), lax.axis_index("tensor")
    mine_out, mine_in = me // 2, lax.rem(me, 2)
    beside = me + 1 - 2 * mine_in
    pieces = len(cfg.piece_rows)
    starts = [sum(cfg.piece_rows[:c]) * experts for c in range(pieces)]

    def peer_of(k):
        place = lax.rem(mine_out + k, outer)
        return place, place * 2 + mine_in

    barrier = pltpu.get_barrier_semaphore()
    pl.semaphore_signal(barrier, inc=1, device_id={"tensor": 1 - core}, device_id_type=MESH)
    pl.semaphore_signal(barrier, inc=1, device_id={"expert": beside}, device_id_type=MESH)

    def greet(k, carry):
        pl.semaphore_signal(barrier, inc=1, device_id={"expert": peer_of(k)[1]}, device_id_type=MESH)
        return carry

    lax.fori_loop(1, outer, greet, 0)

    loads = [
        pltpu.make_async_copy(source, target, r.fetch.at[k])
        for k, (source, target) in enumerate(
            (
                (r.h_rows, r.rows_v),
                (r.h_gate, r.gate_v),
                (r.h_up, r.up_v),
                (r.h_grads, r.grads_v),
                (r.h_inside, r.gate_v),
            )
        )
    ]
    for copy in loads[:4]:
        copy.start()

    r.pack[...] = jnp.zeros_like(r.pack)
    r.pack[:pad, :] = r.mixer_grad[:pad, :side]
    r.pack[pad : 2 * pad, :] = r.mixer_grad[:pad, side:]
    r.pack[2 * pad : 2 * pad + 8, :] = r.rows_grad[:, :side]
    r.pack[2 * pad + 8 : 2 * pad + 16, :] = r.rows_grad[:, side:]
    r.pack[2 * pad + 16 : 3 * pad + 16, :LANES] = r.residual_grad[:pad, :]
    r.pack_out[...] = r.pack[...].astype(bf16)
    pl.semaphore_wait(barrier, outer + 1)
    pack_copy = pltpu.make_async_remote_copy(
        src_ref=r.pack_out,
        dst_ref=r.pack_in,
        send_sem=r.pack_sem.at[0],
        recv_sem=r.pack_sem.at[1],
        device_id={"tensor": 1 - core},
        device_id_type=MESH,
    )
    pack_copy.start()

    def span(start, index, size):
        return pl.ds(pl.multiple_of(start + index * size, 16), size)

    def over_x(stage, c, source, target, from_rows, to_rows):
        return pltpu.make_async_remote_copy(
            src_ref=source.at[from_rows],
            dst_ref=target.at[to_rows],
            send_sem=r.x_send.at[stage, c],
            recv_sem=r.x_recv.at[stage, c],
            device_id={"expert": beside},
            device_id_type=MESH,
        )

    def over_z(stage, c, place, landed, peer, source, target):
        return pltpu.make_async_remote_copy(
            src_ref=source,
            dst_ref=target,
            send_sem=r.z_send.at[stage, c, place],
            recv_sem=r.z_recv.at[stage, c, landed],
            device_id={"expert": peer},
            device_id_type=MESH,
        )

    def half_of(c, which):
        return span(starts[c], which, outer * cfg.piece_rows[c])

    def landing(c):
        return pl.ds(starts[c] // 2, outer * cfg.piece_rows[c])

    def scatter_x(c):
        return over_x(0, c, r.sent, r.x_in, half_of(c, 1 - mine_in), landing(c))

    def gather_x(c, which):
        return over_x(1, c, r.summed, r.summed, half_of(c, which), half_of(c, which))

    def scatter_z(c, place, landed, peer):
        size = cfg.piece_rows[c]
        return over_z(
            0,
            c,
            place,
            landed,
            peer,
            r.z_out.at[span(starts[c] // 2, place, size)],
            r.z_in.at[landed, pl.ds(starts[c] // experts, size)],
        )

    def final(c, place):
        return span(starts[c], mine_in * outer + place, cfg.piece_rows[c])

    def gather_z(c, place, landed, peer):
        rows = final(c, landed)
        return over_z(1, c, place, landed, peer, r.summed.at[rows], r.summed.at[rows])

    def weight_grad(left, right):
        return dot_tn(left.reshape(-1, left.shape[-1]), right.reshape(-1, right.shape[-1]))

    products = ((r.h_da, r.h_o), (r.h_norm, r.h_dv), (r.h_norm, r.h_dk), (r.h_norm, r.h_dq))
    splits = cfg.splits

    def launch(c):
        rows = pl.ds(starts[c], experts * cfg.piece_rows[c])
        if c == pieces - 1:
            pack_copy.wait()
            r.sent[rows, :] = (r.pack[...] + wide(r.pack_in[...])).astype(bf16)
        elif c % splits == 0:
            left, right = products[c // splits]
            value = weight_grad(left[...], right[...])
            covered = splits * experts * cfg.piece_rows[c]
            if value.shape[0] != covered:
                r.sent[pl.ds(starts[c], covered), :] = jnp.zeros((covered, side), bf16)
            r.sent[pl.ds(starts[c], value.shape[0]), :] = value.astype(bf16)
        scatter_x(c).start()

    rows_all = cfg.micro * 2 * cfg.slots
    tile = 256
    steps = []
    for left, right, target in (
        (r.rows_v, r.gate_v, r.gate_grad),
        (r.rows_v, r.up_v, r.up_grad),
        (r.gate_v, r.grads_v, r.down_grad),
    ):
        for t in range(left.shape[-1] // tile):
            needs = ((0, 1), (0, 2), (3, 4))[len(steps) // (width // tile) if target is not r.down_grad else 2]
            steps.append((left, right, target, t, needs))

    loaded = set()
    flying = [None, None]

    def expert_step(index):
        left, right, target, t, needs = steps[index]
        if index == width // tile:
            loads[4].start()
        for k in needs:
            if k not in loaded:
                loads[k].wait()
                loaded.add(k)
        slot = index % 2
        if flying[slot] is not None:
            flying[slot].wait()
        wide_out = right.shape[-1]
        a = left[..., t * tile : (t + 1) * tile].reshape(rows_all, tile)
        r.stage[slot, :, :wide_out] = dot_tn(a, right[...].reshape(rows_all, wide_out)).astype(bf16)
        copy = pltpu.make_async_copy(
            r.stage.at[slot, :, pl.ds(0, wide_out)],
            target.at[pl.ds(t * tile, tile)],
            r.step_sem.at[index],
        )
        copy.start()
        flying[slot] = copy

    def reduce_x(c):
        scatter_x(c).wait_recv()
        rows = landing(c)
        r.z_out[rows, :] = (wide(r.sent[half_of(c, mine_in), :]) + wide(r.x_in[rows, :])).astype(bf16)

        def out_z(k, carry):
            place, peer = peer_of(k)
            scatter_z(c, place, mine_out, peer).start()
            return carry

        lax.fori_loop(1, outer, out_z, 0)

    def reduce_z(c):
        size = cfg.piece_rows[c]

        def add_z(k, total):
            place, peer = peer_of(k)
            scatter_z(c, place, place, peer).wait_recv()
            return total + wide(r.z_in[place, pl.ds(starts[c] // experts, size), :])

        total = lax.fori_loop(1, outer, add_z, wide(r.z_out[span(starts[c] // 2, mine_out, size), :]))
        r.summed[final(c, mine_out), :] = total.astype(bf16)

        def back_z(k, carry):
            place, peer = peer_of(k)
            gather_z(c, place, mine_out, peer).start()
            return carry

        lax.fori_loop(1, outer, back_z, 0)

    def spread_x(c):
        def wait_z(k, carry):
            place, peer = peer_of(k)
            gather_z(c, place, place, peer).wait_recv()
            return carry

        lax.fori_loop(1, outer, wait_z, 0)
        gather_x(c, mine_in).start()

    done = 0
    launch(0)
    launch(1)
    for k in range(pieces + 4):
        if k < pieces:
            reduce_x(k)
        if k + 2 < pieces:
            launch(k + 2)
        if 0 <= k - 2 < pieces:
            reduce_z(k - 2)
        if 0 <= k - 4 < pieces:
            spread_x(k - 4)
        while done < min(len(steps), len(steps) * (k + 1) // pieces):
            expert_step(done)
            done += 1
    for c in range(pieces):
        gather_x(c, 1 - mine_in).wait_recv()
    for c in range(pieces):
        scatter_x(c).wait_send()
        gather_x(c, mine_in).wait_send()

        def sent_z(k, carry, c=c):
            place, peer = peer_of(k)
            scatter_z(c, place, mine_out, peer).wait_send()
            gather_z(c, place, mine_out, peer).wait_send()
            return carry

        lax.fori_loop(1, outer, sent_z, 0)
    for copy in flying:
        copy.wait()


def run_tail(cfg, got):
    vmem, anywhere = pl.BlockSpec(memory_space=pltpu.VMEM), pl.BlockSpec(memory_space=pl.ANY)
    micro, width, inner, slots, experts = cfg.micro, cfg.width, cfg.inner, cfg.slots, cfg.experts
    side, outer = width // 2, experts // 2
    cfg.splits = 2 if width % (32 * experts) == 0 else 1
    piece = -(-width // (16 * cfg.splits * experts)) * 16
    small = -(-(3 * cfg.small_pad + 16) // (16 * experts)) * 16
    cfg.piece_rows = [piece] * (4 * cfg.splits) + [small]
    total = sum(cfg.piece_rows) * experts
    near = dict(
        h_norm=got.h_norm,
        h_da=got.h_da,
        h_o=got.h_o,
        h_dq=got.h_dq,
        h_dk=got.h_dk,
        h_dv=got.h_dv,
        mixer_grad=got.mixer_grad,
        residual_grad=got.residual_grad,
        rows_grad=got.rows_grad,
    )
    far = dict(
        h_rows=got.h_rows,
        h_grads=got.h_grads,
        h_inside=got.h_inside,
        h_up=got.h_up,
        h_gate=got.h_gate,
    )
    shape, dma = jax.ShapeDtypeStruct, pltpu.SemaphoreType.DMA
    outs = dict(
        summed=shape((total, side), bf16),
        gate_grad=shape((width, inner), bf16),
        up_grad=shape((width, inner), bf16),
        down_grad=shape((inner, width), bf16),
    )
    scratch = dict(
        rows_v=pltpu.VMEM((micro, 2, slots, width), bf16),
        grads_v=pltpu.VMEM((micro, 2, slots, width), bf16),
        up_v=pltpu.VMEM((micro, 2 * slots, inner), bf16),
        gate_v=pltpu.VMEM((micro, 2 * slots, inner), bf16),
        sent=pltpu.VMEM((total, side), bf16),
        x_in=pltpu.VMEM((total // 2, side), bf16),
        z_out=pltpu.VMEM((total // 2, side), bf16),
        z_in=pltpu.VMEM((outer, total // experts, side), bf16),
        pack=pltpu.VMEM((small * experts, side), f32),
        pack_out=pltpu.VMEM((small * experts, side), bf16),
        pack_in=pltpu.VMEM((small * experts, side), bf16),
        stage=pltpu.VMEM((2, 256, max(inner, width)), bf16),
        fetch=dma((5,)),
        step_sem=dma(((2 * width + inner) // 256,)),
        pack_sem=dma((2,)),
        x_send=dma((2, len(cfg.piece_rows))),
        x_recv=dma((2, len(cfg.piece_rows))),
        z_send=dma((2, len(cfg.piece_rows), outer)),
        z_recv=dma((2, len(cfg.piece_rows), outer)),
    )
    names = [*near, *far, *outs, *scratch]
    results = pl.pallas_call(
        functools.partial(tail_kernel, cfg, names),
        out_shape=[*outs.values()],
        in_specs=[vmem] * len(near) + [anywhere] * len(far),
        out_specs=[vmem] + [anywhere] * 3,
        scratch_shapes=[*scratch.values()],
        compiler_params=pltpu.CompilerParams(
            collective_id=1, has_side_effects=True, vmem_limit_bytes=60 * 2**20
        ),
        cost_estimate=pl.CostEstimate(
            flops=12 * micro * slots * width * inner, bytes_accessed=40_000_000, transcendentals=0
        ),
    )(*near.values(), *far.values())
    return types.SimpleNamespace(
        **dict(zip(outs, results, strict=True)), pad_rows=piece * cfg.splits * experts
    )


def rope_tables(rows):
    half_width = HEAD_DIM // 2
    frequency = 10000.0 ** (-2.0 * np.arange(half_width, dtype=np.float64) / HEAD_DIM)
    angles = np.arange(rows, dtype=np.float64)[:, None] * frequency[None, :]
    angles = np.tile(angles, (1, LANES // half_width))
    return np.cos(angles).astype(np.float32), np.sin(angles).astype(np.float32)


def local(
    inputs,
    cotangent,
    prev_logits,
    lengths,
    routes,
    slot_order,
    norm_gain1,
    w_query,
    w_key,
    w_value,
    w_out,
    norm_gain2,
    router,
    router_residual,
    const_gate,
    const_value,
    expert_gate,
    expert_up,
    expert_down,
):
    micro, owned, width = inputs.shape
    tensors, peers = lax.axis_size("tensor"), lax.axis_size("expert")
    choices = router.shape[2]
    experts = choices - 4
    assert experts == peers and tensors == 2
    cap = 9 * 2 * owned // (8 * choices) + 1
    main, rem = cap // 16 * 16, cap % 16
    if rem > 2 or not main:
        main, rem = main + (16 if rem else 0), 0
    rem_rows = -(-rem * peers // 16) * 16
    cfg = types.SimpleNamespace(
        micro=micro,
        owned=owned,
        width=width,
        rows=owned * tensors,
        inner=expert_gate.shape[3],
        heads=w_query.shape[2] // HEAD_DIM,
        experts=experts,
        choices=choices,
        cap=cap,
        main=main,
        rem=rem,
        rem_rows=rem_rows,
        half_rows=peers // 2 * main,
        slots=peers * main + rem_rows,
        depth=micro if peers * main <= 512 else 1,
        sections=lax.axis_size("section"),
        seqs=lengths.shape[2] - 1,
        small_pad=-(-(choices + 2) // 16) * 16,
    )
    cfg.chunk = cfg.rows if cfg.depth == micro else owned
    cfg.relay = cfg.depth == micro and cfg.sections == 2 and peers == 8
    cosine, sine = rope_tables(cfg.rows)
    ins = dict(
        lengths=lengths[:, 0],
        inputs=inputs,
        cotangent=cotangent,
        prev_in=jnp.transpose(prev_logits[0], (2, 0, 1)),
        route_row=jnp.swapaxes(routes[0], 1, 2),
        order_row=slot_order[0],
        gain1=norm_gain1,
        gain2=norm_gain2,
        w_query=w_query[0],
        w_key=w_key[0],
        w_value=w_value[0],
        w_out=w_out[0],
        router_in=router[0].T,
        const_gate=const_gate[0],
        residual_in=router_residual[0],
        const_value=const_value[0],
        cosine=jnp.asarray(cosine),
        sine=jnp.asarray(sine),
        gate=expert_gate[0, 0],
        up=expert_up[0, 0],
        down=expert_down[0, 0],
    )
    got = run_chain(cfg, ins)

    tail = run_tail(cfg, got)
    out_grad, value_grad, key_grad, query_grad = (
        wide(tail.summed[c * tail.pad_rows : c * tail.pad_rows + width]) for c in range(4)
    )
    small = wide(tail.summed[4 * tail.pad_rows :])
    pad = cfg.small_pad
    mixer_grad = jnp.concatenate([small[:pad], small[pad : 2 * pad]], axis=1)
    rows_grad = jnp.concatenate([small[2 * pad : 2 * pad + 8], small[2 * pad + 8 : 2 * pad + 16]], axis=1)
    residual_grad = small[2 * pad + 16 : 3 * pad + 16, :LANES]
    return (
        got.layer_out[None],
        got.input_grad[None],
        got.logit_grad[None, :, :, :choices],
        rows_grad[None, 2],
        query_grad[None],
        key_grad[None],
        value_grad[None],
        out_grad.T[None],
        rows_grad[None, 3],
        mixer_grad[:choices].T[None],
        residual_grad[None, :choices, :choices],
        mixer_grad[None, choices : choices + 2],
        rows_grad[None, :2],
        wide(tail.gate_grad)[None, None],
        wide(tail.up_grad)[None, None],
        wide(tail.down_grad)[None, None],
    )


def solution(mesh):
    tokens = ("expert", "tensor")
    in_specs = (
        P(None, tokens, None),
        P(None, tokens, None),
        P("section", None, tokens, None),
        P(None, "expert", None),
        P("section", None, tokens, None),
        P("section", None, tokens, None),
        P("section", None),
        P("section", None, "tensor"),
        P("section", None, "tensor"),
        P("section", None, "tensor"),
        P("section", "tensor", None),
        P("section", None),
        P("section", None, None),
        P("section", None, None),
        P("section", None, None),
        P("section", None, None),
        P("section", "expert", None, "tensor"),
        P("section", "expert", None, "tensor"),
        P("section", "expert", "tensor", None),
    )
    out_specs = (
        P("section", None, tokens, None),
        P("section", None, tokens, None),
        P("section", None, tokens, None),
        P("section", None),
        P("section", None, "tensor"),
        P("section", None, "tensor"),
        P("section", None, "tensor"),
        P("section", "tensor", None),
        P("section", None),
        P("section", None, None),
        P("section", None, None),
        P("section", None, None),
        P("section", None, None),
        P("section", "expert", None, "tensor"),
        P("section", "expert", None, "tensor"),
        P("section", "expert", "tensor", None),
    )
    return jax.shard_map(local, mesh=mesh, in_specs=in_specs, out_specs=out_specs, check_vma=False)
```
